32 devices in a mesh: seq: 4 (over y, x), mp: 8 (over z, core).
Axes of the slice: x: 2, y: 2, z: 4, core: 2. Of those that a mesh axis runs over, the one named last changes fastest.
Arguments:
- queries: bfloat16 [4096, 1024], P(('seq', 'mp')), may hold values from -6 to 6
- keys: bfloat16 [4096, 1024], P(('seq', 'mp')), may hold values from -6 to 6
- values: bfloat16 [4096, 1024], P(('seq', 'mp')), may hold values from -6 to 6
- out_weight: bfloat16 [1024, 1024], P('mp'), may hold values from -0.1875 to 0.1875
- upstream: bfloat16 [4096, 1024], P(('seq', 'mp')), may hold values from -6 to 6
- adjacency: int32 [32, 4], P(('seq', 'mp')), may hold values 0 or 1
- counts: int32 [32], P(('seq', 'mp')), may hold values from 32 to 128, as said below
Outputs:
- mixed_out: bfloat16 [4096, 1024], P(('seq', 'mp'))
- grad_queries: bfloat16 [4096, 1024], P(('seq', 'mp'))
- grad_keys: bfloat16 [4096, 1024], P(('seq', 'mp'))
- grad_values: bfloat16 [4096, 1024], P(('seq', 'mp'))
The draws below stay inside these ranges and needn't reach their ends.
Inputs may be any that keep to these rules, and one draw needn't show every extreme that they name: `counts`: each block has between 32 and 128 valid slots; some block has exactly 128 and some exactly 32.
All inputs are finite; a program needn't handle non-finite values. No bound on the sum of `adjacency` on one device may be relied on, other than what follows from the above.
Results may differ from the reference program's by a relative error of at most 0.023.
Values may be sent and summed in bfloat16 or wider, within the bound.
No kernel may reach another device: no remote copies, remote signals or barrier semaphores. Data moves between devices by JAX's collectives and lax.ppermute only.
A program may use at most 64 MiB of HBM per device.

```python
import jax
import jax.numpy as jnp
from jax import lax

D = 1024
HEADS = 16
HEAD_DIM = 64
TOK_DEV = 128
CYCLE = 4
COLUMNS = 8
BLOCKS = 32
TOKENS = 4096


def drawn_pair(key):
    query_key = jax.random.fold_in(key, 11)
    key_key = jax.random.fold_in(key, 12)
    out_queries = jnp.clip(jax.random.normal(query_key, (TOKENS, D), jnp.float32), -6.0, 6.0)
    out_keys = jnp.clip(jax.random.normal(key_key, (TOKENS, D), jnp.float32), -6.0, 6.0)
    return (out_queries, out_keys)


def draw_queries(key, part):
    return drawn_pair(key)[0].astype(jnp.bfloat16)


def draw_keys(key, part):
    return drawn_pair(key)[1].astype(jnp.bfloat16)


def draw_counts(key, part):
    count_key = jax.random.fold_in(key, 21)
    full_key = jax.random.fold_in(key, 22)
    step_key = jax.random.fold_in(key, 23)
    drawn = jax.random.randint(count_key, (BLOCKS,), TOK_DEV // 4, TOK_DEV + 1)
    full_index = jax.random.randint(full_key, (), 0, BLOCKS)
    least_index = (full_index + 1 + jax.random.randint(step_key, (), 0, BLOCKS - 1)) % BLOCKS
    block_ids = jnp.arange(BLOCKS, dtype=jnp.int32)
    drawn = jnp.where(block_ids == full_index, TOK_DEV, drawn)
    drawn = jnp.where(block_ids == least_index, TOK_DEV // 4, drawn)
    return drawn.astype(jnp.int32)


def plant(values, own_key, smallest, largest):
    place = [jax.random.randint(jax.random.fold_in(own_key, axis), (), 0, length) for axis, length in enumerate(values.shape)]
    widest = values.shape.index(max(values.shape))
    next_to = place[:widest] + [(place[widest] + 1) % values.shape[widest]] + place[widest + 1:]
    return values.at[tuple(place)].set(smallest).at[tuple(next_to)].set(largest)


def block_scale(stream_key, shape, split, least, largest):
    gain = 1.0
    for axis_at, blocks in split:
        heights = jax.random.uniform(jax.random.fold_in(jax.random.fold_in(stream_key, 6), axis_at), (blocks,), jnp.float32, least / len(split), largest / len(split))
        gain = gain * jnp.repeat(jnp.exp(heights), shape[axis_at] // blocks).reshape((-1,) + (1,) * (len(shape) - 1 - axis_at))
    return gain


def gaussian(key, shape, spread, reach, pieces=(), kind=jnp.bfloat16):
    loudness = block_scale(key, shape, pieces, -0.22, 0.18) if pieces else 1.0
    values = jax.random.normal(key, shape, jnp.float32) * spread * loudness
    return jnp.minimum(jnp.maximum(values, -reach), reach).astype(kind)


def setup_inputs(seed: int = 0) -> dict:
    key_of = jax.random.split(jax.random.key(seed), 8)
    queries = draw_queries(jax.random.fold_in(key_of[7], 71), 0)
    keys = draw_keys(jax.random.fold_in(key_of[7], 71), 0)
    values = gaussian(key_of[2], (TOKENS, D), 1.0, 6.0, ((0, 32),))
    out_weight = gaussian(key_of[3], (D, D), D ** -0.5, 0.1875, ((0, 8),))
    upstream = gaussian(key_of[4], (TOKENS, D), 1.0, 6.0, ((0, 32),))
    adjacency = plant((jax.random.randint(key_of[5], (BLOCKS, 4), 0, 3) < 1).astype(jnp.int32), jax.random.fold_in(key_of[5], 1), 0, 1)
    counts = draw_counts(jax.random.fold_in(key_of[7], 71), 0)
    return {"queries": queries, "keys": keys, "values": values, "out_weight": out_weight, "upstream": upstream, "adjacency": adjacency, "counts": counts}


score_scale = 0.125
cycle_offsets = (1, -1, 2, -2)


def to_heads(matrix):
    return matrix.reshape(matrix.shape[:-1] + (HEADS, HEAD_DIM)).astype(jnp.float32)


def rounded(values_in):
    return lax.optimization_barrier(values_in.astype(jnp.bfloat16)).astype(jnp.float32)


def reference(queries, keys, values, out_weight, upstream, adjacency, counts):
    query_blocks = queries.reshape(BLOCKS, TOK_DEV, D)
    key_blocks = keys.reshape(BLOCKS, TOK_DEV, D)
    value_blocks = values.reshape(BLOCKS, TOK_DEV, D)
    offsets = jnp.array(cycle_offsets, dtype=jnp.int32)
    positions = jnp.arange(TOK_DEV, dtype=jnp.int32)

    def key_list(block_index):
        cycle_pos = block_index // COLUMNS
        lane_index = block_index % COLUMNS
        others = ((cycle_pos - offsets) % CYCLE) * COLUMNS + lane_index
        entries = jnp.concatenate([block_index[None], others]).astype(jnp.int32)
        present = jnp.concatenate([jnp.ones((1,), jnp.int32), adjacency[block_index]]) > 0
        return entries, present

    def list_scores(query_heads, key_set, count_set, present):
        scores = jnp.einsum("qhd,jkhd->jhqk", query_heads, to_heads(key_set)) * score_scale
        valid = (positions[None, :] < count_set[:, None]) & present[:, None]
        return jnp.where(valid[:, None, None, :], scores, -jnp.inf)

    def forward_block(block_index):
        entries, present = key_list(block_index)
        query_heads = to_heads(query_blocks[block_index])
        scores = list_scores(query_heads, key_blocks[entries], counts[entries], present)
        maxima = jnp.max(scores, axis=(0, 3))
        expo = jnp.exp(scores - maxima[None, :, :, None])
        totals = jnp.sum(expo, axis=(0, 3))
        probs = rounded(expo / totals[None, :, :, None])
        attended = jnp.einsum("jhqk,jkhd->qhd", probs, to_heads(value_blocks[entries]))
        return attended.reshape(TOK_DEV, D).astype(jnp.bfloat16), maxima, totals

    block_ids = jnp.arange(BLOCKS, dtype=jnp.int32)
    attended_blocks, maxima_all, totals_all = lax.map(forward_block, block_ids)
    attended = attended_blocks.reshape(TOKENS, D)
    mixed_out = jnp.dot(attended, out_weight, preferred_element_type=jnp.float32).astype(jnp.bfloat16)
    grad_attended = jnp.dot(upstream, out_weight.T, preferred_element_type=jnp.float32).astype(jnp.bfloat16)
    grad_blocks = grad_attended.reshape(BLOCKS, TOK_DEV, D)
    delta_all = jnp.einsum("bqhd,bqhd->bhq", to_heads(grad_blocks), to_heads(attended_blocks))

    def query_block_grads(block_index):
        entries, present = key_list(block_index)
        query_heads = to_heads(query_blocks[block_index])
        grad_heads = to_heads(grad_blocks[block_index])
        scores = list_scores(query_heads, key_blocks[entries], counts[entries], present)
        probs = jnp.exp(scores - maxima_all[block_index][None, :, :, None]) / totals_all[block_index][None, :, :, None]
        grad_probs = jnp.einsum("qhd,jkhd->jhqk", grad_heads, to_heads(value_blocks[entries]))
        grad_scores = rounded(probs * (grad_probs - delta_all[block_index][None, :, :, None]))
        query_term = score_scale * jnp.einsum("jhqk,jkhd->qhd", grad_scores, to_heads(key_blocks[entries]))
        return query_term.reshape(TOK_DEV, D).astype(jnp.bfloat16)

    def key_block_grads(block_index):
        cycle_pos = block_index // COLUMNS
        lane_index = block_index % COLUMNS
        sources = ((cycle_pos + offsets) % CYCLE) * COLUMNS + lane_index
        entries = jnp.concatenate([block_index[None], sources]).astype(jnp.int32)
        flags = adjacency[sources, jnp.arange(4, dtype=jnp.int32)] > 0
        present = jnp.concatenate([jnp.ones((1,), dtype=bool), flags])
        query_heads = to_heads(query_blocks[entries])
        grad_heads = to_heads(grad_blocks[entries])
        key_heads = to_heads(key_blocks[block_index])
        value_heads = to_heads(value_blocks[block_index])
        scores = jnp.einsum("jqhd,khd->jhqk", query_heads, key_heads) * score_scale
        valid = (positions < counts[block_index])[None, :] & present[:, None]
        scores = jnp.where(valid[:, None, None, :], scores, -jnp.inf)
        probs = jnp.exp(scores - maxima_all[entries][..., None]) / totals_all[entries][..., None]
        grad_probs = jnp.einsum("jqhd,khd->jhqk", grad_heads, value_heads)
        grad_scores = rounded(probs * (grad_probs - delta_all[entries][..., None]))
        key_terms = score_scale * jnp.einsum("jhqk,jqhd->jkhd", grad_scores, query_heads)
        value_terms = jnp.einsum("jhqk,jqhd->jkhd", rounded(probs), grad_heads)

        def settle(terms):
            terms = terms.reshape(5, TOK_DEV, D)
            return (terms[0] + jnp.sum(rounded(terms[1:]), axis=0)).astype(jnp.bfloat16)

        return settle(key_terms), settle(value_terms)

    grad_queries = lax.map(query_block_grads, block_ids).reshape(TOKENS, D)
    grad_keys, grad_values = lax.map(key_block_grads, block_ids)
    return mixed_out, grad_queries, grad_keys.reshape(TOKENS, D), grad_values.reshape(TOKENS, D)
```

```python
import functools

import jax
import jax.numpy as jnp
from jax import lax
from jax.experimental import pallas as pl
from jax.experimental.pallas import tpu as pltpu
from jax.sharding import PartitionSpec as P

HEADS = 16
HEAD_DIM = 64
META = 32

score_scale = 0.125
log2_scale = 0.125 * 1.4426950408889634
cycle_offsets = (1, -1, 2, -2)
absent = -1e30
bf16 = jnp.bfloat16
f32 = jnp.float32


def dot_nn(a, b):
    return lax.dot_general(a, b, (((1,), (0,)), ((), ())), preferred_element_type=f32)


def dot_nt(a, b):
    return lax.dot_general(a, b, (((1,), (1,)), ((), ())), preferred_element_type=f32)


def vmem():
    return pl.BlockSpec(memory_space=pltpu.VMEM)


def params(mib):
    return pltpu.CompilerParams(vmem_limit_bytes=mib * 1024 * 1024)


def exchange(value, axis, distance):
    count = lax.axis_size(axis)
    return lax.ppermute(value, axis, [(i, i ^ distance) for i in range(count)])


def pack_kernel(cycle, q_ref, k_ref, v_ref, adj_ref, cnt_ref, *outs):
    rows = q_ref.shape[0]
    width = q_ref.shape[1] // cycle
    own = lax.axis_index("seq")
    lines = lax.broadcasted_iota(jnp.int32, (META, width), 0)
    meta = jnp.where(lines == 0, 1, 0)
    for column, offset in enumerate(cycle_offsets):
        named = lax.rem(own - offset + 2 * cycle, cycle)
        meta = meta + jnp.where(
            (lines == lax.bitwise_xor(own, named)) & (adj_ref[0, column] > 0), 1, 0
        )
    meta = jnp.where(lines == META - 1, cnt_ref[0], meta).astype(f32).astype(bf16)
    for place in range(cycle):
        target = lax.bitwise_xor(own, place)
        if width % 128 == 0:
            columns = pl.ds(pl.multiple_of(target * width, width), width)
            for at, ref in enumerate((q_ref, k_ref, v_ref)):
                outs[place][at * rows:(at + 1) * rows, :] = ref[:, columns]
        else:
            for other in range(cycle):
                @pl.when(target == other)
                def _():
                    for at, ref in enumerate((q_ref, k_ref, v_ref)):
                        outs[place][at * rows:(at + 1) * rows, :] = ref[
                            :, other * width:(other + 1) * width
                        ]
        outs[place][3 * rows:, :] = meta


def pack(cycle, queries, keys, values, adjacency, counts):
    rows, model = queries.shape
    width = model // cycle
    smem = pl.BlockSpec(memory_space=pltpu.SMEM)
    return pl.pallas_call(
        functools.partial(pack_kernel, cycle),
        out_shape=[jax.ShapeDtypeStruct((3 * rows + META, width), bf16)] * cycle,
        in_specs=[vmem()] * 3 + [smem] * 2,
        out_specs=[vmem()] * cycle,
        compiler_params=params(32),
        name="pack",
    )(queries, keys, values, adjacency, counts)


def fill(cycle, rows, chunks, bias, *parts):
    for place in range(cycle):
        for at, part in parts:
            part[place * rows:(place + 1) * rows, :] = chunks[place][at * rows:(at + 1) * rows, :]
    lines = lax.broadcasted_iota(jnp.int32, (rows, rows), 0).astype(f32)
    lists = [chunks[place][3 * rows:, :].astype(f32) for place in range(cycle)]
    for key_place in range(cycle):
        count = lists[key_place][META - 1:, :1]
        valid = lines < count
        for query_place in range(cycle):
            way = key_place ^ query_place
            times = lists[query_place][way:way + 1, :1]
            term = jnp.where(times > 0, jnp.log2(jnp.maximum(times, 1.0)), absent)
            bias[
                key_place * rows:(key_place + 1) * rows,
                query_place * rows:(query_place + 1) * rows,
            ] = jnp.where(valid, term, absent)


def head_tile(width):
    return min(128, width)


def only_head(tile, which):
    lanes = lax.broadcasted_iota(jnp.int32, tile.shape, 1)
    inside = (lanes >= which * HEAD_DIM) & (lanes < (which + 1) * HEAD_DIM)
    return jnp.where(inside, tile, jnp.zeros_like(tile))


def forward_kernel(cycle, query_tile, *refs):
    chunks = refs[:cycle]
    outs = refs[cycle:2 * cycle]
    att_t, lse, q_all, k_all, v_all, bias = refs[2 * cycle:]
    width = q_all.shape[1]
    tokens = q_all.shape[0]
    rows = tokens // cycle
    fill(cycle, rows, chunks, bias, (0, q_all), (1, k_all), (2, v_all))
    tile = head_tile(width)
    v_t = v_all[...].astype(f32).T.astype(bf16)
    for start in range(0, tokens, query_tile):
        span = slice(start, start + query_tile)
        for head in range(width // HEAD_DIM):
            at = head * HEAD_DIM // tile * tile
            which = (head * HEAD_DIM - at) // HEAD_DIM
            scores = dot_nt(
                k_all[:, at:at + tile], only_head(q_all[span, at:at + tile], which)
            )
            scores = scores * log2_scale + bias[:, span]
            largest = jnp.max(scores, axis=0, keepdims=True)
            expo = jnp.exp2(scores - largest)
            total = jnp.sum(expo, axis=0, keepdims=True)
            probs = (expo * (1.0 / total)).astype(bf16)
            lse[head:head + 1, span] = largest + jnp.log2(total)
            att_t[head * HEAD_DIM:(head + 1) * HEAD_DIM, span] = dot_nn(
                v_t[head * HEAD_DIM:(head + 1) * HEAD_DIM, :], probs
            )
    attended = att_t[...].T.astype(bf16)
    for place in range(cycle):
        outs[place][...] = attended[place * rows:(place + 1) * rows, :]


def forward(cycle, chunks):
    width = chunks[0].shape[1]
    rows = (chunks[0].shape[0] - META) // 3
    tokens = rows * cycle
    outs = pl.pallas_call(
        functools.partial(forward_kernel, cycle, min(tokens, 512)),
        out_shape=[jax.ShapeDtypeStruct((rows, width), bf16)] * cycle
        + [
            jax.ShapeDtypeStruct((width, tokens), f32),
            jax.ShapeDtypeStruct((8, tokens), f32),
        ],
        in_specs=[vmem()] * cycle,
        out_specs=[vmem()] * (cycle + 2),
        scratch_shapes=[pltpu.VMEM((tokens, width), bf16)] * 3
        + [pltpu.VMEM((tokens, tokens), f32)],
        compiler_params=params(60),
        name="forward",
    )(*chunks)
    return outs[:cycle], outs[cycle], outs[cycle + 1]


def backward_kernel(cycle, query_tile, *refs):
    chunks = refs[:cycle]
    grads = refs[cycle:2 * cycle]
    att_t, lse = refs[2 * cycle:2 * cycle + 2]
    outs = refs[2 * cycle + 2:3 * cycle + 2]
    q_all, k_all, v_all, g_all, dq_t, dk, dv, bias = refs[3 * cycle + 2:]
    width = q_all.shape[1]
    tokens = q_all.shape[0]
    rows = tokens // cycle
    fill(cycle, rows, chunks, bias, (0, q_all), (1, k_all), (2, v_all))
    for place in range(cycle):
        g_all[place * rows:(place + 1) * rows, :] = grads[place][...]
    tile = head_tile(width)
    k_t = k_all[...].astype(f32).T.astype(bf16)
    g_t = g_all[...].astype(f32).T
    product = g_t * att_t[...].astype(bf16).astype(f32)
    for start in range(0, tokens, query_tile):
        span = slice(start, start + query_tile)
        for at in range(0, width, tile):
            dk_tile = dv_tile = None
            for which in range(tile // HEAD_DIM):
                low = at + which * HEAD_DIM
                head = low // HEAD_DIM
                delta = jnp.sum(product[low:low + HEAD_DIM, span], axis=0, keepdims=True)
                q_head = only_head(q_all[span, at:at + tile], which)
                g_head = only_head(g_all[span, at:at + tile], which)
                scores = dot_nt(k_all[:, at:at + tile], q_head)
                probs = jnp.exp2(
                    scores * log2_scale + bias[:, span] - lse[head:head + 1, span]
                )
                grad_probs = dot_nt(v_all[:, at:at + tile], g_head)
                grad_scores = (probs * (grad_probs - delta)).astype(bf16)
                dk_head = dot_nn(grad_scores, q_head)
                dv_head = dot_nn(probs.astype(bf16), g_head)
                dk_tile = dk_head if dk_tile is None else dk_tile + dk_head
                dv_tile = dv_head if dv_tile is None else dv_tile + dv_head
                dq_t[low:low + HEAD_DIM, span] = dot_nn(k_t[low:low + HEAD_DIM, :], grad_scores)
            if start == 0:
                dk[:, at:at + tile] = dk_tile
                dv[:, at:at + tile] = dv_tile
            else:
                dk[:, at:at + tile] += dk_tile
                dv[:, at:at + tile] += dv_tile
    dq = (dq_t[...] * score_scale).T.astype(bf16)
    for place in range(cycle):
        span = slice(place * rows, (place + 1) * rows)
        outs[place][:rows, :] = dq[span, :]
        outs[place][rows:2 * rows, :] = (dk[span, :] * score_scale).astype(bf16)
        outs[place][2 * rows:, :] = dv[span, :].astype(bf16)


def backward(cycle, chunks, grads, att_t, lse):
    rows, width = grads[0].shape
    tokens = rows * cycle
    return pl.pallas_call(
        functools.partial(backward_kernel, cycle, min(tokens, 512)),
        out_shape=[jax.ShapeDtypeStruct((3 * rows, width), bf16)] * cycle,
        in_specs=[vmem()] * (2 * cycle + 2),
        out_specs=[vmem()] * cycle,
        scratch_shapes=[pltpu.VMEM((tokens, width), bf16)] * 4
        + [pltpu.VMEM((width, tokens), f32)]
        + [pltpu.VMEM((tokens, width), f32)] * 2
        + [pltpu.VMEM((tokens, tokens), f32)],
        compiler_params=params(60),
        name="backward",
    )(*chunks, *grads, att_t, lse)


def gather_rows(out_weight):
    count = lax.axis_size("mp")
    chips = count // 2
    pieces = []
    for step in range(chips):
        if step == 0:
            piece = out_weight
        else:
            piece = lax.ppermute(
                out_weight, "mp", [(i, (i - 2 * step) % count) for i in range(count)]
            )
        pieces.append(piece)
    return pieces + [exchange(piece, "mp", 1) for piece in pieces]


def load_rows(pieces, weight, sems):
    rows = pieces[0].shape[0]
    chips = len(pieces) // 2
    own = lax.axis_index("mp")
    chip, core = own // 2, lax.rem(own, 2)
    copies = []
    for at, piece in enumerate(pieces):
        owner = 2 * lax.rem(chip + at % chips, chips) + (core if at < chips else 1 - core)
        first = pl.multiple_of(owner * rows, rows)
        copies.append(
            pltpu.make_async_copy(piece, weight.at[pl.ds(first, rows), :], sems.at[at])
        )
    for copy in copies:
        copy.start()
    for copy in copies:
        copy.wait()


def grad_kernel(cycle, count, up_ref, *refs):
    pieces = refs[:count]
    outs = refs[count:count + cycle]
    weight, sems = refs[count + cycle:]
    load_rows(pieces, weight, sems)
    width = weight.shape[0] // cycle
    own = lax.axis_index("seq")
    for place in range(cycle):
        first = pl.multiple_of(lax.bitwise_xor(own, place) * width, width)
        outs[place][...] = dot_nt(up_ref[...], weight[pl.ds(first, width), :]).astype(bf16)


def project_grad(cycle, upstream, pieces):
    rows, model = upstream.shape
    count = len(pieces)
    return pl.pallas_call(
        functools.partial(grad_kernel, cycle, count),
        out_shape=[jax.ShapeDtypeStruct((rows, model // cycle), bf16)] * cycle,
        in_specs=[vmem()] + [pl.BlockSpec(memory_space=pl.ANY)] * count,
        out_specs=[vmem()] * cycle,
        scratch_shapes=[pltpu.VMEM((model, model), bf16), pltpu.SemaphoreType.DMA((count,))],
        compiler_params=params(32),
        name="project_grad",
    )(upstream, *pieces)


def mixed_kernel(cycle, count, *refs):
    attended = refs[:cycle]
    pieces = refs[cycle:cycle + count]
    out, weight, sems = refs[cycle + count:]
    load_rows(pieces, weight, sems)
    width = weight.shape[0] // cycle
    own = lax.axis_index("seq")
    total = None
    for place in range(cycle):
        first = pl.multiple_of(lax.bitwise_xor(own, place) * width, width)
        term = dot_nn(attended[place][...], weight[pl.ds(first, width), :])
        total = term if total is None else total + term
    out[...] = total.astype(bf16)


def project(cycle, attended, pieces):
    rows = attended[0].shape[0]
    model = attended[0].shape[1] * cycle
    count = len(pieces)
    return pl.pallas_call(
        functools.partial(mixed_kernel, cycle, count),
        out_shape=jax.ShapeDtypeStruct((rows, model), bf16),
        in_specs=[vmem()] * cycle + [pl.BlockSpec(memory_space=pl.ANY)] * count,
        out_specs=vmem(),
        scratch_shapes=[pltpu.VMEM((model, model), bf16), pltpu.SemaphoreType.DMA((count,))],
        compiler_params=params(32),
        name="project",
    )(*attended, *pieces)


def unpack_kernel(cycle, *refs):
    chunks = refs[:cycle]
    outs = refs[cycle:]
    rows = outs[0].shape[0]
    width = outs[0].shape[1] // cycle
    own = lax.axis_index("seq")
    for place in range(cycle):
        source = lax.bitwise_xor(own, place)
        if width % 128 == 0:
            columns = pl.ds(pl.multiple_of(source * width, width), width)
            for at, out in enumerate(outs):
                out[:, columns] = chunks[place][at * rows:(at + 1) * rows, :]
        else:
            for other in range(cycle):
                @pl.when(source == other)
                def _():
                    for at, out in enumerate(outs):
                        out[:, other * width:(other + 1) * width] = chunks[place][
                            at * rows:(at + 1) * rows, :
                        ]


def unpack(cycle, chunks):
    rows = chunks[0].shape[0] // 3
    model = chunks[0].shape[1] * cycle
    return pl.pallas_call(
        functools.partial(unpack_kernel, cycle),
        out_shape=[jax.ShapeDtypeStruct((rows, model), bf16)] * 3,
        in_specs=[vmem()] * cycle,
        out_specs=[vmem()] * 3,
        compiler_params=params(32),
        name="unpack",
    )(*chunks)


def swapped(chunks):
    return [chunks[0]] + [exchange(chunks[k], "seq", k) for k in range(1, len(chunks))]


def local(queries, keys, values, out_weight, upstream, adjacency, counts):
    cycle = lax.axis_size("seq")
    pieces = gather_rows(out_weight)
    chunks = swapped(pack(cycle, queries, keys, values, adjacency, counts))
    attended, att_t, lse = forward(cycle, chunks)
    grads = swapped(project_grad(cycle, upstream, pieces))
    attended = swapped(attended)
    terms = swapped(backward(cycle, chunks, grads, att_t, lse))
    mixed_out = project(cycle, attended, pieces)
    grad_queries, grad_keys, grad_values = unpack(cycle, terms)
    return (mixed_out, grad_queries, grad_keys, grad_values)


def solution(mesh):
    tokens = P(("seq", "mp"), None)
    return jax.shard_map(
        local,
        mesh=mesh,
        in_specs=(tokens, tokens, tokens, P("mp", None), tokens, tokens, P(("seq", "mp"))),
        out_specs=(tokens,) * 4,
        check_vma=False,
    )
```

```python
import functools

import jax
import jax.numpy as jnp
from jax import lax
from jax.experimental import pallas as pl
from jax.experimental.pallas import tpu as pltpu
from jax.sharding import PartitionSpec as P

HEADS = 16
HEAD_DIM = 64
META = 32

score_scale = 0.125
log2_scale = 0.125 * 1.4426950408889634
cycle_offsets = (1, -1, 2, -2)
absent = -1e30
bf16 = jnp.bfloat16
f32 = jnp.float32


def dot_nn(a, b):
    return lax.dot_general(a, b, (((1,), (0,)), ((), ())), preferred_element_type=f32)


def dot_nt(a, b):
    return lax.dot_general(a, b, (((1,), (1,)), ((), ())), preferred_element_type=f32)


def vmem():
    return pl.BlockSpec(memory_space=pltpu.VMEM)


def params(mib):
    return pltpu.CompilerParams(vmem_limit_bytes=mib * 1024 * 1024)


def anywhere():
    return pl.BlockSpec(memory_space=pltpu.HBM)


def exchange(value, axis, distance):
    count = lax.axis_size(axis)
    return lax.ppermute(value, axis, [(i, i ^ distance) for i in range(count)])


def swapped(chunks):
    return [chunks[0]] + [exchange(chunks[k], "seq", k) for k in range(1, len(chunks))]


def group_of(cycle, member, chip):
    turn = (member + chip) % cycle
    if cycle == 4:
        return turn ^ (((turn ^ (turn >> 1)) & 1) * 3)
    return turn


def my_place():
    rank = lax.axis_index("mp")
    return lax.axis_index("seq"), rank // 2, lax.rem(rank, 2)


def columns_at(first, width):
    return pl.ds(pl.multiple_of(first, width), width)


def pack_kernel(cycle, square, q_ref, k_ref, v_ref, w_ref, up_ref, adj_ref, cnt_ref, *refs):
    outs = refs[:cycle]
    sems, w_sem = refs[cycle + 1:]
    rows, model = q_ref.shape
    width = model // cycle
    own, chip, _ = my_place()
    copies = []
    if width % 128 == 0:
        for place in range(cycle):
            group = group_of(cycle, lax.bitwise_xor(own, place), chip)
            for at, ref in enumerate((q_ref, k_ref, v_ref)):
                copies.append(
                    pltpu.make_async_copy(
                        ref.at[:, columns_at(group * width, width)],
                        outs[place].at[at * rows:(at + 1) * rows, :],
                        sems.at[place, at],
                    )
                )
                copies[-1].start()
    copies.append(pltpu.make_async_copy(w_ref, refs[cycle], w_sem))
    copies[-1].start()
    if square:
        for part in range(cycle):
            first = 3 * rows + META + part * rows
            copies.append(
                pltpu.make_async_copy(
                    up_ref.at[:, part * width:(part + 1) * width],
                    outs[1].at[first:first + rows, :],
                    sems.at[part, 3],
                )
            )
            copies[-1].start()
    lines = lax.broadcasted_iota(jnp.int32, (META, width), 0)
    meta = jnp.where(lines == 0, 1, 0)
    for column, offset in enumerate(cycle_offsets):
        named = lax.rem(own - offset + 2 * cycle, cycle)
        meta = meta + jnp.where(
            (lines == lax.bitwise_xor(own, named)) & (adj_ref[0, column] > 0), 1, 0
        )
    meta = jnp.where(lines == META - 1, cnt_ref[0], meta).astype(f32).astype(bf16)
    for place in range(cycle):
        outs[place][3 * rows:3 * rows + META, :] = meta
        if width % 128:
            group = group_of(cycle, lax.bitwise_xor(own, place), chip)
            for other in range(cycle):
                @pl.when(group == other)
                def _():
                    for at, ref in enumerate((q_ref, k_ref, v_ref)):
                        outs[place][at * rows:(at + 1) * rows, :] = ref[
                            :, other * width:(other + 1) * width
                        ]
    for copy in copies:
        copy.wait()


def pack(cycle, square, queries, keys, values, out_weight, upstream, adjacency, counts):
    rows, model = queries.shape
    width = model // cycle
    smem = pl.BlockSpec(memory_space=pltpu.SMEM)
    return pl.pallas_call(
        functools.partial(pack_kernel, cycle, square),
        out_shape=[
            jax.ShapeDtypeStruct(
                (3 * rows + META + (model if square and place == 1 else 0) * rows // width, width), bf16
            )
            for place in range(cycle)
        ]
        + [jax.ShapeDtypeStruct(out_weight.shape, bf16)],
        in_specs=[anywhere() if width % 128 == 0 else vmem()] * 3
        + [anywhere()] * 2
        + [smem] * 2,
        out_specs=[vmem()] * (cycle + 1),
        scratch_shapes=[pltpu.SemaphoreType.DMA((cycle, 4)), pltpu.SemaphoreType.DMA],
        compiler_params=params(62),
        name="pack",
    )(queries, keys, values, out_weight, upstream, adjacency, counts)


def fill(cycle, rows, chunks, bias, *parts):
    for place in range(cycle):
        for at, part in parts:
            part[place * rows:(place + 1) * rows, :] = chunks[place][at * rows:(at + 1) * rows, :]
    lines = lax.broadcasted_iota(jnp.int32, (rows, rows), 0).astype(f32)
    lists = [chunks[place][3 * rows:3 * rows + META, :].astype(f32) for place in range(cycle)]
    for key_place in range(cycle):
        count = lists[key_place][META - 1:, :1]
        valid = lines < count
        for query_place in range(cycle):
            way = key_place ^ query_place
            times = lists[query_place][way:way + 1, :1]
            term = jnp.where(times > 0, jnp.log2(jnp.maximum(times, 1.0)), absent)
            bias[
                key_place * rows:(key_place + 1) * rows,
                query_place * rows:(query_place + 1) * rows,
            ] = jnp.where(valid, term, absent)


def head_tile(width):
    return min(128, width)


def only_head(tile, which):
    lanes = lax.broadcasted_iota(jnp.int32, tile.shape, 1)
    inside = (lanes >= which * HEAD_DIM) & (lanes < (which + 1) * HEAD_DIM)
    return jnp.where(inside, tile, jnp.zeros_like(tile))


def forward_kernel(cycle, query_tile, *refs):
    chunks = refs[:cycle]
    outs = refs[cycle:2 * cycle]
    att_t, lse, q_all, k_all, v_all, bias = refs[2 * cycle:]
    width = q_all.shape[1]
    tokens = q_all.shape[0]
    rows = tokens // cycle
    fill(cycle, rows, chunks, bias, (0, q_all), (1, k_all), (2, v_all))
    tile = head_tile(width)
    v_t = v_all[...].astype(f32).T.astype(bf16)
    for start in range(0, tokens, query_tile):
        span = slice(start, start + query_tile)
        for head in range(width // HEAD_DIM):
            at = head * HEAD_DIM // tile * tile
            which = (head * HEAD_DIM - at) // HEAD_DIM
            scores = dot_nt(
                k_all[:, at:at + tile], only_head(q_all[span, at:at + tile], which)
            )
            scores = scores * log2_scale + bias[:, span]
            largest = jnp.max(scores, axis=0, keepdims=True)
            expo = jnp.exp2(scores - largest)
            total = jnp.sum(expo, axis=0, keepdims=True)
            probs = (expo * (1.0 / total)).astype(bf16)
            lse[head:head + 1, span] = largest + jnp.log2(total)
            att_t[head * HEAD_DIM:(head + 1) * HEAD_DIM, span] = dot_nn(
                v_t[head * HEAD_DIM:(head + 1) * HEAD_DIM, :], probs
            )
    attended = att_t[...].T.astype(bf16)
    for place in range(cycle):
        outs[place][...] = attended[place * rows:(place + 1) * rows, :]


def forward(cycle, chunks):
    width = chunks[0].shape[1]
    rows = (chunks[0].shape[0] - META) // 3
    tokens = rows * cycle
    outs = pl.pallas_call(
        functools.partial(forward_kernel, cycle, min(tokens, 512)),
        out_shape=[jax.ShapeDtypeStruct((rows, width), bf16)] * cycle
        + [
            jax.ShapeDtypeStruct((width, tokens), f32),
            jax.ShapeDtypeStruct((8, tokens), f32),
        ],
        in_specs=[vmem()] * cycle,
        out_specs=[vmem()] * (cycle + 2),
        scratch_shapes=[pltpu.VMEM((tokens, width), bf16)] * 3
        + [pltpu.VMEM((tokens, tokens), f32)],
        compiler_params=params(16 if tokens <= 512 else 60),
        name="forward",
    )(*chunks)
    return outs[:cycle], outs[cycle], outs[cycle + 1]


def backward_kernel(cycle, query_tile, grad_count, *refs):
    chunks = refs[:cycle]
    refs = refs[cycle:]
    grads = refs[:grad_count]
    attended = refs[grad_count:grad_count + cycle]
    refs = refs[grad_count + cycle:]
    att_t, lse = refs[:2]
    outs = refs[2:cycle + 2]
    q_all, k_all, v_all, g_all, dq_t, dk, dv, bias = refs[cycle + 2:]
    width = q_all.shape[1]
    tokens = q_all.shape[0]
    rows = tokens // cycle
    fill(cycle, rows, chunks, bias, (0, q_all), (1, k_all), (2, v_all))
    filled = 0
    for grad in grads:
        g_all[filled:filled + grad.shape[0], :] = grad[...]
        filled += grad.shape[0]
    tile = head_tile(width)
    k_t = k_all[...].astype(f32).T.astype(bf16)
    g_t = g_all[...].astype(f32).T
    product = g_t * att_t[...].astype(bf16).astype(f32)
    for start in range(0, tokens, query_tile):
        span = slice(start, start + query_tile)
        for at in range(0, width, tile):
            dk_tile = dv_tile = None
            for which in range(tile // HEAD_DIM):
                low = at + which * HEAD_DIM
                head = low // HEAD_DIM
                delta = jnp.sum(product[low:low + HEAD_DIM, span], axis=0, keepdims=True)
                q_head = only_head(q_all[span, at:at + tile], which)
                g_head = only_head(g_all[span, at:at + tile], which)
                scores = dot_nt(k_all[:, at:at + tile], q_head)
                probs = jnp.exp2(
                    scores * log2_scale + bias[:, span] - lse[head:head + 1, span]
                )
                grad_probs = dot_nt(v_all[:, at:at + tile], g_head)
                grad_scores = (probs * (grad_probs - delta)).astype(bf16)
                dk_head = dot_nn(grad_scores, q_head)
                dv_head = dot_nn(probs.astype(bf16), g_head)
                dk_tile = dk_head if dk_tile is None else dk_tile + dk_head
                dv_tile = dv_head if dv_tile is None else dv_tile + dv_head
                dq_t[low:low + HEAD_DIM, span] = dot_nn(k_t[low:low + HEAD_DIM, :], grad_scores)
            if start == 0:
                dk[:, at:at + tile] = dk_tile
                dv[:, at:at + tile] = dv_tile
            else:
                dk[:, at:at + tile] += dk_tile
                dv[:, at:at + tile] += dv_tile
    dq = (dq_t[...] * score_scale).T.astype(bf16)
    for place in range(cycle):
        span = slice(place * rows, (place + 1) * rows)
        outs[place][:rows, :] = dq[span, :]
        outs[place][rows:2 * rows, :] = (dk[span, :] * score_scale).astype(bf16)
        outs[place][2 * rows:3 * rows, :] = dv[span, :].astype(bf16)
        outs[place][3 * rows:, :] = attended[place][...]


def backward(cycle, chunks, grads, attended, att_t, lse):
    rows, width = attended[0].shape
    tokens = rows * cycle
    return pl.pallas_call(
        functools.partial(backward_kernel, cycle, min(tokens, 512), len(grads)),
        out_shape=[jax.ShapeDtypeStruct((4 * rows, width), bf16)] * cycle,
        in_specs=[vmem()] * (2 * cycle + len(grads) + 2),
        out_specs=[vmem()] * cycle,
        scratch_shapes=[pltpu.VMEM((tokens, width), bf16)] * 4
        + [pltpu.VMEM((width, tokens), f32)]
        + [pltpu.VMEM((tokens, width), f32)] * 2
        + [pltpu.VMEM((tokens, tokens), f32)],
        compiler_params=params(16 if tokens <= 512 else 60),
        name="backward",
    )(*chunks, *grads, *attended, att_t, lse)


def fetch_rows(out_weight, place):
    cycle, count = lax.axis_size("seq"), lax.axis_size("mp")
    pairs = []
    for member in range(cycle):
        for rank in range(count):
            owner = 2 * group_of(cycle, member ^ place, rank // 2) + rank % 2
            pairs.append((member * count + owner, member * count + rank))
    half = lax.ppermute(out_weight, ("seq", "mp"), pairs)
    return [half, exchange(half, "mp", 1)]


def both_halves(halves, core):
    mine, other = halves[0][...], halves[1][...]
    first = core == 0
    return jnp.concatenate([jnp.where(first, mine, other), jnp.where(first, other, mine)], axis=0)


def near_kernel(up_ref, next_ref, *refs):
    halves = refs[:4]
    near, far, both, sem = refs[-4:]
    rows, model = up_ref.shape
    width = next_ref.shape[1]
    copy = pltpu.make_async_copy(up_ref, both.at[:rows, :], sem)
    copy.start()
    first = next_ref.shape[0] - model // width * rows
    for part in range(model // width):
        both[rows:, part * width:(part + 1) * width] = next_ref[
            first + part * rows:first + (part + 1) * rows, :
        ]
    copy.wait()
    _, _, core = my_place()
    half = halves[0].shape[0]
    for group, out in enumerate((near, far)):
        for side in range(2):
            at = columns_at((core if side == 0 else 1 - core) * half, half)
            out[:, at] = dot_nt(both[...], halves[2 * group + side][...]).astype(bf16)


def near_grads(upstream, neighbour, halves, after):
    rows, width = upstream.shape[0], 2 * halves[0].shape[0]
    return pl.pallas_call(
        near_kernel,
        out_shape=[jax.ShapeDtypeStruct((2 * rows, width), bf16)] * 2,
        in_specs=[anywhere()] + [vmem()] * 5 + [pl.BlockSpec(memory_space=pl.ANY)] * len(after),
        out_specs=[vmem()] * 2,
        scratch_shapes=[
            pltpu.VMEM((2 * rows, upstream.shape[1]), bf16),
            pltpu.SemaphoreType.DMA,
        ],
        compiler_params=params(8),
        name="near_grads",
    )(upstream, neighbour, *halves, *after)


def grad_kernel(cycle, up_ref, *refs):
    _, _, core = my_place()
    outs = refs[2 * cycle:]
    for place in range(cycle):
        rows = both_halves(refs[2 * place:2 * place + 2], core)
        outs[place][...] = dot_nt(up_ref[...], rows).astype(bf16)


def project_grad(cycle, upstream, halves):
    rows, model = upstream.shape
    return pl.pallas_call(
        functools.partial(grad_kernel, cycle),
        out_shape=[jax.ShapeDtypeStruct((rows, model // cycle), bf16)] * cycle,
        in_specs=[vmem()] * (1 + 2 * cycle),
        out_specs=[vmem()] * cycle,
        compiler_params=params(8),
        name="project_grad",
    )(upstream, *halves)


def finish_kernel(cycle, *refs):
    chunks = refs[:cycle]
    halves = refs[cycle:3 * cycle]
    mixed, *outs = refs[3 * cycle:3 * cycle + 4]
    rows, model = mixed.shape
    width = model // cycle
    own, chip, core = my_place()
    copies = []
    total = None
    for place in range(cycle):
        group = group_of(cycle, lax.bitwise_xor(own, place), chip)
        if width % 128 == 0:
            for at, out in enumerate(outs):
                copies.append(
                    pltpu.make_async_copy(
                        chunks[place].at[at * rows:(at + 1) * rows, :],
                        out.at[:, columns_at(group * width, width)],
                        refs[-1].at[place, at],
                    )
                )
                copies[-1].start()
        else:
            for other in range(cycle):
                @pl.when(group == other)
                def _():
                    for at, out in enumerate(outs):
                        out[:, other * width:(other + 1) * width] = chunks[place][
                            at * rows:(at + 1) * rows, :
                        ]
    for place in range(cycle):
        pair = halves[2 * place:2 * place + 2]
        if width % 256 == 0:
            half = width // 2
            terms = [
                dot_nn(
                    chunks[place][3 * rows:, columns_at((core if side == 0 else 1 - core) * half, half)],
                    pair[side][...],
                )
                for side in range(2)
            ]
        else:
            terms = [dot_nn(chunks[place][3 * rows:, :], both_halves(pair, core))]
        for term in terms:
            total = term if total is None else total + term
    mixed[...] = total.astype(bf16)
    for copy in copies:
        copy.wait()


def finish(cycle, chunks, halves):
    rows = chunks[0].shape[0] // 4
    model = chunks[0].shape[1] * cycle
    aligned = model // cycle % 128 == 0
    return pl.pallas_call(
        functools.partial(finish_kernel, cycle),
        out_shape=[jax.ShapeDtypeStruct((rows, model), bf16)] * 4,
        in_specs=[vmem()] * (3 * cycle),
        out_specs=[vmem()] + [anywhere() if aligned else vmem()] * 3,
        scratch_shapes=[pltpu.SemaphoreType.DMA((cycle, 3))],
        compiler_params=params(8),
        name="finish",
    )(*chunks, *halves)


def local(queries, keys, values, out_weight, upstream, adjacency, counts):
    cycle = lax.axis_size("seq")
    square = cycle == 4 and lax.axis_size("mp") == 8
    *chunks, out_weight = pack(
        cycle, square, queries, keys, values, out_weight, upstream, adjacency, counts
    )
    chunks = swapped(chunks)
    halves = {}
    for place in (0, 2, 1, 3) if square else range(cycle):
        halves[place] = fetch_rows(out_weight, place)
    if square:
        near, far = near_grads(upstream, chunks[1], halves[0] + halves[2], chunks[2:])
        grads = [near, exchange(far, "seq", 2)]
    else:
        grads = swapped(project_grad(cycle, upstream, sum((halves[k] for k in range(cycle)), [])))
    attended, att_t, lse = forward(cycle, chunks)
    terms = swapped(backward(cycle, chunks, grads, attended, att_t, lse))
    return tuple(finish(cycle, terms, sum((halves[k] for k in range(cycle)), [])))


def solution(mesh):
    tokens = P(("seq", "mp"), None)
    return jax.shard_map(
        local,
        mesh=mesh,
        in_specs=(tokens, tokens, tokens, P("mp", None), tokens, tokens, P(("seq", "mp"))),
        out_specs=(tokens,) * 4,
        check_vma=False,
    )
```

```python
import functools

import jax
import jax.numpy as jnp
from jax import lax
from jax.experimental import pallas as pl
from jax.experimental.pallas import tpu as pltpu
from jax.sharding import PartitionSpec as P

HEADS = 16
HEAD_DIM = 64
META = 32

score_scale = 0.125
log2_scale = 0.125 * 1.4426950408889634
cycle_offsets = (1, -1, 2, -2)
absent = -1e30
bf16 = jnp.bfloat16
f32 = jnp.float32


def dot_nn(a, b):
    return lax.dot_general(a, b, (((1,), (0,)), ((), ())), preferred_element_type=f32)


def dot_nt(a, b):
    return lax.dot_general(a, b, (((1,), (1,)), ((), ())), preferred_element_type=f32)


def vmem():
    return pl.BlockSpec(memory_space=pltpu.VMEM)


def params(mib):
    return pltpu.CompilerParams(vmem_limit_bytes=mib * 1024 * 1024)


def unread():
    return pl.BlockSpec(memory_space=pl.ANY)


def anywhere():
    return pl.BlockSpec(memory_space=pltpu.HBM)


def cost(micros):
    return pl.CostEstimate(flops=int(micros * 1e9), bytes_accessed=0, transcendentals=0)


def exchange(value, axis, distance):
    count = lax.axis_size(axis)
    return lax.ppermute(value, axis, [(i, i ^ distance) for i in range(count)])


def swapped(chunks):
    return [chunks[0]] + [exchange(chunks[k], "seq", k) for k in range(1, len(chunks))]


def group_of(cycle, member, chip):
    turn = (member + chip) % cycle
    if cycle == 4:
        return turn ^ (((turn ^ (turn >> 1)) & 1) * 3)
    return turn


def my_place():
    rank = lax.axis_index("mp")
    return lax.axis_index("seq"), rank // 2, lax.rem(rank, 2)


def columns_at(first, width):
    return pl.ds(pl.multiple_of(first, width), width)


def pack_kernel(cycle, places, extra, q_ref, k_ref, v_ref, adj_ref, cnt_ref, *refs):
    refs, (sems, more_sems) = refs[:-2], refs[-2:]
    outs = refs[-len(places) - extra:]
    rows, model = q_ref.shape
    width = model // cycle
    own, chip, _ = my_place()
    copies = []
    if width % 128 == 0:
        for place, out in zip(places, outs):
            group = group_of(cycle, lax.bitwise_xor(own, place), chip)
            for at, ref in enumerate((q_ref, k_ref, v_ref)):
                copies.append(
                    pltpu.make_async_copy(
                        ref.at[:, columns_at(group * width, width)],
                        out.at[at * rows:(at + 1) * rows, :],
                        sems.at[place, at],
                    )
                )
                copies[-1].start()
    for at in range(extra):
        copies.append(
            pltpu.make_async_copy(refs[at], outs[len(places) + at], more_sems.at[at])
        )
        copies[-1].start()
    lines = lax.broadcasted_iota(jnp.int32, (META, width), 0)
    meta = jnp.where(lines == 0, 1, 0)
    for column, offset in enumerate(cycle_offsets):
        named = lax.rem(own - offset + 2 * cycle, cycle)
        meta = meta + jnp.where(
            (lines == lax.bitwise_xor(own, named)) & (adj_ref[0, column] > 0), 1, 0
        )
    meta = jnp.where(lines == META - 1, cnt_ref[0], meta).astype(f32).astype(bf16)
    for place, out in zip(places, outs):
        out[3 * rows:, :] = meta
        if width % 128:
            group = group_of(cycle, lax.bitwise_xor(own, place), chip)
            for other in range(cycle):
                @pl.when(group == other)
                def _():
                    for at, ref in enumerate((q_ref, k_ref, v_ref)):
                        out[at * rows:(at + 1) * rows, :] = ref[
                            :, other * width:(other + 1) * width
                        ]
    for copy in copies:
        copy.wait()


def pack(cycle, places, tensors, extra=(), after=()):
    rows, model = tensors[0].shape
    width = model // cycle
    smem = pl.BlockSpec(memory_space=pltpu.SMEM)
    return pl.pallas_call(
        functools.partial(pack_kernel, cycle, places, len(extra)),
        out_shape=[jax.ShapeDtypeStruct((3 * rows + META, width), bf16)] * len(places)
        + [jax.ShapeDtypeStruct(array.shape, bf16) for array in extra],
        in_specs=[anywhere() if width % 128 == 0 else vmem()] * 3
        + [smem] * 2
        + [anywhere()] * len(extra)
        + [unread()] * len(after),
        out_specs=[vmem()] * (len(places) + len(extra)),
        scratch_shapes=[pltpu.SemaphoreType.DMA((cycle, 3)), pltpu.SemaphoreType.DMA((2,))],
        compiler_params=params(8 if extra else 62),
        cost_estimate=cost(5),
        name="pack",
    )(*tensors, *extra, *after)


def gather_kernel(cycle, *refs):
    chunks = refs[:cycle]
    q_all, k_all, v_all, k_t, v_t, bias = refs[cycle:]
    rows = q_all.shape[0] // cycle
    for place in range(cycle):
        for at, part in enumerate((q_all, k_all, v_all)):
            part[place * rows:(place + 1) * rows, :] = chunks[place][at * rows:(at + 1) * rows, :]
    k_t[...] = k_all[...].astype(f32).T.astype(bf16)
    v_t[...] = v_all[...].astype(f32).T.astype(bf16)
    lines = lax.broadcasted_iota(jnp.int32, (rows, rows), 0).astype(f32)
    lists = [chunks[place][3 * rows:, :].astype(f32) for place in range(cycle)]
    for key_place in range(cycle):
        count = lists[key_place][META - 1:, :1]
        valid = lines < count
        for query_place in range(cycle):
            way = key_place ^ query_place
            times = lists[query_place][way:way + 1, :1]
            term = jnp.where(times > 0, jnp.log2(jnp.maximum(times, 1.0)), absent)
            bias[
                key_place * rows:(key_place + 1) * rows,
                query_place * rows:(query_place + 1) * rows,
            ] = jnp.where(valid, term, absent)


def gather(cycle, chunks):
    width = chunks[0].shape[1]
    rows = (chunks[0].shape[0] - META) // 3
    tokens = rows * cycle
    return pl.pallas_call(
        functools.partial(gather_kernel, cycle),
        out_shape=[jax.ShapeDtypeStruct((tokens, width), bf16)] * 3
        + [jax.ShapeDtypeStruct((width, tokens), bf16)] * 2
        + [jax.ShapeDtypeStruct((tokens, tokens), f32)],
        in_specs=[vmem()] * cycle,
        out_specs=[vmem()] * 6,
        compiler_params=params(8 if tokens <= 512 else 40),
        cost_estimate=cost(5),
        name="gather",
    )(*chunks)


def head_tile(width):
    return min(128, width)


def only_head(tile, which):
    lanes = lax.broadcasted_iota(jnp.int32, tile.shape, 1)
    inside = (lanes >= which * HEAD_DIM) & (lanes < (which + 1) * HEAD_DIM)
    return jnp.where(inside, tile, jnp.zeros_like(tile))


def forward_kernel(query_tile, q_all, k_all, v_t, bias, *refs):
    outs = refs[:-2]
    att_t, lse = refs[-2:]
    tokens, width = q_all.shape
    tile = head_tile(width)
    for start in range(0, tokens, query_tile):
        span = slice(start, start + query_tile)
        for head in range(width // HEAD_DIM):
            at = head * HEAD_DIM // tile * tile
            which = (head * HEAD_DIM - at) // HEAD_DIM
            scores = dot_nt(
                k_all[:, at:at + tile], only_head(q_all[span, at:at + tile], which)
            )
            scores = scores * log2_scale + bias[:, span]
            largest = jnp.max(scores, axis=0, keepdims=True)
            expo = jnp.exp2(scores - largest)
            total = jnp.sum(expo, axis=0, keepdims=True)
            probs = (expo * (1.0 / total)).astype(bf16)
            lse[head:head + 1, span] = largest + jnp.log2(total)
            att_t[head * HEAD_DIM:(head + 1) * HEAD_DIM, span] = dot_nn(
                v_t[head * HEAD_DIM:(head + 1) * HEAD_DIM, :], probs
            )
    attended = att_t[...].T.astype(bf16)
    filled = 0
    for out in outs:
        out[...] = attended[filled:filled + out.shape[0], :]
        filled += out.shape[0]


def forward(cycle, together, q_all, k_all, v_t, bias):
    tokens, width = q_all.shape
    rows = tokens // cycle
    parts = cycle // together
    outs = pl.pallas_call(
        functools.partial(forward_kernel, min(tokens, 512)),
        out_shape=[jax.ShapeDtypeStruct((together * rows, width), bf16)] * parts
        + [
            jax.ShapeDtypeStruct((width, tokens), f32),
            jax.ShapeDtypeStruct((8, tokens), f32),
        ],
        in_specs=[vmem()] * 4,
        out_specs=[vmem()] * (parts + 2),
        compiler_params=params(16 if tokens <= 512 else 60),
        cost_estimate=cost(3),
        name="forward",
    )(q_all, k_all, v_t, bias)
    return outs[:parts], outs[parts], outs[parts + 1]


def backward_kernel(cycle, query_tile, grad_count, att_count, *refs):
    q_all, k_all, v_all, k_t, bias, att_t, lse = refs[:7]
    refs = refs[7:]
    grads = refs[:grad_count]
    attended = refs[grad_count:grad_count + att_count]
    outs = refs[-4 - cycle:-4]
    g_all, dq_t, dk, dv = refs[-4:]
    width = q_all.shape[1]
    tokens = q_all.shape[0]
    rows = tokens // cycle
    filled = 0
    for grad in grads:
        g_all[filled:filled + grad.shape[0], :] = grad[...]
        filled += grad.shape[0]
    tile = head_tile(width)
    g_t = g_all[...].astype(f32).T
    product = g_t * att_t[...].astype(bf16).astype(f32)
    for start in range(0, tokens, query_tile):
        span = slice(start, start + query_tile)
        for at in range(0, width, tile):
            dk_tile = dv_tile = None
            for which in range(tile // HEAD_DIM):
                low = at + which * HEAD_DIM
                head = low // HEAD_DIM
                delta = jnp.sum(product[low:low + HEAD_DIM, span], axis=0, keepdims=True)
                q_head = only_head(q_all[span, at:at + tile], which)
                g_head = only_head(g_all[span, at:at + tile], which)
                scores = dot_nt(k_all[:, at:at + tile], q_head)
                probs = jnp.exp2(
                    scores * log2_scale + bias[:, span] - lse[head:head + 1, span]
                )
                grad_probs = dot_nt(v_all[:, at:at + tile], g_head)
                grad_scores = (probs * (grad_probs - delta)).astype(bf16)
                dk_head = dot_nn(grad_scores, q_head)
                dv_head = dot_nn(probs.astype(bf16), g_head)
                dk_tile = dk_head if dk_tile is None else dk_tile + dk_head
                dv_tile = dv_head if dv_tile is None else dv_tile + dv_head
                dq_t[low:low + HEAD_DIM, span] = dot_nn(k_t[low:low + HEAD_DIM, :], grad_scores)
            if start == 0:
                dk[:, at:at + tile] = dk_tile
                dv[:, at:at + tile] = dv_tile
            else:
                dk[:, at:at + tile] += dk_tile
                dv[:, at:at + tile] += dv_tile
    dq = (dq_t[...] * score_scale).T.astype(bf16)
    for place in range(cycle):
        span = slice(place * rows, (place + 1) * rows)
        outs[place][:rows, :] = dq[span, :]
        outs[place][rows:2 * rows, :] = (dk[span, :] * score_scale).astype(bf16)
        outs[place][2 * rows:3 * rows, :] = dv[span, :].astype(bf16)
        if attended:
            outs[place][3 * rows:, :] = attended[place][...]


def backward(cycle, inputs, grads, attended, after):
    tokens, width = inputs[0].shape
    rows = tokens // cycle
    return pl.pallas_call(
        functools.partial(backward_kernel, cycle, min(tokens, 512), len(grads), len(attended)),
        out_shape=[jax.ShapeDtypeStruct(((4 if attended else 3) * rows, width), bf16)] * cycle,
        in_specs=[vmem()] * (len(inputs) + len(grads) + len(attended)) + [unread()] * len(after),
        out_specs=[vmem()] * cycle,
        scratch_shapes=[
            pltpu.VMEM((tokens, width), bf16),
            pltpu.VMEM((width, tokens), f32),
            pltpu.VMEM((tokens, width), f32),
            pltpu.VMEM((tokens, width), f32),
        ],
        compiler_params=params(16 if tokens <= 512 else 60),
        cost_estimate=cost(3),
        name="backward",
    )(*inputs, *grads, *attended, *after)


def fetch_rows(out_weight, place):
    cycle, count = lax.axis_size("seq"), lax.axis_size("mp")
    pairs = []
    for member in range(cycle):
        for rank in range(count):
            owner = 2 * group_of(cycle, member ^ place, rank // 2) + rank % 2
            pairs.append((member * count + owner, member * count + rank))
    return lax.ppermute(out_weight, ("seq", "mp"), pairs)


def with_other_core(half):
    return [half, exchange(half, "mp", 1)]


def both_halves(halves, core):
    mine, other = halves[0][...], halves[1][...]
    first = core == 0
    return jnp.concatenate([jnp.where(first, mine, other), jnp.where(first, other, mine)], axis=0)


def half_columns(halves, core, side):
    half = halves[0].shape[0]
    return columns_at((core if side == 0 else 1 - core) * half, half)


def near_kernel(up_ref, next_ref, *refs):
    halves = refs[:4]
    near, far = refs[-2:]
    rows = up_ref.shape[0]
    _, _, core = my_place()
    for group, out in enumerate((far, near)):
        for side in range(2):
            weight = halves[2 * (1 - group) + side]
            for block, ref in enumerate((up_ref, next_ref)):
                out[block * rows:(block + 1) * rows, half_columns(halves, core, side)] = dot_nt(
                    ref[...], weight[...]
                ).astype(bf16)


def near_grads(upstream, next_upstream, halves, after):
    rows, width = upstream.shape[0], 2 * halves[0].shape[0]
    return pl.pallas_call(
        near_kernel,
        out_shape=[jax.ShapeDtypeStruct((2 * rows, width), bf16)] * 2,
        in_specs=[vmem()] * 6 + [unread()] * len(after),
        out_specs=[vmem()] * 2,
        compiler_params=params(8),
        cost_estimate=cost(1),
        name="near_grads",
    )(upstream, next_upstream, *halves, *after)


def mix_kernel(near_ref, far_ref, *refs):
    halves = refs[:4]
    own, other = refs[-2:]
    rows = own.shape[0]
    _, _, core = my_place()
    total = None
    for group, ref in enumerate((near_ref, far_ref)):
        for side in range(2):
            term = dot_nn(
                ref[:, half_columns(halves, core, side)], halves[2 * group + side][...]
            )
            total = term if total is None else total + term
    own[...] = total[:rows, :]
    other[...] = total[rows:, :].astype(bf16)


def mix(near, far, halves, after):
    rows, model = near.shape[0] // 2, halves[0].shape[1]
    return pl.pallas_call(
        mix_kernel,
        out_shape=[
            jax.ShapeDtypeStruct((rows, model), f32),
            jax.ShapeDtypeStruct((rows, model), bf16),
        ],
        in_specs=[vmem()] * 6 + [unread()] * len(after),
        out_specs=[vmem()] * 2,
        compiler_params=params(8),
        cost_estimate=cost(1),
        name="mix",
    )(near, far, *halves, *after)


def grad_kernel(cycle, up_ref, *refs):
    _, _, core = my_place()
    outs = refs[2 * cycle:]
    for place in range(cycle):
        rows = both_halves(refs[2 * place:2 * place + 2], core)
        outs[place][...] = dot_nt(up_ref[...], rows).astype(bf16)


def project_grad(cycle, upstream, halves):
    rows, model = upstream.shape
    return pl.pallas_call(
        functools.partial(grad_kernel, cycle),
        out_shape=[jax.ShapeDtypeStruct((rows, model // cycle), bf16)] * cycle,
        in_specs=[vmem()] * (1 + 2 * cycle),
        out_specs=[vmem()] * cycle,
        compiler_params=params(8),
        name="project_grad",
    )(upstream, *halves)


def place_columns(chunks, outs, sems):
    cycle = len(chunks)
    rows, model = outs[0].shape
    width = model // cycle
    own, chip, _ = my_place()
    copies = []
    for place in range(cycle):
        group = group_of(cycle, lax.bitwise_xor(own, place), chip)
        if width % 128 == 0:
            for at, out in enumerate(outs):
                copies.append(
                    pltpu.make_async_copy(
                        chunks[place].at[at * rows:(at + 1) * rows, :],
                        out.at[:, columns_at(group * width, width)],
                        sems.at[place, at],
                    )
                )
                copies[-1].start()
        else:
            for other in range(cycle):
                @pl.when(group == other)
                def _():
                    for at, out in enumerate(outs):
                        out[:, other * width:(other + 1) * width] = chunks[place][
                            at * rows:(at + 1) * rows, :
                        ]
    return copies


def finish_kernel(cycle, *refs):
    chunks = refs[:cycle]
    mixed, *outs = refs[-5:-1]
    copies = place_columns(chunks, outs, refs[-1])
    rows = mixed.shape[0]
    if len(refs) == cycle + 7:
        mine, landed = refs[cycle:cycle + 2]
        mixed[...] = (mine[...] + landed[...].astype(f32)).astype(bf16)
    else:
        halves = refs[cycle:3 * cycle]
        _, _, core = my_place()
        total = None
        for place in range(cycle):
            weight = both_halves(halves[2 * place:2 * place + 2], core)
            term = dot_nn(chunks[place][3 * rows:, :], weight)
            total = term if total is None else total + term
        mixed[...] = total.astype(bf16)
    for copy in copies:
        copy.wait()


def finish(cycle, rows, chunks, others):
    model = chunks[0].shape[1] * cycle
    aligned = model // cycle % 128 == 0
    return pl.pallas_call(
        functools.partial(finish_kernel, cycle),
        out_shape=[jax.ShapeDtypeStruct((rows, model), bf16)] * 4,
        in_specs=[vmem()] * (cycle + len(others)),
        out_specs=[vmem()] + [anywhere() if aligned else vmem()] * 3,
        scratch_shapes=[pltpu.SemaphoreType.DMA((cycle, 3))],
        compiler_params=params(8),
        name="finish",
    )(*chunks, *others)


def local(queries, keys, values, out_weight, upstream, adjacency, counts):
    cycle = lax.axis_size("seq")
    rows = queries.shape[0]
    tensors = (queries, keys, values, adjacency, counts)
    if cycle == 4 and lax.axis_size("mp") == 8:
        return square(cycle, rows, tensors, out_weight, upstream)
    chunks = swapped(pack(cycle, range(cycle), tensors))
    halves = []
    for place in range(cycle):
        halves += with_other_core(fetch_rows(out_weight, place))
    q_all, k_all, v_all, k_t, v_t, bias = gather(cycle, chunks)
    attended, att_t, lse = forward(cycle, 1, q_all, k_all, v_t, bias)
    grads = swapped(project_grad(cycle, upstream, halves))
    inputs = (q_all, k_all, v_all, k_t, bias, att_t, lse)
    terms = swapped(backward(cycle, inputs, grads, attended, []))
    return tuple(finish(cycle, rows, terms, halves))


def square(cycle, rows, tensors, out_weight, upstream):
    first = fetch_rows(out_weight, 0)
    sent = list(pack(cycle, range(1, cycle), tensors))
    own_chunk, out_weight, upstream = pack(cycle, [0], tensors, (out_weight, upstream), [first])
    chunks = swapped([own_chunk] + sent)
    second = fetch_rows(out_weight, 2)
    next_upstream = exchange(upstream, "seq", 1)
    halves = with_other_core(first) + with_other_core(second)
    q_all, k_all, v_all, k_t, v_t, bias = gather(cycle, chunks)
    (near_att, far_att), att_t, lse = forward(cycle, 2, q_all, k_all, v_t, bias)
    far_att = exchange(far_att, "seq", 2)
    near, far = near_grads(upstream, next_upstream, halves, [lse])
    grads = [near, exchange(far, "seq", 2)]
    own_mixed, next_mixed = mix(near_att, far_att, halves, [far])
    inputs = (q_all, k_all, v_all, k_t, bias, att_t, lse)
    terms = backward(cycle, inputs, grads, [], [next_mixed])
    next_mixed = exchange(next_mixed, "seq", 1)
    return tuple(finish(cycle, rows, swapped(terms), [own_mixed, next_mixed]))


def solution(mesh):
    tokens = P(("seq", "mp"), None)
    return jax.shard_map(
        local,
        mesh=mesh,
        in_specs=(tokens, tokens, tokens, P("mp", None), tokens, tokens, P(("seq", "mp"))),
        out_specs=(tokens,) * 4,
        check_vma=False,
    )
```

```python
import functools

import jax
import jax.numpy as jnp
from jax import lax
from jax.experimental import pallas as pl
from jax.experimental.pallas import tpu as pltpu
from jax.sharding import PartitionSpec as P

HEADS = 16
HEAD_DIM = 64
META = 32

score_scale = 0.125
log2_scale = 0.125 * 1.4426950408889634
cycle_offsets = (1, -1, 2, -2)
absent = -1e30
bf16 = jnp.bfloat16
f32 = jnp.float32


def dot_nn(a, b):
    return lax.dot_general(a, b, (((1,), (0,)), ((), ())), preferred_element_type=f32)


def dot_nt(a, b):
    return lax.dot_general(a, b, (((1,), (1,)), ((), ())), preferred_element_type=f32)


def vmem():
    return pl.BlockSpec(memory_space=pltpu.VMEM)


def params(mib):
    return pltpu.CompilerParams(vmem_limit_bytes=int(mib * 1024) * 1024)


def unread():
    return pl.BlockSpec(memory_space=pl.ANY)


def anywhere():
    return pl.BlockSpec(memory_space=pltpu.HBM)


def cost(micros):
    return pl.CostEstimate(flops=int(micros * 1e9), bytes_accessed=0, transcendentals=0)


def exchange(value, axis, distance):
    count = lax.axis_size(axis)
    return lax.ppermute(value, axis, [(i, i ^ distance) for i in range(count)])


def exchange_seq(value, distance):
    return exchange(value, "seq", distance)


def turned(distance):
    return distance ^ (((distance ^ (distance >> 1)) & 1) * 3)


def exchange_slot(value, slot):
    count = lax.axis_size("mp")
    pairs = []
    for member in range(lax.axis_size("seq")):
        for rank in range(count):
            partner = member ^ (turned(slot) if rank % 2 else slot)
            pairs.append((member * count + rank, partner * count + rank))
    return lax.ppermute(value, ("seq", "mp"), pairs)


def is_square():
    return lax.axis_size("seq") == 4 and lax.axis_size("mp") == 8


def distance_of(slot):
    if is_square():
        core = lax.rem(lax.axis_index("mp"), 2)
        return jnp.where(core == 0, slot, turned(slot))
    return slot


def swapped(chunks, swap=exchange_seq):
    return [chunks[0]] + [swap(chunks[k], k) for k in range(1, len(chunks))]


def group_of(cycle, member, chip):
    turn = (member + chip) % cycle
    return turned(turn) if cycle == 4 else turn


def my_place():
    rank = lax.axis_index("mp")
    return lax.axis_index("seq"), rank // 2, lax.rem(rank, 2)


def columns_at(first, width):
    return pl.ds(pl.multiple_of(first, width), width)


def pack_kernel(cycle, places, extra, q_ref, k_ref, v_ref, adj_any, cnt_any, *refs):
    refs, (adj_ref, cnt_ref, sems, more_sems) = refs[:-4], refs[-4:]
    outs = refs[-len(places) - extra:]
    rows, model = q_ref.shape
    width = model // cycle
    own, chip, _ = my_place()
    lists = [
        pltpu.make_async_copy(adj_any, adj_ref, more_sems.at[2]),
        pltpu.make_async_copy(cnt_any, cnt_ref, more_sems.at[3]),
    ]
    for copy in lists:
        copy.start()
    copies = []
    if width % 128 == 0:
        for place, out in zip(places, outs):
            group = group_of(cycle, lax.bitwise_xor(own, distance_of(place)), chip)
            for at, ref in enumerate((q_ref, k_ref, v_ref)):
                copies.append(
                    pltpu.make_async_copy(
                        ref.at[:, columns_at(group * width, width)],
                        out.at[at * rows:(at + 1) * rows, :],
                        sems.at[place, at],
                    )
                )
                copies[-1].start()
    for at in range(extra):
        copies.append(
            pltpu.make_async_copy(refs[at], outs[len(places) + at], more_sems.at[at])
        )
        copies[-1].start()
    for copy in lists:
        copy.wait()
    lines = lax.broadcasted_iota(jnp.int32, (META, width), 0)
    meta = jnp.where(lines == 0, 1, 0)
    for column, offset in enumerate(cycle_offsets):
        named = lax.rem(own - offset + 2 * cycle, cycle)
        meta = meta + jnp.where(
            (lines == distance_of(lax.bitwise_xor(own, named))) & (adj_ref[0, column] > 0), 1, 0
        )
    meta = jnp.where(lines == META - 1, cnt_ref[0, 0], meta).astype(f32).astype(bf16)
    for place, out in zip(places, outs):
        out[3 * rows:, :] = meta
        if width % 128:
            group = group_of(cycle, lax.bitwise_xor(own, distance_of(place)), chip)
            for other in range(cycle):
                @pl.when(group == other)
                def _():
                    for at, ref in enumerate((q_ref, k_ref, v_ref)):
                        out[at * rows:(at + 1) * rows, :] = ref[
                            :, other * width:(other + 1) * width
                        ]
    for copy in copies:
        copy.wait()


def hold_kernel(count, *refs):
    outs, sems = refs[-count - 1:-1], refs[-1]
    copies = [pltpu.make_async_copy(refs[at], outs[at], sems.at[at]) for at in range(count)]
    for copy in copies:
        copy.start()
    for copy in copies:
        copy.wait()


def hold(arrays, after):
    count = len(arrays)
    return pl.pallas_call(
        functools.partial(hold_kernel, count),
        out_shape=[jax.ShapeDtypeStruct(array.shape, array.dtype) for array in arrays],
        in_specs=[unread()] * (count + len(after)),
        out_specs=[vmem()] * count,
        scratch_shapes=[pltpu.SemaphoreType.DMA((count,))],
        compiler_params=params(2),
        cost_estimate=cost(1),
        name="hold",
    )(*arrays, *after)


def pack(cycle, places, tensors, extra=()):
    rows, model = tensors[0].shape
    width = model // cycle
    return pl.pallas_call(
        functools.partial(pack_kernel, cycle, places, len(extra)),
        out_shape=[jax.ShapeDtypeStruct((3 * rows + META, width), bf16)] * len(places)
        + [jax.ShapeDtypeStruct(array.shape, bf16) for array in extra],
        in_specs=[anywhere() if width % 128 == 0 else vmem()] * 3
        + [unread()] * 2
        + [anywhere()] * len(extra),
        out_specs=[vmem()] * (len(places) + len(extra)),
        scratch_shapes=[
            pltpu.SMEM(tensors[3].shape, jnp.int32),
            pltpu.SMEM(tensors[4].shape, jnp.int32),
            pltpu.SemaphoreType.DMA((cycle, 3)),
            pltpu.SemaphoreType.DMA((4,)),
        ],
        compiler_params=params(62),
        cost_estimate=cost(5),
        name="pack",
    )(*tensors, *extra)


def gather_kernel(cycle, *refs):
    chunks = refs[:cycle]
    q_all, k_all, v_all, k_t, v_t, bias = refs[-6:]
    rows = q_all.shape[0] // cycle
    for place in range(cycle):
        for at, part in enumerate((q_all, k_all, v_all)):
            part[place * rows:(place + 1) * rows, :] = chunks[place][at * rows:(at + 1) * rows, :]
    k_t[...] = k_all[...].astype(f32).T.astype(bf16)
    v_t[...] = v_all[...].astype(f32).T.astype(bf16)
    lines = lax.broadcasted_iota(jnp.int32, (rows, rows), 0).astype(f32)
    lists = [chunks[place][3 * rows:, :].astype(f32) for place in range(cycle)]
    for key_place in range(cycle):
        count = lists[key_place][META - 1:, :1]
        valid = lines < count
        for query_place in range(cycle):
            way = key_place ^ query_place
            times = lists[query_place][way:way + 1, :1]
            term = jnp.where(times > 0, jnp.log2(jnp.maximum(times, 1.0)), absent)
            bias[
                key_place * rows:(key_place + 1) * rows,
                query_place * rows:(query_place + 1) * rows,
            ] = jnp.where(valid, term, absent)


def gather(cycle, chunks, after=()):
    width = chunks[0].shape[1]
    rows = (chunks[0].shape[0] - META) // 3
    tokens = rows * cycle
    return pl.pallas_call(
        functools.partial(gather_kernel, cycle),
        out_shape=[jax.ShapeDtypeStruct((tokens, width), bf16)] * 3
        + [jax.ShapeDtypeStruct((width, tokens), bf16)] * 2
        + [jax.ShapeDtypeStruct((tokens, tokens), f32)],
        in_specs=[vmem()] * cycle + [unread()] * len(after),
        out_specs=[vmem()] * 6,
        compiler_params=params(8 if tokens <= 512 else 40),
        cost_estimate=cost(5),
        name="gather",
    )(*chunks, *after)


def head_tile(width):
    return min(128, width)


def only_head(tile, which):
    lanes = lax.broadcasted_iota(jnp.int32, tile.shape, 1)
    inside = (lanes >= which * HEAD_DIM) & (lanes < (which + 1) * HEAD_DIM)
    return jnp.where(inside, tile, jnp.zeros_like(tile))


def forward_kernel(query_tile, q_all, k_all, v_t, bias, *refs):
    outs = refs[:-2]
    att_t, lse = refs[-2:]
    tokens, width = q_all.shape
    tile = head_tile(width)
    for start in range(0, tokens, query_tile):
        span = slice(start, start + query_tile)
        for head in range(width // HEAD_DIM):
            at = head * HEAD_DIM // tile * tile
            which = (head * HEAD_DIM - at) // HEAD_DIM
            scores = dot_nt(
                k_all[:, at:at + tile], only_head(q_all[span, at:at + tile], which)
            )
            scores = scores * log2_scale + bias[:, span]
            largest = jnp.max(scores, axis=0, keepdims=True)
            expo = jnp.exp2(scores - largest)
            total = jnp.sum(expo, axis=0, keepdims=True)
            probs = (expo * (1.0 / total)).astype(bf16)
            lse[head:head + 1, span] = largest + jnp.log2(total)
            att_t[head * HEAD_DIM:(head + 1) * HEAD_DIM, span] = dot_nn(
                v_t[head * HEAD_DIM:(head + 1) * HEAD_DIM, :], probs
            )
    attended = att_t[...].T.astype(bf16)
    filled = 0
    for out in outs:
        out[...] = attended[filled:filled + out.shape[0], :]
        filled += out.shape[0]


def forward(cycle, together, q_all, k_all, v_t, bias):
    tokens, width = q_all.shape
    rows = tokens // cycle
    parts = cycle // together
    outs = pl.pallas_call(
        functools.partial(forward_kernel, min(tokens, 512)),
        out_shape=[jax.ShapeDtypeStruct((together * rows, width), bf16)] * parts
        + [
            jax.ShapeDtypeStruct((width, tokens), f32),
            jax.ShapeDtypeStruct((8, tokens), f32),
        ],
        in_specs=[vmem()] * 4,
        out_specs=[vmem()] * (parts + 2),
        compiler_params=params(16 if tokens <= 512 else 60),
        cost_estimate=cost(3),
        name="forward",
    )(q_all, k_all, v_t, bias)
    return outs[:parts], outs[parts], outs[parts + 1]


def backward_kernel(cycle, query_tile, grad_count, att_count, *refs):
    q_all, k_all, v_all, k_t, bias, att_t, lse = refs[:7]
    refs = refs[7:]
    grads = refs[:grad_count]
    attended = refs[grad_count:grad_count + att_count]
    outs = refs[-4 - cycle:-4]
    g_all, dq_t, dk, dv = refs[-4:]
    width = q_all.shape[1]
    tokens = q_all.shape[0]
    rows = tokens // cycle
    filled = 0
    for grad in grads:
        g_all[filled:filled + grad.shape[0], :] = grad[...]
        filled += grad.shape[0]
    tile = head_tile(width)
    g_t = g_all[...].astype(f32).T
    product = g_t * att_t[...].astype(bf16).astype(f32)
    for start in range(0, tokens, query_tile):
        span = slice(start, start + query_tile)
        for at in range(0, width, tile):
            dk_tile = dv_tile = None
            for which in range(tile // HEAD_DIM):
                low = at + which * HEAD_DIM
                head = low // HEAD_DIM
                delta = jnp.sum(product[low:low + HEAD_DIM, span], axis=0, keepdims=True)
                q_head = only_head(q_all[span, at:at + tile], which)
                g_head = only_head(g_all[span, at:at + tile], which)
                scores = dot_nt(k_all[:, at:at + tile], q_head)
                probs = jnp.exp2(
                    scores * log2_scale + bias[:, span] - lse[head:head + 1, span]
                )
                grad_probs = dot_nt(v_all[:, at:at + tile], g_head)
                grad_scores = (probs * (grad_probs - delta)).astype(bf16)
                dk_head = dot_nn(grad_scores, q_head)
                dv_head = dot_nn(probs.astype(bf16), g_head)
                dk_tile = dk_head if dk_tile is None else dk_tile + dk_head
                dv_tile = dv_head if dv_tile is None else dv_tile + dv_head
                dq_t[low:low + HEAD_DIM, span] = dot_nn(k_t[low:low + HEAD_DIM, :], grad_scores)
            if start == 0:
                dk[:, at:at + tile] = dk_tile
                dv[:, at:at + tile] = dv_tile
            else:
                dk[:, at:at + tile] += dk_tile
                dv[:, at:at + tile] += dv_tile
    dq = (dq_t[...] * score_scale).T.astype(bf16)
    for place in range(cycle):
        span = slice(place * rows, (place + 1) * rows)
        outs[place][:rows, :] = dq[span, :]
        outs[place][rows:2 * rows, :] = (dk[span, :] * score_scale).astype(bf16)
        outs[place][2 * rows:3 * rows, :] = dv[span, :].astype(bf16)
        if attended:
            outs[place][3 * rows:, :] = attended[place][...]


def backward(cycle, inputs, grads, attended, after):
    tokens, width = inputs[0].shape
    rows = tokens // cycle
    return pl.pallas_call(
        functools.partial(backward_kernel, cycle, min(tokens, 512), len(grads), len(attended)),
        out_shape=[jax.ShapeDtypeStruct(((4 if attended else 3) * rows, width), bf16)] * cycle,
        in_specs=[vmem()] * (len(inputs) + len(grads) + len(attended)) + [unread()] * len(after),
        out_specs=[vmem()] * cycle,
        scratch_shapes=[
            pltpu.VMEM((tokens, width), bf16),
            pltpu.VMEM((width, tokens), f32),
            pltpu.VMEM((tokens, width), f32),
            pltpu.VMEM((tokens, width), f32),
        ],
        compiler_params=params(16 if tokens <= 512 else 60),
        cost_estimate=cost(3),
        name="backward",
    )(*inputs, *grads, *attended, *after)


def fetch_rows(out_weight, distance, flip=False):
    cycle, count = lax.axis_size("seq"), lax.axis_size("mp")
    pairs = []
    for member in range(cycle):
        for rank in range(count):
            owner = 2 * group_of(cycle, member ^ distance(rank % 2), rank // 2)
            owner += (rank + flip) % 2
            pairs.append((member * count + owner, member * count + rank))
    return lax.ppermute(out_weight, ("seq", "mp"), pairs)


def with_other_core(half):
    return [half, exchange(half, "mp", 1)]


def both_halves(halves, core):
    mine, other = halves[0][...], halves[1][...]
    first = core == 0
    return jnp.concatenate([jnp.where(first, mine, other), jnp.where(first, other, mine)], axis=0)


def half_columns(halves, core, side):
    half = halves[0].shape[0]
    return columns_at((core if side == 0 else 1 - core) * half, half)


def near_kernel(up_ref, next_ref, *refs):
    halves = refs[:4]
    near, far = refs[-2:]
    rows = up_ref.shape[0]
    _, _, core = my_place()
    for group, out in enumerate((far, near)):
        for side in range(2):
            weight = halves[2 * (1 - group) + side]
            for block, ref in enumerate((up_ref, next_ref)):
                out[block * rows:(block + 1) * rows, half_columns(halves, core, side)] = dot_nt(
                    ref[...], weight[...]
                ).astype(bf16)


def near_grads(upstream, next_upstream, halves, after):
    rows, width = upstream.shape[0], 2 * halves[0].shape[0]
    return pl.pallas_call(
        near_kernel,
        out_shape=[jax.ShapeDtypeStruct((2 * rows, width), bf16)] * 2,
        in_specs=[vmem()] * 6 + [unread()] * len(after),
        out_specs=[vmem()] * 2,
        compiler_params=params(8),
        cost_estimate=cost(1),
        name="near_grads",
    )(upstream, next_upstream, *halves, *after)


def mix_kernel(near_ref, far_ref, *refs):
    halves = refs[:4]
    own, other = refs[-2:]
    rows = own.shape[0]
    _, _, core = my_place()
    total = None
    for group, ref in enumerate((near_ref, far_ref)):
        for side in range(2):
            term = dot_nn(
                ref[:, half_columns(halves, core, side)], halves[2 * group + side][...]
            )
            total = term if total is None else total + term
    own[...] = total[:rows, :]
    other[...] = total[rows:, :].astype(bf16)


def mix(near, far, halves, after):
    rows, model = near.shape[0] // 2, halves[0].shape[1]
    return pl.pallas_call(
        mix_kernel,
        out_shape=[
            jax.ShapeDtypeStruct((rows, model), f32),
            jax.ShapeDtypeStruct((rows, model), bf16),
        ],
        in_specs=[vmem()] * 6 + [unread()] * len(after),
        out_specs=[vmem()] * 2,
        compiler_params=params(8),
        cost_estimate=cost(1),
        name="mix",
    )(near, far, *halves, *after)


def grad_kernel(cycle, up_ref, *refs):
    _, _, core = my_place()
    outs = refs[2 * cycle:]
    for place in range(cycle):
        rows = both_halves(refs[2 * place:2 * place + 2], core)
        outs[place][...] = dot_nt(up_ref[...], rows).astype(bf16)


def project_grad(cycle, upstream, halves):
    rows, model = upstream.shape
    return pl.pallas_call(
        functools.partial(grad_kernel, cycle),
        out_shape=[jax.ShapeDtypeStruct((rows, model // cycle), bf16)] * cycle,
        in_specs=[vmem()] * (1 + 2 * cycle),
        out_specs=[vmem()] * cycle,
        compiler_params=params(8),
        name="project_grad",
    )(upstream, *halves)


def place_columns(chunks, outs, sems):
    cycle = len(chunks)
    rows, model = outs[0].shape
    width = model // cycle
    own, chip, _ = my_place()
    copies = []
    for place in range(cycle):
        group = group_of(cycle, lax.bitwise_xor(own, distance_of(place)), chip)
        if width % 128 == 0:
            for at, out in enumerate(outs):
                copies.append(
                    pltpu.make_async_copy(
                        chunks[place].at[at * rows:(at + 1) * rows, :],
                        out.at[:, columns_at(group * width, width)],
                        sems.at[place, at],
                    )
                )
                copies[-1].start()
        else:
            for other in range(cycle):
                @pl.when(group == other)
                def _():
                    for at, out in enumerate(outs):
                        out[:, other * width:(other + 1) * width] = chunks[place][
                            at * rows:(at + 1) * rows, :
                        ]
    return copies


def finish_kernel(cycle, *refs):
    chunks = refs[:cycle]
    mixed, *outs = refs[-5:-1]
    copies = place_columns(chunks, outs, refs[-1])
    rows = mixed.shape[0]
    if len(refs) == cycle + 7:
        mine, landed = refs[cycle:cycle + 2]
        mixed[...] = (mine[...] + landed[...].astype(f32)).astype(bf16)
    else:
        halves = refs[cycle:3 * cycle]
        _, _, core = my_place()
        total = None
        for place in range(cycle):
            weight = both_halves(halves[2 * place:2 * place + 2], core)
            term = dot_nn(chunks[place][3 * rows:, :], weight)
            total = term if total is None else total + term
        mixed[...] = total.astype(bf16)
    for copy in copies:
        copy.wait()


def finish(cycle, rows, chunks, others):
    model = chunks[0].shape[1] * cycle
    aligned = model // cycle % 128 == 0
    return pl.pallas_call(
        functools.partial(finish_kernel, cycle),
        out_shape=[jax.ShapeDtypeStruct((rows, model), bf16)] * 4,
        in_specs=[vmem()] * (cycle + len(others)),
        out_specs=[vmem()] + [anywhere() if aligned else vmem()] * 3,
        scratch_shapes=[pltpu.SemaphoreType.DMA((cycle, 3))],
        compiler_params=params(8),
        name="finish",
    )(*chunks, *others)


def local(queries, keys, values, out_weight, upstream, adjacency, counts):
    cycle = lax.axis_size("seq")
    rows = queries.shape[0]
    tensors = (queries, keys, values, adjacency, counts.reshape(1, 1))
    if is_square():
        return square(cycle, rows, tensors, out_weight, upstream)
    chunks = swapped(pack(cycle, range(cycle), tensors))
    halves = []
    for place in range(cycle):
        halves += with_other_core(fetch_rows(out_weight, lambda core: place))
    q_all, k_all, v_all, k_t, v_t, bias = gather(cycle, chunks)
    attended, att_t, lse = forward(cycle, 1, q_all, k_all, v_t, bias)
    grads = swapped(project_grad(cycle, upstream, halves))
    inputs = (q_all, k_all, v_all, k_t, bias, att_t, lse)
    terms = swapped(backward(cycle, inputs, grads, attended, []))
    return tuple(finish(cycle, rows, terms, halves))


def square(cycle, rows, tensors, out_weight, upstream):
    *chunks, out_weight = pack(cycle, range(cycle), tensors, (out_weight,))
    first = fetch_rows(out_weight, lambda core: 0)
    out_weight, upstream = hold((out_weight, upstream), [first])
    chunks = swapped(chunks, exchange_slot)
    next_upstream = exchange_slot(upstream, 1)
    second = [
        fetch_rows(out_weight, lambda core: turned(2) if core else 2, flip) for flip in (False, True)
    ]
    halves = with_other_core(first) + second
    q_all, k_all, v_all, k_t, v_t, bias = gather(cycle, chunks, [upstream])
    (near_att, far_att), att_t, lse = forward(cycle, 2, q_all, k_all, v_t, bias)
    far_att = exchange_slot(far_att, 2)
    near, far = near_grads(upstream, next_upstream, halves, [lse])
    grads = [near, exchange_slot(far, 2)]
    own_mixed, next_mixed = mix(near_att, far_att, halves, [far])
    inputs = (q_all, k_all, v_all, k_t, bias, att_t, lse)
    terms = backward(cycle, inputs, grads, [], [next_mixed])
    next_mixed = exchange_slot(next_mixed, 1)
    return tuple(
        finish(cycle, rows, swapped(terms, exchange_slot), [own_mixed, next_mixed])
    )


def solution(mesh):
    tokens = P(("seq", "mp"), None)
    return jax.shard_map(
        local,
        mesh=mesh,
        in_specs=(tokens, tokens, tokens, P("mp", None), tokens, tokens, P(("seq", "mp"))),
        out_specs=(tokens,) * 4,
        check_vma=False,
    )
```

```python
import functools

import jax
import jax.numpy as jnp
from jax import lax
from jax.experimental import pallas as pl
from jax.experimental.pallas import tpu as pltpu
from jax.sharding import PartitionSpec as P

HEADS = 16
HEAD_DIM = 64
META = 32

score_scale = 0.125
log2_scale = 0.125 * 1.4426950408889634
cycle_offsets = (1, -1, 2, -2)
absent = -1e30
bf16 = jnp.bfloat16
f32 = jnp.float32


def dot_nn(a, b):
    return lax.dot_general(a, b, (((1,), (0,)), ((), ())), preferred_element_type=f32)


def dot_nt(a, b):
    return lax.dot_general(a, b, (((1,), (1,)), ((), ())), preferred_element_type=f32)


def vmem():
    return pl.BlockSpec(memory_space=pltpu.VMEM)


def params(mib):
    return pltpu.CompilerParams(vmem_limit_bytes=int(mib * 1024) * 1024)


def unread():
    return pl.BlockSpec(memory_space=pl.ANY)


def anywhere():
    return pl.BlockSpec(memory_space=pltpu.HBM)


def cost(micros):
    return pl.CostEstimate(flops=int(micros * 1e9), bytes_accessed=0, transcendentals=0)


def exchange(value, axis, distance):
    count = lax.axis_size(axis)
    return lax.ppermute(value, axis, [(i, i ^ distance) for i in range(count)])


def turned(distance):
    return distance ^ (((distance ^ (distance >> 1)) & 1) * 3)


def is_square():
    return lax.axis_size("seq") == 4 and lax.axis_size("mp") == 8


def swapped(chunks):
    return [chunks[0]] + [exchange(chunks[k], "seq", k) for k in range(1, len(chunks))]


def group_of(cycle, member, chip):
    turn = (member + chip) % cycle
    return turned(turn) if cycle == 4 else turn


def my_place():
    rank = lax.axis_index("mp")
    return lax.axis_index("seq"), rank // 2, lax.rem(rank, 2)


def columns_at(first, width):
    return pl.ds(pl.multiple_of(first, width), width)


def pack_kernel(cycle, places, q_ref, k_ref, v_ref, adj_any, cnt_any, *refs):
    refs, (adj_ref, cnt_ref, sems, more_sems) = refs[:-4], refs[-4:]
    *outs, word = refs
    word[...] = jnp.zeros(word.shape, word.dtype)
    rows, model = q_ref.shape
    width = model // cycle
    own, chip, _ = my_place()
    lists = [
        pltpu.make_async_copy(adj_any, adj_ref, more_sems.at[0]),
        pltpu.make_async_copy(cnt_any, cnt_ref, more_sems.at[1]),
    ]
    for copy in lists:
        copy.start()
    copies = []
    if width % 128 == 0:
        for place, out in zip(places, outs):
            group = group_of(cycle, lax.bitwise_xor(own, place), chip)
            for at, ref in enumerate((q_ref, k_ref, v_ref)):
                copies.append(
                    pltpu.make_async_copy(
                        ref.at[:, columns_at(group * width, width)],
                        out.at[at * rows:(at + 1) * rows, :],
                        sems.at[place, at],
                    )
                )
                copies[-1].start()
    for copy in lists:
        copy.wait()
    lines = lax.broadcasted_iota(jnp.int32, (META, width), 0)
    meta = jnp.where(lines == 0, 1, 0)
    for column, offset in enumerate(cycle_offsets):
        named = lax.rem(own - offset + 2 * cycle, cycle)
        meta = meta + jnp.where(
            (lines == lax.bitwise_xor(own, named)) & (adj_ref[0, column] > 0), 1, 0
        )
    meta = jnp.where(lines == META - 1, cnt_ref[0, 0], meta).astype(f32).astype(bf16)
    for place, out in zip(places, outs):
        out[3 * rows:, :] = meta
        if width % 128:
            group = group_of(cycle, lax.bitwise_xor(own, place), chip)
            for other in range(cycle):
                @pl.when(group == other)
                def _():
                    for at, ref in enumerate((q_ref, k_ref, v_ref)):
                        out[at * rows:(at + 1) * rows, :] = ref[
                            :, other * width:(other + 1) * width
                        ]
    for copy in copies:
        copy.wait()


def hold_kernel(count, *refs):
    outs, sems = refs[-count - 1:-1], refs[-1]
    copies = [pltpu.make_async_copy(refs[at], outs[at], sems.at[at]) for at in range(count)]
    for copy in copies:
        copy.start()
    for copy in copies:
        copy.wait()


def hold(arrays, after):
    count = len(arrays)
    return pl.pallas_call(
        functools.partial(hold_kernel, count),
        out_shape=[jax.ShapeDtypeStruct(array.shape, array.dtype) for array in arrays],
        in_specs=[unread()] * (count + len(after)),
        out_specs=[vmem()] * count,
        scratch_shapes=[pltpu.SemaphoreType.DMA((count,))],
        compiler_params=params(2),
        cost_estimate=cost(1),
        name="hold",
    )(*arrays, *after)


def pack(cycle, places, tensors):
    rows, model = tensors[0].shape
    width = model // cycle
    return pl.pallas_call(
        functools.partial(pack_kernel, cycle, places),
        out_shape=[jax.ShapeDtypeStruct((3 * rows + META, width), bf16)] * len(places)
        + [jax.ShapeDtypeStruct((16, 128), bf16)],
        in_specs=[anywhere() if width % 128 == 0 else vmem()] * 3
        + [unread()] * 2,
        out_specs=[vmem()] * (len(places) + 1),
        scratch_shapes=[
            pltpu.SMEM(tensors[3].shape, jnp.int32),
            pltpu.SMEM(tensors[4].shape, jnp.int32),
            pltpu.SemaphoreType.DMA((cycle, 3)),
            pltpu.SemaphoreType.DMA((2,)),
        ],
        compiler_params=params(62),
        cost_estimate=cost(5),
        name="pack",
    )(*tensors)


def gather_kernel(cycle, *refs):
    chunks = refs[:cycle]
    q_all, k_all, v_all, k_t, v_t, bias = refs[-6:]
    rows = q_all.shape[0] // cycle
    for place in range(cycle):
        for at, part in enumerate((q_all, k_all, v_all)):
            part[place * rows:(place + 1) * rows, :] = chunks[place][at * rows:(at + 1) * rows, :]
    k_t[...] = k_all[...].astype(f32).T.astype(bf16)
    v_t[...] = v_all[...].astype(f32).T.astype(bf16)
    lines = lax.broadcasted_iota(jnp.int32, (rows, rows), 0).astype(f32)
    lists = [chunks[place][3 * rows:, :].astype(f32) for place in range(cycle)]
    for key_place in range(cycle):
        count = lists[key_place][META - 1:, :1]
        valid = lines < count
        for query_place in range(cycle):
            way = key_place ^ query_place
            times = lists[query_place][way:way + 1, :1]
            term = jnp.where(times > 0, jnp.log2(jnp.maximum(times, 1.0)), absent)
            bias[
                key_place * rows:(key_place + 1) * rows,
                query_place * rows:(query_place + 1) * rows,
            ] = jnp.where(valid, term, absent)


def gather(cycle, chunks, after=()):
    width = chunks[0].shape[1]
    rows = (chunks[0].shape[0] - META) // 3
    tokens = rows * cycle
    return pl.pallas_call(
        functools.partial(gather_kernel, cycle),
        out_shape=[jax.ShapeDtypeStruct((tokens, width), bf16)] * 3
        + [jax.ShapeDtypeStruct((width, tokens), bf16)] * 2
        + [jax.ShapeDtypeStruct((tokens, tokens), f32)],
        in_specs=[vmem()] * cycle + [unread()] * len(after),
        out_specs=[vmem()] * 6,
        compiler_params=params(8 if tokens <= 512 else 40),
        cost_estimate=cost(5),
        name="gather",
    )(*chunks, *after)


def head_tile(width):
    return min(128, width)


def only_head(tile, which):
    lanes = lax.broadcasted_iota(jnp.int32, tile.shape, 1)
    inside = (lanes >= which * HEAD_DIM) & (lanes < (which + 1) * HEAD_DIM)
    return jnp.where(inside, tile, jnp.zeros_like(tile))


def forward_kernel(query_tile, q_all, k_all, v_t, bias, *refs):
    outs = refs[:-2]
    att_t, lse = refs[-2:]
    tokens, width = q_all.shape
    tile = head_tile(width)
    for start in range(0, tokens, query_tile):
        span = slice(start, start + query_tile)
        for head in range(width // HEAD_DIM):
            at = head * HEAD_DIM // tile * tile
            which = (head * HEAD_DIM - at) // HEAD_DIM
            scores = dot_nt(
                k_all[:, at:at + tile], only_head(q_all[span, at:at + tile], which)
            )
            scores = scores * log2_scale + bias[:, span]
            largest = jnp.max(scores, axis=0, keepdims=True)
            expo = jnp.exp2(scores - largest)
            total = jnp.sum(expo, axis=0, keepdims=True)
            probs = (expo * (1.0 / total)).astype(bf16)
            lse[head:head + 1, span] = largest + jnp.log2(total)
            att_t[head * HEAD_DIM:(head + 1) * HEAD_DIM, span] = dot_nn(
                v_t[head * HEAD_DIM:(head + 1) * HEAD_DIM, :], probs
            )
    attended = att_t[...].T.astype(bf16)
    filled = 0
    for out in outs:
        out[...] = attended[filled:filled + out.shape[0], :]
        filled += out.shape[0]


def forward(cycle, together, q_all, k_all, v_t, bias):
    tokens, width = q_all.shape
    rows = tokens // cycle
    parts = cycle // together
    outs = pl.pallas_call(
        functools.partial(forward_kernel, min(tokens, 512)),
        out_shape=[jax.ShapeDtypeStruct((together * rows, width), bf16)] * parts
        + [
            jax.ShapeDtypeStruct((width, tokens), f32),
            jax.ShapeDtypeStruct((8, tokens), f32),
        ],
        in_specs=[vmem()] * 4,
        out_specs=[vmem()] * (parts + 2),
        compiler_params=params(16 if tokens <= 512 else 60),
        cost_estimate=cost(3),
        name="forward",
    )(q_all, k_all, v_t, bias)
    return outs[:parts], outs[parts], outs[parts + 1]


def backward_kernel(cycle, query_tile, grad_count, att_count, *refs):
    q_all, k_all, v_all, k_t, bias, att_t, lse = refs[:7]
    refs = refs[7:]
    grads = refs[:grad_count]
    attended = refs[grad_count:grad_count + att_count]
    outs = refs[-4 - cycle:-4]
    g_all, dq_t, dk, dv = refs[-4:]
    width = q_all.shape[1]
    tokens = q_all.shape[0]
    rows = tokens // cycle
    filled = 0
    for grad in grads:
        g_all[filled:filled + grad.shape[0], :] = grad[...]
        filled += grad.shape[0]
    tile = head_tile(width)
    g_t = g_all[...].astype(f32).T
    product = g_t * att_t[...].astype(bf16).astype(f32)
    for start in range(0, tokens, query_tile):
        span = slice(start, start + query_tile)
        for at in range(0, width, tile):
            dk_tile = dv_tile = None
            for which in range(tile // HEAD_DIM):
                low = at + which * HEAD_DIM
                head = low // HEAD_DIM
                delta = jnp.sum(product[low:low + HEAD_DIM, span], axis=0, keepdims=True)
                q_head = only_head(q_all[span, at:at + tile], which)
                g_head = only_head(g_all[span, at:at + tile], which)
                scores = dot_nt(k_all[:, at:at + tile], q_head)
                probs = jnp.exp2(
                    scores * log2_scale + bias[:, span] - lse[head:head + 1, span]
                )
                grad_probs = dot_nt(v_all[:, at:at + tile], g_head)
                grad_scores = (probs * (grad_probs - delta)).astype(bf16)
                dk_head = dot_nn(grad_scores, q_head)
                dv_head = dot_nn(probs.astype(bf16), g_head)
                dk_tile = dk_head if dk_tile is None else dk_tile + dk_head
                dv_tile = dv_head if dv_tile is None else dv_tile + dv_head
                dq_t[low:low + HEAD_DIM, span] = dot_nn(k_t[low:low + HEAD_DIM, :], grad_scores)
            if start == 0:
                dk[:, at:at + tile] = dk_tile
                dv[:, at:at + tile] = dv_tile
            else:
                dk[:, at:at + tile] += dk_tile
                dv[:, at:at + tile] += dv_tile
    dq = (dq_t[...] * score_scale).T.astype(bf16)
    for place in range(cycle):
        span = slice(place * rows, (place + 1) * rows)
        outs[place][:rows, :] = dq[span, :]
        outs[place][rows:2 * rows, :] = (dk[span, :] * score_scale).astype(bf16)
        outs[place][2 * rows:3 * rows, :] = dv[span, :].astype(bf16)
        if attended:
            outs[place][3 * rows:, :] = attended[place][...]


def backward(cycle, inputs, grads, attended, after):
    tokens, width = inputs[0].shape
    rows = tokens // cycle
    return pl.pallas_call(
        functools.partial(backward_kernel, cycle, min(tokens, 512), len(grads), len(attended)),
        out_shape=[jax.ShapeDtypeStruct(((4 if attended else 3) * rows, width), bf16)] * cycle,
        in_specs=[vmem()] * (len(inputs) + len(grads) + len(attended)) + [unread()] * len(after),
        out_specs=[vmem()] * cycle,
        scratch_shapes=[
            pltpu.VMEM((tokens, width), bf16),
            pltpu.VMEM((width, tokens), f32),
            pltpu.VMEM((tokens, width), f32),
            pltpu.VMEM((tokens, width), f32),
        ],
        compiler_params=params(16 if tokens <= 512 else 60),
        cost_estimate=cost(3),
        name="backward",
    )(*inputs, *grads, *attended, *after)


def fetch_rows(out_weight, place):
    cycle, count = lax.axis_size("seq"), lax.axis_size("mp")
    pairs = []
    for member in range(cycle):
        for rank in range(count):
            owner = 2 * group_of(cycle, member ^ place, rank // 2) + rank % 2
            pairs.append((member * count + owner, member * count + rank))
    return lax.ppermute(out_weight, ("seq", "mp"), pairs)


def with_other_core(half):
    return [half, exchange(half, "mp", 1)]


def both_halves(halves, core):
    mine, other = halves[0][...], halves[1][...]
    first = core == 0
    return jnp.concatenate([jnp.where(first, mine, other), jnp.where(first, other, mine)], axis=0)


def half_columns(halves, core, side):
    half = halves[0].shape[0]
    return columns_at((core if side == 0 else 1 - core) * half, half)


def near_kernel(up_ref, next_ref, *refs):
    halves = refs[:4]
    near, far = refs[-2:]
    rows = up_ref.shape[0]
    _, _, core = my_place()
    for group, out in enumerate((far, near)):
        for side in range(2):
            weight = halves[2 * (1 - group) + side]
            for block, ref in enumerate((up_ref, next_ref)):
                out[block * rows:(block + 1) * rows, half_columns(halves, core, side)] = dot_nt(
                    ref[...], weight[...]
                ).astype(bf16)


def near_grads(upstream, next_upstream, halves, after):
    rows, width = upstream.shape[0], 2 * halves[0].shape[0]
    return pl.pallas_call(
        near_kernel,
        out_shape=[jax.ShapeDtypeStruct((2 * rows, width), bf16)] * 2,
        in_specs=[vmem()] * 6 + [unread()] * len(after),
        out_specs=[vmem()] * 2,
        compiler_params=params(8),
        cost_estimate=cost(1),
        name="near_grads",
    )(upstream, next_upstream, *halves, *after)


def mix_kernel(near_ref, far_ref, *refs):
    halves = refs[:4]
    own, other = refs[-2:]
    rows = own.shape[0]
    _, _, core = my_place()
    total = None
    for group, ref in enumerate((near_ref, far_ref)):
        for side in range(2):
            term = dot_nn(
                ref[:, half_columns(halves, core, side)], halves[2 * group + side][...]
            )
            total = term if total is None else total + term
    own[...] = total[:rows, :]
    other[...] = total[rows:, :].astype(bf16)


def mix(near, far, halves, after):
    rows, model = near.shape[0] // 2, halves[0].shape[1]
    return pl.pallas_call(
        mix_kernel,
        out_shape=[
            jax.ShapeDtypeStruct((rows, model), f32),
            jax.ShapeDtypeStruct((rows, model), bf16),
        ],
        in_specs=[vmem()] * 6 + [unread()] * len(after),
        out_specs=[vmem()] * 2,
        compiler_params=params(8),
        cost_estimate=cost(1),
        name="mix",
    )(near, far, *halves, *after)


def grad_kernel(cycle, up_ref, *refs):
    _, _, core = my_place()
    outs = refs[2 * cycle:]
    for place in range(cycle):
        rows = both_halves(refs[2 * place:2 * place + 2], core)
        outs[place][...] = dot_nt(up_ref[...], rows).astype(bf16)


def project_grad(cycle, upstream, halves):
    rows, model = upstream.shape
    return pl.pallas_call(
        functools.partial(grad_kernel, cycle),
        out_shape=[jax.ShapeDtypeStruct((rows, model // cycle), bf16)] * cycle,
        in_specs=[vmem()] * (1 + 2 * cycle),
        out_specs=[vmem()] * cycle,
        compiler_params=params(8),
        name="project_grad",
    )(upstream, *halves)


def place_columns(chunks, outs, sems):
    cycle = len(chunks)
    rows, model = outs[0].shape
    width = model // cycle
    own, chip, _ = my_place()
    copies = []
    for place in range(cycle):
        group = group_of(cycle, lax.bitwise_xor(own, place), chip)
        if width % 128 == 0:
            for at, out in enumerate(outs):
                copies.append(
                    pltpu.make_async_copy(
                        chunks[place].at[at * rows:(at + 1) * rows, :],
                        out.at[:, columns_at(group * width, width)],
                        sems.at[place, at],
                    )
                )
                copies[-1].start()
        else:
            for other in range(cycle):
                @pl.when(group == other)
                def _():
                    for at, out in enumerate(outs):
                        out[:, other * width:(other + 1) * width] = chunks[place][
                            at * rows:(at + 1) * rows, :
                        ]
    return copies


def finish_kernel(cycle, *refs):
    chunks = refs[:cycle]
    mixed, *outs = refs[-5:-1]
    copies = place_columns(chunks, outs, refs[-1])
    rows = mixed.shape[0]
    if len(refs) == cycle + 7:
        mine, landed = refs[cycle:cycle + 2]
        mixed[...] = (mine[...] + landed[...].astype(f32)).astype(bf16)
    else:
        halves = refs[cycle:3 * cycle]
        _, _, core = my_place()
        total = None
        for place in range(cycle):
            weight = both_halves(halves[2 * place:2 * place + 2], core)
            term = dot_nn(chunks[place][3 * rows:, :], weight)
            total = term if total is None else total + term
        mixed[...] = total.astype(bf16)
    for copy in copies:
        copy.wait()


def finish(cycle, rows, chunks, others):
    model = chunks[0].shape[1] * cycle
    aligned = model // cycle % 128 == 0
    return pl.pallas_call(
        functools.partial(finish_kernel, cycle),
        out_shape=[jax.ShapeDtypeStruct((rows, model), bf16)] * 4,
        in_specs=[vmem()] * (cycle + len(others)),
        out_specs=[vmem()] + [anywhere() if aligned else vmem()] * 3,
        scratch_shapes=[pltpu.SemaphoreType.DMA((cycle, 3))],
        compiler_params=params(8),
        name="finish",
    )(*chunks, *others)


def local(queries, keys, values, out_weight, upstream, adjacency, counts):
    cycle = lax.axis_size("seq")
    rows = queries.shape[0]
    tensors = (queries, keys, values, adjacency, counts.reshape(1, 1))
    if is_square():
        return square(cycle, rows, tensors, out_weight, upstream)
    chunks = swapped(pack(cycle, range(cycle), tensors)[:cycle])
    halves = []
    for place in range(cycle):
        halves += with_other_core(fetch_rows(out_weight, place))
    q_all, k_all, v_all, k_t, v_t, bias = gather(cycle, chunks)
    attended, att_t, lse = forward(cycle, 1, q_all, k_all, v_t, bias)
    grads = swapped(project_grad(cycle, upstream, halves))
    inputs = (q_all, k_all, v_all, k_t, bias, att_t, lse)
    terms = swapped(backward(cycle, inputs, grads, attended, []))
    return tuple(finish(cycle, rows, terms, halves))


def square(cycle, rows, tensors, out_weight, upstream):
    chunks = list(pack(cycle, range(cycle), tensors))
    word = exchange(chunks.pop(), "mp", 1)
    chunks = swapped(chunks)
    out_weight, upstream = hold((out_weight, upstream), [word])
    fetched = [fetch_rows(out_weight, place) for place in (0, 2)]
    next_upstream = exchange(upstream, "seq", 1)
    q_all, k_all, v_all, k_t, v_t, bias = gather(cycle, chunks, [upstream])
    (near_att, far_att), att_t, lse = forward(cycle, 2, q_all, k_all, v_t, bias)
    far_att = exchange(far_att, "seq", 2)
    first, second = hold(fetched, [lse])
    halves = with_other_core(first) + with_other_core(second)
    near, far = near_grads(upstream, next_upstream, halves, [])
    grads = [near, exchange(far, "seq", 2)]
    own_mixed, next_mixed = mix(near_att, far_att, halves, [far])
    inputs = (q_all, k_all, v_all, k_t, bias, att_t, lse)
    terms = backward(cycle, inputs, grads, [], [next_mixed])
    next_mixed = exchange(next_mixed, "seq", 1)
    return tuple(finish(cycle, rows, swapped(terms), [own_mixed, next_mixed]))


def solution(mesh):
    tokens = P(("seq", "mp"), None)
    return jax.shard_map(
        local,
        mesh=mesh,
        in_specs=(tokens, tokens, tokens, P("mp", None), tokens, tokens, P(("seq", "mp"))),
        out_specs=(tokens,) * 4,
        check_vma=False,
    )
```

```python
import functools

import jax
import jax.numpy as jnp
from jax import lax
from jax.experimental import pallas as pl
from jax.experimental.pallas import tpu as pltpu
from jax.sharding import PartitionSpec as P

HEADS = 16
HEAD_DIM = 64
META = 32

score_scale = 0.125
log2_scale = 0.125 * 1.4426950408889634
cycle_offsets = (1, -1, 2, -2)
absent = -1e30
bf16 = jnp.bfloat16
f32 = jnp.float32


def dot_nn(a, b):
    return lax.dot_general(a, b, (((1,), (0,)), ((), ())), preferred_element_type=f32)


def dot_nt(a, b):
    return lax.dot_general(a, b, (((1,), (1,)), ((), ())), preferred_element_type=f32)


def vmem():
    return pl.BlockSpec(memory_space=pltpu.VMEM)


def params(mib):
    return pltpu.CompilerParams(vmem_limit_bytes=int(mib * 1024) * 1024)


def unread():
    return pl.BlockSpec(memory_space=pl.ANY)


def anywhere():
    return pl.BlockSpec(memory_space=pltpu.HBM)


def cost(micros):
    return pl.CostEstimate(flops=int(micros * 1e9), bytes_accessed=0, transcendentals=0)


def exchange(value, axis, distance):
    count = lax.axis_size(axis)
    return lax.ppermute(value, axis, [(i, i ^ distance) for i in range(count)])


def exchange_seq(value, distance):
    return exchange(value, "seq", distance)


def turned(distance):
    return distance ^ (((distance ^ (distance >> 1)) & 1) * 3)


def exchange_slot(value, slot):
    count = lax.axis_size("mp")
    pairs = []
    for member in range(lax.axis_size("seq")):
        for rank in range(count):
            partner = member ^ (turned(slot) if rank % 2 else slot)
            pairs.append((member * count + rank, partner * count + rank))
    return lax.ppermute(value, ("seq", "mp"), pairs)


def is_square():
    return lax.axis_size("seq") == 4 and lax.axis_size("mp") == 8


def distance_of(slot):
    if is_square():
        core = lax.rem(lax.axis_index("mp"), 2)
        return jnp.where(core == 0, slot, turned(slot))
    return slot


def swapped(chunks, swap=exchange_seq):
    return [chunks[0]] + [swap(chunks[k], k) for k in range(1, len(chunks))]


def group_of(cycle, member, chip):
    turn = (member + chip) % cycle
    return turned(turn) if cycle == 4 else turn


def my_place():
    rank = lax.axis_index("mp")
    return lax.axis_index("seq"), rank // 2, lax.rem(rank, 2)


def columns_at(first, width):
    return pl.ds(pl.multiple_of(first, width), width)


def pack_kernel(cycle, places, q_ref, k_ref, v_ref, adj_any, cnt_any, *refs):
    refs, (adj_ref, cnt_ref, sems, more_sems) = refs[:-4], refs[-4:]
    outs = refs
    rows, model = q_ref.shape
    width = model // cycle
    own, chip, _ = my_place()
    lists = [
        pltpu.make_async_copy(adj_any, adj_ref, more_sems.at[0]),
        pltpu.make_async_copy(cnt_any, cnt_ref, more_sems.at[1]),
    ]
    for copy in lists:
        copy.start()
    copies = []
    if width % 128 == 0:
        for place, out in zip(places, outs):
            group = group_of(cycle, lax.bitwise_xor(own, distance_of(place)), chip)
            for at, ref in enumerate((q_ref, k_ref, v_ref)):
                copies.append(
                    pltpu.make_async_copy(
                        ref.at[:, columns_at(group * width, width)],
                        out.at[at * rows:(at + 1) * rows, :],
                        sems.at[place, at],
                    )
                )
                copies[-1].start()
    for copy in lists:
        copy.wait()
    lines = lax.broadcasted_iota(jnp.int32, (META, width), 0)
    meta = jnp.where(lines == 0, 1, 0)
    for column, offset in enumerate(cycle_offsets):
        named = lax.rem(own - offset + 2 * cycle, cycle)
        meta = meta + jnp.where(
            (lines == distance_of(lax.bitwise_xor(own, named))) & (adj_ref[0, column] > 0), 1, 0
        )
    meta = jnp.where(lines == META - 1, cnt_ref[0, 0], meta).astype(f32).astype(bf16)
    for place, out in zip(places, outs):
        out[3 * rows:, :] = meta
        if width % 128:
            group = group_of(cycle, lax.bitwise_xor(own, distance_of(place)), chip)
            for other in range(cycle):
                @pl.when(group == other)
                def _():
                    for at, ref in enumerate((q_ref, k_ref, v_ref)):
                        out[at * rows:(at + 1) * rows, :] = ref[
                            :, other * width:(other + 1) * width
                        ]
    for copy in copies:
        copy.wait()


def hold_kernel(count, *refs):
    outs, sems = refs[-count - 1:-1], refs[-1]
    copies = [pltpu.make_async_copy(refs[at], outs[at], sems.at[at]) for at in range(count)]
    for copy in copies:
        copy.start()
    for copy in copies:
        copy.wait()


def hold(arrays, after):
    count = len(arrays)
    return pl.pallas_call(
        functools.partial(hold_kernel, count),
        out_shape=[jax.ShapeDtypeStruct(array.shape, array.dtype) for array in arrays],
        in_specs=[unread()] * (count + len(after)),
        out_specs=[vmem()] * count,
        scratch_shapes=[pltpu.SemaphoreType.DMA((count,))],
        compiler_params=params(2),
        cost_estimate=cost(1),
        name="hold",
    )(*arrays, *after)


def pack(cycle, places, tensors):
    rows, model = tensors[0].shape
    width = model // cycle
    return pl.pallas_call(
        functools.partial(pack_kernel, cycle, places),
        out_shape=[jax.ShapeDtypeStruct((3 * rows + META, width), bf16)] * len(places),
        in_specs=[anywhere() if width % 128 == 0 else vmem()] * 3
        + [unread()] * 2,
        out_specs=[vmem()] * len(places),
        scratch_shapes=[
            pltpu.SMEM(tensors[3].shape, jnp.int32),
            pltpu.SMEM(tensors[4].shape, jnp.int32),
            pltpu.SemaphoreType.DMA((cycle, 3)),
            pltpu.SemaphoreType.DMA((2,)),
        ],
        compiler_params=params(62),
        cost_estimate=cost(5),
        name="pack",
    )(*tensors)


def gather_kernel(cycle, *refs):
    chunks = refs[:cycle]
    q_all, k_all, v_all, k_t, v_t, bias = refs[-6:]
    rows = q_all.shape[0] // cycle
    for place in range(cycle):
        for at, part in enumerate((q_all, k_all, v_all)):
            part[place * rows:(place + 1) * rows, :] = chunks[place][at * rows:(at + 1) * rows, :]
    k_t[...] = k_all[...].astype(f32).T.astype(bf16)
    v_t[...] = v_all[...].astype(f32).T.astype(bf16)
    lines = lax.broadcasted_iota(jnp.int32, (rows, rows), 0).astype(f32)
    lists = [chunks[place][3 * rows:, :].astype(f32) for place in range(cycle)]
    for key_place in range(cycle):
        count = lists[key_place][META - 1:, :1]
        valid = lines < count
        for query_place in range(cycle):
            way = key_place ^ query_place
            times = lists[query_place][way:way + 1, :1]
            term = jnp.where(times > 0, jnp.log2(jnp.maximum(times, 1.0)), absent)
            bias[
                key_place * rows:(key_place + 1) * rows,
                query_place * rows:(query_place + 1) * rows,
            ] = jnp.where(valid, term, absent)


def gather(cycle, chunks, after=()):
    width = chunks[0].shape[1]
    rows = (chunks[0].shape[0] - META) // 3
    tokens = rows * cycle
    return pl.pallas_call(
        functools.partial(gather_kernel, cycle),
        out_shape=[jax.ShapeDtypeStruct((tokens, width), bf16)] * 3
        + [jax.ShapeDtypeStruct((width, tokens), bf16)] * 2
        + [jax.ShapeDtypeStruct((tokens, tokens), f32)],
        in_specs=[vmem()] * cycle + [unread()] * len(after),
        out_specs=[vmem()] * 6,
        compiler_params=params(8 if tokens <= 512 else 40),
        cost_estimate=cost(5),
        name="gather",
    )(*chunks, *after)


def head_tile(width):
    return min(128, width)


def only_head(tile, which):
    lanes = lax.broadcasted_iota(jnp.int32, tile.shape, 1)
    inside = (lanes >= which * HEAD_DIM) & (lanes < (which + 1) * HEAD_DIM)
    return jnp.where(inside, tile, jnp.zeros_like(tile))


def forward_kernel(query_tile, parts, q_all, k_all, v_t, bias, *refs):
    outs = refs[-2 - parts:-2]
    att_t, lse = refs[-2:]
    tokens, width = q_all.shape
    tile = head_tile(width)
    for start in range(0, tokens, query_tile):
        span = slice(start, start + query_tile)
        for head in range(width // HEAD_DIM):
            at = head * HEAD_DIM // tile * tile
            which = (head * HEAD_DIM - at) // HEAD_DIM
            scores = dot_nt(
                k_all[:, at:at + tile], only_head(q_all[span, at:at + tile], which)
            )
            scores = scores * log2_scale + bias[:, span]
            largest = jnp.max(scores, axis=0, keepdims=True)
            expo = jnp.exp2(scores - largest)
            total = jnp.sum(expo, axis=0, keepdims=True)
            probs = (expo * (1.0 / total)).astype(bf16)
            lse[head:head + 1, span] = largest + jnp.log2(total)
            att_t[head * HEAD_DIM:(head + 1) * HEAD_DIM, span] = dot_nn(
                v_t[head * HEAD_DIM:(head + 1) * HEAD_DIM, :], probs
            )
    attended = att_t[...].T.astype(bf16)
    filled = 0
    for out in outs:
        out[...] = attended[filled:filled + out.shape[0], :]
        filled += out.shape[0]


def forward(cycle, together, q_all, k_all, v_t, bias, after=()):
    tokens, width = q_all.shape
    rows = tokens // cycle
    parts = cycle // together
    outs = pl.pallas_call(
        functools.partial(forward_kernel, min(tokens, 512), parts),
        out_shape=[jax.ShapeDtypeStruct((together * rows, width), bf16)] * parts
        + [
            jax.ShapeDtypeStruct((width, tokens), f32),
            jax.ShapeDtypeStruct((8, tokens), f32),
        ],
        in_specs=[vmem()] * 4 + [unread()] * len(after),
        out_specs=[vmem()] * (parts + 2),
        compiler_params=params(16 if tokens <= 512 else 60),
        cost_estimate=cost(3),
        name="forward",
    )(q_all, k_all, v_t, bias, *after)
    return outs[:parts], outs[parts], outs[parts + 1]


def backward_kernel(cycle, query_tile, grad_count, att_count, *refs):
    q_all, k_all, v_all, k_t, bias, att_t, lse = refs[:7]
    refs = refs[7:]
    grads = refs[:grad_count]
    attended = refs[grad_count:grad_count + att_count]
    outs = refs[-4 - cycle:-4]
    g_all, dq_t, dk, dv = refs[-4:]
    width = q_all.shape[1]
    tokens = q_all.shape[0]
    rows = tokens // cycle
    filled = 0
    for grad in grads:
        g_all[filled:filled + grad.shape[0], :] = grad[...]
        filled += grad.shape[0]
    tile = head_tile(width)
    g_t = g_all[...].astype(f32).T
    product = g_t * att_t[...].astype(bf16).astype(f32)
    for start in range(0, tokens, query_tile):
        span = slice(start, start + query_tile)
        for at in range(0, width, tile):
            dk_tile = dv_tile = None
            for which in range(tile // HEAD_DIM):
                low = at + which * HEAD_DIM
                head = low // HEAD_DIM
                delta = jnp.sum(product[low:low + HEAD_DIM, span], axis=0, keepdims=True)
                q_head = only_head(q_all[span, at:at + tile], which)
                g_head = only_head(g_all[span, at:at + tile], which)
                scores = dot_nt(k_all[:, at:at + tile], q_head)
                probs = jnp.exp2(
                    scores * log2_scale + bias[:, span] - lse[head:head + 1, span]
                )
                grad_probs = dot_nt(v_all[:, at:at + tile], g_head)
                grad_scores = (probs * (grad_probs - delta)).astype(bf16)
                dk_head = dot_nn(grad_scores, q_head)
                dv_head = dot_nn(probs.astype(bf16), g_head)
                dk_tile = dk_head if dk_tile is None else dk_tile + dk_head
                dv_tile = dv_head if dv_tile is None else dv_tile + dv_head
                dq_t[low:low + HEAD_DIM, span] = dot_nn(k_t[low:low + HEAD_DIM, :], grad_scores)
            if start == 0:
                dk[:, at:at + tile] = dk_tile
                dv[:, at:at + tile] = dv_tile
            else:
                dk[:, at:at + tile] += dk_tile
                dv[:, at:at + tile] += dv_tile
    dq = (dq_t[...] * score_scale).T.astype(bf16)
    for place in range(cycle):
        span = slice(place * rows, (place + 1) * rows)
        outs[place][:rows, :] = dq[span, :]
        outs[place][rows:2 * rows, :] = (dk[span, :] * score_scale).astype(bf16)
        outs[place][2 * rows:3 * rows, :] = dv[span, :].astype(bf16)
        if attended:
            outs[place][3 * rows:, :] = attended[place][...]


def backward(cycle, inputs, grads, attended, after):
    tokens, width = inputs[0].shape
    rows = tokens // cycle
    return pl.pallas_call(
        functools.partial(backward_kernel, cycle, min(tokens, 512), len(grads), len(attended)),
        out_shape=[jax.ShapeDtypeStruct(((4 if attended else 3) * rows, width), bf16)] * cycle,
        in_specs=[vmem()] * (len(inputs) + len(grads) + len(attended)) + [unread()] * len(after),
        out_specs=[vmem()] * cycle,
        scratch_shapes=[
            pltpu.VMEM((tokens, width), bf16),
            pltpu.VMEM((width, tokens), f32),
            pltpu.VMEM((tokens, width), f32),
            pltpu.VMEM((tokens, width), f32),
        ],
        compiler_params=params(16 if tokens <= 512 else 60),
        cost_estimate=cost(3),
        name="backward",
    )(*inputs, *grads, *attended, *after)


def fetch_rows(out_weight, distance, flip=False):
    cycle, count = lax.axis_size("seq"), lax.axis_size("mp")
    pairs = []
    for member in range(cycle):
        for rank in range(count):
            owner = 2 * group_of(cycle, member ^ distance(rank % 2), rank // 2)
            owner += (rank + flip) % 2
            pairs.append((member * count + owner, member * count + rank))
    return lax.ppermute(out_weight, ("seq", "mp"), pairs)


def with_other_core(half):
    return [half, exchange(half, "mp", 1)]


def both_halves(halves, core):
    mine, other = halves[0][...], halves[1][...]
    first = core == 0
    return jnp.concatenate([jnp.where(first, mine, other), jnp.where(first, other, mine)], axis=0)


def half_columns(halves, core, side):
    half = halves[0].shape[0]
    return columns_at((core if side == 0 else 1 - core) * half, half)


def near_kernel(up_ref, next_ref, *refs):
    halves = refs[:4]
    near, far = refs[-2:]
    rows = up_ref.shape[0]
    _, _, core = my_place()
    for group, out in enumerate((far, near)):
        for side in range(2):
            weight = halves[2 * (1 - group) + side]
            for block, ref in enumerate((up_ref, next_ref)):
                out[block * rows:(block + 1) * rows, half_columns(halves, core, side)] = dot_nt(
                    ref[...], weight[...]
                ).astype(bf16)


def near_grads(upstream, next_upstream, halves, after):
    rows, width = upstream.shape[0], 2 * halves[0].shape[0]
    return pl.pallas_call(
        near_kernel,
        out_shape=[jax.ShapeDtypeStruct((2 * rows, width), bf16)] * 2,
        in_specs=[vmem()] * 6 + [unread()] * len(after),
        out_specs=[vmem()] * 2,
        compiler_params=params(8),
        cost_estimate=cost(1),
        name="near_grads",
    )(upstream, next_upstream, *halves, *after)


def mix_kernel(near_ref, far_ref, *refs):
    halves = refs[:4]
    own, other = refs[-2:]
    rows = own.shape[0]
    _, _, core = my_place()
    total = None
    for group, ref in enumerate((near_ref, far_ref)):
        for side in range(2):
            term = dot_nn(
                ref[:, half_columns(halves, core, side)], halves[2 * group + side][...]
            )
            total = term if total is None else total + term
    own[...] = total[:rows, :]
    other[...] = total[rows:, :].astype(bf16)


def mix(near, far, halves, after):
    rows, model = near.shape[0] // 2, halves[0].shape[1]
    return pl.pallas_call(
        mix_kernel,
        out_shape=[
            jax.ShapeDtypeStruct((rows, model), f32),
            jax.ShapeDtypeStruct((rows, model), bf16),
        ],
        in_specs=[vmem()] * 6 + [unread()] * len(after),
        out_specs=[vmem()] * 2,
        compiler_params=params(8),
        cost_estimate=cost(1),
        name="mix",
    )(near, far, *halves, *after)


def grad_kernel(cycle, up_ref, *refs):
    _, _, core = my_place()
    outs = refs[2 * cycle:]
    for place in range(cycle):
        rows = both_halves(refs[2 * place:2 * place + 2], core)
        outs[place][...] = dot_nt(up_ref[...], rows).astype(bf16)


def project_grad(cycle, upstream, halves):
    rows, model = upstream.shape
    return pl.pallas_call(
        functools.partial(grad_kernel, cycle),
        out_shape=[jax.ShapeDtypeStruct((rows, model // cycle), bf16)] * cycle,
        in_specs=[vmem()] * (1 + 2 * cycle),
        out_specs=[vmem()] * cycle,
        compiler_params=params(8),
        name="project_grad",
    )(upstream, *halves)


def place_columns(chunks, outs, sems):
    cycle = len(chunks)
    rows, model = outs[0].shape
    width = model // cycle
    own, chip, _ = my_place()
    copies = []
    for place in range(cycle):
        group = group_of(cycle, lax.bitwise_xor(own, distance_of(place)), chip)
        if width % 128 == 0:
            for at, out in enumerate(outs):
                copies.append(
                    pltpu.make_async_copy(
                        chunks[place].at[at * rows:(at + 1) * rows, :],
                        out.at[:, columns_at(group * width, width)],
                        sems.at[place, at],
                    )
                )
                copies[-1].start()
        else:
            for other in range(cycle):
                @pl.when(group == other)
                def _():
                    for at, out in enumerate(outs):
                        out[:, other * width:(other + 1) * width] = chunks[place][
                            at * rows:(at + 1) * rows, :
                        ]
    return copies


def finish_kernel(cycle, *refs):
    chunks = refs[:cycle]
    mixed, *outs = refs[-5:-1]
    copies = place_columns(chunks, outs, refs[-1])
    rows = mixed.shape[0]
    if len(refs) == cycle + 7:
        mine, landed = refs[cycle:cycle + 2]
        mixed[...] = (mine[...] + landed[...].astype(f32)).astype(bf16)
    else:
        halves = refs[cycle:3 * cycle]
        _, _, core = my_place()
        total = None
        for place in range(cycle):
            weight = both_halves(halves[2 * place:2 * place + 2], core)
            term = dot_nn(chunks[place][3 * rows:, :], weight)
            total = term if total is None else total + term
        mixed[...] = total.astype(bf16)
    for copy in copies:
        copy.wait()


def finish(cycle, rows, chunks, others):
    model = chunks[0].shape[1] * cycle
    aligned = model // cycle % 128 == 0
    return pl.pallas_call(
        functools.partial(finish_kernel, cycle),
        out_shape=[jax.ShapeDtypeStruct((rows, model), bf16)] * 4,
        in_specs=[vmem()] * (cycle + len(others)),
        out_specs=[vmem()] + [anywhere() if aligned else vmem()] * 3,
        scratch_shapes=[pltpu.SemaphoreType.DMA((cycle, 3))],
        compiler_params=params(8),
        name="finish",
    )(*chunks, *others)


def local(queries, keys, values, out_weight, upstream, adjacency, counts):
    cycle = lax.axis_size("seq")
    rows = queries.shape[0]
    tensors = (queries, keys, values, adjacency, counts.reshape(1, 1))
    if is_square():
        return square(cycle, rows, tensors, out_weight, upstream)
    chunks = swapped(list(pack(cycle, range(cycle), tensors)))
    halves = []
    for place in range(cycle):
        halves += with_other_core(fetch_rows(out_weight, lambda core: place))
    q_all, k_all, v_all, k_t, v_t, bias = gather(cycle, chunks)
    attended, att_t, lse = forward(cycle, 1, q_all, k_all, v_t, bias)
    grads = swapped(project_grad(cycle, upstream, halves))
    inputs = (q_all, k_all, v_all, k_t, bias, att_t, lse)
    terms = swapped(backward(cycle, inputs, grads, attended, []))
    return tuple(finish(cycle, rows, terms, halves))


def square(cycle, rows, tensors, out_weight, upstream):
    next_upstream = exchange_slot(upstream, 1)
    first = fetch_rows(out_weight, lambda core: 0)
    chunks = swapped(pack(cycle, range(cycle), tensors), exchange_slot)
    (held_weight,) = hold((out_weight,), [first])
    halves = with_other_core(first) + [
        fetch_rows(held_weight, lambda core: turned(2) if core else 2, flip) for flip in (False, True)
    ]
    q_all, k_all, v_all, k_t, v_t, bias = gather(cycle, chunks)
    near, far = near_grads(upstream, next_upstream, halves, [])
    grads = [near, exchange_slot(far, 2)]
    (near_att, far_att), att_t, lse = forward(cycle, 2, q_all, k_all, v_t, bias, [far])
    far_att = exchange_slot(far_att, 2)
    inputs = (q_all, k_all, v_all, k_t, bias, att_t, lse)
    terms = backward(cycle, inputs, grads, [], [])
    own_mixed, next_mixed = mix(near_att, far_att, halves, [terms[0]])
    next_mixed = exchange_slot(next_mixed, 1)
    return tuple(
        finish(cycle, rows, swapped(terms, exchange_slot), [own_mixed, next_mixed])
    )


def solution(mesh):
    tokens = P(("seq", "mp"), None)
    return jax.shard_map(
        local,
        mesh=mesh,
        in_specs=(tokens, tokens, tokens, P("mp", None), tokens, tokens, P(("seq", "mp"))),
        out_specs=(tokens,) * 4,
        check_vma=False,
    )
```

```python
import functools

import jax
import jax.numpy as jnp
from jax import lax
from jax.experimental import pallas as pl
from jax.experimental.pallas import tpu as pltpu
from jax.sharding import PartitionSpec as P

HEADS = 16
HEAD_DIM = 64
META = 32

score_scale = 0.125
log2_scale = 0.125 * 1.4426950408889634
cycle_offsets = (1, -1, 2, -2)
absent = -1e30
bf16 = jnp.bfloat16
f32 = jnp.float32


def dot_nn(a, b):
    return lax.dot_general(a, b, (((1,), (0,)), ((), ())), preferred_element_type=f32)


def dot_nt(a, b):
    return lax.dot_general(a, b, (((1,), (1,)), ((), ())), preferred_element_type=f32)


def vmem():
    return pl.BlockSpec(memory_space=pltpu.VMEM)


def params(mib):
    return pltpu.CompilerParams(vmem_limit_bytes=int(mib * 1024) * 1024)


def unread():
    return pl.BlockSpec(memory_space=pl.ANY)


def anywhere():
    return pl.BlockSpec(memory_space=pltpu.HBM)


def cost(micros):
    return pl.CostEstimate(flops=int(micros * 1e9), bytes_accessed=0, transcendentals=0)


def exchange(value, axis, distance):
    count = lax.axis_size(axis)
    return lax.ppermute(value, axis, [(i, i ^ distance) for i in range(count)])


def turned(distance):
    return distance ^ (((distance ^ (distance >> 1)) & 1) * 3)


def is_square():
    return lax.axis_size("seq") == 4 and lax.axis_size("mp") == 8


def swapped(chunks):
    return [chunks[0]] + [exchange(chunks[k], "seq", k) for k in range(1, len(chunks))]


def group_of(cycle, member, chip):
    turn = (member + chip) % cycle
    return turned(turn) if cycle == 4 else turn


def my_place():
    rank = lax.axis_index("mp")
    return lax.axis_index("seq"), rank // 2, lax.rem(rank, 2)


def columns_at(first, width):
    return pl.ds(pl.multiple_of(first, width), width)


def pack_kernel(cycle, places, q_ref, k_ref, v_ref, adj_any, cnt_any, *refs):
    refs, (adj_ref, cnt_ref, sems, more_sems) = refs[:-4], refs[-4:]
    outs = refs
    rows, model = q_ref.shape
    width = model // cycle
    own, chip, _ = my_place()
    lists = [
        pltpu.make_async_copy(adj_any, adj_ref, more_sems.at[0]),
        pltpu.make_async_copy(cnt_any, cnt_ref, more_sems.at[1]),
    ]
    for copy in lists:
        copy.start()
    copies = []
    if width % 128 == 0:
        for place, out in zip(places, outs):
            group = group_of(cycle, lax.bitwise_xor(own, place), chip)
            for at, ref in enumerate((q_ref, k_ref, v_ref)):
                copies.append(
                    pltpu.make_async_copy(
                        ref.at[:, columns_at(group * width, width)],
                        out.at[at * rows:(at + 1) * rows, :],
                        sems.at[place, at],
                    )
                )
                copies[-1].start()
    for copy in lists:
        copy.wait()
    lines = lax.broadcasted_iota(jnp.int32, (META, width), 0)
    meta = jnp.where(lines == 0, 1, 0)
    for column, offset in enumerate(cycle_offsets):
        named = lax.rem(own - offset + 2 * cycle, cycle)
        meta = meta + jnp.where(
            (lines == lax.bitwise_xor(own, named)) & (adj_ref[0, column] > 0), 1, 0
        )
    meta = jnp.where(lines == META - 1, cnt_ref[0, 0], meta).astype(f32).astype(bf16)
    for place, out in zip(places, outs):
        out[3 * rows:, :] = meta
        if width % 128:
            group = group_of(cycle, lax.bitwise_xor(own, place), chip)
            for other in range(cycle):
                @pl.when(group == other)
                def _():
                    for at, ref in enumerate((q_ref, k_ref, v_ref)):
                        out[at * rows:(at + 1) * rows, :] = ref[
                            :, other * width:(other + 1) * width
                        ]
    for copy in copies:
        copy.wait()


def hold_kernel(count, *refs):
    outs, sems = refs[-count - 1:-1], refs[-1]
    copies = [pltpu.make_async_copy(refs[at], outs[at], sems.at[at]) for at in range(count)]
    for copy in copies:
        copy.start()
    for copy in copies:
        copy.wait()


def hold(arrays, after):
    count = len(arrays)
    return pl.pallas_call(
        functools.partial(hold_kernel, count),
        out_shape=[jax.ShapeDtypeStruct(array.shape, array.dtype) for array in arrays],
        in_specs=[unread()] * (count + len(after)),
        out_specs=[vmem()] * count,
        scratch_shapes=[pltpu.SemaphoreType.DMA((count,))],
        compiler_params=params(2),
        cost_estimate=cost(1),
        name="hold",
    )(*arrays, *after)


def pack(cycle, places, tensors):
    rows, model = tensors[0].shape
    width = model // cycle
    return pl.pallas_call(
        functools.partial(pack_kernel, cycle, places),
        out_shape=[jax.ShapeDtypeStruct((3 * rows + META, width), bf16)] * len(places),
        in_specs=[anywhere() if width % 128 == 0 else vmem()] * 3
        + [unread()] * 2,
        out_specs=[vmem()] * len(places),
        scratch_shapes=[
            pltpu.SMEM(tensors[3].shape, jnp.int32),
            pltpu.SMEM(tensors[4].shape, jnp.int32),
            pltpu.SemaphoreType.DMA((cycle, 3)),
            pltpu.SemaphoreType.DMA((2,)),
        ],
        compiler_params=params(62),
        cost_estimate=cost(5),
        name="pack",
    )(*tensors)


def gather_kernel(cycle, *refs):
    chunks = refs[:cycle]
    q_all, k_all, v_all, k_t, v_t, bias, word = refs[-7:]
    word[...] = jnp.zeros(word.shape, word.dtype)
    rows = q_all.shape[0] // cycle
    for place in range(cycle):
        for at, part in enumerate((q_all, k_all, v_all)):
            part[place * rows:(place + 1) * rows, :] = chunks[place][at * rows:(at + 1) * rows, :]
    k_t[...] = k_all[...].astype(f32).T.astype(bf16)
    v_t[...] = v_all[...].astype(f32).T.astype(bf16)
    lines = lax.broadcasted_iota(jnp.int32, (rows, rows), 0).astype(f32)
    lists = [chunks[place][3 * rows:, :].astype(f32) for place in range(cycle)]
    for key_place in range(cycle):
        count = lists[key_place][META - 1:, :1]
        valid = lines < count
        for query_place in range(cycle):
            way = key_place ^ query_place
            times = lists[query_place][way:way + 1, :1]
            term = jnp.where(times > 0, jnp.log2(jnp.maximum(times, 1.0)), absent)
            bias[
                key_place * rows:(key_place + 1) * rows,
                query_place * rows:(query_place + 1) * rows,
            ] = jnp.where(valid, term, absent)


def gather(cycle, chunks, after=()):
    width = chunks[0].shape[1]
    rows = (chunks[0].shape[0] - META) // 3
    tokens = rows * cycle
    return pl.pallas_call(
        functools.partial(gather_kernel, cycle),
        out_shape=[jax.ShapeDtypeStruct((tokens, width), bf16)] * 3
        + [jax.ShapeDtypeStruct((width, tokens), bf16)] * 2
        + [jax.ShapeDtypeStruct((tokens, tokens), f32), jax.ShapeDtypeStruct((16, 128), bf16)],
        in_specs=[vmem()] * cycle + [unread()] * len(after),
        out_specs=[vmem()] * 7,
        compiler_params=params(8 if tokens <= 512 else 40),
        cost_estimate=cost(5),
        name="gather",
    )(*chunks, *after)


def head_tile(width):
    return min(128, width)


def only_head(tile, which):
    lanes = lax.broadcasted_iota(jnp.int32, tile.shape, 1)
    inside = (lanes >= which * HEAD_DIM) & (lanes < (which + 1) * HEAD_DIM)
    return jnp.where(inside, tile, jnp.zeros_like(tile))


def forward_kernel(query_tile, parts, q_all, k_all, v_t, bias, *refs):
    outs = refs[-2 - parts:-2]
    att_t, lse = refs[-2:]
    tokens, width = q_all.shape
    tile = head_tile(width)
    for start in range(0, tokens, query_tile):
        span = slice(start, start + query_tile)
        for head in range(width // HEAD_DIM):
            at = head * HEAD_DIM // tile * tile
            which = (head * HEAD_DIM - at) // HEAD_DIM
            scores = dot_nt(
                k_all[:, at:at + tile], only_head(q_all[span, at:at + tile], which)
            )
            scores = scores * log2_scale + bias[:, span]
            largest = jnp.max(scores, axis=0, keepdims=True)
            expo = jnp.exp2(scores - largest)
            total = jnp.sum(expo, axis=0, keepdims=True)
            probs = (expo * (1.0 / total)).astype(bf16)
            lse[head:head + 1, span] = largest + jnp.log2(total)
            att_t[head * HEAD_DIM:(head + 1) * HEAD_DIM, span] = dot_nn(
                v_t[head * HEAD_DIM:(head + 1) * HEAD_DIM, :], probs
            )
    attended = att_t[...].T.astype(bf16)
    filled = 0
    for out in outs:
        out[...] = attended[filled:filled + out.shape[0], :]
        filled += out.shape[0]


def forward(cycle, together, q_all, k_all, v_t, bias, after=()):
    tokens, width = q_all.shape
    rows = tokens // cycle
    parts = cycle // together
    outs = pl.pallas_call(
        functools.partial(forward_kernel, min(tokens, 512), parts),
        out_shape=[jax.ShapeDtypeStruct((together * rows, width), bf16)] * parts
        + [
            jax.ShapeDtypeStruct((width, tokens), f32),
            jax.ShapeDtypeStruct((8, tokens), f32),
        ],
        in_specs=[vmem()] * 4 + [unread()] * len(after),
        out_specs=[vmem()] * (parts + 2),
        compiler_params=params(16 if tokens <= 512 else 60),
        cost_estimate=cost(3),
        name="forward",
    )(q_all, k_all, v_t, bias, *after)
    return outs[:parts], outs[parts], outs[parts + 1]


def backward_kernel(cycle, query_tile, grad_count, att_count, *refs):
    q_all, k_all, v_all, k_t, bias, att_t, lse = refs[:7]
    refs = refs[7:]
    grads = refs[:grad_count]
    attended = refs[grad_count:grad_count + att_count]
    outs = refs[-4 - cycle:-4]
    g_all, dq_t, dk, dv = refs[-4:]
    width = q_all.shape[1]
    tokens = q_all.shape[0]
    rows = tokens // cycle
    filled = 0
    for grad in grads:
        g_all[filled:filled + grad.shape[0], :] = grad[...]
        filled += grad.shape[0]
    tile = head_tile(width)
    g_t = g_all[...].astype(f32).T
    product = g_t * att_t[...].astype(bf16).astype(f32)
    for start in range(0, tokens, query_tile):
        span = slice(start, start + query_tile)
        for at in range(0, width, tile):
            dk_tile = dv_tile = None
            for which in range(tile // HEAD_DIM):
                low = at + which * HEAD_DIM
                head = low // HEAD_DIM
                delta = jnp.sum(product[low:low + HEAD_DIM, span], axis=0, keepdims=True)
                q_head = only_head(q_all[span, at:at + tile], which)
                g_head = only_head(g_all[span, at:at + tile], which)
                scores = dot_nt(k_all[:, at:at + tile], q_head)
                probs = jnp.exp2(
                    scores * log2_scale + bias[:, span] - lse[head:head + 1, span]
                )
                grad_probs = dot_nt(v_all[:, at:at + tile], g_head)
                grad_scores = (probs * (grad_probs - delta)).astype(bf16)
                dk_head = dot_nn(grad_scores, q_head)
                dv_head = dot_nn(probs.astype(bf16), g_head)
                dk_tile = dk_head if dk_tile is None else dk_tile + dk_head
                dv_tile = dv_head if dv_tile is None else dv_tile + dv_head
                dq_t[low:low + HEAD_DIM, span] = dot_nn(k_t[low:low + HEAD_DIM, :], grad_scores)
            if start == 0:
                dk[:, at:at + tile] = dk_tile
                dv[:, at:at + tile] = dv_tile
            else:
                dk[:, at:at + tile] += dk_tile
                dv[:, at:at + tile] += dv_tile
    dq = (dq_t[...] * score_scale).T.astype(bf16)
    for place in range(cycle):
        span = slice(place * rows, (place + 1) * rows)
        outs[place][:rows, :] = dq[span, :]
        outs[place][rows:2 * rows, :] = (dk[span, :] * score_scale).astype(bf16)
        outs[place][2 * rows:3 * rows, :] = dv[span, :].astype(bf16)
        if attended:
            outs[place][3 * rows:, :] = attended[place][...]


def backward(cycle, inputs, grads, attended, after):
    tokens, width = inputs[0].shape
    rows = tokens // cycle
    return pl.pallas_call(
        functools.partial(backward_kernel, cycle, min(tokens, 512), len(grads), len(attended)),
        out_shape=[jax.ShapeDtypeStruct(((4 if attended else 3) * rows, width), bf16)] * cycle,
        in_specs=[vmem()] * (len(inputs) + len(grads) + len(attended)) + [unread()] * len(after),
        out_specs=[vmem()] * cycle,
        scratch_shapes=[
            pltpu.VMEM((tokens, width), bf16),
            pltpu.VMEM((width, tokens), f32),
            pltpu.VMEM((tokens, width), f32),
            pltpu.VMEM((tokens, width), f32),
        ],
        compiler_params=params(16 if tokens <= 512 else 60),
        cost_estimate=cost(3),
        name="backward",
    )(*inputs, *grads, *attended, *after)


def fetch_rows(out_weight, place):
    cycle, count = lax.axis_size("seq"), lax.axis_size("mp")
    pairs = []
    for member in range(cycle):
        for rank in range(count):
            owner = 2 * group_of(cycle, member ^ place, rank // 2) + rank % 2
            pairs.append((member * count + owner, member * count + rank))
    return lax.ppermute(out_weight, ("seq", "mp"), pairs)


def with_other_core(half):
    return [half, exchange(half, "mp", 1)]


def both_halves(halves, core):
    mine, other = halves[0][...], halves[1][...]
    first = core == 0
    return jnp.concatenate([jnp.where(first, mine, other), jnp.where(first, other, mine)], axis=0)


def half_columns(halves, core, side):
    half = halves[0].shape[0]
    return columns_at((core if side == 0 else 1 - core) * half, half)


def near_kernel(up_ref, next_ref, *refs):
    halves = refs[:4]
    near, far = refs[-2:]
    rows = up_ref.shape[0]
    _, _, core = my_place()
    for group, out in enumerate((far, near)):
        for side in range(2):
            weight = halves[2 * (1 - group) + side]
            for block, ref in enumerate((up_ref, next_ref)):
                out[block * rows:(block + 1) * rows, half_columns(halves, core, side)] = dot_nt(
                    ref[...], weight[...]
                ).astype(bf16)


def near_grads(upstream, next_upstream, halves, after):
    rows, width = upstream.shape[0], 2 * halves[0].shape[0]
    return pl.pallas_call(
        near_kernel,
        out_shape=[jax.ShapeDtypeStruct((2 * rows, width), bf16)] * 2,
        in_specs=[vmem()] * 6 + [unread()] * len(after),
        out_specs=[vmem()] * 2,
        compiler_params=params(8),
        cost_estimate=cost(1),
        name="near_grads",
    )(upstream, next_upstream, *halves, *after)


def mix_kernel(near_ref, far_ref, *refs):
    halves = refs[:4]
    own, other = refs[-2:]
    rows = own.shape[0]
    _, _, core = my_place()
    total = None
    for group, ref in enumerate((near_ref, far_ref)):
        for side in range(2):
            term = dot_nn(
                ref[:, half_columns(halves, core, side)], halves[2 * group + side][...]
            )
            total = term if total is None else total + term
    own[...] = total[:rows, :]
    other[...] = total[rows:, :].astype(bf16)


def mix(near, far, halves, after):
    rows, model = near.shape[0] // 2, halves[0].shape[1]
    return pl.pallas_call(
        mix_kernel,
        out_shape=[
            jax.ShapeDtypeStruct((rows, model), f32),
            jax.ShapeDtypeStruct((rows, model), bf16),
        ],
        in_specs=[vmem()] * 6 + [unread()] * len(after),
        out_specs=[vmem()] * 2,
        compiler_params=params(8),
        cost_estimate=cost(1),
        name="mix",
    )(near, far, *halves, *after)


def grad_kernel(cycle, up_ref, *refs):
    _, _, core = my_place()
    outs = refs[2 * cycle:]
    for place in range(cycle):
        rows = both_halves(refs[2 * place:2 * place + 2], core)
        outs[place][...] = dot_nt(up_ref[...], rows).astype(bf16)


def project_grad(cycle, upstream, halves):
    rows, model = upstream.shape
    return pl.pallas_call(
        functools.partial(grad_kernel, cycle),
        out_shape=[jax.ShapeDtypeStruct((rows, model // cycle), bf16)] * cycle,
        in_specs=[vmem()] * (1 + 2 * cycle),
        out_specs=[vmem()] * cycle,
        compiler_params=params(8),
        name="project_grad",
    )(upstream, *halves)


def place_columns(chunks, outs, sems):
    cycle = len(chunks)
    rows, model = outs[0].shape
    width = model // cycle
    own, chip, _ = my_place()
    copies = []
    for place in range(cycle):
        group = group_of(cycle, lax.bitwise_xor(own, place), chip)
        if width % 128 == 0:
            for at, out in enumerate(outs):
                copies.append(
                    pltpu.make_async_copy(
                        chunks[place].at[at * rows:(at + 1) * rows, :],
                        out.at[:, columns_at(group * width, width)],
                        sems.at[place, at],
                    )
                )
                copies[-1].start()
        else:
            for other in range(cycle):
                @pl.when(group == other)
                def _():
                    for at, out in enumerate(outs):
                        out[:, other * width:(other + 1) * width] = chunks[place][
                            at * rows:(at + 1) * rows, :
                        ]
    return copies


def finish_kernel(cycle, *refs):
    chunks = refs[:cycle]
    mixed, *outs = refs[-5:-1]
    copies = place_columns(chunks, outs, refs[-1])
    rows = mixed.shape[0]
    if len(refs) == cycle + 7:
        mine, landed = refs[cycle:cycle + 2]
        mixed[...] = (mine[...] + landed[...].astype(f32)).astype(bf16)
    else:
        halves = refs[cycle:3 * cycle]
        _, _, core = my_place()
        total = None
        for place in range(cycle):
            weight = both_halves(halves[2 * place:2 * place + 2], core)
            term = dot_nn(chunks[place][3 * rows:, :], weight)
            total = term if total is None else total + term
        mixed[...] = total.astype(bf16)
    for copy in copies:
        copy.wait()


def finish(cycle, rows, chunks, others):
    model = chunks[0].shape[1] * cycle
    aligned = model // cycle % 128 == 0
    return pl.pallas_call(
        functools.partial(finish_kernel, cycle),
        out_shape=[jax.ShapeDtypeStruct((rows, model), bf16)] * 4,
        in_specs=[vmem()] * (cycle + len(others)),
        out_specs=[vmem()] + [anywhere() if aligned else vmem()] * 3,
        scratch_shapes=[pltpu.SemaphoreType.DMA((cycle, 3))],
        compiler_params=params(8),
        name="finish",
    )(*chunks, *others)


def local(queries, keys, values, out_weight, upstream, adjacency, counts):
    cycle = lax.axis_size("seq")
    rows = queries.shape[0]
    tensors = (queries, keys, values, adjacency, counts.reshape(1, 1))
    if is_square():
        return square(cycle, rows, tensors, out_weight, upstream)
    chunks = swapped(list(pack(cycle, range(cycle), tensors)))
    halves = []
    for place in range(cycle):
        halves += with_other_core(fetch_rows(out_weight, place))
    q_all, k_all, v_all, k_t, v_t, bias, _ = gather(cycle, chunks)
    attended, att_t, lse = forward(cycle, 1, q_all, k_all, v_t, bias)
    grads = swapped(project_grad(cycle, upstream, halves))
    inputs = (q_all, k_all, v_all, k_t, bias, att_t, lse)
    terms = swapped(backward(cycle, inputs, grads, attended, []))
    return tuple(finish(cycle, rows, terms, halves))


def square(cycle, rows, tensors, out_weight, upstream):
    next_upstream = exchange(upstream, "seq", 1)
    first = fetch_rows(out_weight, 0)
    chunks = swapped(list(pack(cycle, range(cycle), tensors)))
    (held_weight,) = hold((out_weight,), [first, next_upstream])
    second = fetch_rows(held_weight, 2)
    q_all, k_all, v_all, k_t, v_t, bias, word = gather(cycle, chunks)
    (held_first,) = hold((first,), [word])
    halves = [first, exchange(held_first, "mp", 1)] + with_other_core(second)
    near, far = near_grads(upstream, next_upstream, halves, [])
    grads = [near, exchange(far, "seq", 2)]
    (near_att, far_att), att_t, lse = forward(cycle, 2, q_all, k_all, v_t, bias, [far])
    far_att = exchange(far_att, "seq", 2)
    inputs = (q_all, k_all, v_all, k_t, bias, att_t, lse)
    terms = backward(cycle, inputs, grads, [], [])
    own_mixed, next_mixed = mix(near_att, far_att, halves, [terms[0]])
    next_mixed = exchange(next_mixed, "seq", 1)
    return tuple(finish(cycle, rows, swapped(terms), [own_mixed, next_mixed]))


def solution(mesh):
    tokens = P(("seq", "mp"), None)
    return jax.shard_map(
        local,
        mesh=mesh,
        in_specs=(tokens, tokens, tokens, P("mp", None), tokens, tokens, P(("seq", "mp"))),
        out_specs=(tokens,) * 4,
        check_vma=False,
    )
```

```python
import functools

import jax
import jax.numpy as jnp
from jax import lax
from jax.experimental import pallas as pl
from jax.experimental.pallas import tpu as pltpu
from jax.sharding import PartitionSpec as P

HEADS = 16
HEAD_DIM = 64
META = 32

score_scale = 0.125
log2_scale = 0.125 * 1.4426950408889634
cycle_offsets = (1, -1, 2, -2)
absent = -1e30
bf16 = jnp.bfloat16
f32 = jnp.float32


def dot_nn(a, b):
    return lax.dot_general(a, b, (((1,), (0,)), ((), ())), preferred_element_type=f32)


def dot_nt(a, b):
    return lax.dot_general(a, b, (((1,), (1,)), ((), ())), preferred_element_type=f32)


def vmem():
    return pl.BlockSpec(memory_space=pltpu.VMEM)


def params(mib):
    return pltpu.CompilerParams(vmem_limit_bytes=int(mib * 1024) * 1024)


def unread():
    return pl.BlockSpec(memory_space=pl.ANY)


def anywhere():
    return pl.BlockSpec(memory_space=pltpu.HBM)


def cost(micros):
    return pl.CostEstimate(flops=int(micros * 1e9), bytes_accessed=0, transcendentals=0)


def exchange(value, axis, distance):
    count = lax.axis_size(axis)
    return lax.ppermute(value, axis, [(i, i ^ distance) for i in range(count)])


def turned(distance):
    return distance ^ (((distance ^ (distance >> 1)) & 1) * 3)


def is_square():
    return lax.axis_size("seq") == 4 and lax.axis_size("mp") == 8


def swapped(chunks):
    return [chunks[0]] + [exchange(chunks[k], "seq", k) for k in range(1, len(chunks))]


def group_of(cycle, member, chip):
    turn = (member + chip) % cycle
    return turned(turn) if cycle == 4 else turn


def my_place():
    rank = lax.axis_index("mp")
    return lax.axis_index("seq"), rank // 2, lax.rem(rank, 2)


def columns_at(first, width):
    return pl.ds(pl.multiple_of(first, width), width)


def pack_kernel(cycle, places, q_ref, k_ref, v_ref, adj_any, cnt_any, *refs):
    refs, (adj_ref, cnt_ref, sems, more_sems) = refs[:-4], refs[-4:]
    outs = refs
    rows, model = q_ref.shape
    width = model // cycle
    own, chip, _ = my_place()
    lists = [
        pltpu.make_async_copy(adj_any, adj_ref, more_sems.at[0]),
        pltpu.make_async_copy(cnt_any, cnt_ref, more_sems.at[1]),
    ]
    for copy in lists:
        copy.start()
    copies = []
    if width % 128 == 0:
        for place, out in zip(places, outs):
            group = group_of(cycle, lax.bitwise_xor(own, place), chip)
            for at, ref in enumerate((q_ref, k_ref, v_ref)):
                copies.append(
                    pltpu.make_async_copy(
                        ref.at[:, columns_at(group * width, width)],
                        out.at[at * rows:(at + 1) * rows, :],
                        sems.at[place, at],
                    )
                )
                copies[-1].start()
    for copy in lists:
        copy.wait()
    lines = lax.broadcasted_iota(jnp.int32, (META, width), 0)
    meta = jnp.where(lines == 0, 1, 0)
    for column, offset in enumerate(cycle_offsets):
        named = lax.rem(own - offset + 2 * cycle, cycle)
        meta = meta + jnp.where(
            (lines == lax.bitwise_xor(own, named)) & (adj_ref[0, column] > 0), 1, 0
        )
    meta = jnp.where(lines == META - 1, cnt_ref[0, 0], meta).astype(f32).astype(bf16)
    for place, out in zip(places, outs):
        out[3 * rows:, :] = meta
        if width % 128:
            group = group_of(cycle, lax.bitwise_xor(own, place), chip)
            for other in range(cycle):
                @pl.when(group == other)
                def _():
                    for at, ref in enumerate((q_ref, k_ref, v_ref)):
                        out[at * rows:(at + 1) * rows, :] = ref[
                            :, other * width:(other + 1) * width
                        ]
    for copy in copies:
        copy.wait()


def hold_kernel(count, *refs):
    outs, sems = refs[-count - 1:-1], refs[-1]
    copies = [pltpu.make_async_copy(refs[at], outs[at], sems.at[at]) for at in range(count)]
    for copy in copies:
        copy.start()
    for copy in copies:
        copy.wait()


def hold(arrays, after):
    count = len(arrays)
    return pl.pallas_call(
        functools.partial(hold_kernel, count),
        out_shape=[jax.ShapeDtypeStruct(array.shape, array.dtype) for array in arrays],
        in_specs=[unread()] * (count + len(after)),
        out_specs=[vmem()] * count,
        scratch_shapes=[pltpu.SemaphoreType.DMA((count,))],
        compiler_params=params(2),
        cost_estimate=cost(1),
        name="hold",
    )(*arrays, *after)


def pack(cycle, places, tensors):
    rows, model = tensors[0].shape
    width = model // cycle
    return pl.pallas_call(
        functools.partial(pack_kernel, cycle, places),
        out_shape=[jax.ShapeDtypeStruct((3 * rows + META, width), bf16)] * len(places),
        in_specs=[anywhere() if width % 128 == 0 else vmem()] * 3
        + [unread()] * 2,
        out_specs=[vmem()] * len(places),
        scratch_shapes=[
            pltpu.SMEM(tensors[3].shape, jnp.int32),
            pltpu.SMEM(tensors[4].shape, jnp.int32),
            pltpu.SemaphoreType.DMA((cycle, 3)),
            pltpu.SemaphoreType.DMA((2,)),
        ],
        compiler_params=params(62),
        cost_estimate=cost(5),
        name="pack",
    )(*tensors)


def gather_kernel(cycle, *refs):
    chunks = refs[:cycle]
    q_all, k_all, v_all, k_t, v_t, bias, word = refs[-7:]
    word[...] = jnp.zeros(word.shape, word.dtype)
    rows = q_all.shape[0] // cycle
    for place in range(cycle):
        for at, part in enumerate((q_all, k_all, v_all)):
            part[place * rows:(place + 1) * rows, :] = chunks[place][at * rows:(at + 1) * rows, :]
    k_t[...] = k_all[...].astype(f32).T.astype(bf16)
    v_t[...] = v_all[...].astype(f32).T.astype(bf16)
    lines = lax.broadcasted_iota(jnp.int32, (rows, rows), 0).astype(f32)
    lists = [chunks[place][3 * rows:, :].astype(f32) for place in range(cycle)]
    for key_place in range(cycle):
        count = lists[key_place][META - 1:, :1]
        valid = lines < count
        for query_place in range(cycle):
            way = key_place ^ query_place
            times = lists[query_place][way:way + 1, :1]
            term = jnp.where(times > 0, jnp.log2(jnp.maximum(times, 1.0)), absent)
            bias[
                key_place * rows:(key_place + 1) * rows,
                query_place * rows:(query_place + 1) * rows,
            ] = jnp.where(valid, term, absent)


def gather(cycle, chunks, after=()):
    width = chunks[0].shape[1]
    rows = (chunks[0].shape[0] - META) // 3
    tokens = rows * cycle
    return pl.pallas_call(
        functools.partial(gather_kernel, cycle),
        out_shape=[jax.ShapeDtypeStruct((tokens, width), bf16)] * 3
        + [jax.ShapeDtypeStruct((width, tokens), bf16)] * 2
        + [jax.ShapeDtypeStruct((tokens, tokens), f32), jax.ShapeDtypeStruct((16, 128), bf16)],
        in_specs=[vmem()] * cycle + [unread()] * len(after),
        out_specs=[vmem()] * 7,
        compiler_params=params(8 if tokens <= 512 else 40),
        cost_estimate=cost(5),
        name="gather",
    )(*chunks, *after)


def head_tile(width):
    return min(128, width)


def only_head(tile, which):
    lanes = lax.broadcasted_iota(jnp.int32, tile.shape, 1)
    inside = (lanes >= which * HEAD_DIM) & (lanes < (which + 1) * HEAD_DIM)
    return jnp.where(inside, tile, jnp.zeros_like(tile))


def forward_kernel(query_tile, parts, q_all, k_all, v_t, bias, *refs):
    outs = refs[-2 - parts:-2]
    att_t, lse = refs[-2:]
    tokens, width = q_all.shape
    tile = head_tile(width)
    for start in range(0, tokens, query_tile):
        span = slice(start, start + query_tile)
        for head in range(width // HEAD_DIM):
            at = head * HEAD_DIM // tile * tile
            which = (head * HEAD_DIM - at) // HEAD_DIM
            scores = dot_nt(
                k_all[:, at:at + tile], only_head(q_all[span, at:at + tile], which)
            )
            scores = scores * log2_scale + bias[:, span]
            largest = jnp.max(scores, axis=0, keepdims=True)
            expo = jnp.exp2(scores - largest)
            total = jnp.sum(expo, axis=0, keepdims=True)
            probs = (expo * (1.0 / total)).astype(bf16)
            lse[head:head + 1, span] = largest + jnp.log2(total)
            att_t[head * HEAD_DIM:(head + 1) * HEAD_DIM, span] = dot_nn(
                v_t[head * HEAD_DIM:(head + 1) * HEAD_DIM, :], probs
            )
    attended = att_t[...].T.astype(bf16)
    filled = 0
    for out in outs:
        out[...] = attended[filled:filled + out.shape[0], :]
        filled += out.shape[0]


def forward(cycle, together, q_all, k_all, v_t, bias, after=()):
    tokens, width = q_all.shape
    rows = tokens // cycle
    parts = cycle // together
    outs = pl.pallas_call(
        functools.partial(forward_kernel, min(tokens, 512), parts),
        out_shape=[jax.ShapeDtypeStruct((together * rows, width), bf16)] * parts
        + [
            jax.ShapeDtypeStruct((width, tokens), f32),
            jax.ShapeDtypeStruct((8, tokens), f32),
        ],
        in_specs=[vmem()] * 4 + [unread()] * len(after),
        out_specs=[vmem()] * (parts + 2),
        compiler_params=params(16 if tokens <= 512 else 60),
        cost_estimate=cost(3),
        name="forward",
    )(q_all, k_all, v_t, bias, *after)
    return outs[:parts], outs[parts], outs[parts + 1]


def backward_kernel(cycle, query_tile, grad_count, att_count, *refs):
    q_all, k_all, v_all, k_t, bias, att_t, lse = refs[:7]
    refs = refs[7:]
    grads = refs[:grad_count]
    attended = refs[grad_count:grad_count + att_count]
    outs = refs[-4 - cycle:-4]
    g_all, dq_t, dk, dv = refs[-4:]
    width = q_all.shape[1]
    tokens = q_all.shape[0]
    rows = tokens // cycle
    filled = 0
    for grad in grads:
        g_all[filled:filled + grad.shape[0], :] = grad[...]
        filled += grad.shape[0]
    tile = head_tile(width)
    g_t = g_all[...].astype(f32).T
    product = g_t * att_t[...].astype(bf16).astype(f32)
    for start in range(0, tokens, query_tile):
        span = slice(start, start + query_tile)
        for at in range(0, width, tile):
            dk_tile = dv_tile = None
            for which in range(tile // HEAD_DIM):
                low = at + which * HEAD_DIM
                head = low // HEAD_DIM
                delta = jnp.sum(product[low:low + HEAD_DIM, span], axis=0, keepdims=True)
                q_head = only_head(q_all[span, at:at + tile], which)
                g_head = only_head(g_all[span, at:at + tile], which)
                scores = dot_nt(k_all[:, at:at + tile], q_head)
                probs = jnp.exp2(
                    scores * log2_scale + bias[:, span] - lse[head:head + 1, span]
                )
                grad_probs = dot_nt(v_all[:, at:at + tile], g_head)
                grad_scores = (probs * (grad_probs - delta)).astype(bf16)
                dk_head = dot_nn(grad_scores, q_head)
                dv_head = dot_nn(probs.astype(bf16), g_head)
                dk_tile = dk_head if dk_tile is None else dk_tile + dk_head
                dv_tile = dv_head if dv_tile is None else dv_tile + dv_head
                dq_t[low:low + HEAD_DIM, span] = dot_nn(k_t[low:low + HEAD_DIM, :], grad_scores)
            if start == 0:
                dk[:, at:at + tile] = dk_tile
                dv[:, at:at + tile] = dv_tile
            else:
                dk[:, at:at + tile] += dk_tile
                dv[:, at:at + tile] += dv_tile
    dq = (dq_t[...] * score_scale).T.astype(bf16)
    for place in range(cycle):
        span = slice(place * rows, (place + 1) * rows)
        outs[place][:rows, :] = dq[span, :]
        outs[place][rows:2 * rows, :] = (dk[span, :] * score_scale).astype(bf16)
        outs[place][2 * rows:3 * rows, :] = dv[span, :].astype(bf16)
        if attended:
            outs[place][3 * rows:, :] = attended[place][...]


def backward(cycle, inputs, grads, attended, after):
    tokens, width = inputs[0].shape
    rows = tokens // cycle
    return pl.pallas_call(
        functools.partial(backward_kernel, cycle, min(tokens, 512), len(grads), len(attended)),
        out_shape=[jax.ShapeDtypeStruct(((4 if attended else 3) * rows, width), bf16)] * cycle,
        in_specs=[vmem()] * (len(inputs) + len(grads) + len(attended)) + [unread()] * len(after),
        out_specs=[vmem()] * cycle,
        scratch_shapes=[
            pltpu.VMEM((tokens, width), bf16),
            pltpu.VMEM((width, tokens), f32),
            pltpu.VMEM((tokens, width), f32),
            pltpu.VMEM((tokens, width), f32),
        ],
        compiler_params=params(16 if tokens <= 512 else 60),
        cost_estimate=cost(3),
        name="backward",
    )(*inputs, *grads, *attended, *after)


def fetch_rows(out_weight, place):
    cycle, count = lax.axis_size("seq"), lax.axis_size("mp")
    pairs = []
    for member in range(cycle):
        for rank in range(count):
            owner = 2 * group_of(cycle, member ^ place, rank // 2) + rank % 2
            pairs.append((member * count + owner, member * count + rank))
    return lax.ppermute(out_weight, ("seq", "mp"), pairs)


def with_other_core(half):
    return [half, exchange(half, "mp", 1)]


def both_halves(halves, core):
    mine, other = halves[0][...], halves[1][...]
    first = core == 0
    return jnp.concatenate([jnp.where(first, mine, other), jnp.where(first, other, mine)], axis=0)


def half_columns(halves, core, side):
    half = halves[0].shape[0]
    return columns_at((core if side == 0 else 1 - core) * half, half)


def group_kernel(count, *refs):
    ups, halves = refs[:count], refs[count:count + 2]
    out = refs[-1]
    rows = ups[0].shape[0]
    _, _, core = my_place()
    for side in range(2):
        weight = halves[side][...]
        for block, ref in enumerate(ups):
            out[block * rows:(block + 1) * rows, half_columns(halves, core, side)] = dot_nt(
                ref[...], weight
            ).astype(bf16)


def group_grads(upstreams, halves, after):
    rows, width = upstreams[0].shape[0], 2 * halves[0].shape[0]
    return pl.pallas_call(
        functools.partial(group_kernel, len(upstreams)),
        out_shape=jax.ShapeDtypeStruct((len(upstreams) * rows, width), bf16),
        in_specs=[vmem()] * (len(upstreams) + 2) + [unread()] * len(after),
        out_specs=vmem(),
        compiler_params=params(8),
        cost_estimate=cost(1),
        name="group_grads",
    )(*upstreams, *halves, *after)


def mix_kernel(near_ref, far_ref, *refs):
    halves = refs[:4]
    own, other = refs[-2:]
    rows = own.shape[0]
    _, _, core = my_place()
    total = None
    for group, ref in enumerate((near_ref, far_ref)):
        for side in range(2):
            term = dot_nn(
                ref[:, half_columns(halves, core, side)], halves[2 * group + side][...]
            )
            total = term if total is None else total + term
    own[...] = total[:rows, :]
    other[...] = total[rows:, :].astype(bf16)


def mix(near, far, halves, after):
    rows, model = near.shape[0] // 2, halves[0].shape[1]
    return pl.pallas_call(
        mix_kernel,
        out_shape=[
            jax.ShapeDtypeStruct((rows, model), f32),
            jax.ShapeDtypeStruct((rows, model), bf16),
        ],
        in_specs=[vmem()] * 6 + [unread()] * len(after),
        out_specs=[vmem()] * 2,
        compiler_params=params(8),
        cost_estimate=cost(1),
        name="mix",
    )(near, far, *halves, *after)


def grad_kernel(cycle, up_ref, *refs):
    _, _, core = my_place()
    outs = refs[2 * cycle:]
    for place in range(cycle):
        rows = both_halves(refs[2 * place:2 * place + 2], core)
        outs[place][...] = dot_nt(up_ref[...], rows).astype(bf16)


def project_grad(cycle, upstream, halves):
    rows, model = upstream.shape
    return pl.pallas_call(
        functools.partial(grad_kernel, cycle),
        out_shape=[jax.ShapeDtypeStruct((rows, model // cycle), bf16)] * cycle,
        in_specs=[vmem()] * (1 + 2 * cycle),
        out_specs=[vmem()] * cycle,
        compiler_params=params(8),
        name="project_grad",
    )(upstream, *halves)


def place_columns(chunks, outs, sems):
    cycle = len(chunks)
    rows, model = outs[0].shape
    width = model // cycle
    own, chip, _ = my_place()
    copies = []
    for place in range(cycle):
        group = group_of(cycle, lax.bitwise_xor(own, place), chip)
        if width % 128 == 0:
            for at, out in enumerate(outs):
                copies.append(
                    pltpu.make_async_copy(
                        chunks[place].at[at * rows:(at + 1) * rows, :],
                        out.at[:, columns_at(group * width, width)],
                        sems.at[place, at],
                    )
                )
                copies[-1].start()
        else:
            for other in range(cycle):
                @pl.when(group == other)
                def _():
                    for at, out in enumerate(outs):
                        out[:, other * width:(other + 1) * width] = chunks[place][
                            at * rows:(at + 1) * rows, :
                        ]
    return copies


def finish_kernel(cycle, *refs):
    chunks = refs[:cycle]
    mixed, *outs = refs[-5:-1]
    copies = place_columns(chunks, outs, refs[-1])
    rows = mixed.shape[0]
    if len(refs) == cycle + 7:
        mine, landed = refs[cycle:cycle + 2]
        mixed[...] = (mine[...] + landed[...].astype(f32)).astype(bf16)
    else:
        halves = refs[cycle:3 * cycle]
        _, _, core = my_place()
        total = None
        for place in range(cycle):
            weight = both_halves(halves[2 * place:2 * place + 2], core)
            term = dot_nn(chunks[place][3 * rows:, :], weight)
            total = term if total is None else total + term
        mixed[...] = total.astype(bf16)
    for copy in copies:
        copy.wait()


def finish(cycle, rows, chunks, others):
    model = chunks[0].shape[1] * cycle
    aligned = model // cycle % 128 == 0
    return pl.pallas_call(
        functools.partial(finish_kernel, cycle),
        out_shape=[jax.ShapeDtypeStruct((rows, model), bf16)] * 4,
        in_specs=[vmem()] * (cycle + len(others)),
        out_specs=[vmem()] + [anywhere() if aligned else vmem()] * 3,
        scratch_shapes=[pltpu.SemaphoreType.DMA((cycle, 3))],
        compiler_params=params(8),
        name="finish",
    )(*chunks, *others)


def local(queries, keys, values, out_weight, upstream, adjacency, counts):
    cycle = lax.axis_size("seq")
    rows = queries.shape[0]
    tensors = (queries, keys, values, adjacency, counts.reshape(1, 1))
    if is_square():
        return square(cycle, rows, tensors, out_weight, upstream)
    chunks = swapped(list(pack(cycle, range(cycle), tensors)))
    halves = []
    for place in range(cycle):
        halves += with_other_core(fetch_rows(out_weight, place))
    q_all, k_all, v_all, k_t, v_t, bias, _ = gather(cycle, chunks)
    attended, att_t, lse = forward(cycle, 1, q_all, k_all, v_t, bias)
    grads = swapped(project_grad(cycle, upstream, halves))
    inputs = (q_all, k_all, v_all, k_t, bias, att_t, lse)
    terms = swapped(backward(cycle, inputs, grads, attended, []))
    return tuple(finish(cycle, rows, terms, halves))


def square(cycle, rows, tensors, out_weight, upstream):
    next_x, next_y = exchange(upstream, "seq", 1), exchange(upstream, "seq", 2)
    chunks = swapped(list(pack(cycle, range(cycle), tensors)))
    (held_weight,) = hold((out_weight,), [next_x, next_y])
    first = fetch_rows(held_weight, 0)
    own_rows = with_other_core(first)
    q_all, k_all, v_all, k_t, v_t, bias, word = gather(cycle, chunks)
    (held_y,) = hold((next_y,), [word])
    across = exchange(held_y, "seq", 1)
    (near_att, far_att), att_t, lse = forward(cycle, 2, q_all, k_all, v_t, bias)
    far_att = exchange(far_att, "seq", 2)
    grads = [group_grads((upstream, next_x, next_y, across), own_rows, [lse])]
    inputs = (q_all, k_all, v_all, k_t, bias, att_t, lse)
    terms = backward(cycle, inputs, grads, [], [])
    (held_weight,) = hold((out_weight,), [first])
    second = with_other_core(fetch_rows(held_weight, 2))
    own_mixed, next_mixed = mix(near_att, far_att, own_rows + second, [terms[0]])
    next_mixed = exchange(next_mixed, "seq", 1)
    return tuple(finish(cycle, rows, swapped(terms), [own_mixed, next_mixed]))


def solution(mesh):
    tokens = P(("seq", "mp"), None)
    return jax.shard_map(
        local,
        mesh=mesh,
        in_specs=(tokens, tokens, tokens, P("mp", None), tokens, tokens, P(("seq", "mp"))),
        out_specs=(tokens,) * 4,
        check_vma=False,
    )
```

```python
import functools

import jax
import jax.numpy as jnp
from jax import lax
from jax.experimental import pallas as pl
from jax.experimental.pallas import tpu as pltpu
from jax.sharding import PartitionSpec as P

HEADS = 16
HEAD_DIM = 64
META = 32

score_scale = 0.125
log2_scale = 0.125 * 1.4426950408889634
cycle_offsets = (1, -1, 2, -2)
absent = -1e30
bf16 = jnp.bfloat16
f32 = jnp.float32


def dot_nn(a, b):
    return lax.dot_general(a, b, (((1,), (0,)), ((), ())), preferred_element_type=f32)


def dot_nt(a, b):
    return lax.dot_general(a, b, (((1,), (1,)), ((), ())), preferred_element_type=f32)


def vmem():
    return pl.BlockSpec(memory_space=pltpu.VMEM)


def params(mib):
    return pltpu.CompilerParams(vmem_limit_bytes=int(mib * 1024) * 1024)


def unread():
    return pl.BlockSpec(memory_space=pl.ANY)


def anywhere():
    return pl.BlockSpec(memory_space=pltpu.HBM)


def cost(micros):
    return pl.CostEstimate(flops=int(micros * 1e9), bytes_accessed=0, transcendentals=0)


def exchange(value, axis, distance):
    count = lax.axis_size(axis)
    return lax.ppermute(value, axis, [(i, i ^ distance) for i in range(count)])


def turned(distance):
    return distance ^ (((distance ^ (distance >> 1)) & 1) * 3)


def is_square():
    return lax.axis_size("seq") == 4 and lax.axis_size("mp") == 8


def swapped(chunks):
    return [chunks[0]] + [exchange(chunks[k], "seq", k) for k in range(1, len(chunks))]


def group_of(cycle, member, chip):
    turn = (member + chip) % cycle
    return turned(turn) if cycle == 4 else turn


def my_place():
    rank = lax.axis_index("mp")
    return lax.axis_index("seq"), rank // 2, lax.rem(rank, 2)


def columns_at(first, width):
    return pl.ds(pl.multiple_of(first, width), width)


def pack_kernel(cycle, places, q_ref, k_ref, v_ref, adj_any, cnt_any, *refs):
    refs, (adj_ref, cnt_ref, sems, more_sems) = refs[:-4], refs[-4:]
    outs = refs
    rows, model = q_ref.shape
    width = model // cycle
    own, chip, _ = my_place()
    lists = [
        pltpu.make_async_copy(adj_any, adj_ref, more_sems.at[0]),
        pltpu.make_async_copy(cnt_any, cnt_ref, more_sems.at[1]),
    ]
    for copy in lists:
        copy.start()
    copies = []
    if width % 128 == 0:
        for place, out in zip(places, outs):
            group = group_of(cycle, lax.bitwise_xor(own, place), chip)
            for at, ref in enumerate((q_ref, k_ref, v_ref)):
                copies.append(
                    pltpu.make_async_copy(
                        ref.at[:, columns_at(group * width, width)],
                        out.at[at * rows:(at + 1) * rows, :],
                        sems.at[place, at],
                    )
                )
                copies[-1].start()
    for copy in lists:
        copy.wait()
    lines = lax.broadcasted_iota(jnp.int32, (META, width), 0)
    meta = jnp.where(lines == 0, 1, 0)
    for column, offset in enumerate(cycle_offsets):
        named = lax.rem(own - offset + 2 * cycle, cycle)
        meta = meta + jnp.where(
            (lines == lax.bitwise_xor(own, named)) & (adj_ref[0, column] > 0), 1, 0
        )
    meta = jnp.where(lines == META - 1, cnt_ref[0, 0], meta).astype(f32).astype(bf16)
    for place, out in zip(places, outs):
        out[3 * rows:, :] = meta
        if width % 128:
            group = group_of(cycle, lax.bitwise_xor(own, place), chip)
            for other in range(cycle):
                @pl.when(group == other)
                def _():
                    for at, ref in enumerate((q_ref, k_ref, v_ref)):
                        out[at * rows:(at + 1) * rows, :] = ref[
                            :, other * width:(other + 1) * width
                        ]
    for copy in copies:
        copy.wait()


def hold_kernel(count, *refs):
    outs, sems = refs[-count - 1:-1], refs[-1]
    copies = [pltpu.make_async_copy(refs[at], outs[at], sems.at[at]) for at in range(count)]
    for copy in copies:
        copy.start()
    for copy in copies:
        copy.wait()


def hold(arrays, after):
    count = len(arrays)
    return pl.pallas_call(
        functools.partial(hold_kernel, count),
        out_shape=[jax.ShapeDtypeStruct(array.shape, array.dtype) for array in arrays],
        in_specs=[unread()] * (count + len(after)),
        out_specs=[vmem()] * count,
        scratch_shapes=[pltpu.SemaphoreType.DMA((count,))],
        compiler_params=params(2),
        cost_estimate=cost(1),
        name="hold",
    )(*arrays, *after)


def pack(cycle, places, tensors):
    rows, model = tensors[0].shape
    width = model // cycle
    return pl.pallas_call(
        functools.partial(pack_kernel, cycle, places),
        out_shape=[jax.ShapeDtypeStruct((3 * rows + META, width), bf16)] * len(places),
        in_specs=[anywhere() if width % 128 == 0 else vmem()] * 3
        + [unread()] * 2,
        out_specs=[vmem()] * len(places),
        scratch_shapes=[
            pltpu.SMEM(tensors[3].shape, jnp.int32),
            pltpu.SMEM(tensors[4].shape, jnp.int32),
            pltpu.SemaphoreType.DMA((cycle, 3)),
            pltpu.SemaphoreType.DMA((2,)),
        ],
        compiler_params=params(62),
        cost_estimate=cost(5),
        name="pack",
    )(*tensors)


def gather_kernel(cycle, *refs):
    chunks = refs[:cycle]
    q_all, k_all, v_all, k_t, v_t, bias, word = refs[-7:]
    word[...] = jnp.zeros(word.shape, word.dtype)
    rows = q_all.shape[0] // cycle
    for place in range(cycle):
        for at, part in enumerate((q_all, k_all, v_all)):
            part[place * rows:(place + 1) * rows, :] = chunks[place][at * rows:(at + 1) * rows, :]
    k_t[...] = k_all[...].astype(f32).T.astype(bf16)
    v_t[...] = v_all[...].astype(f32).T.astype(bf16)
    lines = lax.broadcasted_iota(jnp.int32, (rows, rows), 0).astype(f32)
    lists = [chunks[place][3 * rows:, :].astype(f32) for place in range(cycle)]
    for key_place in range(cycle):
        count = lists[key_place][META - 1:, :1]
        valid = lines < count
        for query_place in range(cycle):
            way = key_place ^ query_place
            times = lists[query_place][way:way + 1, :1]
            term = jnp.where(times > 0, jnp.log2(jnp.maximum(times, 1.0)), absent)
            bias[
                key_place * rows:(key_place + 1) * rows,
                query_place * rows:(query_place + 1) * rows,
            ] = jnp.where(valid, term, absent)


def gather(cycle, chunks, after=()):
    width = chunks[0].shape[1]
    rows = (chunks[0].shape[0] - META) // 3
    tokens = rows * cycle
    return pl.pallas_call(
        functools.partial(gather_kernel, cycle),
        out_shape=[jax.ShapeDtypeStruct((tokens, width), bf16)] * 3
        + [jax.ShapeDtypeStruct((width, tokens), bf16)] * 2
        + [jax.ShapeDtypeStruct((tokens, tokens), f32), jax.ShapeDtypeStruct((16, 128), bf16)],
        in_specs=[vmem()] * cycle + [unread()] * len(after),
        out_specs=[vmem()] * 7,
        compiler_params=params(8 if tokens <= 512 else 40),
        cost_estimate=cost(5),
        name="gather",
    )(*chunks, *after)


def head_tile(width):
    return min(128, width)


def only_head(tile, which):
    lanes = lax.broadcasted_iota(jnp.int32, tile.shape, 1)
    inside = (lanes >= which * HEAD_DIM) & (lanes < (which + 1) * HEAD_DIM)
    return jnp.where(inside, tile, jnp.zeros_like(tile))


def forward_kernel(query_tile, parts, q_all, k_all, v_t, bias, *refs):
    outs = refs[-2 - parts:-2]
    att_t, lse = refs[-2:]
    tokens, width = q_all.shape
    tile = head_tile(width)
    for start in range(0, tokens, query_tile):
        span = slice(start, start + query_tile)
        for head in range(width // HEAD_DIM):
            at = head * HEAD_DIM // tile * tile
            which = (head * HEAD_DIM - at) // HEAD_DIM
            scores = dot_nt(
                k_all[:, at:at + tile], only_head(q_all[span, at:at + tile], which)
            )
            scores = scores * log2_scale + bias[:, span]
            largest = jnp.max(scores, axis=0, keepdims=True)
            expo = jnp.exp2(scores - largest)
            total = jnp.sum(expo, axis=0, keepdims=True)
            probs = (expo * (1.0 / total)).astype(bf16)
            lse[head:head + 1, span] = largest + jnp.log2(total)
            att_t[head * HEAD_DIM:(head + 1) * HEAD_DIM, span] = dot_nn(
                v_t[head * HEAD_DIM:(head + 1) * HEAD_DIM, :], probs
            )
    attended = att_t[...].T.astype(bf16)
    filled = 0
    for out in outs:
        out[...] = attended[filled:filled + out.shape[0], :]
        filled += out.shape[0]


def forward(cycle, together, q_all, k_all, v_t, bias, after=()):
    tokens, width = q_all.shape
    rows = tokens // cycle
    parts = cycle // together
    outs = pl.pallas_call(
        functools.partial(forward_kernel, min(tokens, 512), parts),
        out_shape=[jax.ShapeDtypeStruct((together * rows, width), bf16)] * parts
        + [
            jax.ShapeDtypeStruct((width, tokens), f32),
            jax.ShapeDtypeStruct((8, tokens), f32),
        ],
        in_specs=[vmem()] * 4 + [unread()] * len(after),
        out_specs=[vmem()] * (parts + 2),
        compiler_params=params(16 if tokens <= 512 else 60),
        cost_estimate=cost(3),
        name="forward",
    )(q_all, k_all, v_t, bias, *after)
    return outs[:parts], outs[parts], outs[parts + 1]


def backward_kernel(cycle, query_tile, grad_count, att_count, *refs):
    q_all, k_all, v_all, k_t, bias, att_t, lse = refs[:7]
    refs = refs[7:]
    grads = refs[:grad_count]
    attended = refs[grad_count:grad_count + att_count]
    outs = refs[-4 - cycle:-4]
    g_all, dq_t, dk, dv = refs[-4:]
    width = q_all.shape[1]
    tokens = q_all.shape[0]
    rows = tokens // cycle
    filled = 0
    for grad in grads:
        g_all[filled:filled + grad.shape[0], :] = grad[...]
        filled += grad.shape[0]
    tile = head_tile(width)
    g_t = g_all[...].astype(f32).T
    product = g_t * att_t[...].astype(bf16).astype(f32)
    for start in range(0, tokens, query_tile):
        span = slice(start, start + query_tile)
        for at in range(0, width, tile):
            dk_tile = dv_tile = None
            for which in range(tile // HEAD_DIM):
                low = at + which * HEAD_DIM
                head = low // HEAD_DIM
                delta = jnp.sum(product[low:low + HEAD_DIM, span], axis=0, keepdims=True)
                q_head = only_head(q_all[span, at:at + tile], which)
                g_head = only_head(g_all[span, at:at + tile], which)
                scores = dot_nt(k_all[:, at:at + tile], q_head)
                probs = jnp.exp2(
                    scores * log2_scale + bias[:, span] - lse[head:head + 1, span]
                )
                grad_probs = dot_nt(v_all[:, at:at + tile], g_head)
                grad_scores = (probs * (grad_probs - delta)).astype(bf16)
                dk_head = dot_nn(grad_scores, q_head)
                dv_head = dot_nn(probs.astype(bf16), g_head)
                dk_tile = dk_head if dk_tile is None else dk_tile + dk_head
                dv_tile = dv_head if dv_tile is None else dv_tile + dv_head
                dq_t[low:low + HEAD_DIM, span] = dot_nn(k_t[low:low + HEAD_DIM, :], grad_scores)
            if start == 0:
                dk[:, at:at + tile] = dk_tile
                dv[:, at:at + tile] = dv_tile
            else:
                dk[:, at:at + tile] += dk_tile
                dv[:, at:at + tile] += dv_tile
    dq = (dq_t[...] * score_scale).T.astype(bf16)
    for place in range(cycle):
        span = slice(place * rows, (place + 1) * rows)
        outs[place][:rows, :] = dq[span, :]
        outs[place][rows:2 * rows, :] = (dk[span, :] * score_scale).astype(bf16)
        outs[place][2 * rows:3 * rows, :] = dv[span, :].astype(bf16)
        if attended:
            outs[place][3 * rows:, :] = attended[place][...]


def backward(cycle, inputs, grads, attended, after):
    tokens, width = inputs[0].shape
    rows = tokens // cycle
    return pl.pallas_call(
        functools.partial(backward_kernel, cycle, min(tokens, 512), len(grads), len(attended)),
        out_shape=[jax.ShapeDtypeStruct(((4 if attended else 3) * rows, width), bf16)] * cycle,
        in_specs=[vmem()] * (len(inputs) + len(grads) + len(attended)) + [unread()] * len(after),
        out_specs=[vmem()] * cycle,
        scratch_shapes=[
            pltpu.VMEM((tokens, width), bf16),
            pltpu.VMEM((width, tokens), f32),
            pltpu.VMEM((tokens, width), f32),
            pltpu.VMEM((tokens, width), f32),
        ],
        compiler_params=params(16 if tokens <= 512 else 60),
        cost_estimate=cost(3),
        name="backward",
    )(*inputs, *grads, *attended, *after)


def fetch_rows(out_weight, place):
    cycle, count = lax.axis_size("seq"), lax.axis_size("mp")
    pairs = []
    for member in range(cycle):
        for rank in range(count):
            owner = 2 * group_of(cycle, member ^ place, rank // 2) + rank % 2
            pairs.append((member * count + owner, member * count + rank))
    return lax.ppermute(out_weight, ("seq", "mp"), pairs)


def with_other_core(half):
    return [half, exchange(half, "mp", 1)]


def both_halves(halves, core):
    mine, other = halves[0][...], halves[1][...]
    first = core == 0
    return jnp.concatenate([jnp.where(first, mine, other), jnp.where(first, other, mine)], axis=0)


def half_columns(halves, core, side):
    half = halves[0].shape[0]
    return columns_at((core if side == 0 else 1 - core) * half, half)


def group_kernel(count, *refs):
    ups, halves = refs[:count], refs[count:count + 2]
    out = refs[-1]
    rows = ups[0].shape[0]
    _, _, core = my_place()
    for side in range(2):
        weight = halves[side][...]
        for block, ref in enumerate(ups):
            out[block * rows:(block + 1) * rows, half_columns(halves, core, side)] = dot_nt(
                ref[...], weight
            ).astype(bf16)


def group_grads(upstreams, halves, after):
    rows, width = upstreams[0].shape[0], 2 * halves[0].shape[0]
    return pl.pallas_call(
        functools.partial(group_kernel, len(upstreams)),
        out_shape=jax.ShapeDtypeStruct((len(upstreams) * rows, width), bf16),
        in_specs=[vmem()] * (len(upstreams) + 2) + [unread()] * len(after),
        out_specs=vmem(),
        compiler_params=params(8),
        cost_estimate=cost(1),
        name="group_grads",
    )(*upstreams, *halves, *after)


def partial_kernel(att_ref, mine, other, own, *outs):
    rows = own.shape[0]
    _, _, core = my_place()
    weight = both_halves((mine, other), core)
    own[...] = dot_nn(att_ref[:rows, :], weight)
    for block, out in enumerate(outs):
        out[...] = dot_nn(att_ref[(block + 1) * rows:(block + 2) * rows, :], weight).astype(bf16)


def partials(cycle, attended, halves):
    rows, model = attended.shape[0] // cycle, halves[0].shape[1]
    return pl.pallas_call(
        partial_kernel,
        out_shape=[jax.ShapeDtypeStruct((rows, model), f32)]
        + [jax.ShapeDtypeStruct((rows, model), bf16)] * (cycle - 1),
        in_specs=[vmem()] * 3,
        out_specs=[vmem()] * cycle,
        compiler_params=params(12),
        cost_estimate=cost(1),
        name="partials",
    )(attended, *halves)


def grad_kernel(cycle, up_ref, *refs):
    _, _, core = my_place()
    outs = refs[2 * cycle:]
    for place in range(cycle):
        rows = both_halves(refs[2 * place:2 * place + 2], core)
        outs[place][...] = dot_nt(up_ref[...], rows).astype(bf16)


def project_grad(cycle, upstream, halves):
    rows, model = upstream.shape
    return pl.pallas_call(
        functools.partial(grad_kernel, cycle),
        out_shape=[jax.ShapeDtypeStruct((rows, model // cycle), bf16)] * cycle,
        in_specs=[vmem()] * (1 + 2 * cycle),
        out_specs=[vmem()] * cycle,
        compiler_params=params(8),
        name="project_grad",
    )(upstream, *halves)


def place_columns(chunks, outs, sems):
    cycle = len(chunks)
    rows, model = outs[0].shape
    width = model // cycle
    own, chip, _ = my_place()
    copies = []
    for place in range(cycle):
        group = group_of(cycle, lax.bitwise_xor(own, place), chip)
        if width % 128 == 0:
            for at, out in enumerate(outs):
                copies.append(
                    pltpu.make_async_copy(
                        chunks[place].at[at * rows:(at + 1) * rows, :],
                        out.at[:, columns_at(group * width, width)],
                        sems.at[place, at],
                    )
                )
                copies[-1].start()
        else:
            for other in range(cycle):
                @pl.when(group == other)
                def _():
                    for at, out in enumerate(outs):
                        out[:, other * width:(other + 1) * width] = chunks[place][
                            at * rows:(at + 1) * rows, :
                        ]
    return copies


def finish_kernel(cycle, *refs):
    chunks = refs[:cycle]
    mixed, *outs = refs[-5:-1]
    copies = place_columns(chunks, outs, refs[-1])
    rows = mixed.shape[0]
    if len(refs) == 2 * cycle + 5:
        total = refs[cycle][...]
        for landed in refs[cycle + 1:2 * cycle]:
            total = total + landed[...].astype(f32)
        mixed[...] = total.astype(bf16)
    else:
        halves = refs[cycle:3 * cycle]
        _, _, core = my_place()
        total = None
        for place in range(cycle):
            weight = both_halves(halves[2 * place:2 * place + 2], core)
            term = dot_nn(chunks[place][3 * rows:, :], weight)
            total = term if total is None else total + term
        mixed[...] = total.astype(bf16)
    for copy in copies:
        copy.wait()


def finish(cycle, rows, chunks, others):
    model = chunks[0].shape[1] * cycle
    aligned = model // cycle % 128 == 0
    return pl.pallas_call(
        functools.partial(finish_kernel, cycle),
        out_shape=[jax.ShapeDtypeStruct((rows, model), bf16)] * 4,
        in_specs=[vmem()] * (cycle + len(others)),
        out_specs=[vmem()] + [anywhere() if aligned else vmem()] * 3,
        scratch_shapes=[pltpu.SemaphoreType.DMA((cycle, 3))],
        compiler_params=params(8),
        name="finish",
    )(*chunks, *others)


def local(queries, keys, values, out_weight, upstream, adjacency, counts):
    cycle = lax.axis_size("seq")
    rows = queries.shape[0]
    tensors = (queries, keys, values, adjacency, counts.reshape(1, 1))
    if is_square():
        return square(cycle, rows, tensors, out_weight, upstream)
    chunks = swapped(list(pack(cycle, range(cycle), tensors)))
    halves = []
    for place in range(cycle):
        halves += with_other_core(fetch_rows(out_weight, place))
    q_all, k_all, v_all, k_t, v_t, bias, _ = gather(cycle, chunks)
    attended, att_t, lse = forward(cycle, 1, q_all, k_all, v_t, bias)
    grads = swapped(project_grad(cycle, upstream, halves))
    inputs = (q_all, k_all, v_all, k_t, bias, att_t, lse)
    terms = swapped(backward(cycle, inputs, grads, attended, []))
    return tuple(finish(cycle, rows, terms, halves))


def square(cycle, rows, tensors, out_weight, upstream):
    next_x, next_y = exchange(upstream, "seq", 1), exchange(upstream, "seq", 2)
    chunks = swapped(list(pack(cycle, range(cycle), tensors)))
    (held_weight,) = hold((out_weight,), [next_x, next_y])
    own_rows = with_other_core(fetch_rows(held_weight, 0))
    q_all, k_all, v_all, k_t, v_t, bias, word = gather(cycle, chunks)
    (held_y,) = hold((next_y,), [word])
    across = exchange(held_y, "seq", 1)
    (attended,), att_t, lse = forward(cycle, cycle, q_all, k_all, v_t, bias)
    mixed = list(partials(cycle, attended, own_rows))
    grads = [group_grads((upstream, next_x, next_y, across), own_rows, mixed[:1])]
    inputs = (q_all, k_all, v_all, k_t, bias, att_t, lse)
    mixed = swapped(mixed)
    terms = list(backward(cycle, inputs, grads, [], []))
    (terms[3],) = hold((terms[3],), mixed[1:])
    return tuple(finish(cycle, rows, swapped(terms), mixed))


def solution(mesh):
    tokens = P(("seq", "mp"), None)
    return jax.shard_map(
        local,
        mesh=mesh,
        in_specs=(tokens, tokens, tokens, P("mp", None), tokens, tokens, P(("seq", "mp"))),
        out_specs=(tokens,) * 4,
        check_vma=False,
    )
```

```python
import functools

import jax
import jax.numpy as jnp
from jax import lax
from jax.experimental import pallas as pl
from jax.experimental.pallas import tpu as pltpu
from jax.sharding import PartitionSpec as P

HEADS = 16
HEAD_DIM = 64
META = 32

score_scale = 0.125
log2_scale = 0.125 * 1.4426950408889634
cycle_offsets = (1, -1, 2, -2)
absent = -1e30
bf16 = jnp.bfloat16
f32 = jnp.float32


def dot_nn(a, b):
    return lax.dot_general(a, b, (((1,), (0,)), ((), ())), preferred_element_type=f32)


def dot_nt(a, b):
    return lax.dot_general(a, b, (((1,), (1,)), ((), ())), preferred_element_type=f32)


def vmem():
    return pl.BlockSpec(memory_space=pltpu.VMEM)


def params(mib):
    return pltpu.CompilerParams(vmem_limit_bytes=int(mib * 1024) * 1024)


def unread():
    return pl.BlockSpec(memory_space=pl.ANY)


def anywhere():
    return pl.BlockSpec(memory_space=pltpu.HBM)


def cost(micros):
    return pl.CostEstimate(flops=int(micros * 1e9), bytes_accessed=0, transcendentals=0)


def exchange(value, axis, distance):
    count = lax.axis_size(axis)
    return lax.ppermute(value, axis, [(i, i ^ distance) for i in range(count)])


def turned(distance):
    return distance ^ (((distance ^ (distance >> 1)) & 1) * 3)


def exchange_by_core(value, distances):
    count = lax.axis_size("mp")
    pairs = [
        (member * count + rank, (member ^ distances[rank % 2]) * count + rank)
        for member in range(lax.axis_size("seq"))
        for rank in range(count)
    ]
    return lax.ppermute(value, ("seq", "mp"), pairs)


def is_square():
    return lax.axis_size("seq") == 4 and lax.axis_size("mp") == 8


def swapped(chunks):
    return [chunks[0]] + [exchange(chunks[k], "seq", k) for k in range(1, len(chunks))]


def group_of(cycle, member, chip):
    turn = (member + chip) % cycle
    return turned(turn) if cycle == 4 else turn


def my_place():
    rank = lax.axis_index("mp")
    return lax.axis_index("seq"), rank // 2, lax.rem(rank, 2)


def columns_at(first, width):
    return pl.ds(pl.multiple_of(first, width), width)


def pack_kernel(cycle, places, q_ref, k_ref, v_ref, adj_any, cnt_any, *refs):
    refs, (adj_ref, cnt_ref, sems, more_sems) = refs[:-4], refs[-4:]
    outs = refs
    rows, model = q_ref.shape
    width = model // cycle
    own, chip, _ = my_place()
    lists = [
        pltpu.make_async_copy(adj_any, adj_ref, more_sems.at[0]),
        pltpu.make_async_copy(cnt_any, cnt_ref, more_sems.at[1]),
    ]
    for copy in lists:
        copy.start()
    copies = []
    if width % 128 == 0:
        for place, out in zip(places, outs):
            group = group_of(cycle, lax.bitwise_xor(own, place), chip)
            for at, ref in enumerate((q_ref, k_ref, v_ref)):
                copies.append(
                    pltpu.make_async_copy(
                        ref.at[:, columns_at(group * width, width)],
                        out.at[at * rows:(at + 1) * rows, :],
                        sems.at[place, at],
                    )
                )
                copies[-1].start()
    for copy in lists:
        copy.wait()
    lines = lax.broadcasted_iota(jnp.int32, (META, width), 0)
    meta = jnp.where(lines == 0, 1, 0)
    for column, offset in enumerate(cycle_offsets):
        named = lax.rem(own - offset + 2 * cycle, cycle)
        meta = meta + jnp.where(
            (lines == lax.bitwise_xor(own, named)) & (adj_ref[0, column] > 0), 1, 0
        )
    meta = jnp.where(lines == META - 1, cnt_ref[0, 0], meta).astype(f32).astype(bf16)
    for place, out in zip(places, outs):
        out[3 * rows:, :] = meta
        if width % 128:
            group = group_of(cycle, lax.bitwise_xor(own, place), chip)
            for other in range(cycle):
                @pl.when(group == other)
                def _():
                    for at, ref in enumerate((q_ref, k_ref, v_ref)):
                        out[at * rows:(at + 1) * rows, :] = ref[
                            :, other * width:(other + 1) * width
                        ]
    for copy in copies:
        copy.wait()


def hold_kernel(count, *refs):
    outs, sems = refs[-count - 1:-1], refs[-1]
    copies = [pltpu.make_async_copy(refs[at], outs[at], sems.at[at]) for at in range(count)]
    for copy in copies:
        copy.start()
    for copy in copies:
        copy.wait()


def hold(arrays, after):
    count = len(arrays)
    return pl.pallas_call(
        functools.partial(hold_kernel, count),
        out_shape=[jax.ShapeDtypeStruct(array.shape, array.dtype) for array in arrays],
        in_specs=[unread()] * (count + len(after)),
        out_specs=[vmem()] * count,
        scratch_shapes=[pltpu.SemaphoreType.DMA((count,))],
        compiler_params=params(2),
        cost_estimate=cost(1),
        name="hold",
    )(*arrays, *after)


def pack(cycle, places, tensors):
    rows, model = tensors[0].shape
    width = model // cycle
    return pl.pallas_call(
        functools.partial(pack_kernel, cycle, places),
        out_shape=[jax.ShapeDtypeStruct((3 * rows + META, width), bf16)] * len(places),
        in_specs=[anywhere() if width % 128 == 0 else vmem()] * 3
        + [unread()] * 2,
        out_specs=[vmem()] * len(places),
        scratch_shapes=[
            pltpu.SMEM(tensors[3].shape, jnp.int32),
            pltpu.SMEM(tensors[4].shape, jnp.int32),
            pltpu.SemaphoreType.DMA((cycle, 3)),
            pltpu.SemaphoreType.DMA((2,)),
        ],
        compiler_params=params(62),
        cost_estimate=cost(5),
        name="pack",
    )(*tensors)


def gather_kernel(cycle, *refs):
    chunks = refs[:cycle]
    q_all, k_all, v_all, k_t, v_t, bias, word = refs[-7:]
    word[...] = jnp.zeros(word.shape, word.dtype)
    rows = q_all.shape[0] // cycle
    for place in range(cycle):
        for at, part in enumerate((q_all, k_all, v_all)):
            part[place * rows:(place + 1) * rows, :] = chunks[place][at * rows:(at + 1) * rows, :]
    k_t[...] = k_all[...].astype(f32).T.astype(bf16)
    v_t[...] = v_all[...].astype(f32).T.astype(bf16)
    lines = lax.broadcasted_iota(jnp.int32, (rows, rows), 0).astype(f32)
    lists = [chunks[place][3 * rows:, :].astype(f32) for place in range(cycle)]
    for key_place in range(cycle):
        count = lists[key_place][META - 1:, :1]
        valid = lines < count
        for query_place in range(cycle):
            way = key_place ^ query_place
            times = lists[query_place][way:way + 1, :1]
            term = jnp.where(times > 0, jnp.log2(jnp.maximum(times, 1.0)), absent)
            bias[
                key_place * rows:(key_place + 1) * rows,
                query_place * rows:(query_place + 1) * rows,
            ] = jnp.where(valid, term, absent)


def gather(cycle, chunks, after=()):
    width = chunks[0].shape[1]
    rows = (chunks[0].shape[0] - META) // 3
    tokens = rows * cycle
    return pl.pallas_call(
        functools.partial(gather_kernel, cycle),
        out_shape=[jax.ShapeDtypeStruct((tokens, width), bf16)] * 3
        + [jax.ShapeDtypeStruct((width, tokens), bf16)] * 2
        + [jax.ShapeDtypeStruct((tokens, tokens), f32), jax.ShapeDtypeStruct((16, 128), bf16)],
        in_specs=[vmem()] * cycle + [unread()] * len(after),
        out_specs=[vmem()] * 7,
        compiler_params=params(8 if tokens <= 512 else 40),
        cost_estimate=cost(5),
        name="gather",
    )(*chunks, *after)


def head_tile(width):
    return min(128, width)


def only_head(tile, which):
    lanes = lax.broadcasted_iota(jnp.int32, tile.shape, 1)
    inside = (lanes >= which * HEAD_DIM) & (lanes < (which + 1) * HEAD_DIM)
    return jnp.where(inside, tile, jnp.zeros_like(tile))


def forward_kernel(query_tile, parts, q_all, k_all, v_t, bias, *refs):
    outs = refs[-2 - parts:-2]
    att_t, lse = refs[-2:]
    tokens, width = q_all.shape
    tile = head_tile(width)
    for start in range(0, tokens, query_tile):
        span = slice(start, start + query_tile)
        for head in range(width // HEAD_DIM):
            at = head * HEAD_DIM // tile * tile
            which = (head * HEAD_DIM - at) // HEAD_DIM
            scores = dot_nt(
                k_all[:, at:at + tile], only_head(q_all[span, at:at + tile], which)
            )
            scores = scores * log2_scale + bias[:, span]
            largest = jnp.max(scores, axis=0, keepdims=True)
            expo = jnp.exp2(scores - largest)
            total = jnp.sum(expo, axis=0, keepdims=True)
            probs = (expo * (1.0 / total)).astype(bf16)
            lse[head:head + 1, span] = largest + jnp.log2(total)
            att_t[head * HEAD_DIM:(head + 1) * HEAD_DIM, span] = dot_nn(
                v_t[head * HEAD_DIM:(head + 1) * HEAD_DIM, :], probs
            )
    attended = att_t[...].T.astype(bf16)
    filled = 0
    for out in outs:
        out[...] = attended[filled:filled + out.shape[0], :]
        filled += out.shape[0]


def forward(cycle, together, q_all, k_all, v_t, bias, after=()):
    tokens, width = q_all.shape
    rows = tokens // cycle
    parts = cycle // together
    outs = pl.pallas_call(
        functools.partial(forward_kernel, min(tokens, 512), parts),
        out_shape=[jax.ShapeDtypeStruct((together * rows, width), bf16)] * parts
        + [
            jax.ShapeDtypeStruct((width, tokens), f32),
            jax.ShapeDtypeStruct((8, tokens), f32),
        ],
        in_specs=[vmem()] * 4 + [unread()] * len(after),
        out_specs=[vmem()] * (parts + 2),
        compiler_params=params(16 if tokens <= 512 else 60),
        cost_estimate=cost(3),
        name="forward",
    )(q_all, k_all, v_t, bias, *after)
    return outs[:parts], outs[parts], outs[parts + 1]


def backward_kernel(cycle, query_tile, grad_count, att_count, *refs):
    q_all, k_all, v_all, k_t, bias, att_t, lse = refs[:7]
    refs = refs[7:]
    grads = refs[:grad_count]
    attended = refs[grad_count:grad_count + att_count]
    outs = refs[-4 - cycle:-4]
    g_all, dq_t, dk, dv = refs[-4:]
    width = q_all.shape[1]
    tokens = q_all.shape[0]
    rows = tokens // cycle
    filled = 0
    for grad in grads:
        g_all[filled:filled + grad.shape[0], :] = grad[...]
        filled += grad.shape[0]
    tile = head_tile(width)
    g_t = g_all[...].astype(f32).T
    product = g_t * att_t[...].astype(bf16).astype(f32)
    for start in range(0, tokens, query_tile):
        span = slice(start, start + query_tile)
        for at in range(0, width, tile):
            dk_tile = dv_tile = None
            for which in range(tile // HEAD_DIM):
                low = at + which * HEAD_DIM
                head = low // HEAD_DIM
                delta = jnp.sum(product[low:low + HEAD_DIM, span], axis=0, keepdims=True)
                q_head = only_head(q_all[span, at:at + tile], which)
                g_head = only_head(g_all[span, at:at + tile], which)
                scores = dot_nt(k_all[:, at:at + tile], q_head)
                probs = jnp.exp2(
                    scores * log2_scale + bias[:, span] - lse[head:head + 1, span]
                )
                grad_probs = dot_nt(v_all[:, at:at + tile], g_head)
                grad_scores = (probs * (grad_probs - delta)).astype(bf16)
                dk_head = dot_nn(grad_scores, q_head)
                dv_head = dot_nn(probs.astype(bf16), g_head)
                dk_tile = dk_head if dk_tile is None else dk_tile + dk_head
                dv_tile = dv_head if dv_tile is None else dv_tile + dv_head
                dq_t[low:low + HEAD_DIM, span] = dot_nn(k_t[low:low + HEAD_DIM, :], grad_scores)
            if start == 0:
                dk[:, at:at + tile] = dk_tile
                dv[:, at:at + tile] = dv_tile
            else:
                dk[:, at:at + tile] += dk_tile
                dv[:, at:at + tile] += dv_tile
    dq = (dq_t[...] * score_scale).T.astype(bf16)
    for place in range(cycle):
        span = slice(place * rows, (place + 1) * rows)
        outs[place][:rows, :] = dq[span, :]
        outs[place][rows:2 * rows, :] = (dk[span, :] * score_scale).astype(bf16)
        outs[place][2 * rows:3 * rows, :] = dv[span, :].astype(bf16)
        if attended:
            outs[place][3 * rows:, :] = attended[place][...]


def backward(cycle, inputs, grads, attended, after):
    tokens, width = inputs[0].shape
    rows = tokens // cycle
    return pl.pallas_call(
        functools.partial(backward_kernel, cycle, min(tokens, 512), len(grads), len(attended)),
        out_shape=[jax.ShapeDtypeStruct(((4 if attended else 3) * rows, width), bf16)] * cycle,
        in_specs=[vmem()] * (len(inputs) + len(grads) + len(attended)) + [unread()] * len(after),
        out_specs=[vmem()] * cycle,
        scratch_shapes=[
            pltpu.VMEM((tokens, width), bf16),
            pltpu.VMEM((width, tokens), f32),
            pltpu.VMEM((tokens, width), f32),
            pltpu.VMEM((tokens, width), f32),
        ],
        compiler_params=params(16 if tokens <= 512 else 60),
        cost_estimate=cost(3),
        name="backward",
    )(*inputs, *grads, *attended, *after)


def fetch_rows(out_weight, place):
    cycle, count = lax.axis_size("seq"), lax.axis_size("mp")
    pairs = []
    for member in range(cycle):
        for rank in range(count):
            owner = 2 * group_of(cycle, member ^ place, rank // 2) + rank % 2
            pairs.append((member * count + owner, member * count + rank))
    return lax.ppermute(out_weight, ("seq", "mp"), pairs)


def with_other_core(half):
    return [half, exchange(half, "mp", 1)]


def both_halves(halves, core):
    mine, other = halves[0][...], halves[1][...]
    first = core == 0
    return jnp.concatenate([jnp.where(first, mine, other), jnp.where(first, other, mine)], axis=0)


def half_columns(halves, core, side):
    half = halves[0].shape[0]
    return columns_at((core if side == 0 else 1 - core) * half, half)


def group_kernel(count, *refs):
    ups, halves = refs[:count], refs[count:count + 2]
    out = refs[-1]
    rows = ups[0].shape[0]
    _, _, core = my_place()
    for side in range(2):
        weight = halves[side][...]
        for block, ref in enumerate(ups):
            out[block * rows:(block + 1) * rows, half_columns(halves, core, side)] = dot_nt(
                ref[...], weight
            ).astype(bf16)


def group_grads(upstreams, halves, after):
    rows, width = upstreams[0].shape[0], 2 * halves[0].shape[0]
    return pl.pallas_call(
        functools.partial(group_kernel, len(upstreams)),
        out_shape=jax.ShapeDtypeStruct((len(upstreams) * rows, width), bf16),
        in_specs=[vmem()] * (len(upstreams) + 2) + [unread()] * len(after),
        out_specs=vmem(),
        compiler_params=params(8),
        cost_estimate=cost(1),
        name="group_grads",
    )(*upstreams, *halves, *after)


def partial_kernel(att_ref, mine, other, own, kept, sent):
    rows = own.shape[0]
    _, _, core = my_place()
    weight = both_halves((mine, other), core)

    def product(block):
        return dot_nn(att_ref[pl.ds(pl.multiple_of(block * rows, rows), rows), :], weight)

    own[...] = product(0)
    kept[...] = product(1 + core)
    sent[:rows, :] = product(2 - core).astype(bf16)
    sent[rows:, :] = product(3).astype(bf16)


def partials(attended, halves):
    rows, model = attended.shape[0] // 4, halves[0].shape[1]
    return pl.pallas_call(
        partial_kernel,
        out_shape=[jax.ShapeDtypeStruct((rows, model), f32)] * 2
        + [jax.ShapeDtypeStruct((2 * rows, model), bf16)],
        in_specs=[vmem()] * 3,
        out_specs=[vmem()] * 3,
        compiler_params=params(12),
        cost_estimate=cost(1),
        name="partials",
    )(attended, *halves)


def combine_kernel(own, kept, landed, total, sent):
    rows = own.shape[0]
    total[...] = own[...] + landed[:rows, :].astype(f32)
    sent[...] = (kept[...] + landed[rows:, :].astype(f32)).astype(bf16)


def combine(own, kept, landed):
    return pl.pallas_call(
        combine_kernel,
        out_shape=[jax.ShapeDtypeStruct(own.shape, f32), jax.ShapeDtypeStruct(own.shape, bf16)],
        in_specs=[vmem()] * 3,
        out_specs=[vmem()] * 2,
        compiler_params=params(8),
        cost_estimate=cost(1),
        name="combine",
    )(own, kept, landed)


def turn_kernel(w_ref, next_x, next_y, weight, passed, sem):
    copy = pltpu.make_async_copy(w_ref, weight, sem)
    copy.start()
    _, _, core = my_place()
    passed[...] = jnp.where(core == 0, next_y[...], next_x[...])
    copy.wait()


def turn(out_weight, next_x, next_y):
    return pl.pallas_call(
        turn_kernel,
        out_shape=[jax.ShapeDtypeStruct(array.shape, bf16) for array in (out_weight, next_y)],
        in_specs=[unread()] + [vmem()] * 2,
        out_specs=[vmem()] * 2,
        scratch_shapes=[pltpu.SemaphoreType.DMA],
        compiler_params=params(4),
        cost_estimate=cost(1),
        name="turn",
    )(out_weight, next_x, next_y)


def grad_kernel(cycle, up_ref, *refs):
    _, _, core = my_place()
    outs = refs[2 * cycle:]
    for place in range(cycle):
        rows = both_halves(refs[2 * place:2 * place + 2], core)
        outs[place][...] = dot_nt(up_ref[...], rows).astype(bf16)


def project_grad(cycle, upstream, halves):
    rows, model = upstream.shape
    return pl.pallas_call(
        functools.partial(grad_kernel, cycle),
        out_shape=[jax.ShapeDtypeStruct((rows, model // cycle), bf16)] * cycle,
        in_specs=[vmem()] * (1 + 2 * cycle),
        out_specs=[vmem()] * cycle,
        compiler_params=params(8),
        name="project_grad",
    )(upstream, *halves)


def place_columns(chunks, outs, sems):
    cycle = len(chunks)
    rows, model = outs[0].shape
    width = model // cycle
    own, chip, _ = my_place()
    copies = []
    for place in range(cycle):
        group = group_of(cycle, lax.bitwise_xor(own, place), chip)
        if width % 128 == 0:
            for at, out in enumerate(outs):
                copies.append(
                    pltpu.make_async_copy(
                        chunks[place].at[at * rows:(at + 1) * rows, :],
                        out.at[:, columns_at(group * width, width)],
                        sems.at[place, at],
                    )
                )
                copies[-1].start()
        else:
            for other in range(cycle):
                @pl.when(group == other)
                def _():
                    for at, out in enumerate(outs):
                        out[:, other * width:(other + 1) * width] = chunks[place][
                            at * rows:(at + 1) * rows, :
                        ]
    return copies


def finish_kernel(cycle, *refs):
    chunks = refs[:cycle]
    mixed, *outs = refs[-5:-1]
    copies = place_columns(chunks, outs, refs[-1])
    rows = mixed.shape[0]
    if len(refs) == cycle + 7:
        mixed[...] = (refs[cycle][...] + refs[cycle + 1][...].astype(f32)).astype(bf16)
    else:
        halves = refs[cycle:3 * cycle]
        _, _, core = my_place()
        total = None
        for place in range(cycle):
            weight = both_halves(halves[2 * place:2 * place + 2], core)
            term = dot_nn(chunks[place][3 * rows:, :], weight)
            total = term if total is None else total + term
        mixed[...] = total.astype(bf16)
    for copy in copies:
        copy.wait()


def finish(cycle, rows, chunks, others):
    model = chunks[0].shape[1] * cycle
    aligned = model // cycle % 128 == 0
    return pl.pallas_call(
        functools.partial(finish_kernel, cycle),
        out_shape=[jax.ShapeDtypeStruct((rows, model), bf16)] * 4,
        in_specs=[vmem()] * (cycle + len(others)),
        out_specs=[vmem()] + [anywhere() if aligned else vmem()] * 3,
        scratch_shapes=[pltpu.SemaphoreType.DMA((cycle, 3))],
        compiler_params=params(8),
        name="finish",
    )(*chunks, *others)


def local(queries, keys, values, out_weight, upstream, adjacency, counts):
    cycle = lax.axis_size("seq")
    rows = queries.shape[0]
    tensors = (queries, keys, values, adjacency, counts.reshape(1, 1))
    if is_square():
        return square(cycle, rows, tensors, out_weight, upstream)
    chunks = swapped(list(pack(cycle, range(cycle), tensors)))
    halves = []
    for place in range(cycle):
        halves += with_other_core(fetch_rows(out_weight, place))
    q_all, k_all, v_all, k_t, v_t, bias, _ = gather(cycle, chunks)
    attended, att_t, lse = forward(cycle, 1, q_all, k_all, v_t, bias)
    grads = swapped(project_grad(cycle, upstream, halves))
    inputs = (q_all, k_all, v_all, k_t, bias, att_t, lse)
    terms = swapped(backward(cycle, inputs, grads, attended, []))
    return tuple(finish(cycle, rows, terms, halves))


def square(cycle, rows, tensors, out_weight, upstream):
    next_x, next_y = exchange(upstream, "seq", 1), exchange(upstream, "seq", 2)
    chunks = swapped(list(pack(cycle, range(cycle), tensors)))
    held_weight, passed = turn(out_weight, next_x, next_y)
    across = exchange_by_core(passed, (1, 2))
    own_rows = with_other_core(fetch_rows(held_weight, 0))
    q_all, k_all, v_all, k_t, v_t, bias, word = gather(cycle, chunks)
    (attended,), att_t, lse = forward(cycle, cycle, q_all, k_all, v_t, bias, [across])
    own_mixed, kept, sent = partials(attended, own_rows)
    landed = exchange_by_core(sent, (2, 1))
    grads = [group_grads((upstream, next_x, next_y, across), own_rows, [kept])]
    inputs = (q_all, k_all, v_all, k_t, bias, att_t, lse)
    terms = list(backward(cycle, inputs, grads, [], []))
    own_mixed, next_mixed = combine(own_mixed, kept, landed)
    (terms[3],) = hold((terms[3],), [own_mixed])
    next_mixed = exchange_by_core(next_mixed, (1, 2))
    return tuple(finish(cycle, rows, swapped(terms), [own_mixed, next_mixed]))


def solution(mesh):
    tokens = P(("seq", "mp"), None)
    return jax.shard_map(
        local,
        mesh=mesh,
        in_specs=(tokens, tokens, tokens, P("mp", None), tokens, tokens, P(("seq", "mp"))),
        out_specs=(tokens,) * 4,
        check_vma=False,
    )
```

```python
import functools

import jax
import jax.numpy as jnp
from jax import lax
from jax.experimental import pallas as pl
from jax.experimental.pallas import tpu as pltpu
from jax.sharding import PartitionSpec as P

HEADS = 16
HEAD_DIM = 64
META = 32

score_scale = 0.125
log2_scale = 0.125 * 1.4426950408889634
cycle_offsets = (1, -1, 2, -2)
absent = -1e30
bf16 = jnp.bfloat16
f32 = jnp.float32


def dot_nn(a, b):
    return lax.dot_general(a, b, (((1,), (0,)), ((), ())), preferred_element_type=f32)


def dot_nt(a, b):
    return lax.dot_general(a, b, (((1,), (1,)), ((), ())), preferred_element_type=f32)


def vmem():
    return pl.BlockSpec(memory_space=pltpu.VMEM)


def params(mib):
    return pltpu.CompilerParams(vmem_limit_bytes=int(mib * 1024) * 1024)


def unread():
    return pl.BlockSpec(memory_space=pl.ANY)


def anywhere():
    return pl.BlockSpec(memory_space=pltpu.HBM)


def cost(micros):
    return pl.CostEstimate(flops=int(micros * 1e9), bytes_accessed=0, transcendentals=0)


def exchange(value, axis, distance):
    count = lax.axis_size(axis)
    return lax.ppermute(value, axis, [(i, i ^ distance) for i in range(count)])


def turned(distance):
    return distance ^ (((distance ^ (distance >> 1)) & 1) * 3)


def exchange_by_core(value, distances):
    count = lax.axis_size("mp")
    pairs = [
        (member * count + rank, (member ^ distances[rank % 2]) * count + rank)
        for member in range(lax.axis_size("seq"))
        for rank in range(count)
    ]
    return lax.ppermute(value, ("seq", "mp"), pairs)


def is_square():
    return lax.axis_size("seq") == 4 and lax.axis_size("mp") == 8


def swapped(chunks):
    return [chunks[0]] + [exchange(chunks[k], "seq", k) for k in range(1, len(chunks))]


def longest_first(chunks):
    return [chunks[0]] + [chunks[len(chunks) - k] for k in range(1, len(chunks))]


def group_of(cycle, member, chip):
    turn = (member + chip) % cycle
    return turned(turn) if cycle == 4 else turn


def my_place():
    rank = lax.axis_index("mp")
    return lax.axis_index("seq"), rank // 2, lax.rem(rank, 2)


def columns_at(first, width):
    return pl.ds(pl.multiple_of(first, width), width)


def pack_kernel(cycle, places, q_ref, k_ref, v_ref, adj_any, cnt_any, *refs):
    refs, (adj_ref, cnt_ref, sems, more_sems) = refs[:-4], refs[-4:]
    outs = refs
    rows, model = q_ref.shape
    width = model // cycle
    own, chip, _ = my_place()
    lists = [
        pltpu.make_async_copy(adj_any, adj_ref, more_sems.at[0]),
        pltpu.make_async_copy(cnt_any, cnt_ref, more_sems.at[1]),
    ]
    for copy in lists:
        copy.start()
    copies = []
    if width % 128 == 0:
        for place, out in zip(places, outs):
            group = group_of(cycle, lax.bitwise_xor(own, place), chip)
            for at, ref in enumerate((q_ref, k_ref, v_ref)):
                copies.append(
                    pltpu.make_async_copy(
                        ref.at[:, columns_at(group * width, width)],
                        out.at[at * rows:(at + 1) * rows, :],
                        sems.at[place, at],
                    )
                )
                copies[-1].start()
    for copy in lists:
        copy.wait()
    lines = lax.broadcasted_iota(jnp.int32, (META, width), 0)
    meta = jnp.where(lines == 0, 1, 0)
    for column, offset in enumerate(cycle_offsets):
        named = lax.rem(own - offset + 2 * cycle, cycle)
        meta = meta + jnp.where(
            (lines == lax.bitwise_xor(own, named)) & (adj_ref[0, column] > 0), 1, 0
        )
    meta = jnp.where(lines == META - 1, cnt_ref[0, 0], meta).astype(f32).astype(bf16)
    for place, out in zip(places, outs):
        out[3 * rows:, :] = meta
        if width % 128:
            group = group_of(cycle, lax.bitwise_xor(own, place), chip)
            for other in range(cycle):
                @pl.when(group == other)
                def _():
                    for at, ref in enumerate((q_ref, k_ref, v_ref)):
                        out[at * rows:(at + 1) * rows, :] = ref[
                            :, other * width:(other + 1) * width
                        ]
    for copy in copies:
        copy.wait()


def hold_kernel(count, *refs):
    outs, sems = refs[-count - 1:-1], refs[-1]
    copies = [pltpu.make_async_copy(refs[at], outs[at], sems.at[at]) for at in range(count)]
    for copy in copies:
        copy.start()
    for copy in copies:
        copy.wait()


def hold(arrays, after):
    count = len(arrays)
    return pl.pallas_call(
        functools.partial(hold_kernel, count),
        out_shape=[jax.ShapeDtypeStruct(array.shape, array.dtype) for array in arrays],
        in_specs=[unread()] * (count + len(after)),
        out_specs=[vmem()] * count,
        scratch_shapes=[pltpu.SemaphoreType.DMA((count,))],
        compiler_params=params(2),
        cost_estimate=cost(1),
        name="hold",
    )(*arrays, *after)


def pack(cycle, places, tensors):
    rows, model = tensors[0].shape
    width = model // cycle
    return pl.pallas_call(
        functools.partial(pack_kernel, cycle, places),
        out_shape=[jax.ShapeDtypeStruct((3 * rows + META, width), bf16)] * len(places),
        in_specs=[anywhere() if width % 128 == 0 else vmem()] * 3
        + [unread()] * 2,
        out_specs=[vmem()] * len(places),
        scratch_shapes=[
            pltpu.SMEM(tensors[3].shape, jnp.int32),
            pltpu.SMEM(tensors[4].shape, jnp.int32),
            pltpu.SemaphoreType.DMA((cycle, 3)),
            pltpu.SemaphoreType.DMA((2,)),
        ],
        compiler_params=params(62),
        cost_estimate=cost(5),
        name="pack",
    )(*tensors)


def gather_kernel(cycle, *refs):
    chunks = longest_first(refs[:cycle])
    q_all, k_all, v_all, k_t, v_t, bias = refs[-6:]
    rows = q_all.shape[0] // cycle
    for place in range(cycle):
        for at, part in enumerate((q_all, k_all, v_all)):
            part[place * rows:(place + 1) * rows, :] = chunks[place][at * rows:(at + 1) * rows, :]
    k_t[...] = k_all[...].astype(f32).T.astype(bf16)
    v_t[...] = v_all[...].astype(f32).T.astype(bf16)
    lines = lax.broadcasted_iota(jnp.int32, (rows, rows), 0).astype(f32)
    lists = [chunks[place][3 * rows:, :].astype(f32) for place in range(cycle)]
    for key_place in range(cycle):
        count = lists[key_place][META - 1:, :1]
        valid = lines < count
        for query_place in range(cycle):
            way = key_place ^ query_place
            times = lists[query_place][way:way + 1, :1]
            term = jnp.where(times > 0, jnp.log2(jnp.maximum(times, 1.0)), absent)
            bias[
                key_place * rows:(key_place + 1) * rows,
                query_place * rows:(query_place + 1) * rows,
            ] = jnp.where(valid, term, absent)


def gather(cycle, chunks, after=()):
    width = chunks[0].shape[1]
    rows = (chunks[0].shape[0] - META) // 3
    tokens = rows * cycle
    return pl.pallas_call(
        functools.partial(gather_kernel, cycle),
        out_shape=[jax.ShapeDtypeStruct((tokens, width), bf16)] * 3
        + [jax.ShapeDtypeStruct((width, tokens), bf16)] * 2
        + [jax.ShapeDtypeStruct((tokens, tokens), f32)],
        in_specs=[vmem()] * cycle + [unread()] * len(after),
        out_specs=[vmem()] * 6,
        compiler_params=params(8 if tokens <= 512 else 40),
        cost_estimate=cost(5),
        name="gather",
    )(*longest_first(chunks), *after)


def head_tile(width):
    return min(128, width)


def only_head(tile, which):
    lanes = lax.broadcasted_iota(jnp.int32, tile.shape, 1)
    inside = (lanes >= which * HEAD_DIM) & (lanes < (which + 1) * HEAD_DIM)
    return jnp.where(inside, tile, jnp.zeros_like(tile))


def forward_kernel(query_tile, parts, q_all, k_all, v_t, bias, *refs):
    outs = refs[-2 - parts:-2]
    att_t, lse = refs[-2:]
    tokens, width = q_all.shape
    tile = head_tile(width)
    for start in range(0, tokens, query_tile):
        span = slice(start, start + query_tile)
        for head in range(width // HEAD_DIM):
            at = head * HEAD_DIM // tile * tile
            which = (head * HEAD_DIM - at) // HEAD_DIM
            scores = dot_nt(
                k_all[:, at:at + tile], only_head(q_all[span, at:at + tile], which)
            )
            scores = scores * log2_scale + bias[:, span]
            largest = jnp.max(scores, axis=0, keepdims=True)
            expo = jnp.exp2(scores - largest)
            total = jnp.sum(expo, axis=0, keepdims=True)
            probs = (expo * (1.0 / total)).astype(bf16)
            lse[head:head + 1, span] = largest + jnp.log2(total)
            att_t[head * HEAD_DIM:(head + 1) * HEAD_DIM, span] = dot_nn(
                v_t[head * HEAD_DIM:(head + 1) * HEAD_DIM, :], probs
            )
    attended = att_t[...].T.astype(bf16)
    filled = 0
    for out in outs:
        out[...] = attended[filled:filled + out.shape[0], :]
        filled += out.shape[0]


def forward(cycle, together, q_all, k_all, v_t, bias, after=()):
    tokens, width = q_all.shape
    rows = tokens // cycle
    parts = cycle // together
    outs = pl.pallas_call(
        functools.partial(forward_kernel, min(tokens, 512), parts),
        out_shape=[jax.ShapeDtypeStruct((together * rows, width), bf16)] * parts
        + [
            jax.ShapeDtypeStruct((width, tokens), f32),
            jax.ShapeDtypeStruct((8, tokens), f32),
        ],
        in_specs=[vmem()] * 4 + [unread()] * len(after),
        out_specs=[vmem()] * (parts + 2),
        compiler_params=params(16 if tokens <= 512 else 60),
        cost_estimate=cost(3),
        name="forward",
    )(q_all, k_all, v_t, bias, *after)
    return outs[:parts], outs[parts], outs[parts + 1]


def backward_kernel(cycle, query_tile, grad_count, att_count, *refs):
    q_all, k_all, v_all, k_t, bias, att_t, lse = refs[:7]
    refs = refs[7:]
    grads = refs[:grad_count]
    attended = refs[grad_count:grad_count + att_count]
    outs = refs[-4 - cycle:-4]
    g_all, dq_t, dk, dv = refs[-4:]
    width = q_all.shape[1]
    tokens = q_all.shape[0]
    rows = tokens // cycle
    filled = 0
    for grad in grads:
        g_all[filled:filled + grad.shape[0], :] = grad[...]
        filled += grad.shape[0]
    tile = head_tile(width)
    g_t = g_all[...].astype(f32).T
    product = g_t * att_t[...].astype(bf16).astype(f32)
    for start in range(0, tokens, query_tile):
        span = slice(start, start + query_tile)
        for at in range(0, width, tile):
            dk_tile = dv_tile = None
            for which in range(tile // HEAD_DIM):
                low = at + which * HEAD_DIM
                head = low // HEAD_DIM
                delta = jnp.sum(product[low:low + HEAD_DIM, span], axis=0, keepdims=True)
                q_head = only_head(q_all[span, at:at + tile], which)
                g_head = only_head(g_all[span, at:at + tile], which)
                scores = dot_nt(k_all[:, at:at + tile], q_head)
                probs = jnp.exp2(
                    scores * log2_scale + bias[:, span] - lse[head:head + 1, span]
                )
                grad_probs = dot_nt(v_all[:, at:at + tile], g_head)
                grad_scores = (probs * (grad_probs - delta)).astype(bf16)
                dk_head = dot_nn(grad_scores, q_head)
                dv_head = dot_nn(probs.astype(bf16), g_head)
                dk_tile = dk_head if dk_tile is None else dk_tile + dk_head
                dv_tile = dv_head if dv_tile is None else dv_tile + dv_head
                dq_t[low:low + HEAD_DIM, span] = dot_nn(k_t[low:low + HEAD_DIM, :], grad_scores)
            if start == 0:
                dk[:, at:at + tile] = dk_tile
                dv[:, at:at + tile] = dv_tile
            else:
                dk[:, at:at + tile] += dk_tile
                dv[:, at:at + tile] += dv_tile
    dq = (dq_t[...] * score_scale).T.astype(bf16)
    for place in range(cycle):
        span = slice(place * rows, (place + 1) * rows)
        outs[place][:rows, :] = dq[span, :]
        outs[place][rows:2 * rows, :] = (dk[span, :] * score_scale).astype(bf16)
        outs[place][2 * rows:3 * rows, :] = dv[span, :].astype(bf16)
        if attended:
            outs[place][3 * rows:, :] = attended[place][...]


def backward(cycle, inputs, grads, attended, after):
    tokens, width = inputs[0].shape
    rows = tokens // cycle
    return pl.pallas_call(
        functools.partial(backward_kernel, cycle, min(tokens, 512), len(grads), len(attended)),
        out_shape=[jax.ShapeDtypeStruct(((4 if attended else 3) * rows, width), bf16)] * cycle,
        in_specs=[vmem()] * (len(inputs) + len(grads) + len(attended)) + [unread()] * len(after),
        out_specs=[vmem()] * cycle,
        scratch_shapes=[
            pltpu.VMEM((tokens, width), bf16),
            pltpu.VMEM((width, tokens), f32),
            pltpu.VMEM((tokens, width), f32),
            pltpu.VMEM((tokens, width), f32),
        ],
        compiler_params=params(16 if tokens <= 512 else 60),
        cost_estimate=cost(3),
        name="backward",
    )(*inputs, *grads, *attended, *after)


def fetch_rows(out_weight, place):
    cycle, count = lax.axis_size("seq"), lax.axis_size("mp")
    pairs = []
    for member in range(cycle):
        for rank in range(count):
            owner = 2 * group_of(cycle, member ^ place, rank // 2) + rank % 2
            pairs.append((member * count + owner, member * count + rank))
    return lax.ppermute(out_weight, ("seq", "mp"), pairs)


def with_other_core(half):
    return [half, exchange(half, "mp", 1)]


def both_halves(halves, core):
    mine, other = halves[0][...], halves[1][...]
    first = core == 0
    return jnp.concatenate([jnp.where(first, mine, other), jnp.where(first, other, mine)], axis=0)


def half_columns(halves, core, side):
    half = halves[0].shape[0]
    return columns_at((core if side == 0 else 1 - core) * half, half)


def group_kernel(count, *refs):
    ups, halves = refs[:count], refs[count:count + 2]
    out = refs[-1]
    rows = ups[0].shape[0]
    _, _, core = my_place()
    for side in range(2):
        weight = halves[side][...]
        for block, ref in enumerate(ups):
            out[block * rows:(block + 1) * rows, half_columns(halves, core, side)] = dot_nt(
                ref[...], weight
            ).astype(bf16)


def group_grads(upstreams, halves, after):
    rows, width = upstreams[0].shape[0], 2 * halves[0].shape[0]
    return pl.pallas_call(
        functools.partial(group_kernel, len(upstreams)),
        out_shape=jax.ShapeDtypeStruct((len(upstreams) * rows, width), bf16),
        in_specs=[vmem()] * (len(upstreams) + 2) + [unread()] * len(after),
        out_specs=vmem(),
        compiler_params=params(8),
        cost_estimate=cost(1),
        name="group_grads",
    )(*upstreams, *halves, *after)


def partial_kernel(att_ref, mine, other, *refs):
    own, kept, sent = refs[-3:]
    rows = own.shape[0]
    _, _, core = my_place()
    weight = both_halves((mine, other), core)

    def product(block):
        return dot_nn(att_ref[pl.ds(pl.multiple_of(block * rows, rows), rows), :], weight)

    own[...] = product(0)
    kept[...] = product(1 + core)
    sent[:rows, :] = product(2 - core).astype(bf16)
    sent[rows:, :] = product(3).astype(bf16)


def partials(attended, halves, after):
    rows, model = attended.shape[0] // 4, halves[0].shape[1]
    return pl.pallas_call(
        partial_kernel,
        out_shape=[jax.ShapeDtypeStruct((rows, model), f32)] * 2
        + [jax.ShapeDtypeStruct((2 * rows, model), bf16)],
        in_specs=[vmem()] * 3 + [unread()] * len(after),
        out_specs=[vmem()] * 3,
        compiler_params=params(12),
        cost_estimate=cost(1),
        name="partials",
    )(attended, *halves, *after)


def combine_kernel(own, kept, landed, total, *sent):
    rows = own.shape[0]
    total[...] = own[...] + landed[:rows, :].astype(f32)
    part = rows // len(sent)
    for at, out in enumerate(sent):
        span = slice(at * part, (at + 1) * part)
        out[...] = (
            kept[span, :] + landed[rows + at * part:rows + (at + 1) * part, :].astype(f32)
        ).astype(bf16)


def combine(own, kept, landed):
    return pl.pallas_call(
        combine_kernel,
        out_shape=[jax.ShapeDtypeStruct(own.shape, f32)]
        + [jax.ShapeDtypeStruct((own.shape[0] // 2, own.shape[1]), bf16)] * 2,
        in_specs=[vmem()] * 3,
        out_specs=[vmem()] * 3,
        compiler_params=params(8),
        cost_estimate=cost(1),
        name="combine",
    )(own, kept, landed)


def turn_kernel(w_ref, next_x, next_y, weight, passed, sem):
    copy = pltpu.make_async_copy(w_ref, weight, sem)
    copy.start()
    _, _, core = my_place()
    passed[...] = jnp.where(core == 0, next_y[...], next_x[...])
    copy.wait()


def turn(out_weight, next_x, next_y):
    return pl.pallas_call(
        turn_kernel,
        out_shape=[jax.ShapeDtypeStruct(array.shape, bf16) for array in (out_weight, next_y)],
        in_specs=[unread()] + [vmem()] * 2,
        out_specs=[vmem()] * 2,
        scratch_shapes=[pltpu.SemaphoreType.DMA],
        compiler_params=params(4),
        cost_estimate=cost(1),
        name="turn",
    )(out_weight, next_x, next_y)


def grad_kernel(cycle, up_ref, *refs):
    _, _, core = my_place()
    outs = refs[2 * cycle:]
    for place in range(cycle):
        rows = both_halves(refs[2 * place:2 * place + 2], core)
        outs[place][...] = dot_nt(up_ref[...], rows).astype(bf16)


def project_grad(cycle, upstream, halves):
    rows, model = upstream.shape
    return pl.pallas_call(
        functools.partial(grad_kernel, cycle),
        out_shape=[jax.ShapeDtypeStruct((rows, model // cycle), bf16)] * cycle,
        in_specs=[vmem()] * (1 + 2 * cycle),
        out_specs=[vmem()] * cycle,
        compiler_params=params(8),
        name="project_grad",
    )(upstream, *halves)


def place_columns(chunks, outs, sems):
    cycle = len(chunks)
    rows, model = outs[0].shape
    width = model // cycle
    own, chip, _ = my_place()
    copies = []
    for place in range(cycle):
        group = group_of(cycle, lax.bitwise_xor(own, place), chip)
        if width % 128 == 0:
            for at, out in enumerate(outs):
                copies.append(
                    pltpu.make_async_copy(
                        chunks[place].at[at * rows:(at + 1) * rows, :],
                        out.at[:, columns_at(group * width, width)],
                        sems.at[place, at],
                    )
                )
                copies[-1].start()
        else:
            for other in range(cycle):
                @pl.when(group == other)
                def _():
                    for at, out in enumerate(outs):
                        out[:, other * width:(other + 1) * width] = chunks[place][
                            at * rows:(at + 1) * rows, :
                        ]
    return copies


def finish_kernel(cycle, *refs):
    chunks = longest_first(refs[:cycle])
    mixed, *outs = refs[-5:-1]
    copies = place_columns(chunks, outs, refs[-1])
    rows = mixed.shape[0]
    if len(refs) == cycle + 8:
        for at in range(2):
            span = slice(at * rows // 2, (at + 1) * rows // 2)
            mixed[span, :] = (
                refs[cycle][span, :] + refs[cycle + 1 + at][...].astype(f32)
            ).astype(bf16)
    else:
        halves = refs[cycle:3 * cycle]
        _, _, core = my_place()
        total = None
        for place in range(cycle):
            weight = both_halves(halves[2 * place:2 * place + 2], core)
            term = dot_nn(chunks[place][3 * rows:, :], weight)
            total = term if total is None else total + term
        mixed[...] = total.astype(bf16)
    for copy in copies:
        copy.wait()


def finish(cycle, rows, chunks, others):
    model = chunks[0].shape[1] * cycle
    aligned = model // cycle % 128 == 0
    return pl.pallas_call(
        functools.partial(finish_kernel, cycle),
        out_shape=[jax.ShapeDtypeStruct((rows, model), bf16)] * 4,
        in_specs=[vmem()] * (cycle + len(others)),
        out_specs=[vmem()] + [anywhere() if aligned else vmem()] * 3,
        scratch_shapes=[pltpu.SemaphoreType.DMA((cycle, 3))],
        compiler_params=params(8),
        name="finish",
    )(*longest_first(chunks), *others)


def local(queries, keys, values, out_weight, upstream, adjacency, counts):
    cycle = lax.axis_size("seq")
    rows = queries.shape[0]
    tensors = (queries, keys, values, adjacency, counts.reshape(1, 1))
    if is_square():
        return square(cycle, rows, tensors, out_weight, upstream)
    chunks = swapped(list(pack(cycle, range(cycle), tensors)))
    halves = []
    for place in range(cycle):
        halves += with_other_core(fetch_rows(out_weight, place))
    q_all, k_all, v_all, k_t, v_t, bias = gather(cycle, chunks)
    attended, att_t, lse = forward(cycle, 1, q_all, k_all, v_t, bias)
    grads = swapped(project_grad(cycle, upstream, halves))
    inputs = (q_all, k_all, v_all, k_t, bias, att_t, lse)
    terms = swapped(backward(cycle, inputs, grads, attended, []))
    return tuple(finish(cycle, rows, terms, halves))


def square(cycle, rows, tensors, out_weight, upstream):
    next_x, next_y = exchange(upstream, "seq", 1), exchange(upstream, "seq", 2)
    chunks = swapped(list(pack(cycle, range(cycle), tensors)))
    held_weight, passed = turn(out_weight, next_x, next_y)
    across = exchange_by_core(passed, (1, 2))
    own_rows = with_other_core(fetch_rows(held_weight, 0))
    q_all, k_all, v_all, k_t, v_t, bias = gather(cycle, chunks)
    (attended,), att_t, lse = forward(cycle, cycle, q_all, k_all, v_t, bias, [across])
    own_mixed, kept, sent = partials(attended, own_rows, [])
    landed = exchange_by_core(sent, (2, 1))
    grads = [group_grads((upstream, next_x, next_y, across), own_rows, [kept])]
    inputs = (q_all, k_all, v_all, k_t, bias, att_t, lse)
    terms = list(backward(cycle, inputs, grads, [], []))
    own_mixed, *next_mixed = combine(own_mixed, kept, landed)
    next_mixed = [exchange_by_core(part, (1, 2)) for part in next_mixed]
    return tuple(finish(cycle, rows, swapped(terms), [own_mixed] + next_mixed))


def solution(mesh):
    tokens = P(("seq", "mp"), None)
    return jax.shard_map(
        local,
        mesh=mesh,
        in_specs=(tokens, tokens, tokens, P("mp", None), tokens, tokens, P(("seq", "mp"))),
        out_specs=(tokens,) * 4,
        check_vma=False,
    )
```

```python
import functools

import jax
import jax.numpy as jnp
from jax import lax
from jax.experimental import pallas as pl
from jax.experimental.pallas import tpu as pltpu
from jax.sharding import PartitionSpec as P

HEADS = 16
HEAD_DIM = 64
META = 32

score_scale = 0.125
log2_scale = 0.125 * 1.4426950408889634
cycle_offsets = (1, -1, 2, -2)
absent = -1e30
bf16 = jnp.bfloat16
f32 = jnp.float32


def dot_nn(a, b):
    return lax.dot_general(a, b, (((1,), (0,)), ((), ())), preferred_element_type=f32)


def dot_nt(a, b):
    return lax.dot_general(a, b, (((1,), (1,)), ((), ())), preferred_element_type=f32)


def vmem():
    return pl.BlockSpec(memory_space=pltpu.VMEM)


def params(mib):
    return pltpu.CompilerParams(vmem_limit_bytes=int(mib * 1024) * 1024)


def unread():
    return pl.BlockSpec(memory_space=pl.ANY)


def anywhere():
    return pl.BlockSpec(memory_space=pltpu.HBM)


def cost(micros):
    return pl.CostEstimate(flops=int(micros * 1e9), bytes_accessed=0, transcendentals=0)


def exchange(value, axis, distance):
    count = lax.axis_size(axis)
    return lax.ppermute(value, axis, [(i, i ^ distance) for i in range(count)])


def turned(distance):
    return distance ^ (((distance ^ (distance >> 1)) & 1) * 3)


def exchange_by_core(value, distances):
    count = lax.axis_size("mp")
    pairs = [
        (member * count + rank, (member ^ distances[rank % 2]) * count + rank)
        for member in range(lax.axis_size("seq"))
        for rank in range(count)
    ]
    return lax.ppermute(value, ("seq", "mp"), pairs)


def is_square():
    return lax.axis_size("seq") == 4 and lax.axis_size("mp") == 8


def distance_of(slot):
    if is_square():
        return jnp.where(lax.rem(lax.axis_index("mp"), 2) == 0, slot, turned(slot))
    return slot


def swapped(chunks):
    if is_square():
        return [chunks[0]] + [
            exchange_by_core(chunks[k], (k, turned(k))) for k in range(1, len(chunks))
        ]
    return [chunks[0]] + [exchange(chunks[k], "seq", k) for k in range(1, len(chunks))]


def group_of(cycle, member, chip):
    turn = (member + chip) % cycle
    return turned(turn) if cycle == 4 else turn


def my_place():
    rank = lax.axis_index("mp")
    return lax.axis_index("seq"), rank // 2, lax.rem(rank, 2)


def columns_at(first, width):
    return pl.ds(pl.multiple_of(first, width), width)


def pack_kernel(cycle, places, q_ref, k_ref, v_ref, adj_any, cnt_any, *refs):
    refs, (adj_ref, cnt_ref, sems, more_sems) = refs[:-4], refs[-4:]
    outs = refs
    rows, model = q_ref.shape
    width = model // cycle
    own, chip, _ = my_place()
    lists = [
        pltpu.make_async_copy(adj_any, adj_ref, more_sems.at[0]),
        pltpu.make_async_copy(cnt_any, cnt_ref, more_sems.at[1]),
    ]
    for copy in lists:
        copy.start()
    copies = []
    if width % 128 == 0:
        for place, out in zip(places, outs):
            group = group_of(cycle, lax.bitwise_xor(own, distance_of(place)), chip)
            for at, ref in enumerate((q_ref, k_ref, v_ref)):
                copies.append(
                    pltpu.make_async_copy(
                        ref.at[:, columns_at(group * width, width)],
                        out.at[at * rows:(at + 1) * rows, :],
                        sems.at[place, at],
                    )
                )
                copies[-1].start()
    for copy in lists:
        copy.wait()
    lines = lax.broadcasted_iota(jnp.int32, (META, width), 0)
    meta = jnp.where(lines == 0, 1, 0)
    for column, offset in enumerate(cycle_offsets):
        named = lax.rem(own - offset + 2 * cycle, cycle)
        meta = meta + jnp.where(
            (lines == distance_of(lax.bitwise_xor(own, named))) & (adj_ref[0, column] > 0), 1, 0
        )
    meta = jnp.where(lines == META - 1, cnt_ref[0, 0], meta).astype(f32).astype(bf16)
    for place, out in zip(places, outs):
        out[3 * rows:, :] = meta
        if width % 128:
            group = group_of(cycle, lax.bitwise_xor(own, distance_of(place)), chip)
            for other in range(cycle):
                @pl.when(group == other)
                def _():
                    for at, ref in enumerate((q_ref, k_ref, v_ref)):
                        out[at * rows:(at + 1) * rows, :] = ref[
                            :, other * width:(other + 1) * width
                        ]
    for copy in copies:
        copy.wait()


def hold_kernel(count, *refs):
    outs, sems = refs[-count - 1:-1], refs[-1]
    copies = [pltpu.make_async_copy(refs[at], outs[at], sems.at[at]) for at in range(count)]
    for copy in copies:
        copy.start()
    for copy in copies:
        copy.wait()


def hold(arrays, after):
    count = len(arrays)
    return pl.pallas_call(
        functools.partial(hold_kernel, count),
        out_shape=[jax.ShapeDtypeStruct(array.shape, array.dtype) for array in arrays],
        in_specs=[unread()] * (count + len(after)),
        out_specs=[vmem()] * count,
        scratch_shapes=[pltpu.SemaphoreType.DMA((count,))],
        compiler_params=params(2),
        cost_estimate=cost(1),
        name="hold",
    )(*arrays, *after)


def pack(cycle, places, tensors):
    rows, model = tensors[0].shape
    width = model // cycle
    return pl.pallas_call(
        functools.partial(pack_kernel, cycle, places),
        out_shape=[jax.ShapeDtypeStruct((3 * rows + META, width), bf16)] * len(places),
        in_specs=[anywhere() if width % 128 == 0 else vmem()] * 3
        + [unread()] * 2,
        out_specs=[vmem()] * len(places),
        scratch_shapes=[
            pltpu.SMEM(tensors[3].shape, jnp.int32),
            pltpu.SMEM(tensors[4].shape, jnp.int32),
            pltpu.SemaphoreType.DMA((cycle, 3)),
            pltpu.SemaphoreType.DMA((2,)),
        ],
        compiler_params=params(62),
        cost_estimate=cost(5),
        name="pack",
    )(*tensors)


def gather_kernel(cycle, *refs):
    chunks = refs[:cycle]
    q_all, k_all, v_all, k_t, v_t, bias = refs[-6:]
    rows = q_all.shape[0] // cycle
    for place in range(cycle):
        for at, part in enumerate((q_all, k_all, v_all)):
            part[place * rows:(place + 1) * rows, :] = chunks[place][at * rows:(at + 1) * rows, :]
    k_t[...] = k_all[...].astype(f32).T.astype(bf16)
    v_t[...] = v_all[...].astype(f32).T.astype(bf16)
    lines = lax.broadcasted_iota(jnp.int32, (rows, rows), 0).astype(f32)
    lists = [chunks[place][3 * rows:, :].astype(f32) for place in range(cycle)]
    for key_place in range(cycle):
        count = lists[key_place][META - 1:, :1]
        valid = lines < count
        for query_place in range(cycle):
            way = key_place ^ query_place
            times = lists[query_place][way:way + 1, :1]
            term = jnp.where(times > 0, jnp.log2(jnp.maximum(times, 1.0)), absent)
            bias[
                key_place * rows:(key_place + 1) * rows,
                query_place * rows:(query_place + 1) * rows,
            ] = jnp.where(valid, term, absent)


def gather(cycle, chunks, after=()):
    width = chunks[0].shape[1]
    rows = (chunks[0].shape[0] - META) // 3
    tokens = rows * cycle
    return pl.pallas_call(
        functools.partial(gather_kernel, cycle),
        out_shape=[jax.ShapeDtypeStruct((tokens, width), bf16)] * 3
        + [jax.ShapeDtypeStruct((width, tokens), bf16)] * 2
        + [jax.ShapeDtypeStruct((tokens, tokens), f32)],
        in_specs=[vmem()] * cycle + [unread()] * len(after),
        out_specs=[vmem()] * 6,
        compiler_params=params(8 if tokens <= 512 else 40),
        cost_estimate=cost(5),
        name="gather",
    )(*chunks, *after)


def head_tile(width):
    return min(128, width)


def only_head(tile, which):
    lanes = lax.broadcasted_iota(jnp.int32, tile.shape, 1)
    inside = (lanes >= which * HEAD_DIM) & (lanes < (which + 1) * HEAD_DIM)
    return jnp.where(inside, tile, jnp.zeros_like(tile))


def forward_kernel(query_tile, parts, q_all, k_all, v_t, bias, *refs):
    outs = refs[-2 - parts:-2]
    att_t, lse = refs[-2:]
    tokens, width = q_all.shape
    tile = head_tile(width)
    for start in range(0, tokens, query_tile):
        span = slice(start, start + query_tile)
        for head in range(width // HEAD_DIM):
            at = head * HEAD_DIM // tile * tile
            which = (head * HEAD_DIM - at) // HEAD_DIM
            scores = dot_nt(
                k_all[:, at:at + tile], only_head(q_all[span, at:at + tile], which)
            )
            scores = scores * log2_scale + bias[:, span]
            largest = jnp.max(scores, axis=0, keepdims=True)
            expo = jnp.exp2(scores - largest)
            total = jnp.sum(expo, axis=0, keepdims=True)
            probs = (expo * (1.0 / total)).astype(bf16)
            lse[head:head + 1, span] = largest + jnp.log2(total)
            att_t[head * HEAD_DIM:(head + 1) * HEAD_DIM, span] = dot_nn(
                v_t[head * HEAD_DIM:(head + 1) * HEAD_DIM, :], probs
            )
    attended = att_t[...].T.astype(bf16)
    filled = 0
    for out in outs:
        out[...] = attended[filled:filled + out.shape[0], :]
        filled += out.shape[0]


def forward(cycle, together, q_all, k_all, v_t, bias, after=()):
    tokens, width = q_all.shape
    rows = tokens // cycle
    parts = cycle // together
    outs = pl.pallas_call(
        functools.partial(forward_kernel, min(tokens, 512), parts),
        out_shape=[jax.ShapeDtypeStruct((together * rows, width), bf16)] * parts
        + [
            jax.ShapeDtypeStruct((width, tokens), f32),
            jax.ShapeDtypeStruct((8, tokens), f32),
        ],
        in_specs=[vmem()] * 4 + [unread()] * len(after),
        out_specs=[vmem()] * (parts + 2),
        compiler_params=params(16 if tokens <= 512 else 60),
        cost_estimate=cost(3),
        name="forward",
    )(q_all, k_all, v_t, bias, *after)
    return outs[:parts], outs[parts], outs[parts + 1]


def backward_kernel(cycle, query_tile, grad_count, att_count, *refs):
    q_all, k_all, v_all, k_t, bias, att_t, lse = refs[:7]
    refs = refs[7:]
    grads = refs[:grad_count]
    attended = refs[grad_count:grad_count + att_count]
    outs = refs[-4 - cycle:-4]
    g_all, dq_t, dk, dv = refs[-4:]
    width = q_all.shape[1]
    tokens = q_all.shape[0]
    rows = tokens // cycle
    filled = 0
    for grad in grads:
        g_all[filled:filled + grad.shape[0], :] = grad[...]
        filled += grad.shape[0]
    tile = head_tile(width)
    g_t = g_all[...].astype(f32).T
    product = g_t * att_t[...].astype(bf16).astype(f32)
    for start in range(0, tokens, query_tile):
        span = slice(start, start + query_tile)
        for at in range(0, width, tile):
            dk_tile = dv_tile = None
            for which in range(tile // HEAD_DIM):
                low = at + which * HEAD_DIM
                head = low // HEAD_DIM
                delta = jnp.sum(product[low:low + HEAD_DIM, span], axis=0, keepdims=True)
                q_head = only_head(q_all[span, at:at + tile], which)
                g_head = only_head(g_all[span, at:at + tile], which)
                scores = dot_nt(k_all[:, at:at + tile], q_head)
                probs = jnp.exp2(
                    scores * log2_scale + bias[:, span] - lse[head:head + 1, span]
                )
                grad_probs = dot_nt(v_all[:, at:at + tile], g_head)
                grad_scores = (probs * (grad_probs - delta)).astype(bf16)
                dk_head = dot_nn(grad_scores, q_head)
                dv_head = dot_nn(probs.astype(bf16), g_head)
                dk_tile = dk_head if dk_tile is None else dk_tile + dk_head
                dv_tile = dv_head if dv_tile is None else dv_tile + dv_head
                dq_t[low:low + HEAD_DIM, span] = dot_nn(k_t[low:low + HEAD_DIM, :], grad_scores)
            if start == 0:
                dk[:, at:at + tile] = dk_tile
                dv[:, at:at + tile] = dv_tile
            else:
                dk[:, at:at + tile] += dk_tile
                dv[:, at:at + tile] += dv_tile
    dq = (dq_t[...] * score_scale).T.astype(bf16)
    for place in range(cycle):
        span = slice(place * rows, (place + 1) * rows)
        outs[place][:rows, :] = dq[span, :]
        outs[place][rows:2 * rows, :] = (dk[span, :] * score_scale).astype(bf16)
        outs[place][2 * rows:3 * rows, :] = dv[span, :].astype(bf16)
        if attended:
            outs[place][3 * rows:, :] = attended[place][...]


def backward(cycle, inputs, grads, attended, after):
    tokens, width = inputs[0].shape
    rows = tokens // cycle
    return pl.pallas_call(
        functools.partial(backward_kernel, cycle, min(tokens, 512), len(grads), len(attended)),
        out_shape=[jax.ShapeDtypeStruct(((4 if attended else 3) * rows, width), bf16)] * cycle,
        in_specs=[vmem()] * (len(inputs) + len(grads) + len(attended)) + [unread()] * len(after),
        out_specs=[vmem()] * cycle,
        scratch_shapes=[
            pltpu.VMEM((tokens, width), bf16),
            pltpu.VMEM((width, tokens), f32),
            pltpu.VMEM((tokens, width), f32),
            pltpu.VMEM((tokens, width), f32),
        ],
        compiler_params=params(16 if tokens <= 512 else 60),
        cost_estimate=cost(3),
        name="backward",
    )(*inputs, *grads, *attended, *after)


def fetch_rows(out_weight, place):
    cycle, count = lax.axis_size("seq"), lax.axis_size("mp")
    pairs = []
    for member in range(cycle):
        for rank in range(count):
            owner = 2 * group_of(cycle, member ^ place, rank // 2) + rank % 2
            pairs.append((member * count + owner, member * count + rank))
    return lax.ppermute(out_weight, ("seq", "mp"), pairs)


def with_other_core(half):
    return [half, exchange(half, "mp", 1)]


def rows_in_order(mine, others, core):
    first = core == 0
    mine, other = mine[...], jnp.concatenate([ref[...] for ref in others], axis=0)
    return jnp.concatenate([jnp.where(first, mine, other), jnp.where(first, other, mine)], axis=0)


def both_halves(halves, core):
    mine, other = halves[0][...], halves[1][...]
    first = core == 0
    return jnp.concatenate([jnp.where(first, mine, other), jnp.where(first, other, mine)], axis=0)


def group_kernel(count, *refs):
    ups, out = refs[:count], refs[-1]
    rows = ups[0].shape[0]
    _, _, core = my_place()
    weight = rows_in_order(refs[count], refs[count + 1:count + 2], core)
    for block, ref in enumerate(ups):
        out[block * rows:(block + 1) * rows, :] = dot_nt(ref[...], weight).astype(bf16)


def group_grads(upstreams, pieces, after):
    rows, width = upstreams[0].shape[0], 2 * pieces[0].shape[0]
    return pl.pallas_call(
        functools.partial(group_kernel, len(upstreams)),
        out_shape=jax.ShapeDtypeStruct((len(upstreams) * rows, width), bf16),
        in_specs=[vmem()] * (len(upstreams) + 2) + [unread()] * len(after),
        out_specs=vmem(),
        compiler_params=params(8),
        cost_estimate=cost(1),
        name="group_grads",
    )(*upstreams, *pieces, *after)


def partial_kernel(att_ref, mine, *refs):
    own, kept, sent = refs[-3:]
    rows = own.shape[0]
    _, _, core = my_place()
    weight = rows_in_order(mine, refs[:1], core)
    own[...] = dot_nn(att_ref[:rows, :], weight)
    kept[...] = dot_nn(att_ref[rows:2 * rows, :], weight)
    sent[...] = dot_nn(att_ref[2 * rows:, :], weight).astype(bf16)


def partials(attended, pieces, after):
    rows, model = attended.shape[0] // 4, pieces[0].shape[1]
    return pl.pallas_call(
        partial_kernel,
        out_shape=[jax.ShapeDtypeStruct((rows, model), f32)] * 2
        + [jax.ShapeDtypeStruct((2 * rows, model), bf16)],
        in_specs=[vmem()] * 3 + [unread()] * len(after),
        out_specs=[vmem()] * 3,
        compiler_params=params(12),
        cost_estimate=cost(1),
        name="partials",
    )(attended, *pieces, *after)


def combine_kernel(own, kept, landed, total, *sent):
    rows = own.shape[0]
    total[...] = own[...] + landed[:rows, :].astype(f32)
    part = rows // len(sent)
    for at, out in enumerate(sent):
        span = slice(at * part, (at + 1) * part)
        out[...] = (
            kept[span, :] + landed[rows + at * part:rows + (at + 1) * part, :].astype(f32)
        ).astype(bf16)


def combine(own, kept, landed):
    return pl.pallas_call(
        combine_kernel,
        out_shape=[jax.ShapeDtypeStruct(own.shape, f32)]
        + [jax.ShapeDtypeStruct((own.shape[0] // 2, own.shape[1]), bf16)] * 2,
        in_specs=[vmem()] * 3,
        out_specs=[vmem()] * 3,
        compiler_params=params(8),
        cost_estimate=cost(1),
        name="combine",
    )(own, kept, landed)


def grad_kernel(cycle, up_ref, *refs):
    _, _, core = my_place()
    outs = refs[2 * cycle:]
    for place in range(cycle):
        rows = both_halves(refs[2 * place:2 * place + 2], core)
        outs[place][...] = dot_nt(up_ref[...], rows).astype(bf16)


def project_grad(cycle, upstream, halves):
    rows, model = upstream.shape
    return pl.pallas_call(
        functools.partial(grad_kernel, cycle),
        out_shape=[jax.ShapeDtypeStruct((rows, model // cycle), bf16)] * cycle,
        in_specs=[vmem()] * (1 + 2 * cycle),
        out_specs=[vmem()] * cycle,
        compiler_params=params(8),
        name="project_grad",
    )(upstream, *halves)


def place_columns(chunks, outs, sems):
    cycle = len(chunks)
    rows, model = outs[0].shape
    width = model // cycle
    own, chip, _ = my_place()
    copies = []
    for place in range(cycle):
        group = group_of(cycle, lax.bitwise_xor(own, distance_of(place)), chip)
        if width % 128 == 0:
            for at, out in enumerate(outs):
                copies.append(
                    pltpu.make_async_copy(
                        chunks[place].at[at * rows:(at + 1) * rows, :],
                        out.at[:, columns_at(group * width, width)],
                        sems.at[place, at],
                    )
                )
                copies[-1].start()
        else:
            for other in range(cycle):
                @pl.when(group == other)
                def _():
                    for at, out in enumerate(outs):
                        out[:, other * width:(other + 1) * width] = chunks[place][
                            at * rows:(at + 1) * rows, :
                        ]
    return copies


def finish_kernel(cycle, *refs):
    chunks = refs[:cycle]
    mixed, *outs = refs[-5:-1]
    copies = place_columns(chunks, outs, refs[-1])
    rows = mixed.shape[0]
    if len(refs) == cycle + 8:
        for at in range(2):
            span = slice(at * rows // 2, (at + 1) * rows // 2)
            mixed[span, :] = (
                refs[cycle][span, :] + refs[cycle + 1 + at][...].astype(f32)
            ).astype(bf16)
    else:
        halves = refs[cycle:3 * cycle]
        _, _, core = my_place()
        total = None
        for place in range(cycle):
            weight = both_halves(halves[2 * place:2 * place + 2], core)
            term = dot_nn(chunks[place][3 * rows:, :], weight)
            total = term if total is None else total + term
        mixed[...] = total.astype(bf16)
    for copy in copies:
        copy.wait()


def finish(cycle, rows, chunks, others):
    model = chunks[0].shape[1] * cycle
    aligned = model // cycle % 128 == 0
    return pl.pallas_call(
        functools.partial(finish_kernel, cycle),
        out_shape=[jax.ShapeDtypeStruct((rows, model), bf16)] * 4,
        in_specs=[vmem()] * (cycle + len(others)),
        out_specs=[vmem()] + [anywhere() if aligned else vmem()] * 3,
        scratch_shapes=[pltpu.SemaphoreType.DMA((cycle, 3))],
        compiler_params=params(8),
        name="finish",
    )(*chunks, *others)


def local(queries, keys, values, out_weight, upstream, adjacency, counts):
    cycle = lax.axis_size("seq")
    rows = queries.shape[0]
    tensors = (queries, keys, values, adjacency, counts.reshape(1, 1))
    if is_square():
        return square(cycle, rows, tensors, out_weight, upstream)
    chunks = swapped(list(pack(cycle, range(cycle), tensors)))
    halves = []
    for place in range(cycle):
        halves += with_other_core(fetch_rows(out_weight, place))
    q_all, k_all, v_all, k_t, v_t, bias = gather(cycle, chunks)
    attended, att_t, lse = forward(cycle, 1, q_all, k_all, v_t, bias)
    grads = swapped(project_grad(cycle, upstream, halves))
    inputs = (q_all, k_all, v_all, k_t, bias, att_t, lse)
    terms = swapped(backward(cycle, inputs, grads, attended, []))
    return tuple(finish(cycle, rows, terms, halves))


def square(cycle, rows, tensors, out_weight, upstream):
    nexts = swapped([upstream] * 3)[1:]
    chunks = swapped(list(pack(cycle, range(cycle), tensors)))
    held_weight, passed = hold((out_weight, nexts[1]), [nexts[0]])
    across = exchange_by_core(passed, (1, 2))
    own_rows = with_other_core(fetch_rows(held_weight, 0))
    q_all, k_all, v_all, k_t, v_t, bias = gather(cycle, chunks)
    (attended,), att_t, lse = forward(cycle, cycle, q_all, k_all, v_t, bias, [across])
    own_mixed, kept, sent = partials(attended, own_rows, [])
    landed = exchange_by_core(sent, (2, 1))
    grads = [group_grads((upstream, *nexts, across), own_rows, [kept])]
    inputs = (q_all, k_all, v_all, k_t, bias, att_t, lse)
    terms = swapped(list(backward(cycle, inputs, grads, [], [])))
    own_mixed, *next_mixed = combine(own_mixed, kept, landed)
    next_mixed = [exchange_by_core(part, (1, 2)) for part in next_mixed]
    return tuple(finish(cycle, rows, terms, [own_mixed] + next_mixed))


def solution(mesh):
    tokens = P(("seq", "mp"), None)
    return jax.shard_map(
        local,
        mesh=mesh,
        in_specs=(tokens, tokens, tokens, P("mp", None), tokens, tokens, P(("seq", "mp"))),
        out_specs=(tokens,) * 4,
        check_vma=False,
    )
```

```python
import functools

import jax
import jax.numpy as jnp
from jax import lax
from jax.experimental import pallas as pl
from jax.experimental.pallas import tpu as pltpu
from jax.sharding import PartitionSpec as P

HEADS = 16
HEAD_DIM = 64
META = 32

score_scale = 0.125
log2_scale = 0.125 * 1.4426950408889634
cycle_offsets = (1, -1, 2, -2)
absent = -1e30
bf16 = jnp.bfloat16
f32 = jnp.float32


def dot_nn(a, b):
    return lax.dot_general(a, b, (((1,), (0,)), ((), ())), preferred_element_type=f32)


def dot_nt(a, b):
    return lax.dot_general(a, b, (((1,), (1,)), ((), ())), preferred_element_type=f32)


def vmem():
    return pl.BlockSpec(memory_space=pltpu.VMEM)


def params(mib):
    return pltpu.CompilerParams(vmem_limit_bytes=int(mib * 1024) * 1024)


def unread():
    return pl.BlockSpec(memory_space=pl.ANY)


def anywhere():
    return pl.BlockSpec(memory_space=pltpu.HBM)


def cost(micros):
    return pl.CostEstimate(flops=int(micros * 1e9), bytes_accessed=0, transcendentals=0)


def exchange(value, axis, distance):
    count = lax.axis_size(axis)
    return lax.ppermute(value, axis, [(i, i ^ distance) for i in range(count)])


def turned(distance):
    return distance ^ (((distance ^ (distance >> 1)) & 1) * 3)


def exchange_by_core(value, distances):
    count = lax.axis_size("mp")
    pairs = [
        (member * count + rank, (member ^ distances[rank % 2]) * count + rank)
        for member in range(lax.axis_size("seq"))
        for rank in range(count)
    ]
    return lax.ppermute(value, ("seq", "mp"), pairs)


def is_square():
    return lax.axis_size("seq") == 4 and lax.axis_size("mp") == 8


def distance_of(slot):
    if is_square():
        return jnp.where(lax.rem(lax.axis_index("mp"), 2) == 0, slot, turned(slot))
    return slot


def swapped(chunks):
    if is_square():
        return [chunks[0]] + [
            exchange_by_core(chunks[k], (k, turned(k))) for k in range(1, len(chunks))
        ]
    return [chunks[0]] + [exchange(chunks[k], "seq", k) for k in range(1, len(chunks))]


def group_of(cycle, member, chip):
    turn = (member + chip) % cycle
    return turned(turn) if cycle == 4 else turn


def my_place():
    rank = lax.axis_index("mp")
    return lax.axis_index("seq"), rank // 2, lax.rem(rank, 2)


def columns_at(first, width):
    return pl.ds(pl.multiple_of(first, width), width)


def pack_kernel(cycle, places, q_ref, k_ref, v_ref, adj_any, cnt_any, *refs):
    refs, (adj_ref, cnt_ref, sems, more_sems) = refs[:-4], refs[-4:]
    outs = refs
    rows, model = q_ref.shape
    width = model // cycle
    own, chip, _ = my_place()
    lists = [
        pltpu.make_async_copy(adj_any, adj_ref, more_sems.at[0]),
        pltpu.make_async_copy(cnt_any, cnt_ref, more_sems.at[1]),
    ]
    for copy in lists:
        copy.start()
    copies = []
    if width % 128 == 0:
        for place, out in zip(places, outs):
            group = group_of(cycle, lax.bitwise_xor(own, distance_of(place)), chip)
            for at, ref in enumerate((q_ref, k_ref, v_ref)):
                copies.append(
                    pltpu.make_async_copy(
                        ref.at[:, columns_at(group * width, width)],
                        out.at[at * rows:(at + 1) * rows, :],
                        sems.at[place, at],
                    )
                )
                copies[-1].start()
    for copy in lists:
        copy.wait()
    lines = lax.broadcasted_iota(jnp.int32, (META, width), 0)
    meta = jnp.where(lines == 0, 1, 0)
    for column, offset in enumerate(cycle_offsets):
        named = lax.rem(own - offset + 2 * cycle, cycle)
        meta = meta + jnp.where(
            (lines == distance_of(lax.bitwise_xor(own, named))) & (adj_ref[0, column] > 0), 1, 0
        )
    meta = jnp.where(lines == META - 1, cnt_ref[0, 0], meta).astype(f32).astype(bf16)
    for place, out in zip(places, outs):
        out[3 * rows:, :] = meta
        if width % 128:
            group = group_of(cycle, lax.bitwise_xor(own, distance_of(place)), chip)
            for other in range(cycle):
                @pl.when(group == other)
                def _():
                    for at, ref in enumerate((q_ref, k_ref, v_ref)):
                        out[at * rows:(at + 1) * rows, :] = ref[
                            :, other * width:(other + 1) * width
                        ]
    for copy in copies:
        copy.wait()


def hold_kernel(count, *refs):
    outs, sems = refs[-count - 1:-1], refs[-1]
    copies = [pltpu.make_async_copy(refs[at], outs[at], sems.at[at]) for at in range(count)]
    for copy in copies:
        copy.start()
    for copy in copies:
        copy.wait()


def hold(arrays, after):
    count = len(arrays)
    return pl.pallas_call(
        functools.partial(hold_kernel, count),
        out_shape=[jax.ShapeDtypeStruct(array.shape, array.dtype) for array in arrays],
        in_specs=[unread()] * (count + len(after)),
        out_specs=[vmem()] * count,
        scratch_shapes=[pltpu.SemaphoreType.DMA((count,))],
        compiler_params=params(2),
        cost_estimate=cost(1),
        name="hold",
    )(*arrays, *after)


def pack(cycle, places, tensors):
    rows, model = tensors[0].shape
    width = model // cycle
    return pl.pallas_call(
        functools.partial(pack_kernel, cycle, places),
        out_shape=[jax.ShapeDtypeStruct((3 * rows + META, width), bf16)] * len(places),
        in_specs=[anywhere() if width % 128 == 0 else vmem()] * 3
        + [unread()] * 2,
        out_specs=[vmem()] * len(places),
        scratch_shapes=[
            pltpu.SMEM(tensors[3].shape, jnp.int32),
            pltpu.SMEM(tensors[4].shape, jnp.int32),
            pltpu.SemaphoreType.DMA((cycle, 3)),
            pltpu.SemaphoreType.DMA((2,)),
        ],
        compiler_params=params(62),
        cost_estimate=cost(5),
        name="pack",
    )(*tensors)


def gather_kernel(cycle, *refs):
    chunks = refs[:cycle]
    q_all, k_all, v_all, k_t, v_t, bias = refs[-6:]
    rows = q_all.shape[0] // cycle
    for place in range(cycle):
        for at, part in enumerate((q_all, k_all, v_all)):
            part[place * rows:(place + 1) * rows, :] = chunks[place][at * rows:(at + 1) * rows, :]
    k_t[...] = k_all[...].astype(f32).T.astype(bf16)
    v_t[...] = v_all[...].astype(f32).T.astype(bf16)
    lines = lax.broadcasted_iota(jnp.int32, (rows, rows), 0).astype(f32)
    lists = [chunks[place][3 * rows:, :].astype(f32) for place in range(cycle)]
    for key_place in range(cycle):
        count = lists[key_place][META - 1:, :1]
        valid = lines < count
        for query_place in range(cycle):
            way = key_place ^ query_place
            times = lists[query_place][way:way + 1, :1]
            term = jnp.where(times > 0, jnp.log2(jnp.maximum(times, 1.0)), absent)
            bias[
                key_place * rows:(key_place + 1) * rows,
                query_place * rows:(query_place + 1) * rows,
            ] = jnp.where(valid, term, absent)


def gather(cycle, chunks, after=()):
    width = chunks[0].shape[1]
    rows = (chunks[0].shape[0] - META) // 3
    tokens = rows * cycle
    return pl.pallas_call(
        functools.partial(gather_kernel, cycle),
        out_shape=[jax.ShapeDtypeStruct((tokens, width), bf16)] * 3
        + [jax.ShapeDtypeStruct((width, tokens), bf16)] * 2
        + [jax.ShapeDtypeStruct((tokens, tokens), f32)],
        in_specs=[vmem()] * cycle + [unread()] * len(after),
        out_specs=[vmem()] * 6,
        compiler_params=params(8 if tokens <= 512 else 40),
        cost_estimate=cost(5),
        name="gather",
    )(*chunks, *after)


def head_tile(width):
    return min(128, width)


def only_head(tile, which):
    lanes = lax.broadcasted_iota(jnp.int32, tile.shape, 1)
    inside = (lanes >= which * HEAD_DIM) & (lanes < (which + 1) * HEAD_DIM)
    return jnp.where(inside, tile, jnp.zeros_like(tile))


def forward_kernel(query_tile, parts, q_all, k_all, v_t, bias, *refs):
    outs = refs[-2 - parts:-2]
    att_t, lse = refs[-2:]
    tokens, width = q_all.shape
    tile = head_tile(width)
    for start in range(0, tokens, query_tile):
        span = slice(start, start + query_tile)
        for head in range(width // HEAD_DIM):
            at = head * HEAD_DIM // tile * tile
            which = (head * HEAD_DIM - at) // HEAD_DIM
            scores = dot_nt(
                k_all[:, at:at + tile], only_head(q_all[span, at:at + tile], which)
            )
            scores = scores * log2_scale + bias[:, span]
            largest = jnp.max(scores, axis=0, keepdims=True)
            expo = jnp.exp2(scores - largest)
            total = jnp.sum(expo, axis=0, keepdims=True)
            lse[head:head + 1, span] = largest + jnp.log2(total)
            att_t[head * HEAD_DIM:(head + 1) * HEAD_DIM, span] = dot_nn(
                v_t[head * HEAD_DIM:(head + 1) * HEAD_DIM, :], expo.astype(bf16)
            ) * (1.0 / total)
    attended = att_t[...].T.astype(bf16)
    filled = 0
    for out in outs:
        out[...] = attended[filled:filled + out.shape[0], :]
        filled += out.shape[0]


def forward(cycle, together, q_all, k_all, v_t, bias, after=()):
    tokens, width = q_all.shape
    rows = tokens // cycle
    parts = cycle // together
    outs = pl.pallas_call(
        functools.partial(forward_kernel, min(tokens, 512), parts),
        out_shape=[jax.ShapeDtypeStruct((together * rows, width), bf16)] * parts
        + [
            jax.ShapeDtypeStruct((width, tokens), f32),
            jax.ShapeDtypeStruct((8, tokens), f32),
        ],
        in_specs=[vmem()] * 4 + [unread()] * len(after),
        out_specs=[vmem()] * (parts + 2),
        compiler_params=params(16 if tokens <= 512 else 60),
        cost_estimate=cost(3),
        name="forward",
    )(q_all, k_all, v_t, bias, *after)
    return outs[:parts], outs[parts], outs[parts + 1]


def backward_kernel(cycle, query_tile, grad_count, att_count, *refs):
    q_all, k_all, v_all, k_t, bias, att_t, lse = refs[:7]
    refs = refs[7:]
    grads = refs[:grad_count]
    attended = refs[grad_count:grad_count + att_count]
    outs = refs[-4 - cycle:-4]
    g_all, dq_t, dk, dv = refs[-4:]
    width = q_all.shape[1]
    tokens = q_all.shape[0]
    rows = tokens // cycle
    filled = 0
    for grad in grads:
        g_all[filled:filled + grad.shape[0], :] = grad[...]
        filled += grad.shape[0]
    tile = head_tile(width)
    g_t = g_all[...].astype(f32).T
    product = g_t * att_t[...].astype(bf16).astype(f32)
    for start in range(0, tokens, query_tile):
        span = slice(start, start + query_tile)
        for at in range(0, width, tile):
            dk_tile = dv_tile = None
            for which in range(tile // HEAD_DIM):
                low = at + which * HEAD_DIM
                head = low // HEAD_DIM
                delta = jnp.sum(product[low:low + HEAD_DIM, span], axis=0, keepdims=True)
                q_head = only_head(q_all[span, at:at + tile], which)
                g_head = only_head(g_all[span, at:at + tile], which)
                scores = dot_nt(k_all[:, at:at + tile], q_head)
                probs = jnp.exp2(
                    scores * log2_scale + bias[:, span] - lse[head:head + 1, span]
                )
                grad_probs = dot_nt(v_all[:, at:at + tile], g_head)
                grad_scores = (probs * (grad_probs - delta)).astype(bf16)
                dk_head = dot_nn(grad_scores, q_head)
                dv_head = dot_nn(probs.astype(bf16), g_head)
                dk_tile = dk_head if dk_tile is None else dk_tile + dk_head
                dv_tile = dv_head if dv_tile is None else dv_tile + dv_head
                dq_t[low:low + HEAD_DIM, span] = dot_nn(k_t[low:low + HEAD_DIM, :], grad_scores)
            if start == 0:
                dk[:, at:at + tile] = dk_tile
                dv[:, at:at + tile] = dv_tile
            else:
                dk[:, at:at + tile] += dk_tile
                dv[:, at:at + tile] += dv_tile
    dq = (dq_t[...] * score_scale).T.astype(bf16)
    for place in range(cycle):
        span = slice(place * rows, (place + 1) * rows)
        outs[place][:rows, :] = dq[span, :]
        outs[place][rows:2 * rows, :] = (dk[span, :] * score_scale).astype(bf16)
        outs[place][2 * rows:3 * rows, :] = dv[span, :].astype(bf16)
        if attended:
            outs[place][3 * rows:, :] = attended[place][...]


def backward(cycle, inputs, grads, attended, after):
    tokens, width = inputs[0].shape
    rows = tokens // cycle
    return pl.pallas_call(
        functools.partial(backward_kernel, cycle, min(tokens, 512), len(grads), len(attended)),
        out_shape=[jax.ShapeDtypeStruct(((4 if attended else 3) * rows, width), bf16)] * cycle,
        in_specs=[vmem()] * (len(inputs) + len(grads) + len(attended)) + [unread()] * len(after),
        out_specs=[vmem()] * cycle,
        scratch_shapes=[
            pltpu.VMEM((tokens, width), bf16),
            pltpu.VMEM((width, tokens), f32),
            pltpu.VMEM((tokens, width), f32),
            pltpu.VMEM((tokens, width), f32),
        ],
        compiler_params=params(16 if tokens <= 512 else 60),
        cost_estimate=cost(3),
        name="backward",
    )(*inputs, *grads, *attended, *after)


def fetch_rows(out_weight, place):
    cycle, count = lax.axis_size("seq"), lax.axis_size("mp")
    pairs = []
    for member in range(cycle):
        for rank in range(count):
            owner = 2 * group_of(cycle, member ^ place, rank // 2) + rank % 2
            pairs.append((member * count + owner, member * count + rank))
    return lax.ppermute(out_weight, ("seq", "mp"), pairs)


def with_other_core(half):
    return [half, exchange(half, "mp", 1)]


def rows_in_order(mine, others, core):
    first = core == 0
    mine, other = mine[...], jnp.concatenate([ref[...] for ref in others], axis=0)
    return jnp.concatenate([jnp.where(first, mine, other), jnp.where(first, other, mine)], axis=0)


def both_halves(halves, core):
    mine, other = halves[0][...], halves[1][...]
    first = core == 0
    return jnp.concatenate([jnp.where(first, mine, other), jnp.where(first, other, mine)], axis=0)


def group_kernel(count, *refs):
    ups, out = refs[:count], refs[-1]
    rows = ups[0].shape[0]
    _, _, core = my_place()
    weight = rows_in_order(refs[count], refs[count + 1:count + 2], core)
    for block, ref in enumerate(ups):
        out[block * rows:(block + 1) * rows, :] = dot_nt(ref[...], weight).astype(bf16)


def group_grads(upstreams, pieces, after):
    rows, width = upstreams[0].shape[0], 2 * pieces[0].shape[0]
    return pl.pallas_call(
        functools.partial(group_kernel, len(upstreams)),
        out_shape=jax.ShapeDtypeStruct((len(upstreams) * rows, width), bf16),
        in_specs=[vmem()] * (len(upstreams) + 2) + [unread()] * len(after),
        out_specs=vmem(),
        compiler_params=params(8),
        cost_estimate=cost(1),
        name="group_grads",
    )(*upstreams, *pieces, *after)


def partial_kernel(att_ref, mine, *refs):
    own, kept, sent = refs[-3:]
    rows = own.shape[0]
    _, _, core = my_place()
    weight = rows_in_order(mine, refs[:1], core)
    own[...] = dot_nn(att_ref[:rows, :], weight)
    kept[...] = dot_nn(att_ref[rows:2 * rows, :], weight)
    sent[...] = dot_nn(att_ref[2 * rows:, :], weight).astype(bf16)


def partials(attended, pieces, after):
    rows, model = attended.shape[0] // 4, pieces[0].shape[1]
    return pl.pallas_call(
        partial_kernel,
        out_shape=[jax.ShapeDtypeStruct((rows, model), f32)] * 2
        + [jax.ShapeDtypeStruct((2 * rows, model), bf16)],
        in_specs=[vmem()] * 3 + [unread()] * len(after),
        out_specs=[vmem()] * 3,
        compiler_params=params(12),
        cost_estimate=cost(1),
        name="partials",
    )(attended, *pieces, *after)


def combine_kernel(own, kept, landed, total, *sent):
    rows = own.shape[0]
    total[...] = own[...] + landed[:rows, :].astype(f32)
    part = rows // len(sent)
    for at, out in enumerate(sent):
        span = slice(at * part, (at + 1) * part)
        out[...] = (
            kept[span, :] + landed[rows + at * part:rows + (at + 1) * part, :].astype(f32)
        ).astype(bf16)


def combine(own, kept, landed):
    return pl.pallas_call(
        combine_kernel,
        out_shape=[jax.ShapeDtypeStruct(own.shape, f32)]
        + [jax.ShapeDtypeStruct((own.shape[0] // 2, own.shape[1]), bf16)] * 2,
        in_specs=[vmem()] * 3,
        out_specs=[vmem()] * 3,
        compiler_params=params(8),
        cost_estimate=cost(1),
        name="combine",
    )(own, kept, landed)


def grad_kernel(cycle, up_ref, *refs):
    _, _, core = my_place()
    outs = refs[2 * cycle:]
    for place in range(cycle):
        rows = both_halves(refs[2 * place:2 * place + 2], core)
        outs[place][...] = dot_nt(up_ref[...], rows).astype(bf16)


def project_grad(cycle, upstream, halves):
    rows, model = upstream.shape
    return pl.pallas_call(
        functools.partial(grad_kernel, cycle),
        out_shape=[jax.ShapeDtypeStruct((rows, model // cycle), bf16)] * cycle,
        in_specs=[vmem()] * (1 + 2 * cycle),
        out_specs=[vmem()] * cycle,
        compiler_params=params(8),
        name="project_grad",
    )(upstream, *halves)


def place_columns(chunks, outs, sems):
    cycle = len(chunks)
    rows, model = outs[0].shape
    width = model // cycle
    own, chip, _ = my_place()
    copies = []
    for place in range(cycle):
        group = group_of(cycle, lax.bitwise_xor(own, distance_of(place)), chip)
        if width % 128 == 0:
            for at, out in enumerate(outs):
                copies.append(
                    pltpu.make_async_copy(
                        chunks[place].at[at * rows:(at + 1) * rows, :],
                        out.at[:, columns_at(group * width, width)],
                        sems.at[place, at],
                    )
                )
                copies[-1].start()
        else:
            for other in range(cycle):
                @pl.when(group == other)
                def _():
                    for at, out in enumerate(outs):
                        out[:, other * width:(other + 1) * width] = chunks[place][
                            at * rows:(at + 1) * rows, :
                        ]
    return copies


def finish_kernel(cycle, *refs):
    chunks = refs[:cycle]
    outs, word = refs[-5:-2], refs[-2]
    word[...] = jnp.zeros(word.shape, word.dtype)
    rows = outs[0].shape[0]
    copies = place_columns(chunks, outs, refs[-1])
    if len(refs) > cycle + 5:
        halves = refs[cycle:3 * cycle]
        _, _, core = my_place()
        total = None
        for place in range(cycle):
            weight = both_halves(halves[2 * place:2 * place + 2], core)
            term = dot_nn(chunks[place][3 * rows:, :], weight)
            total = term if total is None else total + term
        refs[-6][...] = total.astype(bf16)
    for copy in copies:
        copy.wait()


def finish(cycle, rows, chunks, others):
    model = chunks[0].shape[1] * cycle
    aligned = model // cycle % 128 == 0
    return pl.pallas_call(
        functools.partial(finish_kernel, cycle),
        out_shape=[jax.ShapeDtypeStruct((rows, model), bf16)] * (4 if others else 3)
        + [jax.ShapeDtypeStruct((16, 128), bf16)],
        in_specs=[vmem()] * (cycle + len(others)),
        out_specs=[vmem()] * (1 if others else 0)
        + [anywhere() if aligned else vmem()] * 3
        + [vmem()],
        scratch_shapes=[pltpu.SemaphoreType.DMA((cycle, 3))],
        compiler_params=params(8),
        name="finish",
    )(*chunks, *others)


def sum_kernel(own, *refs):
    out = refs[-1]
    part = own.shape[0] // 2
    for at in range(2):
        span = slice(at * part, (at + 1) * part)
        out[span, :] = (own[span, :] + refs[at][...].astype(f32)).astype(bf16)


def last_sum(own, landed, after):
    return pl.pallas_call(
        sum_kernel,
        out_shape=jax.ShapeDtypeStruct(own.shape, bf16),
        in_specs=[vmem()] * 3 + [unread()] * len(after),
        out_specs=vmem(),
        compiler_params=params(8),
        name="last_sum",
    )(own, *landed, *after)


def local(queries, keys, values, out_weight, upstream, adjacency, counts):
    cycle = lax.axis_size("seq")
    rows = queries.shape[0]
    tensors = (queries, keys, values, adjacency, counts.reshape(1, 1))
    if is_square():
        return square(cycle, rows, tensors, out_weight, upstream)
    chunks = swapped(list(pack(cycle, range(cycle), tensors)))
    halves = []
    for place in range(cycle):
        halves += with_other_core(fetch_rows(out_weight, place))
    q_all, k_all, v_all, k_t, v_t, bias = gather(cycle, chunks)
    attended, att_t, lse = forward(cycle, 1, q_all, k_all, v_t, bias)
    grads = swapped(project_grad(cycle, upstream, halves))
    inputs = (q_all, k_all, v_all, k_t, bias, att_t, lse)
    terms = swapped(backward(cycle, inputs, grads, attended, []))
    return tuple(finish(cycle, rows, terms, halves)[:4])


def square(cycle, rows, tensors, out_weight, upstream):
    nexts = swapped([upstream] * 3)[1:]
    chunks = swapped(list(pack(cycle, range(cycle), tensors)))
    held_weight, passed = hold((out_weight, nexts[1]), [nexts[0]])
    across = exchange_by_core(passed, (1, 2))
    own_rows = with_other_core(fetch_rows(held_weight, 0))
    q_all, k_all, v_all, k_t, v_t, bias = gather(cycle, chunks)
    (attended,), att_t, lse = forward(cycle, cycle, q_all, k_all, v_t, bias)
    own_mixed, kept, sent = partials(attended, own_rows, [across])
    landed = exchange_by_core(sent, (2, 1))
    grads = [group_grads((upstream, *nexts, across), own_rows, [kept])]
    inputs = (q_all, k_all, v_all, k_t, bias, att_t, lse)
    terms = swapped(list(backward(cycle, inputs, grads, [], [])))
    own_mixed, *next_mixed = combine(own_mixed, kept, landed)
    next_mixed = [exchange_by_core(part, (1, 2)) for part in next_mixed]
    *grads, word = finish(cycle, rows, terms, [])
    return (last_sum(own_mixed, next_mixed, [word]), *grads)


def solution(mesh):
    tokens = P(("seq", "mp"), None)
    return jax.shard_map(
        local,
        mesh=mesh,
        in_specs=(tokens, tokens, tokens, P("mp", None), tokens, tokens, P(("seq", "mp"))),
        out_specs=(tokens,) * 4,
        check_vma=False,
    )
```

```python
import functools

import jax
import jax.numpy as jnp
from jax import lax
from jax.experimental import pallas as pl
from jax.experimental.pallas import tpu as pltpu
from jax.sharding import PartitionSpec as P

HEADS = 16
HEAD_DIM = 64
META = 32

score_scale = 0.125
log2_scale = 0.125 * 1.4426950408889634
cycle_offsets = (1, -1, 2, -2)
absent = -1e30
bf16 = jnp.bfloat16
f32 = jnp.float32


def dot_nn(a, b):
    return lax.dot_general(a, b, (((1,), (0,)), ((), ())), preferred_element_type=f32)


def dot_nt(a, b):
    return lax.dot_general(a, b, (((1,), (1,)), ((), ())), preferred_element_type=f32)


def vmem():
    return pl.BlockSpec(memory_space=pltpu.VMEM)


def params(mib):
    return pltpu.CompilerParams(vmem_limit_bytes=int(mib * 1024) * 1024)


def unread():
    return pl.BlockSpec(memory_space=pl.ANY)


def anywhere():
    return pl.BlockSpec(memory_space=pltpu.HBM)


def cost(micros):
    return pl.CostEstimate(flops=int(micros * 1e9), bytes_accessed=0, transcendentals=0)


def exchange(value, axis, distance):
    count = lax.axis_size(axis)
    return lax.ppermute(value, axis, [(i, i ^ distance) for i in range(count)])


def turned(distance):
    return distance ^ (((distance ^ (distance >> 1)) & 1) * 3)


def exchange_by_core(value, distances):
    count = lax.axis_size("mp")
    pairs = [
        (member * count + rank, (member ^ distances[rank % 2]) * count + rank)
        for member in range(lax.axis_size("seq"))
        for rank in range(count)
    ]
    return lax.ppermute(value, ("seq", "mp"), pairs)


def is_square():
    return lax.axis_size("seq") == 4 and lax.axis_size("mp") == 8


def distance_of(slot):
    if is_square():
        return jnp.where(lax.rem(lax.axis_index("mp"), 2) == 0, slot, turned(slot))
    return slot


def swapped(chunks):
    if is_square():
        return [chunks[0]] + [
            exchange_by_core(chunks[k], (k, turned(k))) for k in range(1, len(chunks))
        ]
    return [chunks[0]] + [exchange(chunks[k], "seq", k) for k in range(1, len(chunks))]


def group_of(cycle, member, chip):
    turn = (member + chip) % cycle
    return turned(turn) if cycle == 4 else turn


def my_place():
    rank = lax.axis_index("mp")
    return lax.axis_index("seq"), rank // 2, lax.rem(rank, 2)


def columns_at(first, width):
    return pl.ds(pl.multiple_of(first, width), width)


def pack_kernel(cycle, places, q_ref, k_ref, v_ref, adj_any, cnt_any, *refs):
    refs, (adj_ref, cnt_ref, sems, more_sems) = refs[:-4], refs[-4:]
    outs = refs
    rows, model = q_ref.shape
    width = model // cycle
    own, chip, _ = my_place()
    lists = [
        pltpu.make_async_copy(adj_any, adj_ref, more_sems.at[0]),
        pltpu.make_async_copy(cnt_any, cnt_ref, more_sems.at[1]),
    ]
    for copy in lists:
        copy.start()
    copies = []
    if width % 128 == 0:
        for place, out in zip(places, outs):
            group = group_of(cycle, lax.bitwise_xor(own, distance_of(place)), chip)
            for at, ref in enumerate((q_ref, k_ref, v_ref)):
                copies.append(
                    pltpu.make_async_copy(
                        ref.at[:, columns_at(group * width, width)],
                        out.at[at * rows:(at + 1) * rows, :],
                        sems.at[place, at],
                    )
                )
                copies[-1].start()
    for copy in lists:
        copy.wait()
    lines = lax.broadcasted_iota(jnp.int32, (META, width), 0)
    meta = jnp.where(lines == 0, 1, 0)
    for column, offset in enumerate(cycle_offsets):
        named = lax.rem(own - offset + 2 * cycle, cycle)
        meta = meta + jnp.where(
            (lines == distance_of(lax.bitwise_xor(own, named))) & (adj_ref[0, column] > 0), 1, 0
        )
    meta = jnp.where(lines == META - 1, cnt_ref[0, 0], meta).astype(f32).astype(bf16)
    for place, out in zip(places, outs):
        out[3 * rows:, :] = meta
        if width % 128:
            group = group_of(cycle, lax.bitwise_xor(own, distance_of(place)), chip)
            for other in range(cycle):
                @pl.when(group == other)
                def _():
                    for at, ref in enumerate((q_ref, k_ref, v_ref)):
                        out[at * rows:(at + 1) * rows, :] = ref[
                            :, other * width:(other + 1) * width
                        ]
    for copy in copies:
        copy.wait()


def hold_kernel(count, *refs):
    outs, sems = refs[-count - 1:-1], refs[-1]
    copies = [pltpu.make_async_copy(refs[at], outs[at], sems.at[at]) for at in range(count)]
    for copy in copies:
        copy.start()
    for copy in copies:
        copy.wait()


def hold(arrays, after):
    count = len(arrays)
    return pl.pallas_call(
        functools.partial(hold_kernel, count),
        out_shape=[jax.ShapeDtypeStruct(array.shape, array.dtype) for array in arrays],
        in_specs=[unread()] * (count + len(after)),
        out_specs=[vmem()] * count,
        scratch_shapes=[pltpu.SemaphoreType.DMA((count,))],
        compiler_params=params(2),
        cost_estimate=cost(1),
        name="hold",
    )(*arrays, *after)


def pack(cycle, places, tensors):
    rows, model = tensors[0].shape
    width = model // cycle
    return pl.pallas_call(
        functools.partial(pack_kernel, cycle, places),
        out_shape=[jax.ShapeDtypeStruct((3 * rows + META, width), bf16)] * len(places),
        in_specs=[anywhere() if width % 128 == 0 else vmem()] * 3
        + [unread()] * 2,
        out_specs=[vmem()] * len(places),
        scratch_shapes=[
            pltpu.SMEM(tensors[3].shape, jnp.int32),
            pltpu.SMEM(tensors[4].shape, jnp.int32),
            pltpu.SemaphoreType.DMA((cycle, 3)),
            pltpu.SemaphoreType.DMA((2,)),
        ],
        compiler_params=params(62),
        cost_estimate=cost(5),
        name="pack",
    )(*tensors)


def gather_kernel(cycle, *refs):
    chunks = refs[:cycle]
    q_all, k_all, v_all, k_t, v_t, bias = refs[-6:]
    rows = q_all.shape[0] // cycle
    for place in range(cycle):
        for at, part in enumerate((q_all, k_all, v_all)):
            part[place * rows:(place + 1) * rows, :] = chunks[place][at * rows:(at + 1) * rows, :]
    k_t[...] = k_all[...].astype(f32).T.astype(bf16)
    v_t[...] = v_all[...].astype(f32).T.astype(bf16)
    lines = lax.broadcasted_iota(jnp.int32, (rows, rows), 0).astype(f32)
    lists = [chunks[place][3 * rows:, :].astype(f32) for place in range(cycle)]
    for key_place in range(cycle):
        count = lists[key_place][META - 1:, :1]
        valid = lines < count
        for query_place in range(cycle):
            way = key_place ^ query_place
            times = lists[query_place][way:way + 1, :1]
            term = jnp.where(times > 0, jnp.log2(jnp.maximum(times, 1.0)), absent)
            bias[
                key_place * rows:(key_place + 1) * rows,
                query_place * rows:(query_place + 1) * rows,
            ] = jnp.where(valid, term, absent)


def gather(cycle, chunks, after=()):
    width = chunks[0].shape[1]
    rows = (chunks[0].shape[0] - META) // 3
    tokens = rows * cycle
    return pl.pallas_call(
        functools.partial(gather_kernel, cycle),
        out_shape=[jax.ShapeDtypeStruct((tokens, width), bf16)] * 3
        + [jax.ShapeDtypeStruct((width, tokens), bf16)] * 2
        + [jax.ShapeDtypeStruct((tokens, tokens), f32)],
        in_specs=[vmem()] * cycle + [unread()] * len(after),
        out_specs=[vmem()] * 6,
        compiler_params=params(8 if tokens <= 512 else 40),
        cost_estimate=cost(5),
        name="gather",
    )(*chunks, *after)


def head_tile(width):
    return min(128, width)


def only_head(tile, which):
    lanes = lax.broadcasted_iota(jnp.int32, tile.shape, 1)
    inside = (lanes >= which * HEAD_DIM) & (lanes < (which + 1) * HEAD_DIM)
    return jnp.where(inside, tile, jnp.zeros_like(tile))


def forward_kernel(query_tile, parts, q_all, k_all, v_t, bias, *refs):
    outs = refs[-2 - parts:-2]
    att_t, lse = refs[-2:]
    tokens, width = q_all.shape
    tile = head_tile(width)
    for start in range(0, tokens, query_tile):
        span = slice(start, start + query_tile)
        for head in range(width // HEAD_DIM):
            at = head * HEAD_DIM // tile * tile
            which = (head * HEAD_DIM - at) // HEAD_DIM
            scores = dot_nt(
                k_all[:, at:at + tile], only_head(q_all[span, at:at + tile], which)
            )
            scores = scores * log2_scale + bias[:, span]
            largest = jnp.max(scores, axis=0, keepdims=True)
            expo = jnp.exp2(scores - largest)
            total = jnp.sum(expo, axis=0, keepdims=True)
            lse[head:head + 1, span] = largest + jnp.log2(total)
            att_t[head * HEAD_DIM:(head + 1) * HEAD_DIM, span] = dot_nn(
                v_t[head * HEAD_DIM:(head + 1) * HEAD_DIM, :], expo.astype(bf16)
            ) * (1.0 / total)
    attended = att_t[...].T.astype(bf16)
    filled = 0
    for out in outs:
        out[...] = attended[filled:filled + out.shape[0], :]
        filled += out.shape[0]


def forward(cycle, together, q_all, k_all, v_t, bias, after=()):
    tokens, width = q_all.shape
    rows = tokens // cycle
    parts = cycle // together
    outs = pl.pallas_call(
        functools.partial(forward_kernel, min(tokens, 512), parts),
        out_shape=[jax.ShapeDtypeStruct((together * rows, width), bf16)] * parts
        + [
            jax.ShapeDtypeStruct((width, tokens), f32),
            jax.ShapeDtypeStruct((8, tokens), f32),
        ],
        in_specs=[vmem()] * 4 + [unread()] * len(after),
        out_specs=[vmem()] * (parts + 2),
        compiler_params=params(16 if tokens <= 512 else 60),
        cost_estimate=cost(3),
        name="forward",
    )(q_all, k_all, v_t, bias, *after)
    return outs[:parts], outs[parts], outs[parts + 1]


def backward_kernel(cycle, query_tile, grad_count, att_count, *refs):
    q_all, k_all, v_all, k_t, bias, att_t, lse = refs[:7]
    refs = refs[7:]
    grads = refs[:grad_count]
    attended = refs[grad_count:grad_count + att_count]
    outs = refs[-4 - cycle:-4]
    g_all, dq_t, dk, dv = refs[-4:]
    width = q_all.shape[1]
    tokens = q_all.shape[0]
    rows = tokens // cycle
    filled = 0
    for grad in grads:
        g_all[filled:filled + grad.shape[0], :] = grad[...]
        filled += grad.shape[0]
    tile = head_tile(width)
    g_t = g_all[...].astype(f32).T
    product = g_t * att_t[...].astype(bf16).astype(f32)
    for start in range(0, tokens, query_tile):
        span = slice(start, start + query_tile)
        for at in range(0, width, tile):
            dk_tile = dv_tile = None
            for which in range(tile // HEAD_DIM):
                low = at + which * HEAD_DIM
                head = low // HEAD_DIM
                delta = jnp.sum(product[low:low + HEAD_DIM, span], axis=0, keepdims=True)
                q_head = only_head(q_all[span, at:at + tile], which)
                g_head = only_head(g_all[span, at:at + tile], which)
                scores = dot_nt(k_all[:, at:at + tile], q_head)
                probs = jnp.exp2(
                    scores * log2_scale + bias[:, span] - lse[head:head + 1, span]
                )
                grad_probs = dot_nt(v_all[:, at:at + tile], g_head)
                grad_scores = (probs * (grad_probs - delta)).astype(bf16)
                dk_head = dot_nn(grad_scores, q_head)
                dv_head = dot_nn(probs.astype(bf16), g_head)
                dk_tile = dk_head if dk_tile is None else dk_tile + dk_head
                dv_tile = dv_head if dv_tile is None else dv_tile + dv_head
                dq_t[low:low + HEAD_DIM, span] = dot_nn(k_t[low:low + HEAD_DIM, :], grad_scores)
            if start == 0:
                dk[:, at:at + tile] = dk_tile
                dv[:, at:at + tile] = dv_tile
            else:
                dk[:, at:at + tile] += dk_tile
                dv[:, at:at + tile] += dv_tile
    dq = (dq_t[...] * score_scale).T.astype(bf16)
    for place in range(cycle):
        span = slice(place * rows, (place + 1) * rows)
        outs[place][:rows, :] = dq[span, :]
        outs[place][rows:2 * rows, :] = (dk[span, :] * score_scale).astype(bf16)
        outs[place][2 * rows:3 * rows, :] = dv[span, :].astype(bf16)
        if attended:
            outs[place][3 * rows:, :] = attended[place][...]


def backward(cycle, inputs, grads, attended, after):
    tokens, width = inputs[0].shape
    rows = tokens // cycle
    return pl.pallas_call(
        functools.partial(backward_kernel, cycle, min(tokens, 512), len(grads), len(attended)),
        out_shape=[jax.ShapeDtypeStruct(((4 if attended else 3) * rows, width), bf16)] * cycle,
        in_specs=[vmem()] * (len(inputs) + len(grads) + len(attended)) + [unread()] * len(after),
        out_specs=[vmem()] * cycle,
        scratch_shapes=[
            pltpu.VMEM((tokens, width), bf16),
            pltpu.VMEM((width, tokens), f32),
            pltpu.VMEM((tokens, width), f32),
            pltpu.VMEM((tokens, width), f32),
        ],
        compiler_params=params(16 if tokens <= 512 else 60),
        cost_estimate=cost(3),
        name="backward",
    )(*inputs, *grads, *attended, *after)


def fetch_rows(out_weight, place):
    cycle, count = lax.axis_size("seq"), lax.axis_size("mp")
    pairs = []
    for member in range(cycle):
        for rank in range(count):
            owner = 2 * group_of(cycle, member ^ place, rank // 2) + rank % 2
            pairs.append((member * count + owner, member * count + rank))
    return lax.ppermute(out_weight, ("seq", "mp"), pairs)


def with_other_core(half):
    return [half, exchange(half, "mp", 1)]


def rows_in_order(mine, others, core):
    first = core == 0
    mine, other = mine[...], jnp.concatenate([ref[...] for ref in others], axis=0)
    return jnp.concatenate([jnp.where(first, mine, other), jnp.where(first, other, mine)], axis=0)


def both_halves(halves, core):
    mine, other = halves[0][...], halves[1][...]
    first = core == 0
    return jnp.concatenate([jnp.where(first, mine, other), jnp.where(first, other, mine)], axis=0)


def group_kernel(count, *refs):
    ups, out = refs[:count], refs[-1]
    _, _, core = my_place()
    weight = rows_in_order(refs[count], refs[count + 1:count + 2], core)
    out[...] = dot_nt(jnp.concatenate([ref[...] for ref in ups], axis=0), weight).astype(bf16)


def group_grads(upstreams, pieces, after):
    rows, width = upstreams[0].shape[0], 2 * pieces[0].shape[0]
    return pl.pallas_call(
        functools.partial(group_kernel, len(upstreams)),
        out_shape=jax.ShapeDtypeStruct((len(upstreams) * rows, width), bf16),
        in_specs=[vmem()] * (len(upstreams) + 2) + [unread()] * len(after),
        out_specs=vmem(),
        compiler_params=params(8),
        cost_estimate=cost(1),
        name="group_grads",
    )(*upstreams, *pieces, *after)


def partial_kernel(att_ref, mine, *refs):
    own, kept, sent = refs[-3:]
    rows = own.shape[0]
    _, _, core = my_place()
    weight = rows_in_order(mine, refs[:1], core)
    product = dot_nn(att_ref[...], weight)
    own[...] = product[:rows, :]
    kept[...] = product[rows:2 * rows, :]
    sent[...] = product[2 * rows:, :].astype(bf16)


def partials(attended, pieces, after):
    rows, model = attended.shape[0] // 4, pieces[0].shape[1]
    return pl.pallas_call(
        partial_kernel,
        out_shape=[jax.ShapeDtypeStruct((rows, model), f32)] * 2
        + [jax.ShapeDtypeStruct((2 * rows, model), bf16)],
        in_specs=[vmem()] * 3 + [unread()] * len(after),
        out_specs=[vmem()] * 3,
        compiler_params=params(12),
        cost_estimate=cost(1),
        name="partials",
    )(attended, *pieces, *after)


def combine_kernel(own, kept, landed, total, *sent):
    rows = own.shape[0]
    total[...] = own[...] + landed[:rows, :].astype(f32)
    part = rows // len(sent)
    for at, out in enumerate(sent):
        span = slice(at * part, (at + 1) * part)
        out[...] = (
            kept[span, :] + landed[rows + at * part:rows + (at + 1) * part, :].astype(f32)
        ).astype(bf16)


def combine(own, kept, landed):
    return pl.pallas_call(
        combine_kernel,
        out_shape=[jax.ShapeDtypeStruct(own.shape, f32)]
        + [jax.ShapeDtypeStruct((own.shape[0] // 2, own.shape[1]), bf16)] * 2,
        in_specs=[vmem()] * 3,
        out_specs=[vmem()] * 3,
        compiler_params=params(8),
        cost_estimate=cost(1),
        name="combine",
    )(own, kept, landed)


def grad_kernel(cycle, up_ref, *refs):
    _, _, core = my_place()
    outs = refs[2 * cycle:]
    for place in range(cycle):
        rows = both_halves(refs[2 * place:2 * place + 2], core)
        outs[place][...] = dot_nt(up_ref[...], rows).astype(bf16)


def project_grad(cycle, upstream, halves):
    rows, model = upstream.shape
    return pl.pallas_call(
        functools.partial(grad_kernel, cycle),
        out_shape=[jax.ShapeDtypeStruct((rows, model // cycle), bf16)] * cycle,
        in_specs=[vmem()] * (1 + 2 * cycle),
        out_specs=[vmem()] * cycle,
        compiler_params=params(8),
        name="project_grad",
    )(upstream, *halves)


def place_columns(chunks, outs, sems):
    cycle = len(chunks)
    rows, model = outs[0].shape
    width = model // cycle
    own, chip, _ = my_place()
    copies = []
    for place in range(cycle):
        group = group_of(cycle, lax.bitwise_xor(own, distance_of(place)), chip)
        if width % 128 == 0:
            for at, out in enumerate(outs):
                copies.append(
                    pltpu.make_async_copy(
                        chunks[place].at[at * rows:(at + 1) * rows, :],
                        out.at[:, columns_at(group * width, width)],
                        sems.at[place, at],
                    )
                )
                copies[-1].start()
        else:
            for other in range(cycle):
                @pl.when(group == other)
                def _():
                    for at, out in enumerate(outs):
                        out[:, other * width:(other + 1) * width] = chunks[place][
                            at * rows:(at + 1) * rows, :
                        ]
    return copies


def finish_kernel(cycle, *refs):
    chunks = refs[:cycle]
    outs, word = refs[-5:-2], refs[-2]
    word[...] = jnp.zeros(word.shape, word.dtype)
    rows = outs[0].shape[0]
    copies = place_columns(chunks, outs, refs[-1])
    if len(refs) > cycle + 5:
        halves = refs[cycle:3 * cycle]
        _, _, core = my_place()
        total = None
        for place in range(cycle):
            weight = both_halves(halves[2 * place:2 * place + 2], core)
            term = dot_nn(chunks[place][3 * rows:, :], weight)
            total = term if total is None else total + term
        refs[-6][...] = total.astype(bf16)
    for copy in copies:
        copy.wait()


def finish(cycle, rows, chunks, others):
    model = chunks[0].shape[1] * cycle
    aligned = model // cycle % 128 == 0
    return pl.pallas_call(
        functools.partial(finish_kernel, cycle),
        out_shape=[jax.ShapeDtypeStruct((rows, model), bf16)] * (4 if others else 3)
        + [jax.ShapeDtypeStruct((16, 128), bf16)],
        in_specs=[vmem()] * (cycle + len(others)),
        out_specs=[vmem()] * (1 if others else 0)
        + [anywhere() if aligned else vmem()] * 3
        + [vmem()],
        scratch_shapes=[pltpu.SemaphoreType.DMA((cycle, 3))],
        compiler_params=params(8),
        name="finish",
    )(*chunks, *others)


def sum_kernel(own, *refs):
    out = refs[-1]
    part = own.shape[0] // 2
    for at in range(2):
        span = slice(at * part, (at + 1) * part)
        out[span, :] = (own[span, :] + refs[at][...].astype(f32)).astype(bf16)


def last_sum(own, landed, after):
    return pl.pallas_call(
        sum_kernel,
        out_shape=jax.ShapeDtypeStruct(own.shape, bf16),
        in_specs=[vmem()] * 3 + [unread()] * len(after),
        out_specs=vmem(),
        compiler_params=params(8),
        name="last_sum",
    )(own, *landed, *after)


def local(queries, keys, values, out_weight, upstream, adjacency, counts):
    cycle = lax.axis_size("seq")
    rows = queries.shape[0]
    tensors = (queries, keys, values, adjacency, counts.reshape(1, 1))
    if is_square():
        return square(cycle, rows, tensors, out_weight, upstream)
    chunks = swapped(list(pack(cycle, range(cycle), tensors)))
    halves = []
    for place in range(cycle):
        halves += with_other_core(fetch_rows(out_weight, place))
    q_all, k_all, v_all, k_t, v_t, bias = gather(cycle, chunks)
    attended, att_t, lse = forward(cycle, 1, q_all, k_all, v_t, bias)
    grads = swapped(project_grad(cycle, upstream, halves))
    inputs = (q_all, k_all, v_all, k_t, bias, att_t, lse)
    terms = swapped(backward(cycle, inputs, grads, attended, []))
    return tuple(finish(cycle, rows, terms, halves)[:4])


def square(cycle, rows, tensors, out_weight, upstream):
    nexts = swapped([upstream] * 3)[1:]
    chunks = swapped(list(pack(cycle, range(cycle), tensors)))
    held_weight, passed = hold((out_weight, nexts[1]), [nexts[0]])
    across = exchange_by_core(passed, (1, 2))
    own_rows = with_other_core(fetch_rows(held_weight, 0))
    q_all, k_all, v_all, k_t, v_t, bias = gather(cycle, chunks)
    (attended,), att_t, lse = forward(cycle, cycle, q_all, k_all, v_t, bias, [across])
    own_mixed, kept, sent = partials(attended, own_rows, [])
    landed = exchange_by_core(sent, (2, 1))
    grads = [group_grads((upstream, *nexts, across), own_rows, [kept])]
    inputs = (q_all, k_all, v_all, k_t, bias, att_t, lse)
    terms = swapped(list(backward(cycle, inputs, grads, [], [])))
    own_mixed, *next_mixed = combine(own_mixed, kept, landed)
    next_mixed = [exchange_by_core(part, (1, 2)) for part in next_mixed]
    *grads, word = finish(cycle, rows, terms, [])
    return (last_sum(own_mixed, next_mixed, [word]), *grads)


def solution(mesh):
    tokens = P(("seq", "mp"), None)
    return jax.shard_map(
        local,
        mesh=mesh,
        in_specs=(tokens, tokens, tokens, P("mp", None), tokens, tokens, P(("seq", "mp"))),
        out_specs=(tokens,) * 4,
        check_vma=False,
    )
```

```python
import functools

import jax
import jax.numpy as jnp
from jax import lax
from jax.experimental import pallas as pl
from jax.experimental.pallas import tpu as pltpu
from jax.sharding import PartitionSpec as P

HEADS = 16
HEAD_DIM = 64
META = 32

score_scale = 0.125
log2_scale = 0.125 * 1.4426950408889634
cycle_offsets = (1, -1, 2, -2)
absent = -1e30
bf16 = jnp.bfloat16
f32 = jnp.float32


def dot_nn(a, b):
    return lax.dot_general(a, b, (((1,), (0,)), ((), ())), preferred_element_type=f32)


def dot_nt(a, b):
    return lax.dot_general(a, b, (((1,), (1,)), ((), ())), preferred_element_type=f32)


def vmem():
    return pl.BlockSpec(memory_space=pltpu.VMEM)


def params(mib):
    return pltpu.CompilerParams(vmem_limit_bytes=int(mib * 1024) * 1024)


def unread():
    return pl.BlockSpec(memory_space=pl.ANY)


def anywhere():
    return pl.BlockSpec(memory_space=pltpu.HBM)


def cost(micros):
    return pl.CostEstimate(flops=int(micros * 1e9), bytes_accessed=0, transcendentals=0)


def exchange(value, axis, distance):
    count = lax.axis_size(axis)
    return lax.ppermute(value, axis, [(i, i ^ distance) for i in range(count)])


def turned(distance):
    return distance ^ (((distance ^ (distance >> 1)) & 1) * 3)


def exchange_by_core(value, distances):
    count = lax.axis_size("mp")
    pairs = [
        (member * count + rank, (member ^ distances[rank % 2]) * count + rank)
        for member in range(lax.axis_size("seq"))
        for rank in range(count)
    ]
    return lax.ppermute(value, ("seq", "mp"), pairs)


def is_square():
    return lax.axis_size("seq") == 4 and lax.axis_size("mp") == 8


def distance_of(slot):
    if is_square():
        return jnp.where(lax.rem(lax.axis_index("mp"), 2) == 0, slot, turned(slot))
    return slot


def swapped(chunks):
    if is_square():
        return [chunks[0]] + [
            exchange_by_core(chunks[k], (k, turned(k))) for k in range(1, len(chunks))
        ]
    return [chunks[0]] + [exchange(chunks[k], "seq", k) for k in range(1, len(chunks))]


def group_of(cycle, member, chip):
    turn = (member + chip) % cycle
    return turned(turn) if cycle == 4 else turn


def my_place():
    rank = lax.axis_index("mp")
    return lax.axis_index("seq"), rank // 2, lax.rem(rank, 2)


def columns_at(first, width):
    return pl.ds(pl.multiple_of(first, width), width)


def pack_kernel(cycle, places, q_ref, k_ref, v_ref, adj_any, cnt_any, *refs):
    refs, (adj_ref, cnt_ref, sems, more_sems) = refs[:-4], refs[-4:]
    outs = refs
    rows, model = q_ref.shape
    width = model // cycle
    own, chip, _ = my_place()
    lists = [
        pltpu.make_async_copy(adj_any, adj_ref, more_sems.at[0]),
        pltpu.make_async_copy(cnt_any, cnt_ref, more_sems.at[1]),
    ]
    for copy in lists:
        copy.start()
    copies = []
    if width % 128 == 0:
        for place, out in zip(places, outs):
            group = group_of(cycle, lax.bitwise_xor(own, distance_of(place)), chip)
            for at, ref in enumerate((q_ref, k_ref, v_ref)):
                copies.append(
                    pltpu.make_async_copy(
                        ref.at[:, columns_at(group * width, width)],
                        out.at[at * rows:(at + 1) * rows, :],
                        sems.at[place, at],
                    )
                )
                copies[-1].start()
    for copy in lists:
        copy.wait()
    lines = lax.broadcasted_iota(jnp.int32, (META, width), 0)
    meta = jnp.where(lines == 0, 1, 0)
    for column, offset in enumerate(cycle_offsets):
        named = lax.rem(own - offset + 2 * cycle, cycle)
        meta = meta + jnp.where(
            (lines == distance_of(lax.bitwise_xor(own, named))) & (adj_ref[0, column] > 0), 1, 0
        )
    meta = jnp.where(lines == META - 1, cnt_ref[0, 0], meta).astype(f32).astype(bf16)
    for place, out in zip(places, outs):
        out[3 * rows:, :] = meta
        if width % 128:
            group = group_of(cycle, lax.bitwise_xor(own, distance_of(place)), chip)
            for other in range(cycle):
                @pl.when(group == other)
                def _():
                    for at, ref in enumerate((q_ref, k_ref, v_ref)):
                        out[at * rows:(at + 1) * rows, :] = ref[
                            :, other * width:(other + 1) * width
                        ]
    for copy in copies:
        copy.wait()


def hold_kernel(count, *refs):
    outs, sems = refs[-count - 1:-1], refs[-1]
    copies = [pltpu.make_async_copy(refs[at], outs[at], sems.at[at]) for at in range(count)]
    for copy in copies:
        copy.start()
    for copy in copies:
        copy.wait()


def hold(arrays, after):
    count = len(arrays)
    return pl.pallas_call(
        functools.partial(hold_kernel, count),
        out_shape=[jax.ShapeDtypeStruct(array.shape, array.dtype) for array in arrays],
        in_specs=[unread()] * (count + len(after)),
        out_specs=[vmem()] * count,
        scratch_shapes=[pltpu.SemaphoreType.DMA((count,))],
        compiler_params=params(2),
        cost_estimate=cost(1),
        name="hold",
    )(*arrays, *after)


def pack(cycle, places, tensors):
    rows, model = tensors[0].shape
    width = model // cycle
    return pl.pallas_call(
        functools.partial(pack_kernel, cycle, places),
        out_shape=[jax.ShapeDtypeStruct((3 * rows + META, width), bf16)] * len(places),
        in_specs=[anywhere() if width % 128 == 0 else vmem()] * 3
        + [unread()] * 2,
        out_specs=[vmem()] * len(places),
        scratch_shapes=[
            pltpu.SMEM(tensors[3].shape, jnp.int32),
            pltpu.SMEM(tensors[4].shape, jnp.int32),
            pltpu.SemaphoreType.DMA((cycle, 3)),
            pltpu.SemaphoreType.DMA((2,)),
        ],
        compiler_params=params(62),
        cost_estimate=cost(5),
        name="pack",
    )(*tensors)


def gather_kernel(cycle, *refs):
    chunks = refs[:cycle]
    q_all, k_all, v_all, k_t, v_t, bias = refs[-6:]
    rows = q_all.shape[0] // cycle
    for place in range(cycle):
        for at, part in enumerate((q_all, k_all, v_all)):
            part[place * rows:(place + 1) * rows, :] = chunks[place][at * rows:(at + 1) * rows, :]
    k_t[...] = k_all[...].astype(f32).T.astype(bf16)
    v_t[...] = v_all[...].astype(f32).T.astype(bf16)
    lines = lax.broadcasted_iota(jnp.int32, (rows, rows), 0).astype(f32)
    lists = [chunks[place][3 * rows:, :].astype(f32) for place in range(cycle)]
    for key_place in range(cycle):
        count = lists[key_place][META - 1:, :1]
        valid = lines < count
        for query_place in range(cycle):
            way = key_place ^ query_place
            times = lists[query_place][way:way + 1, :1]
            term = jnp.where(times > 0, jnp.log2(jnp.maximum(times, 1.0)), absent)
            bias[
                key_place * rows:(key_place + 1) * rows,
                query_place * rows:(query_place + 1) * rows,
            ] = jnp.where(valid, term, absent)


def gather(cycle, chunks, after=()):
    width = chunks[0].shape[1]
    rows = (chunks[0].shape[0] - META) // 3
    tokens = rows * cycle
    return pl.pallas_call(
        functools.partial(gather_kernel, cycle),
        out_shape=[jax.ShapeDtypeStruct((tokens, width), bf16)] * 3
        + [jax.ShapeDtypeStruct((width, tokens), bf16)] * 2
        + [jax.ShapeDtypeStruct((tokens, tokens), f32)],
        in_specs=[vmem()] * cycle + [unread()] * len(after),
        out_specs=[vmem()] * 6,
        compiler_params=params(8 if tokens <= 512 else 40),
        cost_estimate=cost(5),
        name="gather",
    )(*chunks, *after)


def head_tile(width):
    return min(128, width)


def only_head(tile, which):
    lanes = lax.broadcasted_iota(jnp.int32, tile.shape, 1)
    inside = (lanes >= which * HEAD_DIM) & (lanes < (which + 1) * HEAD_DIM)
    return jnp.where(inside, tile, jnp.zeros_like(tile))


def forward_kernel(query_tile, parts, q_all, k_all, v_t, bias, *refs):
    outs = refs[-3 - parts:-3]
    att_t, inverse, weights = refs[-3:]
    tokens, width = q_all.shape
    tile = head_tile(width)
    for start in range(0, tokens, query_tile):
        span = slice(start, start + query_tile)
        for head in range(width // HEAD_DIM):
            at = head * HEAD_DIM // tile * tile
            which = (head * HEAD_DIM - at) // HEAD_DIM
            scores = dot_nt(
                k_all[:, at:at + tile], only_head(q_all[span, at:at + tile], which)
            )
            scores = scores * log2_scale + bias[:, span]
            largest = jnp.max(scores, axis=0, keepdims=True)
            expo = jnp.exp2(scores - largest)
            total = jnp.sum(expo, axis=0, keepdims=True)
            share = 1.0 / total
            expo = expo.astype(bf16)
            inverse[head:head + 1, span] = share
            weights[head * tokens:(head + 1) * tokens, span] = expo
            att_t[head * HEAD_DIM:(head + 1) * HEAD_DIM, span] = (
                dot_nn(v_t[head * HEAD_DIM:(head + 1) * HEAD_DIM, :], expo) * share
            )
    attended = att_t[...].T.astype(bf16)
    filled = 0
    for out in outs:
        out[...] = attended[filled:filled + out.shape[0], :]
        filled += out.shape[0]


def forward(cycle, together, q_all, k_all, v_t, bias, after=()):
    tokens, width = q_all.shape
    rows = tokens // cycle
    parts = cycle // together
    outs = pl.pallas_call(
        functools.partial(forward_kernel, min(tokens, 512), parts),
        out_shape=[jax.ShapeDtypeStruct((together * rows, width), bf16)] * parts
        + [
            jax.ShapeDtypeStruct((width, tokens), f32),
            jax.ShapeDtypeStruct((8, tokens), f32),
            jax.ShapeDtypeStruct((width // HEAD_DIM * tokens, tokens), bf16),
        ],
        in_specs=[vmem()] * 4 + [unread()] * len(after),
        out_specs=[vmem()] * (parts + 3),
        compiler_params=params(16 if tokens <= 512 else 60),
        cost_estimate=cost(3),
        name="forward",
    )(q_all, k_all, v_t, bias, *after)
    return outs[:parts], *outs[parts:]


def backward_kernel(cycle, query_tile, grad_count, att_count, *refs):
    q_all, k_all, v_all, k_t, att_t, inverse, weights = refs[:7]
    refs = refs[7:]
    grads = refs[:grad_count]
    attended = refs[grad_count:grad_count + att_count]
    outs = refs[-5 - cycle:-5]
    g_all, g_t, dq_t, dk, dv = refs[-5:]
    tokens, width = q_all.shape
    rows = tokens // cycle
    if grad_count == 1:
        turned_grad = grads[0][...].astype(f32)
    else:
        for place, grad in enumerate(grads):
            g_all[place * rows:(place + 1) * rows, :] = grad[...]
        turned_grad = g_all[...].astype(f32).T
    shares = [
        turned_grad[low:low + HEAD_DIM, :] * inverse[low // HEAD_DIM:low // HEAD_DIM + 1, :]
        for low in range(0, width, HEAD_DIM)
    ]
    g_t[...] = jnp.concatenate(shares, axis=0).astype(bf16)
    g_wide = g_t[...].astype(f32)
    g_all[...] = g_wide.T.astype(bf16)
    product = g_wide * att_t[...].astype(bf16).astype(f32)
    tile = head_tile(width)
    for start in range(0, tokens, query_tile):
        span = slice(start, start + query_tile)
        for at in range(0, width, tile):
            dk_tile = dv_tile = None
            for which in range(tile // HEAD_DIM):
                low = at + which * HEAD_DIM
                head = low // HEAD_DIM
                delta = jnp.sum(product[low:low + HEAD_DIM, span], axis=0, keepdims=True)
                grad_probs = dot_nn(
                    only_head(v_all[:, at:at + tile], which), g_t[at:at + tile, span]
                )
                expo = weights[head * tokens:(head + 1) * tokens, span]
                grad_scores = (expo.astype(f32) * (grad_probs - delta)).astype(bf16)
                dk_head = dot_nn(grad_scores, only_head(q_all[span, at:at + tile], which))
                dv_head = dot_nn(expo, only_head(g_all[span, at:at + tile], which))
                dk_tile = dk_head if dk_tile is None else dk_tile + dk_head
                dv_tile = dv_head if dv_tile is None else dv_tile + dv_head
                dq_head = dot_nn(k_t[low:low + HEAD_DIM, :], grad_scores)
                dq_t[low:low + HEAD_DIM, span] = dq_head
            if start == 0:
                dk[:, at:at + tile] = dk_tile
                dv[:, at:at + tile] = dv_tile
            else:
                dk[:, at:at + tile] += dk_tile
                dv[:, at:at + tile] += dv_tile
    dq = (dq_t[...] * score_scale).T.astype(bf16)
    for place in range(cycle):
        span = slice(place * rows, (place + 1) * rows)
        outs[place][:rows, :] = dq[span, :]
        outs[place][rows:2 * rows, :] = (dk[span, :] * score_scale).astype(bf16)
        outs[place][2 * rows:3 * rows, :] = dv[span, :].astype(bf16)
        if attended:
            outs[place][3 * rows:, :] = attended[place][...]


def backward(cycle, inputs, grads, attended):
    tokens, width = inputs[0].shape
    rows = tokens // cycle
    return pl.pallas_call(
        functools.partial(backward_kernel, cycle, min(tokens, 512), len(grads), len(attended)),
        out_shape=[jax.ShapeDtypeStruct(((4 if attended else 3) * rows, width), bf16)] * cycle,
        in_specs=[vmem()] * (len(inputs) + len(grads) + len(attended)),
        out_specs=[vmem()] * cycle,
        scratch_shapes=[
            pltpu.VMEM((tokens, width), bf16),
            pltpu.VMEM((width, tokens), bf16),
            pltpu.VMEM((width, tokens), f32),
            pltpu.VMEM((tokens, width), f32),
            pltpu.VMEM((tokens, width), f32),
        ],
        compiler_params=params(16 if tokens <= 512 else 60),
        cost_estimate=cost(3),
        name="backward",
    )(*inputs, *grads, *attended)


def fetch_rows(out_weight, place):
    cycle, count = lax.axis_size("seq"), lax.axis_size("mp")
    pairs = []
    for member in range(cycle):
        for rank in range(count):
            owner = 2 * group_of(cycle, member ^ place, rank // 2) + rank % 2
            pairs.append((member * count + owner, member * count + rank))
    return lax.ppermute(out_weight, ("seq", "mp"), pairs)


def with_other_core(half):
    return [half, exchange(half, "mp", 1)]


def rows_in_order(mine, others, core):
    first = core == 0
    mine, other = mine[...], jnp.concatenate([ref[...] for ref in others], axis=0)
    return jnp.concatenate([jnp.where(first, mine, other), jnp.where(first, other, mine)], axis=0)


def both_halves(halves, core):
    mine, other = halves[0][...], halves[1][...]
    first = core == 0
    return jnp.concatenate([jnp.where(first, mine, other), jnp.where(first, other, mine)], axis=0)


def group_kernel(count, *refs):
    ups, out = refs[:count], refs[-1]
    _, _, core = my_place()
    weight = rows_in_order(refs[count], refs[count + 1:count + 2], core)
    out[...] = dot_nt(weight, jnp.concatenate([ref[...] for ref in ups], axis=0)).astype(bf16)


def group_grads(upstreams, pieces, after):
    rows, width = upstreams[0].shape[0], 2 * pieces[0].shape[0]
    return pl.pallas_call(
        functools.partial(group_kernel, len(upstreams)),
        out_shape=jax.ShapeDtypeStruct((width, len(upstreams) * rows), bf16),
        in_specs=[vmem()] * (len(upstreams) + 2) + [unread()] * len(after),
        out_specs=vmem(),
        compiler_params=params(8),
        cost_estimate=cost(1),
        name="group_grads",
    )(*upstreams, *pieces, *after)


def partial_kernel(att_ref, mine, *refs):
    own, kept, sent = refs[-3:]
    rows = own.shape[0]
    _, _, core = my_place()
    weight = rows_in_order(mine, refs[:1], core)
    product = dot_nn(att_ref[...], weight)
    own[...] = product[:rows, :]
    kept[...] = product[rows:2 * rows, :]
    sent[...] = product[2 * rows:, :].astype(bf16)


def partials(attended, pieces, after):
    rows, model = attended.shape[0] // 4, pieces[0].shape[1]
    return pl.pallas_call(
        partial_kernel,
        out_shape=[jax.ShapeDtypeStruct((rows, model), f32)] * 2
        + [jax.ShapeDtypeStruct((2 * rows, model), bf16)],
        in_specs=[vmem()] * 3 + [unread()] * len(after),
        out_specs=[vmem()] * 3,
        compiler_params=params(12),
        cost_estimate=cost(1),
        name="partials",
    )(attended, *pieces, *after)


def combine_kernel(own, kept, landed, total, *sent):
    rows = own.shape[0]
    total[...] = own[...] + landed[:rows, :].astype(f32)
    part = rows // len(sent)
    for at, out in enumerate(sent):
        span = slice(at * part, (at + 1) * part)
        out[...] = (
            kept[span, :] + landed[rows + at * part:rows + (at + 1) * part, :].astype(f32)
        ).astype(bf16)


def combine(own, kept, landed):
    return pl.pallas_call(
        combine_kernel,
        out_shape=[jax.ShapeDtypeStruct(own.shape, f32)]
        + [jax.ShapeDtypeStruct((own.shape[0] // 2, own.shape[1]), bf16)] * 2,
        in_specs=[vmem()] * 3,
        out_specs=[vmem()] * 3,
        compiler_params=params(8),
        cost_estimate=cost(1),
        name="combine",
    )(own, kept, landed)


def grad_kernel(cycle, up_ref, *refs):
    _, _, core = my_place()
    outs = refs[2 * cycle:]
    for place in range(cycle):
        rows = both_halves(refs[2 * place:2 * place + 2], core)
        outs[place][...] = dot_nt(up_ref[...], rows).astype(bf16)


def project_grad(cycle, upstream, halves):
    rows, model = upstream.shape
    return pl.pallas_call(
        functools.partial(grad_kernel, cycle),
        out_shape=[jax.ShapeDtypeStruct((rows, model // cycle), bf16)] * cycle,
        in_specs=[vmem()] * (1 + 2 * cycle),
        out_specs=[vmem()] * cycle,
        compiler_params=params(8),
        name="project_grad",
    )(upstream, *halves)


def place_columns(chunks, outs, sems):
    cycle = len(chunks)
    rows, model = outs[0].shape
    width = model // cycle
    own, chip, _ = my_place()
    copies = []
    for place in range(cycle):
        group = group_of(cycle, lax.bitwise_xor(own, distance_of(place)), chip)
        if width % 128 == 0:
            for at, out in enumerate(outs):
                copies.append(
                    pltpu.make_async_copy(
                        chunks[place].at[at * rows:(at + 1) * rows, :],
                        out.at[:, columns_at(group * width, width)],
                        sems.at[place, at],
                    )
                )
                copies[-1].start()
        else:
            for other in range(cycle):
                @pl.when(group == other)
                def _():
                    for at, out in enumerate(outs):
                        out[:, other * width:(other + 1) * width] = chunks[place][
                            at * rows:(at + 1) * rows, :
                        ]
    return copies


def finish_kernel(cycle, *refs):
    chunks = refs[:cycle]
    outs, word = refs[-5:-2], refs[-2]
    word[...] = jnp.zeros(word.shape, word.dtype)
    rows = outs[0].shape[0]
    copies = place_columns(chunks, outs, refs[-1])
    if len(refs) > cycle + 5:
        halves = refs[cycle:3 * cycle]
        _, _, core = my_place()
        total = None
        for place in range(cycle):
            weight = both_halves(halves[2 * place:2 * place + 2], core)
            term = dot_nn(chunks[place][3 * rows:, :], weight)
            total = term if total is None else total + term
        refs[-6][...] = total.astype(bf16)
    for copy in copies:
        copy.wait()


def finish(cycle, rows, chunks, others):
    model = chunks[0].shape[1] * cycle
    aligned = model // cycle % 128 == 0
    return pl.pallas_call(
        functools.partial(finish_kernel, cycle),
        out_shape=[jax.ShapeDtypeStruct((rows, model), bf16)] * (4 if others else 3)
        + [jax.ShapeDtypeStruct((16, 128), bf16)],
        in_specs=[vmem()] * (cycle + len(others)),
        out_specs=[vmem()] * (1 if others else 0)
        + [anywhere() if aligned else vmem()] * 3
        + [vmem()],
        scratch_shapes=[pltpu.SemaphoreType.DMA((cycle, 3))],
        compiler_params=params(8),
        name="finish",
    )(*chunks, *others)


def sum_kernel(own, *refs):
    out = refs[-1]
    part = own.shape[0] // 2
    for at in range(2):
        span = slice(at * part, (at + 1) * part)
        out[span, :] = (own[span, :] + refs[at][...].astype(f32)).astype(bf16)


def last_sum(own, landed, after):
    return pl.pallas_call(
        sum_kernel,
        out_shape=jax.ShapeDtypeStruct(own.shape, bf16),
        in_specs=[vmem()] * 3 + [unread()] * len(after),
        out_specs=vmem(),
        compiler_params=params(8),
        name="last_sum",
    )(own, *landed, *after)


def local(queries, keys, values, out_weight, upstream, adjacency, counts):
    cycle = lax.axis_size("seq")
    rows = queries.shape[0]
    tensors = (queries, keys, values, adjacency, counts.reshape(1, 1))
    if is_square():
        return square(cycle, rows, tensors, out_weight, upstream)
    chunks = swapped(list(pack(cycle, range(cycle), tensors)))
    halves = []
    for place in range(cycle):
        halves += with_other_core(fetch_rows(out_weight, place))
    q_all, k_all, v_all, k_t, v_t, bias = gather(cycle, chunks)
    attended, att_t, inverse, weights = forward(cycle, 1, q_all, k_all, v_t, bias)
    grads = swapped(project_grad(cycle, upstream, halves))
    inputs = (q_all, k_all, v_all, k_t, att_t, inverse, weights)
    terms = swapped(backward(cycle, inputs, grads, attended))
    return tuple(finish(cycle, rows, terms, halves)[:4])


def square(cycle, rows, tensors, out_weight, upstream):
    nexts = swapped([upstream] * 3)[1:]
    chunks = swapped(list(pack(cycle, range(cycle), tensors)))
    held_weight, passed = hold((out_weight, nexts[1]), [nexts[0]])
    across = exchange_by_core(passed, (1, 2))
    own_rows = with_other_core(fetch_rows(held_weight, 0))
    q_all, k_all, v_all, k_t, v_t, bias = gather(cycle, chunks)
    (attended,), att_t, inverse, weights = forward(
        cycle, cycle, q_all, k_all, v_t, bias, [across]
    )
    own_mixed, kept, sent = partials(attended, own_rows, [])
    landed = exchange_by_core(sent, (2, 1))
    grads = [group_grads((upstream, *nexts, across), own_rows, [kept])]
    inputs = (q_all, k_all, v_all, k_t, att_t, inverse, weights)
    terms = swapped(list(backward(cycle, inputs, grads, [])))
    own_mixed, *next_mixed = combine(own_mixed, kept, landed)
    next_mixed = [exchange_by_core(part, (1, 2)) for part in next_mixed]
    *grads, word = finish(cycle, rows, terms, [])
    return (last_sum(own_mixed, next_mixed, [word]), *grads)


def solution(mesh):
    tokens = P(("seq", "mp"), None)
    return jax.shard_map(
        local,
        mesh=mesh,
        in_specs=(tokens, tokens, tokens, P("mp", None), tokens, tokens, P(("seq", "mp"))),
        out_specs=(tokens,) * 4,
        check_vma=False,
    )
```

```python
import functools

import jax
import jax.numpy as jnp
from jax import lax
from jax.experimental import pallas as pl
from jax.experimental.pallas import tpu as pltpu
from jax.sharding import PartitionSpec as P

HEADS = 16
HEAD_DIM = 64
META = 32

score_scale = 0.125
log2_scale = 0.125 * 1.4426950408889634
cycle_offsets = (1, -1, 2, -2)
absent = -1e30
bf16 = jnp.bfloat16
f32 = jnp.float32


def dot_nn(a, b):
    return lax.dot_general(a, b, (((1,), (0,)), ((), ())), preferred_element_type=f32)


def dot_nt(a, b):
    return lax.dot_general(a, b, (((1,), (1,)), ((), ())), preferred_element_type=f32)


def vmem():
    return pl.BlockSpec(memory_space=pltpu.VMEM)


def params(mib):
    return pltpu.CompilerParams(vmem_limit_bytes=int(mib * 1024) * 1024)


def unread():
    return pl.BlockSpec(memory_space=pl.ANY)


def anywhere():
    return pl.BlockSpec(memory_space=pltpu.HBM)


def cost(micros):
    return pl.CostEstimate(flops=int(micros * 1e9), bytes_accessed=0, transcendentals=0)


def exchange(value, axis, distance):
    count = lax.axis_size(axis)
    return lax.ppermute(value, axis, [(i, i ^ distance) for i in range(count)])


def turned(distance):
    return distance ^ (((distance ^ (distance >> 1)) & 1) * 3)


def exchange_by_core(value, distances):
    count = lax.axis_size("mp")
    pairs = [
        (member * count + rank, (member ^ distances[rank % 2]) * count + rank)
        for member in range(lax.axis_size("seq"))
        for rank in range(count)
    ]
    return lax.ppermute(value, ("seq", "mp"), pairs)


def is_square():
    return lax.axis_size("seq") == 4 and lax.axis_size("mp") == 8


def distance_of(slot):
    if is_square():
        return jnp.where(lax.rem(lax.axis_index("mp"), 2) == 0, slot, turned(slot))
    return slot


def swapped(chunks):
    if is_square():
        return [chunks[0]] + [
            exchange_by_core(chunks[k], (k, turned(k))) for k in range(1, len(chunks))
        ]
    return [chunks[0]] + [exchange(chunks[k], "seq", k) for k in range(1, len(chunks))]


def group_of(cycle, member, chip):
    turn = (member + chip) % cycle
    return turned(turn) if cycle == 4 else turn


def my_place():
    rank = lax.axis_index("mp")
    return lax.axis_index("seq"), rank // 2, lax.rem(rank, 2)


def columns_at(first, width):
    return pl.ds(pl.multiple_of(first, width), width)


def pack_kernel(cycle, places, q_ref, k_ref, v_ref, adj_any, cnt_any, *refs):
    refs, (adj_ref, cnt_ref, sems, more_sems) = refs[:-4], refs[-4:]
    outs = refs
    rows, model = q_ref.shape
    width = model // cycle
    own, chip, _ = my_place()
    lists = [
        pltpu.make_async_copy(adj_any, adj_ref, more_sems.at[0]),
        pltpu.make_async_copy(cnt_any, cnt_ref, more_sems.at[1]),
    ]
    for copy in lists:
        copy.start()
    copies = []
    if width % 128 == 0:
        for place, out in zip(places, outs):
            group = group_of(cycle, lax.bitwise_xor(own, distance_of(place)), chip)
            for at, ref in enumerate((q_ref, k_ref, v_ref)):
                copies.append(
                    pltpu.make_async_copy(
                        ref.at[:, columns_at(group * width, width)],
                        out.at[at * rows:(at + 1) * rows, :],
                        sems.at[place, at],
                    )
                )
                copies[-1].start()
    for copy in lists:
        copy.wait()
    lines = lax.broadcasted_iota(jnp.int32, (META, width), 0)
    meta = jnp.where(lines == 0, 1, 0)
    for column, offset in enumerate(cycle_offsets):
        named = lax.rem(own - offset + 2 * cycle, cycle)
        meta = meta + jnp.where(
            (lines == distance_of(lax.bitwise_xor(own, named))) & (adj_ref[0, column] > 0), 1, 0
        )
    meta = jnp.where(lines == META - 1, cnt_ref[0, 0], meta).astype(f32).astype(bf16)
    for place, out in zip(places, outs):
        out[3 * rows:, :] = meta
        if width % 128:
            group = group_of(cycle, lax.bitwise_xor(own, distance_of(place)), chip)
            for other in range(cycle):
                @pl.when(group == other)
                def _():
                    for at, ref in enumerate((q_ref, k_ref, v_ref)):
                        out[at * rows:(at + 1) * rows, :] = ref[
                            :, other * width:(other + 1) * width
                        ]
    for copy in copies:
        copy.wait()


def hold_kernel(count, *refs):
    outs, sems = refs[-count - 1:-1], refs[-1]
    copies = [pltpu.make_async_copy(refs[at], outs[at], sems.at[at]) for at in range(count)]
    for copy in copies:
        copy.start()
    for copy in copies:
        copy.wait()


def hold(arrays, after):
    count = len(arrays)
    return pl.pallas_call(
        functools.partial(hold_kernel, count),
        out_shape=[jax.ShapeDtypeStruct(array.shape, array.dtype) for array in arrays],
        in_specs=[unread()] * (count + len(after)),
        out_specs=[vmem()] * count,
        scratch_shapes=[pltpu.SemaphoreType.DMA((count,))],
        compiler_params=params(2),
        cost_estimate=cost(1),
        name="hold",
    )(*arrays, *after)


def pack(cycle, places, tensors):
    rows, model = tensors[0].shape
    width = model // cycle
    return pl.pallas_call(
        functools.partial(pack_kernel, cycle, places),
        out_shape=[jax.ShapeDtypeStruct((3 * rows + META, width), bf16)] * len(places),
        in_specs=[anywhere() if width % 128 == 0 else vmem()] * 3
        + [unread()] * 2,
        out_specs=[vmem()] * len(places),
        scratch_shapes=[
            pltpu.SMEM(tensors[3].shape, jnp.int32),
            pltpu.SMEM(tensors[4].shape, jnp.int32),
            pltpu.SemaphoreType.DMA((cycle, 3)),
            pltpu.SemaphoreType.DMA((2,)),
        ],
        compiler_params=params(62),
        cost_estimate=cost(5),
        name="pack",
    )(*tensors)


def gather_kernel(cycle, *refs):
    chunks = refs[:cycle]
    q_all, k_all, v_all, k_t, v_t, bias = refs[-6:]
    rows = q_all.shape[0] // cycle
    for place in range(cycle):
        for at, part in enumerate((q_all, k_all, v_all)):
            part[place * rows:(place + 1) * rows, :] = chunks[place][at * rows:(at + 1) * rows, :]
    k_t[...] = k_all[...].astype(f32).T.astype(bf16)
    v_t[...] = v_all[...].astype(f32).T.astype(bf16)
    lines = lax.broadcasted_iota(jnp.int32, (rows, rows), 0).astype(f32)
    lists = [chunks[place][3 * rows:, :].astype(f32) for place in range(cycle)]
    for key_place in range(cycle):
        count = lists[key_place][META - 1:, :1]
        valid = lines < count
        for query_place in range(cycle):
            way = key_place ^ query_place
            times = lists[query_place][way:way + 1, :1]
            term = jnp.where(times > 0, jnp.log2(jnp.maximum(times, 1.0)), absent)
            bias[
                key_place * rows:(key_place + 1) * rows,
                query_place * rows:(query_place + 1) * rows,
            ] = jnp.where(valid, term, absent)


def gather(cycle, chunks, after=()):
    width = chunks[0].shape[1]
    rows = (chunks[0].shape[0] - META) // 3
    tokens = rows * cycle
    return pl.pallas_call(
        functools.partial(gather_kernel, cycle),
        out_shape=[jax.ShapeDtypeStruct((tokens, width), bf16)] * 3
        + [jax.ShapeDtypeStruct((width, tokens), bf16)] * 2
        + [jax.ShapeDtypeStruct((tokens, tokens), f32)],
        in_specs=[vmem()] * cycle + [unread()] * len(after),
        out_specs=[vmem()] * 6,
        compiler_params=params(8 if tokens <= 512 else 40),
        cost_estimate=cost(5),
        name="gather",
    )(*chunks, *after)


def head_tile(width):
    return min(128, width)


def only_head(tile, which):
    lanes = lax.broadcasted_iota(jnp.int32, tile.shape, 1)
    inside = (lanes >= which * HEAD_DIM) & (lanes < (which + 1) * HEAD_DIM)
    return jnp.where(inside, tile, jnp.zeros_like(tile))


def forward_kernel(query_tile, parts, q_all, k_all, v_t, bias, *refs):
    outs = refs[-3 - parts:-3]
    att_t, inverse, weights = refs[-3:]
    tokens, width = q_all.shape
    tile = head_tile(width)
    for start in range(0, tokens, query_tile):
        span = slice(start, start + query_tile)
        for head in range(width // HEAD_DIM):
            at = head * HEAD_DIM // tile * tile
            which = (head * HEAD_DIM - at) // HEAD_DIM
            scores = dot_nt(
                k_all[:, at:at + tile], only_head(q_all[span, at:at + tile], which)
            )
            scores = scores * log2_scale + bias[:, span]
            largest = jnp.max(scores, axis=0, keepdims=True)
            expo = jnp.exp2(scores - largest)
            total = jnp.sum(expo, axis=0, keepdims=True)
            share = 1.0 / total
            expo = expo.astype(bf16)
            inverse[head:head + 1, span] = share
            weights[head * tokens:(head + 1) * tokens, span] = expo
            att_t[head * HEAD_DIM:(head + 1) * HEAD_DIM, span] = (
                dot_nn(v_t[head * HEAD_DIM:(head + 1) * HEAD_DIM, :], expo) * share
            )
    attended = att_t[...].T.astype(bf16)
    filled = 0
    for out in outs:
        out[...] = attended[filled:filled + out.shape[0], :]
        filled += out.shape[0]


def forward(cycle, together, q_all, k_all, v_t, bias, after=()):
    tokens, width = q_all.shape
    rows = tokens // cycle
    parts = cycle // together
    outs = pl.pallas_call(
        functools.partial(forward_kernel, min(tokens, 512), parts),
        out_shape=[jax.ShapeDtypeStruct((together * rows, width), bf16)] * parts
        + [
            jax.ShapeDtypeStruct((width, tokens), f32),
            jax.ShapeDtypeStruct((8, tokens), f32),
            jax.ShapeDtypeStruct((width // HEAD_DIM * tokens, tokens), bf16),
        ],
        in_specs=[vmem()] * 4 + [unread()] * len(after),
        out_specs=[vmem()] * (parts + 3),
        compiler_params=params(16 if tokens <= 512 else 60),
        cost_estimate=cost(3),
        name="forward",
    )(q_all, k_all, v_t, bias, *after)
    return outs[:parts], *outs[parts:]


def backward_kernel(cycle, query_tile, grad_count, att_count, *refs):
    q_all, k_all, v_all, k_t, att_t, inverse, weights = refs[:7]
    refs = refs[7:]
    grads = refs[:grad_count]
    attended = refs[grad_count:grad_count + att_count]
    outs = refs[-5 - cycle:-5]
    g_all, g_t, dq_t, dk, dv = refs[-5:]
    tokens, width = q_all.shape
    rows = tokens // cycle
    if grad_count == 1:
        turned_grad = grads[0][...].astype(f32)
    else:
        for place, grad in enumerate(grads):
            g_all[place * rows:(place + 1) * rows, :] = grad[...]
        turned_grad = g_all[...].astype(f32).T
    shares = [
        turned_grad[low:low + HEAD_DIM, :] * inverse[low // HEAD_DIM:low // HEAD_DIM + 1, :]
        for low in range(0, width, HEAD_DIM)
    ]
    g_t[...] = jnp.concatenate(shares, axis=0).astype(bf16)
    g_wide = g_t[...].astype(f32)
    g_all[...] = g_wide.T.astype(bf16)
    product = g_wide * att_t[...].astype(bf16).astype(f32)
    tile = head_tile(width)
    for start in range(0, tokens, query_tile):
        span = slice(start, start + query_tile)
        for at in range(0, width, tile):
            dk_tile = dv_tile = None
            for which in range(tile // HEAD_DIM):
                low = at + which * HEAD_DIM
                head = low // HEAD_DIM
                delta = jnp.sum(product[low:low + HEAD_DIM, span], axis=0, keepdims=True)
                grad_probs = dot_nn(
                    only_head(v_all[:, at:at + tile], which), g_t[at:at + tile, span]
                )
                expo = weights[head * tokens:(head + 1) * tokens, span]
                grad_scores = (expo.astype(f32) * (grad_probs - delta)).astype(bf16)
                dk_head = dot_nn(grad_scores, only_head(q_all[span, at:at + tile], which))
                dv_head = dot_nn(expo, only_head(g_all[span, at:at + tile], which))
                dk_tile = dk_head if dk_tile is None else dk_tile + dk_head
                dv_tile = dv_head if dv_tile is None else dv_tile + dv_head
                dq_head = dot_nn(k_t[low:low + HEAD_DIM, :], grad_scores)
                dq_t[low:low + HEAD_DIM, span] = dq_head
            if start == 0:
                dk[:, at:at + tile] = dk_tile
                dv[:, at:at + tile] = dv_tile
            else:
                dk[:, at:at + tile] += dk_tile
                dv[:, at:at + tile] += dv_tile
    dq = (dq_t[...] * score_scale).T.astype(bf16)
    for place in range(cycle):
        span = slice(place * rows, (place + 1) * rows)
        outs[place][:rows, :] = dq[span, :]
        outs[place][rows:2 * rows, :] = (dk[span, :] * score_scale).astype(bf16)
        outs[place][2 * rows:3 * rows, :] = dv[span, :].astype(bf16)
        if attended:
            outs[place][3 * rows:, :] = attended[place][...]


def backward(cycle, inputs, grads, attended):
    tokens, width = inputs[0].shape
    rows = tokens // cycle
    return pl.pallas_call(
        functools.partial(backward_kernel, cycle, min(tokens, 512), len(grads), len(attended)),
        out_shape=[jax.ShapeDtypeStruct(((4 if attended else 3) * rows, width), bf16)] * cycle,
        in_specs=[vmem()] * (len(inputs) + len(grads) + len(attended)),
        out_specs=[vmem()] * cycle,
        scratch_shapes=[
            pltpu.VMEM((tokens, width), bf16),
            pltpu.VMEM((width, tokens), bf16),
            pltpu.VMEM((width, tokens), f32),
            pltpu.VMEM((tokens, width), f32),
            pltpu.VMEM((tokens, width), f32),
        ],
        compiler_params=params(16 if tokens <= 512 else 60),
        cost_estimate=cost(3),
        name="backward",
    )(*inputs, *grads, *attended)


def fetch_rows(out_weight, place):
    cycle, count = lax.axis_size("seq"), lax.axis_size("mp")
    pairs = []
    for member in range(cycle):
        for rank in range(count):
            owner = 2 * group_of(cycle, member ^ place, rank // 2) + rank % 2
            pairs.append((member * count + owner, member * count + rank))
    return lax.ppermute(out_weight, ("seq", "mp"), pairs)


def with_other_core(half):
    return [half, exchange(half, "mp", 1)]


def rows_in_order(mine, others, core):
    first = core == 0
    mine, other = mine[...], jnp.concatenate([ref[...] for ref in others], axis=0)
    return jnp.concatenate([jnp.where(first, mine, other), jnp.where(first, other, mine)], axis=0)


def both_halves(halves, core):
    mine, other = halves[0][...], halves[1][...]
    first = core == 0
    return jnp.concatenate([jnp.where(first, mine, other), jnp.where(first, other, mine)], axis=0)


def group_kernel(count, *refs):
    ups, out = refs[:count], refs[-1]
    _, _, core = my_place()
    weight = rows_in_order(refs[count], refs[count + 1:count + 2], core)
    out[...] = dot_nt(weight, jnp.concatenate([ref[...] for ref in ups], axis=0)).astype(bf16)


def group_grads(upstreams, pieces, after):
    rows, width = upstreams[0].shape[0], 2 * pieces[0].shape[0]
    return pl.pallas_call(
        functools.partial(group_kernel, len(upstreams)),
        out_shape=jax.ShapeDtypeStruct((width, len(upstreams) * rows), bf16),
        in_specs=[vmem()] * (len(upstreams) + 2) + [unread()] * len(after),
        out_specs=vmem(),
        compiler_params=params(8),
        cost_estimate=cost(1),
        name="group_grads",
    )(*upstreams, *pieces, *after)


def partial_kernel(att_ref, mine, *refs):
    own, kept, sent = refs[-3:]
    rows = own.shape[0]
    _, _, core = my_place()
    weight = rows_in_order(mine, refs[:1], core)
    product = dot_nn(att_ref[...], weight)
    own[...] = product[:rows, :]
    kept[...] = product[rows:2 * rows, :]
    sent[...] = product[2 * rows:, :].astype(bf16)


def partials(attended, pieces, after):
    rows, model = attended.shape[0] // 4, pieces[0].shape[1]
    return pl.pallas_call(
        partial_kernel,
        out_shape=[jax.ShapeDtypeStruct((rows, model), f32)] * 2
        + [jax.ShapeDtypeStruct((2 * rows, model), bf16)],
        in_specs=[vmem()] * 3 + [unread()] * len(after),
        out_specs=[vmem()] * 3,
        compiler_params=params(12),
        cost_estimate=cost(1),
        name="partials",
    )(attended, *pieces, *after)


def combine_kernel(own, kept, landed, total, *sent):
    rows = own.shape[0]
    total[...] = own[...] + landed[:rows, :].astype(f32)
    part = rows // len(sent)
    for at, out in enumerate(sent):
        span = slice(at * part, (at + 1) * part)
        out[...] = (
            kept[span, :] + landed[rows + at * part:rows + (at + 1) * part, :].astype(f32)
        ).astype(bf16)


def combine(own, kept, landed):
    return pl.pallas_call(
        combine_kernel,
        out_shape=[jax.ShapeDtypeStruct(own.shape, f32)]
        + [jax.ShapeDtypeStruct((own.shape[0] // 2, own.shape[1]), bf16)] * 2,
        in_specs=[vmem()] * 3,
        out_specs=[vmem()] * 3,
        compiler_params=params(8),
        cost_estimate=cost(1),
        name="combine",
    )(own, kept, landed)


def grad_kernel(cycle, up_ref, *refs):
    _, _, core = my_place()
    outs = refs[2 * cycle:]
    for place in range(cycle):
        rows = both_halves(refs[2 * place:2 * place + 2], core)
        outs[place][...] = dot_nt(up_ref[...], rows).astype(bf16)


def project_grad(cycle, upstream, halves):
    rows, model = upstream.shape
    return pl.pallas_call(
        functools.partial(grad_kernel, cycle),
        out_shape=[jax.ShapeDtypeStruct((rows, model // cycle), bf16)] * cycle,
        in_specs=[vmem()] * (1 + 2 * cycle),
        out_specs=[vmem()] * cycle,
        compiler_params=params(8),
        name="project_grad",
    )(upstream, *halves)


def place_columns(chunks, outs, sems):
    cycle = len(chunks)
    rows, model = outs[0].shape
    width = model // cycle
    own, chip, _ = my_place()
    copies = []
    for place in range(cycle):
        group = group_of(cycle, lax.bitwise_xor(own, distance_of(place)), chip)
        if width % 128 == 0:
            for at, out in enumerate(outs):
                copies.append(
                    pltpu.make_async_copy(
                        chunks[place].at[at * rows:(at + 1) * rows, :],
                        out.at[:, columns_at(group * width, width)],
                        sems.at[place, at],
                    )
                )
                copies[-1].start()
        else:
            for other in range(cycle):
                @pl.when(group == other)
                def _():
                    for at, out in enumerate(outs):
                        out[:, other * width:(other + 1) * width] = chunks[place][
                            at * rows:(at + 1) * rows, :
                        ]
    return copies


def finish_kernel(cycle, *refs):
    chunks = refs[:cycle]
    outs, word = refs[-5:-2], refs[-2]
    word[...] = jnp.zeros(word.shape, word.dtype)
    rows = outs[0].shape[0]
    copies = place_columns(chunks, outs, refs[-1])
    if len(refs) > cycle + 5:
        halves = refs[cycle:3 * cycle]
        _, _, core = my_place()
        total = None
        for place in range(cycle):
            weight = both_halves(halves[2 * place:2 * place + 2], core)
            term = dot_nn(chunks[place][3 * rows:, :], weight)
            total = term if total is None else total + term
        refs[-6][...] = total.astype(bf16)
    for copy in copies:
        copy.wait()


def finish(cycle, rows, chunks, others):
    model = chunks[0].shape[1] * cycle
    aligned = model // cycle % 128 == 0
    return pl.pallas_call(
        functools.partial(finish_kernel, cycle),
        out_shape=[jax.ShapeDtypeStruct((rows, model), bf16)] * (4 if others else 3)
        + [jax.ShapeDtypeStruct((16, 128), bf16)],
        in_specs=[vmem()] * (cycle + len(others)),
        out_specs=[vmem()] * (1 if others else 0)
        + [anywhere() if aligned else vmem()] * 3
        + [vmem()],
        scratch_shapes=[pltpu.SemaphoreType.DMA((cycle, 3))],
        compiler_params=params(8),
        name="finish",
    )(*chunks, *others)


def sum_kernel(own, *refs):
    out = refs[-1]
    part = own.shape[0] // 2
    for at in range(2):
        span = slice(at * part, (at + 1) * part)
        out[span, :] = (own[span, :] + refs[at][...].astype(f32)).astype(bf16)


def last_sum(own, landed, after):
    return pl.pallas_call(
        sum_kernel,
        out_shape=jax.ShapeDtypeStruct(own.shape, bf16),
        in_specs=[vmem()] * 3 + [unread()] * len(after),
        out_specs=vmem(),
        compiler_params=params(8),
        name="last_sum",
    )(own, *landed, *after)


def local(queries, keys, values, out_weight, upstream, adjacency, counts):
    cycle = lax.axis_size("seq")
    rows = queries.shape[0]
    tensors = (queries, keys, values, adjacency, counts.reshape(1, 1))
    if is_square():
        return square(cycle, rows, tensors, out_weight, upstream)
    chunks = swapped(list(pack(cycle, range(cycle), tensors)))
    halves = []
    for place in range(cycle):
        halves += with_other_core(fetch_rows(out_weight, place))
    q_all, k_all, v_all, k_t, v_t, bias = gather(cycle, chunks)
    attended, att_t, inverse, weights = forward(cycle, 1, q_all, k_all, v_t, bias)
    grads = swapped(project_grad(cycle, upstream, halves))
    inputs = (q_all, k_all, v_all, k_t, att_t, inverse, weights)
    terms = swapped(backward(cycle, inputs, grads, attended))
    return tuple(finish(cycle, rows, terms, halves)[:4])


def square(cycle, rows, tensors, out_weight, upstream):
    nexts = swapped([upstream] * 3)[1:]
    chunks = swapped(list(pack(cycle, range(cycle), tensors)))
    (held_weight,) = hold((out_weight,), nexts)
    (passed,) = hold((nexts[1],), [chunks[1]])
    across = exchange_by_core(passed, (1, 2))
    own_rows = with_other_core(fetch_rows(held_weight, 0))
    q_all, k_all, v_all, k_t, v_t, bias = gather(cycle, chunks)
    (attended,), att_t, inverse, weights = forward(cycle, cycle, q_all, k_all, v_t, bias)
    own_mixed, kept, sent = partials(attended, own_rows, [])
    landed = exchange_by_core(sent, (2, 1))
    grads = [group_grads((upstream, *nexts, across), own_rows, [kept])]
    inputs = (q_all, k_all, v_all, k_t, att_t, inverse, weights)
    terms = swapped(list(backward(cycle, inputs, grads, [])))
    own_mixed, *next_mixed = combine(own_mixed, kept, landed)
    next_mixed = [exchange_by_core(part, (1, 2)) for part in next_mixed]
    *grads, word = finish(cycle, rows, terms, [])
    return (last_sum(own_mixed, next_mixed, [word]), *grads)


def solution(mesh):
    tokens = P(("seq", "mp"), None)
    return jax.shard_map(
        local,
        mesh=mesh,
        in_specs=(tokens, tokens, tokens, P("mp", None), tokens, tokens, P(("seq", "mp"))),
        out_specs=(tokens,) * 4,
        check_vma=False,
    )
```

```python
import functools

import jax
import jax.numpy as jnp
from jax import lax
from jax.experimental import pallas as pl
from jax.experimental.pallas import tpu as pltpu
from jax.sharding import PartitionSpec as P

HEADS = 16
HEAD_DIM = 64
META = 32

score_scale = 0.125
log2_scale = 0.125 * 1.4426950408889634
cycle_offsets = (1, -1, 2, -2)
absent = -1e30
bf16 = jnp.bfloat16
f32 = jnp.float32


def dot_nn(a, b):
    return lax.dot_general(a, b, (((1,), (0,)), ((), ())), preferred_element_type=f32)


def dot_nt(a, b):
    return lax.dot_general(a, b, (((1,), (1,)), ((), ())), preferred_element_type=f32)


def vmem():
    return pl.BlockSpec(memory_space=pltpu.VMEM)


def params(mib):
    return pltpu.CompilerParams(vmem_limit_bytes=int(mib * 1024) * 1024)


def unread():
    return pl.BlockSpec(memory_space=pl.ANY)


def anywhere():
    return pl.BlockSpec(memory_space=pltpu.HBM)


def cost(micros):
    return pl.CostEstimate(flops=int(micros * 1e9), bytes_accessed=0, transcendentals=0)


def exchange(value, axis, distance):
    count = lax.axis_size(axis)
    return lax.ppermute(value, axis, [(i, i ^ distance) for i in range(count)])


def turned(distance):
    return distance ^ (((distance ^ (distance >> 1)) & 1) * 3)


def exchange_by_core(value, distances):
    count = lax.axis_size("mp")
    pairs = [
        (member * count + rank, (member ^ distances[rank % 2]) * count + rank)
        for member in range(lax.axis_size("seq"))
        for rank in range(count)
    ]
    return lax.ppermute(value, ("seq", "mp"), pairs)


def is_square():
    return lax.axis_size("seq") == 4 and lax.axis_size("mp") == 8


def distance_of(slot):
    if is_square():
        return jnp.where(lax.rem(lax.axis_index("mp"), 2) == 0, slot, turned(slot))
    return slot


def swapped(chunks):
    if is_square():
        return [chunks[0]] + [
            exchange_by_core(chunks[k], (k, turned(k))) for k in range(1, len(chunks))
        ]
    return [chunks[0]] + [exchange(chunks[k], "seq", k) for k in range(1, len(chunks))]


def group_of(cycle, member, chip):
    turn = (member + chip) % cycle
    return turned(turn) if cycle == 4 else turn


def my_place():
    rank = lax.axis_index("mp")
    return lax.axis_index("seq"), rank // 2, lax.rem(rank, 2)


def columns_at(first, width):
    return pl.ds(pl.multiple_of(first, width), width)


def pack_kernel(cycle, places, q_ref, k_ref, v_ref, adj_any, cnt_any, *refs):
    refs, (adj_ref, cnt_ref, sems, more_sems) = refs[:-4], refs[-4:]
    outs = refs
    rows, model = q_ref.shape
    width = model // cycle
    own, chip, _ = my_place()
    lists = [
        pltpu.make_async_copy(adj_any, adj_ref, more_sems.at[0]),
        pltpu.make_async_copy(cnt_any, cnt_ref, more_sems.at[1]),
    ]
    for copy in lists:
        copy.start()
    copies = []
    if width % 128 == 0:
        for place, out in zip(places, outs):
            group = group_of(cycle, lax.bitwise_xor(own, distance_of(place)), chip)
            for at, ref in enumerate((q_ref, k_ref, v_ref)):
                copies.append(
                    pltpu.make_async_copy(
                        ref.at[:, columns_at(group * width, width)],
                        out.at[at * rows:(at + 1) * rows, :],
                        sems.at[place, at],
                    )
                )
                copies[-1].start()
    for copy in lists:
        copy.wait()
    lines = lax.broadcasted_iota(jnp.int32, (META, width), 0)
    meta = jnp.where(lines == 0, 1, 0)
    for column, offset in enumerate(cycle_offsets):
        named = lax.rem(own - offset + 2 * cycle, cycle)
        meta = meta + jnp.where(
            (lines == distance_of(lax.bitwise_xor(own, named))) & (adj_ref[0, column] > 0), 1, 0
        )
    meta = jnp.where(lines == META - 1, cnt_ref[0, 0], meta).astype(f32).astype(bf16)
    for place, out in zip(places, outs):
        out[3 * rows:, :] = meta
        if width % 128:
            group = group_of(cycle, lax.bitwise_xor(own, distance_of(place)), chip)
            for other in range(cycle):
                @pl.when(group == other)
                def _():
                    for at, ref in enumerate((q_ref, k_ref, v_ref)):
                        out[at * rows:(at + 1) * rows, :] = ref[
                            :, other * width:(other + 1) * width
                        ]
    for copy in copies:
        copy.wait()


def hold_kernel(count, *refs):
    outs, sems = refs[-count - 1:-1], refs[-1]
    copies = [pltpu.make_async_copy(refs[at], outs[at], sems.at[at]) for at in range(count)]
    for copy in copies:
        copy.start()
    for copy in copies:
        copy.wait()


def hold(arrays, after):
    count = len(arrays)
    return pl.pallas_call(
        functools.partial(hold_kernel, count),
        out_shape=[jax.ShapeDtypeStruct(array.shape, array.dtype) for array in arrays],
        in_specs=[unread()] * (count + len(after)),
        out_specs=[vmem()] * count,
        scratch_shapes=[pltpu.SemaphoreType.DMA((count,))],
        compiler_params=params(2),
        cost_estimate=cost(1),
        name="hold",
    )(*arrays, *after)


def pack(cycle, places, tensors):
    rows, model = tensors[0].shape
    width = model // cycle
    return pl.pallas_call(
        functools.partial(pack_kernel, cycle, places),
        out_shape=[jax.ShapeDtypeStruct((3 * rows + META, width), bf16)] * len(places),
        in_specs=[anywhere() if width % 128 == 0 else vmem()] * 3
        + [unread()] * 2,
        out_specs=[vmem()] * len(places),
        scratch_shapes=[
            pltpu.SMEM(tensors[3].shape, jnp.int32),
            pltpu.SMEM(tensors[4].shape, jnp.int32),
            pltpu.SemaphoreType.DMA((cycle, 3)),
            pltpu.SemaphoreType.DMA((2,)),
        ],
        compiler_params=params(62),
        cost_estimate=cost(5),
        name="pack",
    )(*tensors)


def gather_kernel(cycle, *refs):
    chunks = refs[:cycle]
    q_all, k_all, v_all, k_t, v_t, bias = refs[-6:]
    rows = q_all.shape[0] // cycle
    for place in range(cycle):
        for at, part in enumerate((q_all, k_all, v_all)):
            part[place * rows:(place + 1) * rows, :] = chunks[place][at * rows:(at + 1) * rows, :]
    k_t[...] = k_all[...].astype(f32).T.astype(bf16)
    v_t[...] = v_all[...].astype(f32).T.astype(bf16)
    lines = lax.broadcasted_iota(jnp.int32, (rows, rows), 0).astype(f32)
    lists = [chunks[place][3 * rows:, :].astype(f32) for place in range(cycle)]
    for key_place in range(cycle):
        count = lists[key_place][META - 1:, :1]
        valid = lines < count
        for query_place in range(cycle):
            way = key_place ^ query_place
            times = lists[query_place][way:way + 1, :1]
            term = jnp.where(times > 0, jnp.log2(jnp.maximum(times, 1.0)), absent)
            bias[
                key_place * rows:(key_place + 1) * rows,
                query_place * rows:(query_place + 1) * rows,
            ] = jnp.where(valid, term, absent)


def gather(cycle, chunks, after=()):
    width = chunks[0].shape[1]
    rows = (chunks[0].shape[0] - META) // 3
    tokens = rows * cycle
    return pl.pallas_call(
        functools.partial(gather_kernel, cycle),
        out_shape=[jax.ShapeDtypeStruct((tokens, width), bf16)] * 3
        + [jax.ShapeDtypeStruct((width, tokens), bf16)] * 2
        + [jax.ShapeDtypeStruct((tokens, tokens), f32)],
        in_specs=[vmem()] * cycle + [unread()] * len(after),
        out_specs=[vmem()] * 6,
        compiler_params=params(8 if tokens <= 512 else 40),
        cost_estimate=cost(5),
        name="gather",
    )(*chunks, *after)


def head_tile(width):
    return min(128, width)


def only_head(tile, which):
    lanes = lax.broadcasted_iota(jnp.int32, tile.shape, 1)
    inside = (lanes >= which * HEAD_DIM) & (lanes < (which + 1) * HEAD_DIM)
    return jnp.where(inside, tile, jnp.zeros_like(tile))


def forward_kernel(query_tile, parts, q_all, k_all, v_t, bias, *refs):
    outs = refs[-3 - parts:-3]
    att_t, inverse, weights = refs[-3:]
    tokens, width = q_all.shape
    tile = head_tile(width)
    for start in range(0, tokens, query_tile):
        span = slice(start, start + query_tile)
        for head in range(width // HEAD_DIM):
            at = head * HEAD_DIM // tile * tile
            which = (head * HEAD_DIM - at) // HEAD_DIM
            scores = dot_nt(
                k_all[:, at:at + tile], only_head(q_all[span, at:at + tile], which)
            )
            scores = scores * log2_scale + bias[:, span]
            largest = jnp.max(scores, axis=0, keepdims=True)
            expo = jnp.exp2(scores - largest)
            total = jnp.sum(expo, axis=0, keepdims=True)
            share = 1.0 / total
            expo = expo.astype(bf16)
            inverse[head:head + 1, span] = share
            weights[head * tokens:(head + 1) * tokens, span] = expo
            att_t[head * HEAD_DIM:(head + 1) * HEAD_DIM, span] = (
                dot_nn(v_t[head * HEAD_DIM:(head + 1) * HEAD_DIM, :], expo) * share
            )
    attended = att_t[...].T.astype(bf16)
    filled = 0
    for out in outs:
        out[...] = attended[filled:filled + out.shape[0], :]
        filled += out.shape[0]


def forward(cycle, together, q_all, k_all, v_t, bias, after=()):
    tokens, width = q_all.shape
    rows = tokens // cycle
    parts = cycle // together
    outs = pl.pallas_call(
        functools.partial(forward_kernel, min(tokens, 512), parts),
        out_shape=[jax.ShapeDtypeStruct((together * rows, width), bf16)] * parts
        + [
            jax.ShapeDtypeStruct((width, tokens), f32),
            jax.ShapeDtypeStruct((8, tokens), f32),
            jax.ShapeDtypeStruct((width // HEAD_DIM * tokens, tokens), bf16),
        ],
        in_specs=[vmem()] * 4 + [unread()] * len(after),
        out_specs=[vmem()] * (parts + 3),
        compiler_params=params(16 if tokens <= 512 else 60),
        cost_estimate=cost(3),
        name="forward",
    )(q_all, k_all, v_t, bias, *after)
    return outs[:parts], *outs[parts:]


def backward_kernel(cycle, query_tile, grad_count, att_count, *refs):
    q_all, k_all, v_all, k_t, att_t, inverse, weights = refs[:7]
    refs = refs[7:]
    grads = refs[:grad_count]
    attended = refs[grad_count:grad_count + att_count]
    outs = refs[-5 - cycle:-5]
    g_all, g_t, dq_t, dk, dv = refs[-5:]
    tokens, width = q_all.shape
    rows = tokens // cycle
    if grad_count == 1:
        turned_grad = grads[0][...].astype(f32)
    else:
        for place, grad in enumerate(grads):
            g_all[place * rows:(place + 1) * rows, :] = grad[...]
        turned_grad = g_all[...].astype(f32).T
    shares = [
        turned_grad[low:low + HEAD_DIM, :] * inverse[low // HEAD_DIM:low // HEAD_DIM + 1, :]
        for low in range(0, width, HEAD_DIM)
    ]
    g_t[...] = jnp.concatenate(shares, axis=0).astype(bf16)
    g_wide = g_t[...].astype(f32)
    g_all[...] = g_wide.T.astype(bf16)
    product = g_wide * att_t[...].astype(bf16).astype(f32)
    tile = head_tile(width)
    for start in range(0, tokens, query_tile):
        span = slice(start, start + query_tile)
        for at in range(0, width, tile):
            dk_tile = dv_tile = None
            for which in range(tile // HEAD_DIM):
                low = at + which * HEAD_DIM
                head = low // HEAD_DIM
                delta = jnp.sum(product[low:low + HEAD_DIM, span], axis=0, keepdims=True)
                grad_probs = dot_nn(
                    only_head(v_all[:, at:at + tile], which), g_t[at:at + tile, span]
                )
                expo = weights[head * tokens:(head + 1) * tokens, span]
                grad_scores = (expo.astype(f32) * (grad_probs - delta)).astype(bf16)
                dk_head = dot_nn(grad_scores, only_head(q_all[span, at:at + tile], which))
                dv_head = dot_nn(expo, only_head(g_all[span, at:at + tile], which))
                dk_tile = dk_head if dk_tile is None else dk_tile + dk_head
                dv_tile = dv_head if dv_tile is None else dv_tile + dv_head
                dq_head = dot_nn(k_t[low:low + HEAD_DIM, :], grad_scores)
                dq_t[low:low + HEAD_DIM, span] = dq_head
            if start == 0:
                dk[:, at:at + tile] = dk_tile
                dv[:, at:at + tile] = dv_tile
            else:
                dk[:, at:at + tile] += dk_tile
                dv[:, at:at + tile] += dv_tile
    dq = (dq_t[...] * score_scale).T.astype(bf16)
    for place in range(cycle):
        span = slice(place * rows, (place + 1) * rows)
        outs[place][:rows, :] = dq[span, :]
        outs[place][rows:2 * rows, :] = (dk[span, :] * score_scale).astype(bf16)
        outs[place][2 * rows:3 * rows, :] = dv[span, :].astype(bf16)
        if attended:
            outs[place][3 * rows:, :] = attended[place][...]


def backward(cycle, inputs, grads, attended):
    tokens, width = inputs[0].shape
    rows = tokens // cycle
    return pl.pallas_call(
        functools.partial(backward_kernel, cycle, min(tokens, 512), len(grads), len(attended)),
        out_shape=[jax.ShapeDtypeStruct(((4 if attended else 3) * rows, width), bf16)] * cycle,
        in_specs=[vmem()] * (len(inputs) + len(grads) + len(attended)),
        out_specs=[vmem()] * cycle,
        scratch_shapes=[
            pltpu.VMEM((tokens, width), bf16),
            pltpu.VMEM((width, tokens), bf16),
            pltpu.VMEM((width, tokens), f32),
            pltpu.VMEM((tokens, width), f32),
            pltpu.VMEM((tokens, width), f32),
        ],
        compiler_params=params(16 if tokens <= 512 else 60),
        cost_estimate=cost(3),
        name="backward",
    )(*inputs, *grads, *attended)


def fetch_rows(out_weight, place):
    cycle, count = lax.axis_size("seq"), lax.axis_size("mp")
    pairs = []
    for member in range(cycle):
        for rank in range(count):
            owner = 2 * group_of(cycle, member ^ place, rank // 2) + rank % 2
            pairs.append((member * count + owner, member * count + rank))
    return lax.ppermute(out_weight, ("seq", "mp"), pairs)


def with_other_core(half):
    return [half, exchange(half, "mp", 1)]


def rows_in_order(mine, others, core):
    first = core == 0
    mine, other = mine[...], jnp.concatenate([ref[...] for ref in others], axis=0)
    return jnp.concatenate([jnp.where(first, mine, other), jnp.where(first, other, mine)], axis=0)


def both_halves(halves, core):
    mine, other = halves[0][...], halves[1][...]
    first = core == 0
    return jnp.concatenate([jnp.where(first, mine, other), jnp.where(first, other, mine)], axis=0)


def group_kernel(count, *refs):
    ups, out = refs[:count], refs[-1]
    _, _, core = my_place()
    weight = rows_in_order(refs[count], refs[count + 1:count + 2], core)
    out[...] = dot_nt(weight, jnp.concatenate([ref[...] for ref in ups], axis=0)).astype(bf16)


def group_grads(upstreams, pieces, after):
    rows, width = upstreams[0].shape[0], 2 * pieces[0].shape[0]
    return pl.pallas_call(
        functools.partial(group_kernel, len(upstreams)),
        out_shape=jax.ShapeDtypeStruct((width, len(upstreams) * rows), bf16),
        in_specs=[vmem()] * (len(upstreams) + 2) + [unread()] * len(after),
        out_specs=vmem(),
        compiler_params=params(8),
        cost_estimate=cost(1),
        name="group_grads",
    )(*upstreams, *pieces, *after)


def partial_kernel(att_ref, mine, *refs):
    own, kept, near, across = refs[-4:]
    rows = own.shape[0]
    _, _, core = my_place()
    weight = rows_in_order(mine, refs[:1], core)
    product = dot_nn(att_ref[...], weight)
    own[...] = product[:rows, :]
    kept[...] = product[rows:2 * rows, :]
    near[...] = product[2 * rows:3 * rows, :].astype(bf16)
    across[...] = product[3 * rows:, :].astype(bf16)


def partials(attended, pieces, after):
    rows, model = attended.shape[0] // 4, pieces[0].shape[1]
    return pl.pallas_call(
        partial_kernel,
        out_shape=[jax.ShapeDtypeStruct((rows, model), f32)] * 2
        + [jax.ShapeDtypeStruct((rows, model), bf16)] * 2,
        in_specs=[vmem()] * 3 + [unread()] * len(after),
        out_specs=[vmem()] * 4,
        compiler_params=params(12),
        cost_estimate=cost(1),
        name="partials",
    )(attended, *pieces, *after)


def combine_kernel(kept, landed, *sent):
    part = kept.shape[0] // len(sent)
    for at, out in enumerate(sent):
        span = slice(at * part, (at + 1) * part)
        out[...] = (kept[span, :] + landed[span, :].astype(f32)).astype(bf16)


def combine(kept, landed):
    return pl.pallas_call(
        combine_kernel,
        out_shape=[jax.ShapeDtypeStruct((kept.shape[0] // 2, kept.shape[1]), bf16)] * 2,
        in_specs=[vmem()] * 2,
        out_specs=[vmem()] * 2,
        compiler_params=params(8),
        cost_estimate=cost(1),
        name="combine",
    )(kept, landed)


def grad_kernel(cycle, up_ref, *refs):
    _, _, core = my_place()
    outs = refs[2 * cycle:]
    for place in range(cycle):
        rows = both_halves(refs[2 * place:2 * place + 2], core)
        outs[place][...] = dot_nt(up_ref[...], rows).astype(bf16)


def project_grad(cycle, upstream, halves):
    rows, model = upstream.shape
    return pl.pallas_call(
        functools.partial(grad_kernel, cycle),
        out_shape=[jax.ShapeDtypeStruct((rows, model // cycle), bf16)] * cycle,
        in_specs=[vmem()] * (1 + 2 * cycle),
        out_specs=[vmem()] * cycle,
        compiler_params=params(8),
        name="project_grad",
    )(upstream, *halves)


def place_columns(chunks, outs, sems):
    cycle = len(chunks)
    rows, model = outs[0].shape
    width = model // cycle
    own, chip, _ = my_place()
    copies = []
    for place in range(cycle):
        group = group_of(cycle, lax.bitwise_xor(own, distance_of(place)), chip)
        if width % 128 == 0:
            for at, out in enumerate(outs):
                copies.append(
                    pltpu.make_async_copy(
                        chunks[place].at[at * rows:(at + 1) * rows, :],
                        out.at[:, columns_at(group * width, width)],
                        sems.at[place, at],
                    )
                )
                copies[-1].start()
        else:
            for other in range(cycle):
                @pl.when(group == other)
                def _():
                    for at, out in enumerate(outs):
                        out[:, other * width:(other + 1) * width] = chunks[place][
                            at * rows:(at + 1) * rows, :
                        ]
    return copies


def finish_kernel(cycle, product, *refs):
    chunks = refs[:cycle]
    outs = refs[-4:-1]
    rows = outs[0].shape[0]
    copies = place_columns(chunks, outs, refs[-1])
    if product:
        halves = refs[cycle:3 * cycle]
        _, _, core = my_place()
        total = None
        for place in range(cycle):
            weight = both_halves(halves[2 * place:2 * place + 2], core)
            term = dot_nn(chunks[place][3 * rows:, :], weight)
            total = term if total is None else total + term
        refs[-5][...] = total.astype(bf16)
    for copy in copies:
        copy.wait()


def finish(cycle, rows, chunks, others, after=()):
    model = chunks[0].shape[1] * cycle
    aligned = model // cycle % 128 == 0
    return pl.pallas_call(
        functools.partial(finish_kernel, cycle, len(others) > 0),
        out_shape=[jax.ShapeDtypeStruct((rows, model), bf16)] * (4 if others else 3),
        in_specs=[vmem()] * (cycle + len(others)) + [unread()] * len(after),
        out_specs=[vmem()] * (1 if others else 0)
        + [anywhere() if aligned else vmem()] * 3,
        scratch_shapes=[pltpu.SemaphoreType.DMA((cycle, 3))],
        compiler_params=params(8),
        name="finish",
    )(*chunks, *others, *after)


def sum_kernel(own, *refs):
    near, out, word = refs[-3:]
    word[...] = jnp.zeros(word.shape, word.dtype)
    part = own.shape[0] // 2
    for at in range(2):
        span = slice(at * part, (at + 1) * part)
        total = own[span, :] + near[span, :].astype(f32) + refs[at][...].astype(f32)
        out[span, :] = total.astype(bf16)


def last_sum(own, near, landed):
    return pl.pallas_call(
        sum_kernel,
        out_shape=[
            jax.ShapeDtypeStruct(own.shape, bf16),
            jax.ShapeDtypeStruct((16, 128), bf16),
        ],
        in_specs=[vmem()] * 4,
        out_specs=[vmem()] * 2,
        compiler_params=params(8),
        name="last_sum",
    )(own, *landed, near)


def local(queries, keys, values, out_weight, upstream, adjacency, counts):
    cycle = lax.axis_size("seq")
    rows = queries.shape[0]
    tensors = (queries, keys, values, adjacency, counts.reshape(1, 1))
    if is_square():
        return square(cycle, rows, tensors, out_weight, upstream)
    chunks = swapped(list(pack(cycle, range(cycle), tensors)))
    halves = []
    for place in range(cycle):
        halves += with_other_core(fetch_rows(out_weight, place))
    q_all, k_all, v_all, k_t, v_t, bias = gather(cycle, chunks)
    attended, att_t, inverse, weights = forward(cycle, 1, q_all, k_all, v_t, bias)
    grads = swapped(project_grad(cycle, upstream, halves))
    inputs = (q_all, k_all, v_all, k_t, att_t, inverse, weights)
    terms = swapped(backward(cycle, inputs, grads, attended))
    return tuple(finish(cycle, rows, terms, halves))


def square(cycle, rows, tensors, out_weight, upstream):
    nexts = swapped([upstream] * 3)[1:]
    chunks = swapped(list(pack(cycle, range(cycle), tensors)))
    (held_weight,) = hold((out_weight,), nexts)
    (passed,) = hold((nexts[1],), [chunks[1]])
    across = exchange_by_core(passed, (1, 2))
    own_rows = with_other_core(fetch_rows(held_weight, 0))
    q_all, k_all, v_all, k_t, v_t, bias = gather(cycle, chunks)
    (attended,), att_t, inverse, weights = forward(cycle, cycle, q_all, k_all, v_t, bias)
    own_mixed, kept, near_mixed, passed_mixed = partials(attended, own_rows, [])
    passed_mixed = exchange_by_core(passed_mixed, (2, 1))
    near_mixed = exchange_by_core(near_mixed, (2, 1))
    grads = [group_grads((upstream, *nexts, across), own_rows, [kept])]
    inputs = (q_all, k_all, v_all, k_t, att_t, inverse, weights)
    terms = swapped(list(backward(cycle, inputs, grads, [])))
    next_mixed = [exchange_by_core(part, (1, 2)) for part in combine(kept, passed_mixed)]
    mixed_out, word = last_sum(own_mixed, near_mixed, next_mixed)
    return (mixed_out, *finish(cycle, rows, terms, [], [word]))


def solution(mesh):
    tokens = P(("seq", "mp"), None)
    return jax.shard_map(
        local,
        mesh=mesh,
        in_specs=(tokens, tokens, tokens, P("mp", None), tokens, tokens, P(("seq", "mp"))),
        out_specs=(tokens,) * 4,
        check_vma=False,
    )
```

```python
import functools

import jax
import jax.numpy as jnp
from jax import lax
from jax.experimental import pallas as pl
from jax.experimental.pallas import tpu as pltpu
from jax.sharding import PartitionSpec as P

HEADS = 16
HEAD_DIM = 64
META = 32

score_scale = 0.125
log2_scale = 0.125 * 1.4426950408889634
cycle_offsets = (1, -1, 2, -2)
absent = -1e30
bf16 = jnp.bfloat16
f32 = jnp.float32


def dot_nn(a, b):
    return lax.dot_general(a, b, (((1,), (0,)), ((), ())), preferred_element_type=f32)


def dot_nt(a, b):
    return lax.dot_general(a, b, (((1,), (1,)), ((), ())), preferred_element_type=f32)


def vmem():
    return pl.BlockSpec(memory_space=pltpu.VMEM)


def params(mib):
    return pltpu.CompilerParams(vmem_limit_bytes=int(mib * 1024) * 1024)


def unread():
    return pl.BlockSpec(memory_space=pl.ANY)


def anywhere():
    return pl.BlockSpec(memory_space=pltpu.HBM)


def cost(micros):
    return pl.CostEstimate(flops=int(micros * 1e9), bytes_accessed=0, transcendentals=0)


def exchange(value, axis, distance):
    count = lax.axis_size(axis)
    return lax.ppermute(value, axis, [(i, i ^ distance) for i in range(count)])


def turned(distance):
    return distance ^ (((distance ^ (distance >> 1)) & 1) * 3)


def exchange_by_core(value, distances):
    count = lax.axis_size("mp")
    pairs = [
        (member * count + rank, (member ^ distances[rank % 2]) * count + rank)
        for member in range(lax.axis_size("seq"))
        for rank in range(count)
    ]
    return lax.ppermute(value, ("seq", "mp"), pairs)


def is_square():
    return lax.axis_size("seq") == 4 and lax.axis_size("mp") == 8


def distance_of(slot):
    if is_square():
        return jnp.where(lax.rem(lax.axis_index("mp"), 2) == 0, slot, turned(slot))
    return slot


def swapped(chunks):
    if is_square():
        return [chunks[0]] + [
            exchange_by_core(chunks[k], (k, turned(k))) for k in range(1, len(chunks))
        ]
    return [chunks[0]] + [exchange(chunks[k], "seq", k) for k in range(1, len(chunks))]


def group_of(cycle, member, chip):
    turn = (member + chip) % cycle
    return turned(turn) if cycle == 4 else turn


def my_place():
    rank = lax.axis_index("mp")
    return lax.axis_index("seq"), rank // 2, lax.rem(rank, 2)


def columns_at(first, width):
    return pl.ds(pl.multiple_of(first, width), width)


def pack_kernel(cycle, places, q_ref, k_ref, v_ref, adj_any, cnt_any, *refs):
    refs, (adj_ref, cnt_ref, sems, more_sems) = refs[:-4], refs[-4:]
    outs = refs
    rows, model = q_ref.shape
    width = model // cycle
    own, chip, _ = my_place()
    lists = [
        pltpu.make_async_copy(adj_any, adj_ref, more_sems.at[0]),
        pltpu.make_async_copy(cnt_any, cnt_ref, more_sems.at[1]),
    ]
    for copy in lists:
        copy.start()
    copies = []
    if width % 128 == 0:
        for place, out in zip(places, outs):
            group = group_of(cycle, lax.bitwise_xor(own, distance_of(place)), chip)
            for at, ref in enumerate((q_ref, k_ref, v_ref)):
                copies.append(
                    pltpu.make_async_copy(
                        ref.at[:, columns_at(group * width, width)],
                        out.at[at * rows:(at + 1) * rows, :],
                        sems.at[place, at],
                    )
                )
                copies[-1].start()
    for copy in lists:
        copy.wait()
    lines = lax.broadcasted_iota(jnp.int32, (META, width), 0)
    meta = jnp.where(lines == 0, 1, 0)
    for column, offset in enumerate(cycle_offsets):
        named = lax.rem(own - offset + 2 * cycle, cycle)
        meta = meta + jnp.where(
            (lines == distance_of(lax.bitwise_xor(own, named))) & (adj_ref[0, column] > 0), 1, 0
        )
    meta = jnp.where(lines == META - 1, cnt_ref[0, 0], meta).astype(f32).astype(bf16)
    for place, out in zip(places, outs):
        out[3 * rows:, :] = meta
        if width % 128:
            group = group_of(cycle, lax.bitwise_xor(own, distance_of(place)), chip)
            for other in range(cycle):
                @pl.when(group == other)
                def _():
                    for at, ref in enumerate((q_ref, k_ref, v_ref)):
                        out[at * rows:(at + 1) * rows, :] = ref[
                            :, other * width:(other + 1) * width
                        ]
    for copy in copies:
        copy.wait()


def hold_kernel(count, *refs):
    outs, sems = refs[-count - 1:-1], refs[-1]
    copies = [pltpu.make_async_copy(refs[at], outs[at], sems.at[at]) for at in range(count)]
    for copy in copies:
        copy.start()
    for copy in copies:
        copy.wait()


def hold(arrays, after):
    count = len(arrays)
    return pl.pallas_call(
        functools.partial(hold_kernel, count),
        out_shape=[jax.ShapeDtypeStruct(array.shape, array.dtype) for array in arrays],
        in_specs=[unread()] * (count + len(after)),
        out_specs=[vmem()] * count,
        scratch_shapes=[pltpu.SemaphoreType.DMA((count,))],
        compiler_params=params(2),
        cost_estimate=cost(1),
        name="hold",
    )(*arrays, *after)


def pack(cycle, places, tensors):
    rows, model = tensors[0].shape
    width = model // cycle
    return pl.pallas_call(
        functools.partial(pack_kernel, cycle, places),
        out_shape=[jax.ShapeDtypeStruct((3 * rows + META, width), bf16)] * len(places),
        in_specs=[anywhere() if width % 128 == 0 else vmem()] * 3
        + [unread()] * 2,
        out_specs=[vmem()] * len(places),
        scratch_shapes=[
            pltpu.SMEM(tensors[3].shape, jnp.int32),
            pltpu.SMEM(tensors[4].shape, jnp.int32),
            pltpu.SemaphoreType.DMA((cycle, 3)),
            pltpu.SemaphoreType.DMA((2,)),
        ],
        compiler_params=params(62),
        cost_estimate=cost(5),
        name="pack",
    )(*tensors)


def gather_kernel(cycle, *refs):
    chunks = refs[:cycle]
    q_all, k_all, v_all, k_t, v_t, bias = refs[-6:]
    rows = q_all.shape[0] // cycle
    for place in range(cycle):
        for at, part in enumerate((q_all, k_all, v_all)):
            part[place * rows:(place + 1) * rows, :] = chunks[place][at * rows:(at + 1) * rows, :]
    k_t[...] = k_all[...].astype(f32).T.astype(bf16)
    v_t[...] = v_all[...].astype(f32).T.astype(bf16)
    lines = lax.broadcasted_iota(jnp.int32, (rows, rows), 0).astype(f32)
    lists = [chunks[place][3 * rows:, :].astype(f32) for place in range(cycle)]
    for key_place in range(cycle):
        count = lists[key_place][META - 1:, :1]
        valid = lines < count
        for query_place in range(cycle):
            way = key_place ^ query_place
            times = lists[query_place][way:way + 1, :1]
            term = jnp.where(times > 0, jnp.log2(jnp.maximum(times, 1.0)), absent)
            bias[
                key_place * rows:(key_place + 1) * rows,
                query_place * rows:(query_place + 1) * rows,
            ] = jnp.where(valid, term, absent)


def gather(cycle, chunks, after=()):
    width = chunks[0].shape[1]
    rows = (chunks[0].shape[0] - META) // 3
    tokens = rows * cycle
    return pl.pallas_call(
        functools.partial(gather_kernel, cycle),
        out_shape=[jax.ShapeDtypeStruct((tokens, width), bf16)] * 3
        + [jax.ShapeDtypeStruct((width, tokens), bf16)] * 2
        + [jax.ShapeDtypeStruct((tokens, tokens), f32)],
        in_specs=[vmem()] * cycle + [unread()] * len(after),
        out_specs=[vmem()] * 6,
        compiler_params=params(8 if tokens <= 512 else 40),
        cost_estimate=cost(5),
        name="gather",
    )(*chunks, *after)


def head_tile(width):
    return min(128, width)


def only_head(tile, which):
    lanes = lax.broadcasted_iota(jnp.int32, tile.shape, 1)
    inside = (lanes >= which * HEAD_DIM) & (lanes < (which + 1) * HEAD_DIM)
    return jnp.where(inside, tile, jnp.zeros_like(tile))


def forward_kernel(query_tile, parts, q_all, k_all, v_t, bias, *refs):
    outs = refs[-3 - parts:-3]
    att_t, inverse, weights = refs[-3:]
    tokens, width = q_all.shape
    tile = head_tile(width)
    for start in range(0, tokens, query_tile):
        span = slice(start, start + query_tile)
        for head in range(width // HEAD_DIM):
            at = head * HEAD_DIM // tile * tile
            which = (head * HEAD_DIM - at) // HEAD_DIM
            scores = dot_nt(
                k_all[:, at:at + tile], only_head(q_all[span, at:at + tile], which)
            )
            scores = scores * log2_scale + bias[:, span]
            largest = jnp.max(scores, axis=0, keepdims=True)
            expo = jnp.exp2(scores - largest)
            total = jnp.sum(expo, axis=0, keepdims=True)
            share = 1.0 / total
            expo = expo.astype(bf16)
            inverse[head:head + 1, span] = share
            weights[head * tokens:(head + 1) * tokens, span] = expo
            att_t[head * HEAD_DIM:(head + 1) * HEAD_DIM, span] = (
                dot_nn(v_t[head * HEAD_DIM:(head + 1) * HEAD_DIM, :], expo) * share
            )
    attended = att_t[...].T.astype(bf16)
    filled = 0
    for out in outs:
        out[...] = attended[filled:filled + out.shape[0], :]
        filled += out.shape[0]


def forward(cycle, together, q_all, k_all, v_t, bias, after=()):
    tokens, width = q_all.shape
    rows = tokens // cycle
    parts = cycle // together
    outs = pl.pallas_call(
        functools.partial(forward_kernel, min(tokens, 512), parts),
        out_shape=[jax.ShapeDtypeStruct((together * rows, width), bf16)] * parts
        + [
            jax.ShapeDtypeStruct((width, tokens), f32),
            jax.ShapeDtypeStruct((8, tokens), f32),
            jax.ShapeDtypeStruct((width // HEAD_DIM * tokens, tokens), bf16),
        ],
        in_specs=[vmem()] * 4 + [unread()] * len(after),
        out_specs=[vmem()] * (parts + 3),
        compiler_params=params(16 if tokens <= 512 else 60),
        cost_estimate=cost(3),
        name="forward",
    )(q_all, k_all, v_t, bias, *after)
    return outs[:parts], *outs[parts:]


def backward_kernel(cycle, query_tile, grad_count, att_count, *refs):
    q_all, k_all, v_all, k_t, att_t, inverse, weights = refs[:7]
    refs = refs[7:]
    grads = refs[:grad_count]
    attended = refs[grad_count:grad_count + att_count]
    outs = refs[-5 - cycle:-5]
    g_all, g_t, dq_t, dk, dv = refs[-5:]
    tokens, width = q_all.shape
    rows = tokens // cycle
    if grad_count == 1:
        turned_grad = grads[0][...].astype(f32)
    else:
        for place, grad in enumerate(grads):
            g_all[place * rows:(place + 1) * rows, :] = grad[...]
        turned_grad = g_all[...].astype(f32).T
    shares = [
        turned_grad[low:low + HEAD_DIM, :] * inverse[low // HEAD_DIM:low // HEAD_DIM + 1, :]
        for low in range(0, width, HEAD_DIM)
    ]
    g_t[...] = jnp.concatenate(shares, axis=0).astype(bf16)
    g_wide = g_t[...].astype(f32)
    g_all[...] = g_wide.T.astype(bf16)
    product = g_wide * att_t[...].astype(bf16).astype(f32)
    tile = head_tile(width)
    for start in range(0, tokens, query_tile):
        span = slice(start, start + query_tile)
        for at in range(0, width, tile):
            dk_tile = dv_tile = None
            for which in range(tile // HEAD_DIM):
                low = at + which * HEAD_DIM
                head = low // HEAD_DIM
                delta = jnp.sum(product[low:low + HEAD_DIM, span], axis=0, keepdims=True)
                grad_probs = dot_nn(
                    only_head(v_all[:, at:at + tile], which), g_t[at:at + tile, span]
                )
                expo = weights[head * tokens:(head + 1) * tokens, span]
                grad_scores = (expo.astype(f32) * (grad_probs - delta)).astype(bf16)
                dk_head = dot_nn(grad_scores, only_head(q_all[span, at:at + tile], which))
                dv_head = dot_nn(expo, only_head(g_all[span, at:at + tile], which))
                dk_tile = dk_head if dk_tile is None else dk_tile + dk_head
                dv_tile = dv_head if dv_tile is None else dv_tile + dv_head
                dq_head = dot_nn(k_t[low:low + HEAD_DIM, :], grad_scores)
                dq_t[low:low + HEAD_DIM, span] = dq_head
            if start == 0:
                dk[:, at:at + tile] = dk_tile
                dv[:, at:at + tile] = dv_tile
            else:
                dk[:, at:at + tile] += dk_tile
                dv[:, at:at + tile] += dv_tile
    dq = (dq_t[...] * score_scale).T.astype(bf16)
    for place in range(cycle):
        span = slice(place * rows, (place + 1) * rows)
        outs[place][:rows, :] = dq[span, :]
        outs[place][rows:2 * rows, :] = (dk[span, :] * score_scale).astype(bf16)
        outs[place][2 * rows:3 * rows, :] = dv[span, :].astype(bf16)
        if attended:
            outs[place][3 * rows:, :] = attended[place][...]


def backward(cycle, inputs, grads, attended):
    tokens, width = inputs[0].shape
    rows = tokens // cycle
    return pl.pallas_call(
        functools.partial(backward_kernel, cycle, min(tokens, 512), len(grads), len(attended)),
        out_shape=[jax.ShapeDtypeStruct(((4 if attended else 3) * rows, width), bf16)] * cycle,
        in_specs=[vmem()] * (len(inputs) + len(grads) + len(attended)),
        out_specs=[vmem()] * cycle,
        scratch_shapes=[
            pltpu.VMEM((tokens, width), bf16),
            pltpu.VMEM((width, tokens), bf16),
            pltpu.VMEM((width, tokens), f32),
            pltpu.VMEM((tokens, width), f32),
            pltpu.VMEM((tokens, width), f32),
        ],
        compiler_params=params(16 if tokens <= 512 else 60),
        cost_estimate=cost(3),
        name="backward",
    )(*inputs, *grads, *attended)


def fetch_rows(out_weight, place):
    cycle, count = lax.axis_size("seq"), lax.axis_size("mp")
    pairs = []
    for member in range(cycle):
        for rank in range(count):
            owner = 2 * group_of(cycle, member ^ place, rank // 2) + rank % 2
            pairs.append((member * count + owner, member * count + rank))
    return lax.ppermute(out_weight, ("seq", "mp"), pairs)


def with_other_core(half):
    return [half, exchange(half, "mp", 1)]


def rows_in_order(mine, others, core):
    first = core == 0
    mine, other = mine[...], jnp.concatenate([ref[...] for ref in others], axis=0)
    return jnp.concatenate([jnp.where(first, mine, other), jnp.where(first, other, mine)], axis=0)


def both_halves(halves, core):
    mine, other = halves[0][...], halves[1][...]
    first = core == 0
    return jnp.concatenate([jnp.where(first, mine, other), jnp.where(first, other, mine)], axis=0)


def group_kernel(count, *refs):
    ups, out = refs[:count], refs[-1]
    _, _, core = my_place()
    weight = rows_in_order(refs[count], refs[count + 1:count + 2], core)
    out[...] = dot_nt(weight, jnp.concatenate([ref[...] for ref in ups], axis=0)).astype(bf16)


def group_grads(upstreams, pieces, after):
    rows, width = upstreams[0].shape[0], 2 * pieces[0].shape[0]
    return pl.pallas_call(
        functools.partial(group_kernel, len(upstreams)),
        out_shape=jax.ShapeDtypeStruct((width, len(upstreams) * rows), bf16),
        in_specs=[vmem()] * (len(upstreams) + 2) + [unread()] * len(after),
        out_specs=vmem(),
        compiler_params=params(8),
        cost_estimate=cost(1),
        name="group_grads",
    )(*upstreams, *pieces, *after)


def partial_kernel(att_ref, mine, *refs):
    own, kept, near, across = refs[-4:]
    rows = own.shape[0]
    _, _, core = my_place()
    weight = rows_in_order(mine, refs[:1], core)
    product = dot_nn(att_ref[...], weight)
    own[...] = product[:rows, :]
    kept[...] = product[rows:2 * rows, :]
    near[...] = product[2 * rows:3 * rows, :].astype(bf16)
    across[...] = product[3 * rows:, :].astype(bf16)


def partials(attended, pieces, after):
    rows, model = attended.shape[0] // 4, pieces[0].shape[1]
    return pl.pallas_call(
        partial_kernel,
        out_shape=[jax.ShapeDtypeStruct((rows, model), f32)] * 2
        + [jax.ShapeDtypeStruct((rows, model), bf16)] * 2,
        in_specs=[vmem()] * 3 + [unread()] * len(after),
        out_specs=[vmem()] * 4,
        compiler_params=params(12),
        cost_estimate=cost(1),
        name="partials",
    )(attended, *pieces, *after)


def combine_kernel(kept, landed, unused, sent):
    sent[...] = (kept[...] + landed[...].astype(f32)).astype(bf16)


def combine(kept, landed, after):
    return pl.pallas_call(
        combine_kernel,
        out_shape=jax.ShapeDtypeStruct(kept.shape, bf16),
        in_specs=[vmem()] * 2 + [unread()],
        out_specs=vmem(),
        compiler_params=params(8),
        cost_estimate=cost(1),
        name="combine",
    )(kept, landed, after)


def grad_kernel(cycle, up_ref, *refs):
    _, _, core = my_place()
    outs = refs[2 * cycle:]
    for place in range(cycle):
        rows = both_halves(refs[2 * place:2 * place + 2], core)
        outs[place][...] = dot_nt(up_ref[...], rows).astype(bf16)


def project_grad(cycle, upstream, halves):
    rows, model = upstream.shape
    return pl.pallas_call(
        functools.partial(grad_kernel, cycle),
        out_shape=[jax.ShapeDtypeStruct((rows, model // cycle), bf16)] * cycle,
        in_specs=[vmem()] * (1 + 2 * cycle),
        out_specs=[vmem()] * cycle,
        compiler_params=params(8),
        name="project_grad",
    )(upstream, *halves)


def place_columns(chunks, outs, sems):
    cycle = len(chunks)
    rows, model = outs[0].shape
    width = model // cycle
    own, chip, _ = my_place()
    copies = []
    for place in range(cycle):
        group = group_of(cycle, lax.bitwise_xor(own, distance_of(place)), chip)
        if width % 128 == 0:
            for at, out in enumerate(outs):
                copies.append(
                    pltpu.make_async_copy(
                        chunks[place].at[at * rows:(at + 1) * rows, :],
                        out.at[:, columns_at(group * width, width)],
                        sems.at[place, at],
                    )
                )
                copies[-1].start()
        else:
            for other in range(cycle):
                @pl.when(group == other)
                def _():
                    for at, out in enumerate(outs):
                        out[:, other * width:(other + 1) * width] = chunks[place][
                            at * rows:(at + 1) * rows, :
                        ]
    return copies


def finish_kernel(cycle, product, *refs):
    chunks = refs[:cycle]
    outs = refs[-4:-1]
    rows = outs[0].shape[0]
    copies = place_columns(chunks, outs, refs[-1])
    if product:
        halves = refs[cycle:3 * cycle]
        _, _, core = my_place()
        total = None
        for place in range(cycle):
            weight = both_halves(halves[2 * place:2 * place + 2], core)
            term = dot_nn(chunks[place][3 * rows:, :], weight)
            total = term if total is None else total + term
        refs[-5][...] = total.astype(bf16)
    for copy in copies:
        copy.wait()


def finish(cycle, rows, chunks, others, after=()):
    model = chunks[0].shape[1] * cycle
    aligned = model // cycle % 128 == 0
    return pl.pallas_call(
        functools.partial(finish_kernel, cycle, len(others) > 0),
        out_shape=[jax.ShapeDtypeStruct((rows, model), bf16)] * (4 if others else 3),
        in_specs=[vmem()] * (cycle + len(others)) + [unread()] * len(after),
        out_specs=[vmem()] * (1 if others else 0)
        + [anywhere() if aligned else vmem()] * 3,
        scratch_shapes=[pltpu.SemaphoreType.DMA((cycle, 3))],
        compiler_params=params(8),
        name="finish",
    )(*chunks, *others, *after)


def sum_kernel(own, landed, near, out, word):
    word[...] = jnp.zeros(word.shape, word.dtype)
    total = own[...] + near[...].astype(f32) + landed[...].astype(f32)
    out[...] = total.astype(bf16)


def last_sum(own, near, landed):
    return pl.pallas_call(
        sum_kernel,
        out_shape=[
            jax.ShapeDtypeStruct(own.shape, bf16),
            jax.ShapeDtypeStruct((16, 128), bf16),
        ],
        in_specs=[vmem()] * 3,
        out_specs=[vmem()] * 2,
        compiler_params=params(8),
        name="last_sum",
    )(own, landed, near)


def local(queries, keys, values, out_weight, upstream, adjacency, counts):
    cycle = lax.axis_size("seq")
    rows = queries.shape[0]
    tensors = (queries, keys, values, adjacency, counts.reshape(1, 1))
    if is_square():
        return square(cycle, rows, tensors, out_weight, upstream)
    chunks = swapped(list(pack(cycle, range(cycle), tensors)))
    halves = []
    for place in range(cycle):
        halves += with_other_core(fetch_rows(out_weight, place))
    q_all, k_all, v_all, k_t, v_t, bias = gather(cycle, chunks)
    attended, att_t, inverse, weights = forward(cycle, 1, q_all, k_all, v_t, bias)
    grads = swapped(project_grad(cycle, upstream, halves))
    inputs = (q_all, k_all, v_all, k_t, att_t, inverse, weights)
    terms = swapped(backward(cycle, inputs, grads, attended))
    return tuple(finish(cycle, rows, terms, halves))


def square(cycle, rows, tensors, out_weight, upstream):
    nexts = swapped([upstream] * 3)[1:]
    chunks = swapped(list(pack(cycle, range(cycle), tensors)))
    (held_weight,) = hold((out_weight,), nexts)
    (passed,) = hold((nexts[1],), [chunks[1]])
    across = exchange_by_core(passed, (1, 2))
    own_rows = with_other_core(fetch_rows(held_weight, 0))
    q_all, k_all, v_all, k_t, v_t, bias = gather(cycle, chunks)
    (attended,), att_t, inverse, weights = forward(cycle, cycle, q_all, k_all, v_t, bias)
    own_mixed, kept, near_mixed, passed_mixed = partials(attended, own_rows, [])
    passed_mixed = exchange_by_core(passed_mixed, (2, 1))
    near_mixed = exchange_by_core(near_mixed, (2, 1))
    grads = [group_grads((upstream, *nexts, across), own_rows, [kept])]
    inputs = (q_all, k_all, v_all, k_t, att_t, inverse, weights)
    terms = swapped(list(backward(cycle, inputs, grads, [])))
    next_mixed = exchange_by_core(combine(kept, passed_mixed, terms[0]), (1, 2))
    mixed_out, word = last_sum(own_mixed, near_mixed, next_mixed)
    return (mixed_out, *finish(cycle, rows, terms, [], [word]))


def solution(mesh):
    tokens = P(("seq", "mp"), None)
    return jax.shard_map(
        local,
        mesh=mesh,
        in_specs=(tokens, tokens, tokens, P("mp", None), tokens, tokens, P(("seq", "mp"))),
        out_specs=(tokens,) * 4,
        check_vma=False,
    )
```

```python
import functools

import jax
import jax.numpy as jnp
from jax import lax
from jax.experimental import pallas as pl
from jax.experimental.pallas import tpu as pltpu
from jax.sharding import PartitionSpec as P

HEADS = 16
HEAD_DIM = 64
META = 32

score_scale = 0.125
log2_scale = 0.125 * 1.4426950408889634
cycle_offsets = (1, -1, 2, -2)
absent = -1e30
bf16 = jnp.bfloat16
f32 = jnp.float32


def dot_nn(a, b):
    return lax.dot_general(a, b, (((1,), (0,)), ((), ())), preferred_element_type=f32)


def dot_nt(a, b):
    return lax.dot_general(a, b, (((1,), (1,)), ((), ())), preferred_element_type=f32)


def vmem():
    return pl.BlockSpec(memory_space=pltpu.VMEM)


def params(mib):
    return pltpu.CompilerParams(vmem_limit_bytes=int(mib * 1024) * 1024)


def unread():
    return pl.BlockSpec(memory_space=pl.ANY)


def anywhere():
    return pl.BlockSpec(memory_space=pltpu.HBM)


def cost(micros):
    return pl.CostEstimate(flops=int(micros * 1e9), bytes_accessed=0, transcendentals=0)


def exchange(value, axis, distance):
    count = lax.axis_size(axis)
    return lax.ppermute(value, axis, [(i, i ^ distance) for i in range(count)])


def turned(distance):
    return distance ^ (((distance ^ (distance >> 1)) & 1) * 3)


def exchange_by_core(value, distances):
    count = lax.axis_size("mp")
    pairs = [
        (member * count + rank, (member ^ distances[rank % 2]) * count + rank)
        for member in range(lax.axis_size("seq"))
        for rank in range(count)
    ]
    return lax.ppermute(value, ("seq", "mp"), pairs)


def is_square():
    return lax.axis_size("seq") == 4 and lax.axis_size("mp") == 8


def distance_of(slot):
    if is_square():
        return jnp.where(lax.rem(lax.axis_index("mp"), 2) == 0, slot, turned(slot))
    return slot


def swapped(chunks):
    if is_square():
        return [chunks[0]] + [
            exchange_by_core(chunks[k], (k, turned(k))) for k in range(1, len(chunks))
        ]
    return [chunks[0]] + [exchange(chunks[k], "seq", k) for k in range(1, len(chunks))]


def group_of(cycle, member, chip):
    turn = (member + chip) % cycle
    return turned(turn) if cycle == 4 else turn


def my_place():
    rank = lax.axis_index("mp")
    return lax.axis_index("seq"), rank // 2, lax.rem(rank, 2)


def columns_at(first, width):
    return pl.ds(pl.multiple_of(first, width), width)


def pack_kernel(cycle, places, q_ref, k_ref, v_ref, adj_any, cnt_any, *refs):
    refs, (adj_ref, cnt_ref, sems, more_sems) = refs[:-4], refs[-4:]
    outs = refs
    rows, model = q_ref.shape
    width = model // cycle
    own, chip, _ = my_place()
    lists = [
        pltpu.make_async_copy(adj_any, adj_ref, more_sems.at[0]),
        pltpu.make_async_copy(cnt_any, cnt_ref, more_sems.at[1]),
    ]
    for copy in lists:
        copy.start()
    copies = []
    if width % 128 == 0:
        for place, out in zip(places, outs):
            group = group_of(cycle, lax.bitwise_xor(own, distance_of(place)), chip)
            for at, ref in enumerate((q_ref, k_ref, v_ref)):
                copies.append(
                    pltpu.make_async_copy(
                        ref.at[:, columns_at(group * width, width)],
                        out.at[at * rows:(at + 1) * rows, :],
                        sems.at[place, at],
                    )
                )
                copies[-1].start()
    for copy in lists:
        copy.wait()
    lines = lax.broadcasted_iota(jnp.int32, (META, width), 0)
    meta = jnp.where(lines == 0, 1, 0)
    for column, offset in enumerate(cycle_offsets):
        named = lax.rem(own - offset + 2 * cycle, cycle)
        meta = meta + jnp.where(
            (lines == distance_of(lax.bitwise_xor(own, named))) & (adj_ref[0, column] > 0), 1, 0
        )
    meta = jnp.where(lines == META - 1, cnt_ref[0, 0], meta).astype(f32).astype(bf16)
    for place, out in zip(places, outs):
        out[3 * rows:, :] = meta
        if width % 128:
            group = group_of(cycle, lax.bitwise_xor(own, distance_of(place)), chip)
            for other in range(cycle):
                @pl.when(group == other)
                def _():
                    for at, ref in enumerate((q_ref, k_ref, v_ref)):
                        out[at * rows:(at + 1) * rows, :] = ref[
                            :, other * width:(other + 1) * width
                        ]
    for copy in copies:
        copy.wait()


def hold_kernel(count, *refs):
    outs, sems = refs[-count - 1:-1], refs[-1]
    copies = [pltpu.make_async_copy(refs[at], outs[at], sems.at[at]) for at in range(count)]
    for copy in copies:
        copy.start()
    for copy in copies:
        copy.wait()


def hold(arrays, after):
    count = len(arrays)
    return pl.pallas_call(
        functools.partial(hold_kernel, count),
        out_shape=[jax.ShapeDtypeStruct(array.shape, array.dtype) for array in arrays],
        in_specs=[unread()] * (count + len(after)),
        out_specs=[vmem()] * count,
        scratch_shapes=[pltpu.SemaphoreType.DMA((count,))],
        compiler_params=params(2),
        cost_estimate=cost(1),
        name="hold",
    )(*arrays, *after)


def pack(cycle, places, tensors):
    rows, model = tensors[0].shape
    width = model // cycle
    return pl.pallas_call(
        functools.partial(pack_kernel, cycle, places),
        out_shape=[jax.ShapeDtypeStruct((3 * rows + META, width), bf16)] * len(places),
        in_specs=[anywhere() if width % 128 == 0 else vmem()] * 3
        + [unread()] * 2,
        out_specs=[vmem()] * len(places),
        scratch_shapes=[
            pltpu.SMEM(tensors[3].shape, jnp.int32),
            pltpu.SMEM(tensors[4].shape, jnp.int32),
            pltpu.SemaphoreType.DMA((cycle, 3)),
            pltpu.SemaphoreType.DMA((2,)),
        ],
        compiler_params=params(62),
        cost_estimate=cost(5),
        name="pack",
    )(*tensors)


def gather_kernel(cycle, *refs):
    chunks = refs[:cycle]
    q_all, k_all, v_all, k_t, v_t, bias = refs[-6:]
    rows = q_all.shape[0] // cycle
    for place in range(cycle):
        for at, part in enumerate((q_all, k_all, v_all)):
            part[place * rows:(place + 1) * rows, :] = chunks[place][at * rows:(at + 1) * rows, :]
    k_t[...] = k_all[...].astype(f32).T.astype(bf16)
    v_t[...] = v_all[...].astype(f32).T.astype(bf16)
    lines = lax.broadcasted_iota(jnp.int32, (rows, rows), 0).astype(f32)
    lists = [chunks[place][3 * rows:, :].astype(f32) for place in range(cycle)]
    for key_place in range(cycle):
        count = lists[key_place][META - 1:, :1]
        valid = lines < count
        for query_place in range(cycle):
            way = key_place ^ query_place
            times = lists[query_place][way:way + 1, :1]
            term = jnp.where(times > 0, jnp.log2(jnp.maximum(times, 1.0)), absent)
            bias[
                key_place * rows:(key_place + 1) * rows,
                query_place * rows:(query_place + 1) * rows,
            ] = jnp.where(valid, term, absent)


def gather(cycle, chunks, after=()):
    width = chunks[0].shape[1]
    rows = (chunks[0].shape[0] - META) // 3
    tokens = rows * cycle
    return pl.pallas_call(
        functools.partial(gather_kernel, cycle),
        out_shape=[jax.ShapeDtypeStruct((tokens, width), bf16)] * 3
        + [jax.ShapeDtypeStruct((width, tokens), bf16)] * 2
        + [jax.ShapeDtypeStruct((tokens, tokens), f32)],
        in_specs=[vmem()] * cycle + [unread()] * len(after),
        out_specs=[vmem()] * 6,
        compiler_params=params(8 if tokens <= 512 else 40),
        cost_estimate=cost(5),
        name="gather",
    )(*chunks, *after)


def head_tile(width):
    return min(128, width)


def only_head(tile, which):
    lanes = lax.broadcasted_iota(jnp.int32, tile.shape, 1)
    inside = (lanes >= which * HEAD_DIM) & (lanes < (which + 1) * HEAD_DIM)
    return jnp.where(inside, tile, jnp.zeros_like(tile))


def forward_kernel(query_tile, parts, q_all, k_all, v_t, bias, *refs):
    outs = refs[-2 - parts:-2]
    att_t, lse = refs[-2:]
    tokens, width = q_all.shape
    tile = head_tile(width)
    for start in range(0, tokens, query_tile):
        span = slice(start, start + query_tile)
        for head in range(width // HEAD_DIM):
            at = head * HEAD_DIM // tile * tile
            which = (head * HEAD_DIM - at) // HEAD_DIM
            scores = dot_nt(
                k_all[:, at:at + tile], only_head(q_all[span, at:at + tile], which)
            )
            scores = scores * log2_scale + bias[:, span]
            largest = jnp.max(scores, axis=0, keepdims=True)
            expo = jnp.exp2(scores - largest)
            total = jnp.sum(expo, axis=0, keepdims=True)
            lse[head:head + 1, span] = largest + jnp.log2(total)
            att_t[head * HEAD_DIM:(head + 1) * HEAD_DIM, span] = dot_nn(
                v_t[head * HEAD_DIM:(head + 1) * HEAD_DIM, :], expo.astype(bf16)
            ) * (1.0 / total)
    attended = att_t[...].T.astype(bf16)
    filled = 0
    for out in outs:
        out[...] = attended[filled:filled + out.shape[0], :]
        filled += out.shape[0]


def forward(cycle, together, q_all, k_all, v_t, bias, after=()):
    tokens, width = q_all.shape
    rows = tokens // cycle
    parts = cycle // together
    outs = pl.pallas_call(
        functools.partial(forward_kernel, min(tokens, 512), parts),
        out_shape=[jax.ShapeDtypeStruct((together * rows, width), bf16)] * parts
        + [
            jax.ShapeDtypeStruct((width, tokens), f32),
            jax.ShapeDtypeStruct((8, tokens), f32),
        ],
        in_specs=[vmem()] * 4 + [unread()] * len(after),
        out_specs=[vmem()] * (parts + 2),
        compiler_params=params(16 if tokens <= 512 else 60),
        cost_estimate=cost(3),
        name="forward",
    )(q_all, k_all, v_t, bias, *after)
    return outs[:parts], outs[parts], outs[parts + 1]


def backward_kernel(cycle, query_tile, grad_count, att_count, *refs):
    q_all, k_all, v_all, k_t, bias, att_t, lse = refs[:7]
    refs = refs[7:]
    grads = refs[:grad_count]
    attended = refs[grad_count:grad_count + att_count]
    outs = refs[-4 - cycle:-4]
    g_all, dq_t, dk, dv = refs[-4:]
    width = q_all.shape[1]
    tokens = q_all.shape[0]
    rows = tokens // cycle
    filled = 0
    for grad in grads:
        g_all[filled:filled + grad.shape[0], :] = grad[...]
        filled += grad.shape[0]
    tile = head_tile(width)
    g_t = g_all[...].astype(f32).T
    product = g_t * att_t[...].astype(bf16).astype(f32)
    for start in range(0, tokens, query_tile):
        span = slice(start, start + query_tile)
        for at in range(0, width, tile):
            dk_tile = dv_tile = None
            for which in range(tile // HEAD_DIM):
                low = at + which * HEAD_DIM
                head = low // HEAD_DIM
                delta = jnp.sum(product[low:low + HEAD_DIM, span], axis=0, keepdims=True)
                q_head = only_head(q_all[span, at:at + tile], which)
                g_head = only_head(g_all[span, at:at + tile], which)
                scores = dot_nt(k_all[:, at:at + tile], q_head)
                probs = jnp.exp2(
                    scores * log2_scale + bias[:, span] - lse[head:head + 1, span]
                )
                grad_probs = dot_nt(v_all[:, at:at + tile], g_head)
                grad_scores = (probs * (grad_probs - delta)).astype(bf16)
                dk_head = dot_nn(grad_scores, q_head)
                dv_head = dot_nn(probs.astype(bf16), g_head)
                dk_tile = dk_head if dk_tile is None else dk_tile + dk_head
                dv_tile = dv_head if dv_tile is None else dv_tile + dv_head
                dq_t[low:low + HEAD_DIM, span] = dot_nn(k_t[low:low + HEAD_DIM, :], grad_scores)
            if start == 0:
                dk[:, at:at + tile] = dk_tile
                dv[:, at:at + tile] = dv_tile
            else:
                dk[:, at:at + tile] += dk_tile
                dv[:, at:at + tile] += dv_tile
    dq = (dq_t[...] * score_scale).T.astype(bf16)
    for place in range(cycle):
        span = slice(place * rows, (place + 1) * rows)
        outs[place][:rows, :] = dq[span, :]
        outs[place][rows:2 * rows, :] = (dk[span, :] * score_scale).astype(bf16)
        outs[place][2 * rows:3 * rows, :] = dv[span, :].astype(bf16)
        if attended:
            outs[place][3 * rows:, :] = attended[place][...]


def backward(cycle, inputs, grads, attended, after):
    tokens, width = inputs[0].shape
    rows = tokens // cycle
    return pl.pallas_call(
        functools.partial(backward_kernel, cycle, min(tokens, 512), len(grads), len(attended)),
        out_shape=[jax.ShapeDtypeStruct(((4 if attended else 3) * rows, width), bf16)] * cycle,
        in_specs=[vmem()] * (len(inputs) + len(grads) + len(attended)) + [unread()] * len(after),
        out_specs=[vmem()] * cycle,
        scratch_shapes=[
            pltpu.VMEM((tokens, width), bf16),
            pltpu.VMEM((width, tokens), f32),
            pltpu.VMEM((tokens, width), f32),
            pltpu.VMEM((tokens, width), f32),
        ],
        compiler_params=params(16 if tokens <= 512 else 60),
        cost_estimate=cost(3),
        name="backward",
    )(*inputs, *grads, *attended, *after)


def fetch_rows(out_weight, place):
    cycle, count = lax.axis_size("seq"), lax.axis_size("mp")
    pairs = []
    for member in range(cycle):
        for rank in range(count):
            owner = 2 * group_of(cycle, member ^ place, rank // 2) + rank % 2
            pairs.append((member * count + owner, member * count + rank))
    return lax.ppermute(out_weight, ("seq", "mp"), pairs)


def with_other_core(half):
    return [half, exchange(half, "mp", 1)]


def rows_in_order(mine, others, core):
    first = core == 0
    mine, other = mine[...], jnp.concatenate([ref[...] for ref in others], axis=0)
    return jnp.concatenate([jnp.where(first, mine, other), jnp.where(first, other, mine)], axis=0)


def both_halves(halves, core):
    mine, other = halves[0][...], halves[1][...]
    first = core == 0
    return jnp.concatenate([jnp.where(first, mine, other), jnp.where(first, other, mine)], axis=0)


def group_kernel(count, *refs):
    ups, out = refs[:count], refs[-1]
    _, _, core = my_place()
    weight = rows_in_order(refs[count], refs[count + 1:count + 2], core)
    out[...] = dot_nt(jnp.concatenate([ref[...] for ref in ups], axis=0), weight).astype(bf16)


def group_grads(upstreams, pieces, after):
    rows, width = upstreams[0].shape[0], 2 * pieces[0].shape[0]
    return pl.pallas_call(
        functools.partial(group_kernel, len(upstreams)),
        out_shape=jax.ShapeDtypeStruct((len(upstreams) * rows, width), bf16),
        in_specs=[vmem()] * (len(upstreams) + 2) + [unread()] * len(after),
        out_specs=vmem(),
        compiler_params=params(8),
        cost_estimate=cost(1),
        name="group_grads",
    )(*upstreams, *pieces, *after)


def partial_kernel(att_ref, mine, *refs):
    own, kept, sent = refs[-3:]
    rows = own.shape[0]
    _, _, core = my_place()
    weight = rows_in_order(mine, refs[:1], core)
    product = dot_nn(att_ref[...], weight)
    own[...] = product[:rows, :]
    kept[...] = product[rows:2 * rows, :]
    sent[...] = product[2 * rows:, :].astype(bf16)


def partials(attended, pieces, after):
    rows, model = attended.shape[0] // 4, pieces[0].shape[1]
    return pl.pallas_call(
        partial_kernel,
        out_shape=[jax.ShapeDtypeStruct((rows, model), f32)] * 2
        + [jax.ShapeDtypeStruct((2 * rows, model), bf16)],
        in_specs=[vmem()] * 3 + [unread()] * len(after),
        out_specs=[vmem()] * 3,
        compiler_params=params(12),
        cost_estimate=cost(1),
        name="partials",
    )(attended, *pieces, *after)


def combine_kernel(own, kept, landed, total, *sent):
    rows = own.shape[0]
    total[...] = own[...] + landed[:rows, :].astype(f32)
    part = rows // len(sent)
    for at, out in enumerate(sent):
        span = slice(at * part, (at + 1) * part)
        out[...] = (
            kept[span, :] + landed[rows + at * part:rows + (at + 1) * part, :].astype(f32)
        ).astype(bf16)


def combine(own, kept, landed):
    return pl.pallas_call(
        combine_kernel,
        out_shape=[jax.ShapeDtypeStruct(own.shape, f32)]
        + [jax.ShapeDtypeStruct((own.shape[0] // 2, own.shape[1]), bf16)] * 2,
        in_specs=[vmem()] * 3,
        out_specs=[vmem()] * 3,
        compiler_params=params(8),
        cost_estimate=cost(1),
        name="combine",
    )(own, kept, landed)


def grad_kernel(cycle, up_ref, *refs):
    _, _, core = my_place()
    outs = refs[2 * cycle:]
    for place in range(cycle):
        rows = both_halves(refs[2 * place:2 * place + 2], core)
        outs[place][...] = dot_nt(up_ref[...], rows).astype(bf16)


def project_grad(cycle, upstream, halves):
    rows, model = upstream.shape
    return pl.pallas_call(
        functools.partial(grad_kernel, cycle),
        out_shape=[jax.ShapeDtypeStruct((rows, model // cycle), bf16)] * cycle,
        in_specs=[vmem()] * (1 + 2 * cycle),
        out_specs=[vmem()] * cycle,
        compiler_params=params(8),
        name="project_grad",
    )(upstream, *halves)


def place_columns(chunks, outs, sems):
    cycle = len(chunks)
    rows, model = outs[0].shape
    width = model // cycle
    own, chip, _ = my_place()
    copies = []
    for place in range(cycle):
        group = group_of(cycle, lax.bitwise_xor(own, distance_of(place)), chip)
        if width % 128 == 0:
            for at, out in enumerate(outs):
                copies.append(
                    pltpu.make_async_copy(
                        chunks[place].at[at * rows:(at + 1) * rows, :],
                        out.at[:, columns_at(group * width, width)],
                        sems.at[place, at],
                    )
                )
                copies[-1].start()
        else:
            for other in range(cycle):
                @pl.when(group == other)
                def _():
                    for at, out in enumerate(outs):
                        out[:, other * width:(other + 1) * width] = chunks[place][
                            at * rows:(at + 1) * rows, :
                        ]
    return copies


def finish_kernel(cycle, *refs):
    chunks = refs[:cycle]
    outs, word = refs[-5:-2], refs[-2]
    word[...] = jnp.zeros(word.shape, word.dtype)
    rows = outs[0].shape[0]
    copies = place_columns(chunks, outs, refs[-1])
    if len(refs) > cycle + 5:
        halves = refs[cycle:3 * cycle]
        _, _, core = my_place()
        total = None
        for place in range(cycle):
            weight = both_halves(halves[2 * place:2 * place + 2], core)
            term = dot_nn(chunks[place][3 * rows:, :], weight)
            total = term if total is None else total + term
        refs[-6][...] = total.astype(bf16)
    for copy in copies:
        copy.wait()


def finish(cycle, rows, chunks, others):
    model = chunks[0].shape[1] * cycle
    aligned = model // cycle % 128 == 0
    return pl.pallas_call(
        functools.partial(finish_kernel, cycle),
        out_shape=[jax.ShapeDtypeStruct((rows, model), bf16)] * (4 if others else 3)
        + [jax.ShapeDtypeStruct((16, 128), bf16)],
        in_specs=[vmem()] * (cycle + len(others)),
        out_specs=[vmem()] * (1 if others else 0)
        + [anywhere() if aligned else vmem()] * 3
        + [vmem()],
        scratch_shapes=[pltpu.SemaphoreType.DMA((cycle, 3))],
        compiler_params=params(8),
        name="finish",
    )(*chunks, *others)


def sum_kernel(half, own, landed, unused, out, total, sem):
    part = total.shape[0]
    span = slice(half * part, (half + 1) * part)
    total[...] = (own[span, :] + landed[...].astype(f32)).astype(bf16)
    copy = pltpu.make_async_copy(total, out.at[span, :], sem)
    copy.start()
    copy.wait()


def half_sum(half, own, landed, before):
    return pl.pallas_call(
        functools.partial(sum_kernel, half),
        out_shape=jax.ShapeDtypeStruct(own.shape, bf16),
        in_specs=[vmem()] * 2 + [anywhere() if half else unread()],
        out_specs=anywhere(),
        scratch_shapes=[pltpu.VMEM(landed.shape, bf16), pltpu.SemaphoreType.DMA],
        input_output_aliases={2: 0} if half else {},
        compiler_params=params(8),
        name="half_sum",
    )(own, landed, before)


def local(queries, keys, values, out_weight, upstream, adjacency, counts):
    cycle = lax.axis_size("seq")
    rows = queries.shape[0]
    tensors = (queries, keys, values, adjacency, counts.reshape(1, 1))
    if is_square():
        return square(cycle, rows, tensors, out_weight, upstream)
    chunks = swapped(list(pack(cycle, range(cycle), tensors)))
    halves = []
    for place in range(cycle):
        halves += with_other_core(fetch_rows(out_weight, place))
    q_all, k_all, v_all, k_t, v_t, bias = gather(cycle, chunks)
    attended, att_t, lse = forward(cycle, 1, q_all, k_all, v_t, bias)
    grads = swapped(project_grad(cycle, upstream, halves))
    inputs = (q_all, k_all, v_all, k_t, bias, att_t, lse)
    terms = swapped(backward(cycle, inputs, grads, attended, []))
    return tuple(finish(cycle, rows, terms, halves)[:4])


def square(cycle, rows, tensors, out_weight, upstream):
    nexts = swapped([upstream] * 3)[1:]
    chunks = swapped(list(pack(cycle, range(cycle), tensors)))
    held_weight, passed = hold((out_weight, nexts[1]), [nexts[0]])
    across = exchange_by_core(passed, (1, 2))
    own_rows = with_other_core(fetch_rows(held_weight, 0))
    q_all, k_all, v_all, k_t, v_t, bias = gather(cycle, chunks)
    (attended,), att_t, lse = forward(cycle, cycle, q_all, k_all, v_t, bias, [across])
    own_mixed, kept, sent = partials(attended, own_rows, [])
    landed = exchange_by_core(sent, (2, 1))
    grads = [group_grads((upstream, *nexts, across), own_rows, [kept])]
    inputs = (q_all, k_all, v_all, k_t, bias, att_t, lse)
    terms = swapped(list(backward(cycle, inputs, grads, [], [])))
    own_mixed, *next_mixed = combine(own_mixed, kept, landed)
    next_mixed = [exchange_by_core(part, (1, 2)) for part in next_mixed]
    *grads, word = finish(cycle, rows, terms, [])
    mixed_out = half_sum(0, own_mixed, next_mixed[0], word)
    mixed_out = half_sum(1, own_mixed, next_mixed[1], mixed_out)
    return (mixed_out, *grads)


def solution(mesh):
    tokens = P(("seq", "mp"), None)
    return jax.shard_map(
        local,
        mesh=mesh,
        in_specs=(tokens, tokens, tokens, P("mp", None), tokens, tokens, P(("seq", "mp"))),
        out_specs=(tokens,) * 4,
        check_vma=False,
    )
```
